32 devices in a mesh: dp: 4 (over z), row: 2 (over core), col: 4 (over y, x).
Axes of the slice: x: 2, y: 2, z: 4, core: 2. Of those that a mesh axis runs over, the one named last changes fastest.
Arguments:
- tokens: bfloat16 [6144, 2560], P(('dp', 'row'), 'col'), may hold values from -6 to 6
- cotangent: bfloat16 [6144, 2560], P(('dp', 'row'), 'col'), may hold values from -6 to 6
- rec_in: bfloat16 [2, 2560, 2560], P(None, 'col', 'row'), may hold values from -0.125 to 0.125
- rec_out: bfloat16 [2560, 2560], P('row', 'col'), may hold values from -0.5 to 0.5
- gates: bfloat16 [2, 10, 256, 256], P(None, 'row'), may hold values from -0.375 to 0.375
- gate_bias: float32 [2, 2560], P(None, 'row'), may hold values from -3 to 3
- decay: float32 [2560], P('row')
- conv_w: float32 [4, 2560], P(None, 'row'), may hold values from -3 to 3
- conv_b: float32 [2560], P('row'), may hold values from -3 to 3
- gains: float32 [2, 2560], P(None, 'col'), may hold values from 0.5 to 1.5
- mlp_in: bfloat16 [2, 2560, 7680], P(None, 'col', 'row'), may hold values from -0.125 to 0.125
- mlp_out: bfloat16 [7680, 2560], P('row', 'col'), may hold values from -0.125 to 0.125
- lengths: int32 [16], replicated, may hold values from 1 to 1024, as said below
- order: int32 [16], replicated, may hold values from 0 to 15, as said below
Outputs:
- result: bfloat16 [6144, 2560], P(('dp', 'row'), 'col')
- grad_input: bfloat16 [6144, 2560], P(('dp', 'row'), 'col')
- grad_rec_in: float32 [2, 2560, 2560], P(None, ('col', 'dp'), 'row')
- grad_rec_out: float32 [2560, 2560], P('row', ('col', 'dp'))
- grad_gates: float32 [2, 10, 256, 256], P(None, 'row')
- grad_gate_bias: float32 [2, 2560], P(None, 'row')
- grad_decay: float32 [2560], P('row')
- grad_conv_w: float32 [4, 2560], P(None, 'row')
- grad_conv_b: float32 [2560], P('row')
- grad_gains: float32 [2, 2560], P(None, 'col')
- grad_mlp_in: float32 [2, 2560, 7680], P(None, ('col', 'dp'), 'row')
- grad_mlp_out: float32 [7680, 2560], P('row', ('col', 'dp'))
- stats: float32 [4], replicated
The draws below stay inside these ranges and needn't reach their ends.
Inputs may be any that keep to these rules, and one draw needn't show every extreme that they name: Group g takes the sequences order[4 * g] to order[4 g + 3] in that order; their lengths add up to exactly 1536 in every group, and every group has one sequence of 1024 tokens. `order`: A permutation of the sequence numbers.
All inputs are finite; a program needn't handle non-finite values.
Results may differ from the reference program's by a relative error of at most 0.013.
Values may be sent and summed in bfloat16 or wider, within the bound.
A program may use at most 320 MiB of HBM per device.

```python
import jax
import jax.numpy as jnp
from jax import lax

NB = 10
BW = 256
D = 2560
FF = 7680
CW = 4
TOK_GRP = 1536
LMAX = 1024
NSEQ = 16
TOKENS = 6144
N_DP = 4


def seq_layout(key):
    quarter = TOK_GRP // 4
    groups = NSEQ // 4
    first_key, second_key, third_key = jax.random.split(key, 3)
    heads = jax.random.randint(first_key, (groups,), quarter // 3 + 1, quarter)
    remain = TOK_GRP - LMAX - heads
    middle = jax.random.randint(second_key, (groups,), 1, remain)
    longest = jnp.full((groups,), LMAX, jnp.int32)
    group_lengths = jnp.stack([heads, longest, middle, remain - middle], axis=1).reshape(-1).astype(jnp.int32)
    order = jax.random.permutation(third_key, NSEQ).astype(jnp.int32)
    lengths = jnp.zeros((NSEQ,), jnp.int32).at[order].set(group_lengths)
    return (lengths, order)


def draw_lengths(key, part):
    lengths, order = seq_layout(key)
    return lengths


def draw_order(key, part):
    lengths, order = seq_layout(key)
    return order


def draw_decay(key, part):
    key = jax.random.fold_in(key, 7)
    values = jax.random.uniform(key, (D,), jnp.float32, -9.0, -3.5)
    return values


def block_levels(own_key, extent, cuts, low, high):
    loudness = 1.0
    for position, shards_of in cuts:
        draws = jax.random.uniform(jax.random.fold_in(jax.random.fold_in(own_key, 6), position), (shards_of,), jnp.float32, low / len(cuts), high / len(cuts))
        loudness = loudness * jnp.repeat(jnp.exp(draws), extent[position] // shards_of).reshape((-1,) + (1,) * (len(extent) - 1 - position))
    return loudness


def centred(key, extent, spread, reach, cuts=(), kind=jnp.bfloat16):
    array = jax.random.normal(key, extent, jnp.float32) * spread
    if len(cuts) > 0:
        array = block_levels(key, extent, cuts, -0.22, 0.18) * array
    return jnp.clip(array, min=-reach, max=reach).astype(kind)


def setup_inputs(seed: int = 0) -> dict:
    seeds = jax.random.split(jax.random.key(seed), 15)
    return {
        "tokens": centred(seeds[0], (TOKENS, D), 1.0, 6.0, ((0, 8), (1, 4))),
        "cotangent": centred(seeds[1], (TOKENS, D), 1.0, 6.0, ((0, 8), (1, 4))),
        "rec_in": centred(seeds[2], (2, D, D), D ** -0.5, 0.125, ((1, 4), (2, 2))),
        "rec_out": centred(seeds[3], (D, D), (D // 16) ** -0.5, 0.5, ((0, 2), (1, 4))),
        "gates": centred(seeds[4], (2, NB, BW, BW), BW ** -0.5, 0.375, ((1, 2),)),
        "gate_bias": centred(seeds[5], (2, D), 0.5, 3.0, ((1, 2),), jnp.float32),
        "decay": draw_decay(jax.random.fold_in(seeds[14], 71), 0),
        "conv_w": centred(seeds[7], (CW, D), 0.5, 3.0, ((1, 2),), jnp.float32),
        "conv_b": centred(seeds[8], (D,), 0.5, 3.0, ((0, 2),), jnp.float32),
        "gains": jnp.clip(1.0 + 0.1 * jax.random.normal(seeds[9], (2, D), jnp.float32), 0.5, 1.5),
        "mlp_in": centred(seeds[10], (2, D, FF), D ** -0.5, 0.125, ((1, 4), (2, 2))),
        "mlp_out": centred(seeds[11], (FF, D), (FF // 4) ** -0.5, 0.125, ((0, 2), (1, 4))),
        "lengths": draw_lengths(jax.random.fold_in(seeds[14], 71), 0),
        "order": draw_order(jax.random.fold_in(seeds[14], 71), 0),
    }


epsilon = 1e-06
highest = lax.Precision.HIGHEST

@jax.custom_vjp
def low(v):
    return lax.optimization_barrier(v.astype(jnp.bfloat16)).astype(jnp.float32)

@jax.custom_vjp
def low_back(v):
    return v

def low_keep(v):
    return (low(v), None)

def low_pass(kept, grad):
    return (grad,)

def back_keep(v):
    return (v, None)

def back_low(kept, grad):
    return (low(grad),)
low.defvjp(low_keep, low_pass)
low_back.defvjp(back_keep, back_low)

def compose(first, second):
    return (first[0] * second[0], second[0] * first[1] + second[1])

def matmul_hi(left, right):
    return jnp.dot(left, right, precision=highest)

def seq_tables(lengths, order):
    number = lengths.shape[0]
    slots = jnp.arange(number, dtype=jnp.int32)
    chosen = (order[:, None] == slots[None, :]).astype(jnp.int32)
    group_lengths = lax.optimization_barrier(jnp.sum(chosen * lengths[None, :], axis=1)).astype(jnp.int32)
    input_offsets = (jnp.cumsum(lengths) - lengths).astype(jnp.int32)
    group_offsets = (jnp.cumsum(group_lengths) - group_lengths).astype(jnp.int32)
    input_starts = lax.optimization_barrier(jnp.sum(chosen * input_offsets[None, :], axis=1)).astype(jnp.int32)
    inverse = lax.optimization_barrier(jnp.sum(chosen * slots[:, None], axis=0)).astype(jnp.int32)
    return (slots, input_offsets, group_offsets, input_starts, inverse)

def locate(rows, tables):
    slots, input_offsets, group_offsets, input_starts, inverse = tables
    which = lax.optimization_barrier(jnp.sum((rows[:, None] >= group_offsets[None, :]).astype(jnp.int32), axis=1)) - 1
    match = (which[:, None] == slots[None, :]).astype(jnp.int32)
    places = (rows - lax.optimization_barrier(jnp.sum(match * group_offsets[None, :], axis=1))).astype(jnp.int32)
    source = (lax.optimization_barrier(jnp.sum(match * input_starts[None, :], axis=1)) + places).astype(jnp.int32)
    return (source, places)

def lru_coeffs(pre, inputs, decay, reset):
    input_gate = jax.nn.sigmoid(pre[0])
    rate_gate = jax.nn.sigmoid(pre[1])
    log_decay = -8.0 * rate_gate * jax.nn.softplus(decay)
    decay_factor = jnp.where(reset, 0.0, jnp.exp(log_decay))
    scaling = jnp.where(reset, 1.0, jnp.sqrt(-jnp.expm1(2.0 * log_decay)))
    return (decay_factor, inputs * input_gate * scaling)

def forward(params, tokens, places):
    rec_in, rec_out, gates, gate_bias, decay, conv_w, conv_b, gains, mlp_in, mlp_out = params
    length = tokens.shape[0]
    width = tokens.shape[1]
    taps = conv_w.shape[0]
    blocks = gates.shape[1]
    block_width = gates.shape[2]
    scale_one = lax.rsqrt(lax.optimization_barrier(jnp.mean(tokens * tokens, axis=-1, keepdims=True)) + epsilon)
    normed_one = low(tokens * scale_one * gains[0])
    x_branch = low_back(matmul_hi(normed_one, rec_in[0]))
    y_branch = low_back(matmul_hi(normed_one, rec_in[1]))
    padded = jnp.concatenate([jnp.zeros((taps - 1, width), tokens.dtype), x_branch], axis=0)
    mixed = conv_b[None, :] + jnp.zeros_like(x_branch)
    for tap_index in range(taps):
        lagged = padded[taps - 1 - tap_index:taps - 1 - tap_index + length]
        mixed = mixed + jnp.where((places >= tap_index)[:, None], conv_w[tap_index][None, :] * lagged, 0.0)
    conv_out = low(mixed)
    pre = jnp.einsum('tnb,jnbc->jtnc', conv_out.reshape(length, blocks, block_width), gates, precision=highest).reshape(2, length, width) + gate_bias[:, None, :]
    pre = low_back(pre)
    reset = (places == 0)[:, None]
    decay_factor, inject = lru_coeffs(pre, conv_out, decay, reset)
    _, state = lax.associative_scan(compose, (decay_factor, inject))
    branch = low(state * jax.nn.gelu(y_branch, approximate=True))
    out_one = low_back(matmul_hi(branch, rec_out))
    resid = tokens + out_one
    scale_two = lax.rsqrt(lax.optimization_barrier(jnp.mean(resid * resid, axis=-1, keepdims=True)) + epsilon)
    normed_two = low(resid * scale_two * gains[1])
    gate_part = low_back(matmul_hi(normed_two, mlp_in[0]))
    up_part = low_back(matmul_hi(normed_two, mlp_in[1]))
    hidden = low(jax.nn.gelu(gate_part, approximate=True) * up_part)
    out_two = low_back(matmul_hi(hidden, mlp_out))
    sums = jnp.stack([jnp.sum(tokens * tokens), jnp.sum(out_one * out_one), jnp.sum(resid * resid), jnp.sum(out_two * out_two)])
    return (resid + out_two, sums)

def reference(tokens, cotangent, rec_in, rec_out, gates, gate_bias, decay, conv_w, conv_b, gains, mlp_in, mlp_out, lengths, order):
    width = tokens.shape[1]
    tables = seq_tables(lengths, order)
    rows = jnp.arange(TOKENS, dtype=jnp.int32)
    source, places = locate(rows, tables)
    grouped = jnp.take(tokens, source, axis=0).astype(jnp.float32).reshape(N_DP, TOK_GRP, width)
    upstream = jnp.take(cotangent, source, axis=0).astype(jnp.float32).reshape(N_DP, TOK_GRP, width)
    group_places = places.reshape(N_DP, TOK_GRP)
    params = tuple((item.astype(jnp.float32) for item in (rec_in, rec_out, gates, gate_bias, decay, conv_w, conv_b, gains, mlp_in, mlp_out)))

    def whole(params, grouped):

        def step(carry, item):
            output, sums = jax.checkpoint(forward)(params, item[0], item[1])
            return (carry + sums, output)
        sums, output = lax.scan(step, jnp.zeros((4,), jnp.float32), (grouped, group_places))
        return (output, sums)
    output, backward, sums = jax.vjp(whole, params, grouped, has_aux=True)
    grad_params, grad_grouped = backward(upstream)
    flat = output.reshape(TOKENS, width)
    result = jnp.zeros_like(flat).at[source].set(flat)
    grad_flat = grad_grouped.reshape(TOKENS, width)
    grad_input = jnp.zeros_like(grad_flat).at[source].set(grad_flat)
    stats = jnp.sqrt(sums / (TOKENS * width))
    return (result.astype(jnp.bfloat16), grad_input.astype(jnp.bfloat16), grad_params[0], grad_params[1], grad_params[2], grad_params[3], grad_params[4], grad_params[5], grad_params[6], grad_params[7], grad_params[8], grad_params[9], stats)
```

```python
import functools

import jax
import jax.numpy as jnp
from jax import lax
from jax.experimental import pallas as pl
from jax.experimental.pallas import tpu as pltpu
from jax.sharding import PartitionSpec as P

epsilon = 1e-06
LANES = 128
MESH = pl.DeviceIdType.MESH
low = jnp.bfloat16
f32 = jnp.float32


def gelu(values):
    return jax.nn.gelu(values, approximate=True)


def window_tile(col, tiles, n_col, wide):
    spare = wide * n_col - tiles
    return col * wide - jnp.maximum(col - (n_col - 1 - spare), 0)


def spare_window(col, tiles, n_col, wide):
    spare = wide * n_col - tiles
    return col > n_col - 1 - spare


def weights_kernel(
    geo, rec_in, rec_out, mlp_in, mlp_out, w_rec, w_out, w_in, w_down, send, recv, local
):
    n_col, part, bw, tiles, wide = geo
    col = lax.axis_index("col")
    barrier = pltpu.get_barrier_semaphore()
    for k in range(1, n_col):
        pl.semaphore_signal(
            barrier, inc=1, device_id={"col": lax.rem(col + k, n_col)}, device_id_type=MESH
        )
    pl.semaphore_wait(barrier, n_col - 1)
    shared = n_col * bw
    span = wide * LANES
    here = pl.ds(pl.multiple_of(col * part, LANES), part)

    def pieces(dest):
        blk = pl.multiple_of(dest * bw, LANES)
        tile = pl.multiple_of(shared + lax.div(dest, 2) * LANES, LANES)
        win = pl.multiple_of(window_tile(dest, tiles, n_col, wide) * LANES, LANES)
        return [
            (mlp_in.at[:, :, pl.ds(win, span)], w_in.at[:, here, :]),
            (mlp_out.at[pl.ds(win, span), :], w_down.at[:, here]),
            (rec_in.at[0, :, pl.ds(blk, bw)], w_rec.at[here, pl.ds(0, bw)]),
            (rec_in.at[0, :, pl.ds(shared, bw)], w_rec.at[here, pl.ds(bw, bw)]),
            (rec_in.at[1, :, pl.ds(blk, bw)], w_rec.at[here, pl.ds(2 * bw, bw)]),
            (rec_in.at[1, :, pl.ds(tile, LANES)], w_rec.at[here, pl.ds(3 * bw, LANES)]),
            (rec_out.at[pl.ds(blk, bw), :], w_out.at[pl.ds(0, bw), here]),
            (rec_out.at[pl.ds(tile, LANES), :], w_out.at[pl.ds(bw, LANES), here]),
        ]

    copies = []
    for k in range(1, n_col):
        dest = lax.rem(col + k, n_col)
        for i, (src, dst) in enumerate(pieces(dest)):
            copy = pltpu.make_async_remote_copy(
                src_ref=src,
                dst_ref=dst,
                send_sem=send.at[k - 1, i],
                recv_sem=recv.at[k - 1, i],
                device_id={"col": dest},
                device_id_type=MESH,
            )
            copy.start()
            copies.append(copy)
    for i, (src, dst) in enumerate(pieces(col)):
        copy = pltpu.make_async_copy(src, dst, local.at[i])
        copy.start()
        copies.append(copy)
    for copy in copies:
        copy.wait()


def gather_weights(rec_in, rec_out, mlp_in, mlp_out, n_col, bw, wide):
    part = rec_in.shape[1]
    width = part * n_col
    tiles = mlp_out.shape[0] // LANES
    span = wide * LANES
    geo = (n_col, part, bw, tiles, wide)
    anywhere = pl.BlockSpec(memory_space=pl.ANY)
    return pl.pallas_call(
        functools.partial(weights_kernel, geo),
        out_shape=(
            jax.ShapeDtypeStruct((width, 3 * bw + LANES), low),
            jax.ShapeDtypeStruct((bw + LANES, width), low),
            jax.ShapeDtypeStruct((2, width, span), low),
            jax.ShapeDtypeStruct((span, width), low),
        ),
        in_specs=[anywhere] * 4,
        out_specs=(anywhere,) * 4,
        scratch_shapes=[
            pltpu.SemaphoreType.DMA((n_col - 1, 8)),
            pltpu.SemaphoreType.DMA((n_col - 1, 8)),
            pltpu.SemaphoreType.DMA((8,)),
        ],
        compiler_params=pltpu.CompilerParams(collective_id=1, has_side_effects=True),
        name="weights",
    )(rec_in, rec_out, mlp_in, mlp_out)


def scan_kernel(reverse, a_ref, u_ref, h_ref, p_ref, carry):
    step = pl.program_id(0)
    rows = a_ref.shape[0]

    @pl.when(step == 0)
    def _():
        carry[0:1] = jnp.zeros_like(carry[0:1])
        carry[1:2] = jnp.ones_like(carry[1:2])

    for lane in range(a_ref.shape[1] // LANES):
        at = slice(lane * LANES, (lane + 1) * LANES)
        a = a_ref[:, at]
        u = u_ref[:, at]
        index = lax.broadcasted_iota(jnp.int32, a.shape, 0)
        by = 1
        while by < rows:
            turn = rows - by if reverse else by
            inside = index < rows - by if reverse else index >= by
            a_far = jnp.where(inside, pltpu.roll(a, turn, 0), 1.0)
            u_far = jnp.where(inside, pltpu.roll(u, turn, 0), 0.0)
            u = u + a * u_far
            a = a * a_far
            by *= 2
        h = u + a * carry[0:1, at]
        p = a * carry[1:2, at]
        h_ref[:, at] = h
        p_ref[:, at] = p
        edge = 0 if reverse else rows - 1
        carry[0:1, at] = h[edge : edge + 1]
        carry[1:2, at] = p[edge : edge + 1]


def scan_rows(decay, inject, reverse, rows=256):
    length, channels = decay.shape
    steps = length // rows
    block = pl.BlockSpec((rows, channels), lambda i: (steps - 1 - i if reverse else i, 0))
    shape = jax.ShapeDtypeStruct(decay.shape, f32)
    return pl.pallas_call(
        functools.partial(scan_kernel, reverse),
        grid=(steps,),
        out_shape=(shape, shape),
        in_specs=[block, block],
        out_specs=(block, block),
        scratch_shapes=[pltpu.VMEM((8, channels), f32)],
        name="scan_back" if reverse else "scan",
    )(decay, inject)


def outer_kernel(n_dp, left_ref, right_ref, out_ref):
    total = lax.dot_general(
        left_ref[...], right_ref[...], (((0,), (0,)), ((), ())), preferred_element_type=f32
    )
    rows = total.shape[0] // n_dp
    for k in range(n_dp):
        out_ref[k, 0] = total[k * rows : (k + 1) * rows].astype(out_ref.dtype)


def outer(left, right, n_dp, n_col, columns):
    length, width = left.shape
    part = width // n_col
    count = right.shape[1]
    return pl.pallas_call(
        functools.partial(outer_kernel, n_dp),
        grid=(n_col, count // columns),
        out_shape=jax.ShapeDtypeStruct((n_dp, n_col, part // n_dp, count), low),
        in_specs=[
            pl.BlockSpec((length, part), lambda i, j: (0, i)),
            pl.BlockSpec((length, columns), lambda i, j: (0, j)),
        ],
        out_specs=pl.BlockSpec((n_dp, 1, part // n_dp, columns), lambda i, j: (0, i, 0, j)),
        compiler_params=pltpu.CompilerParams(vmem_limit_bytes=48 * 1024 * 1024),
        cost_estimate=pl.CostEstimate(
            flops=2 * length * width * count,
            bytes_accessed=2 * (length * width + length * count + width * count),
            transcendentals=0,
        ),
        name="outer",
    )(left, right)


def deal_back(grads, n_col):
    summed = lax.psum_scatter(grads, "dp", scatter_dimension=0, tiled=False)
    return lax.all_to_all(summed, "col", 0, 0, tiled=False)


def gather_rows(local):
    return lax.all_gather(local, ("row", "col"), axis=0, tiled=True)


def scatter_rows(partial):
    return lax.psum_scatter(
        partial.astype(low), ("row", "col"), scatter_dimension=0, tiled=True
    ).astype(f32)


def dot(a, b, dims=((1,), (0,))):
    return lax.dot_general(a, b, (dims, ((), ())), preferred_element_type=f32)


def neighbour(x, axis, by):
    length = lax.axis_size(axis)
    pairs = [(i, i + by) for i in range(length) if 0 <= i + by < length]
    return lax.ppermute(x, axis, pairs)


def places_of(rows, lengths):
    ends = jnp.cumsum(lengths)
    starts = ends - lengths
    inside = (rows[:, None] >= starts[None, :]) & (rows[:, None] < ends[None, :])
    return rows - jnp.sum(jnp.where(inside, starts[None, :], 0), axis=1)


def lru_coeffs(pre_in, pre_rate, inputs, decay, reset):
    input_gate = jax.nn.sigmoid(pre_in)
    rate_gate = jax.nn.sigmoid(pre_rate)
    log_decay = -8.0 * rate_gate * jax.nn.softplus(decay)
    decay_factor = jnp.where(reset, 0.0, jnp.exp(log_decay))
    scaling = jnp.where(reset, 1.0, jnp.sqrt(-jnp.expm1(2.0 * log_decay)))
    return (decay_factor, inputs * input_gate * scaling)


def body(
    tokens,
    cotangent,
    rec_in,
    rec_out,
    gates,
    gate_bias,
    decay,
    conv_w,
    conv_b,
    gains,
    mlp_in,
    mlp_out,
    lengths,
    order,
):
    n_dp, n_row, n_col = (lax.axis_size(a) for a in ("dp", "row", "col"))
    dp, row, col = (lax.axis_index(a) for a in ("dp", "row", "col"))
    given, part = tokens.shape
    own = given // n_col
    group = given * n_row
    width = part * n_col
    taps = conv_w.shape[0]
    blocks, bw = gates.shape[1], gates.shape[2]
    half = rec_out.shape[0]
    hidden_half = mlp_out.shape[0]
    tiles = hidden_half // LANES
    wide = -(-tiles // n_col)
    span = wide * LANES
    shared = n_col * bw
    chans = bw + LANES

    w_rec, w_out, w_in, w_down = gather_weights(rec_in, rec_out, mlp_in, mlp_out, n_col, bw, wide)
    w_x, w_y = w_rec[:, : 2 * bw], w_rec[:, 2 * bw :]

    def own_rows(x):
        dealt = lax.all_to_all(x.reshape(n_col, own, part), "col", 0, 0)
        return dealt.transpose(1, 0, 2).reshape(own, width)

    def home_rows(x):
        dealt = lax.all_to_all(x.reshape(own, n_col, part).transpose(1, 0, 2), "col", 0, 0)
        return dealt.reshape(given, part)

    tile_at = shared + (col // 2) * LANES
    tile_owner = col % 2 == 0

    def own_channels(x):
        blk = lax.dynamic_slice_in_dim(x, col * bw, bw, axis=-1)
        tile = lax.dynamic_slice_in_dim(x, tile_at, LANES, axis=-1)
        return jnp.concatenate([blk, tile], axis=-1)

    def block_channels(x):
        blk = lax.dynamic_slice_in_dim(x, col * bw, bw, axis=-1)
        return jnp.concatenate([blk, x[..., shared:]], axis=-1)

    bias = own_channels(gate_bias)
    decay_o = own_channels(decay)
    conv_w_c = block_channels(conv_w)
    conv_b_c = block_channels(conv_b)
    conv_w_o = own_channels(conv_w)
    gates_blk = lax.dynamic_index_in_dim(gates, col, axis=1, keepdims=False)
    gates_five = gates[:, n_col]
    gates_tile = lax.dynamic_slice_in_dim(gates_five, (col // 2) * LANES, LANES, axis=2)
    gates_rows = lax.dynamic_slice_in_dim(gates_five, (col // 2) * LANES, LANES, axis=1)
    channel_ok = (jnp.arange(chans) < bw) | tile_owner
    hidden_ok = (jnp.arange(span) >= LANES) | ~spare_window(col, tiles, n_col, wide)

    base = dp * group
    places_ext = places_of(base + jnp.arange(group + taps - 1, dtype=jnp.int32), lengths)
    places = places_ext[:group]
    reset = (places == 0)[:, None]
    gains_all = lax.all_gather(gains, "col", axis=1, tiled=True)

    inputs = own_rows(tokens).astype(f32)
    upstream_low = own_rows(cotangent)
    upstream = upstream_low.astype(f32)
    sumsq_one = jnp.sum(inputs * inputs, axis=-1, keepdims=True)
    scale_one = lax.rsqrt(sumsq_one / width + epsilon)
    normed_one = (inputs * scale_one * gains_all[0]).astype(low)
    n1 = gather_rows(normed_one)
    n1_before = neighbour(n1[group - 16 :], "dp", 1)
    x_branch = dot(n1, w_x)
    y_branch = dot(n1, w_y)
    x_before = dot(n1_before, w_x)[16 - (taps - 1) :]
    x_ext = jnp.concatenate([x_before, x_branch], axis=0)
    mixed = conv_b_c[None, :] + jnp.zeros_like(x_branch)
    for t in range(taps):
        lagged = x_ext[taps - 1 - t : taps - 1 - t + group]
        mixed = mixed + jnp.where((places >= t)[:, None], conv_w_c[t][None, :] * lagged, 0.0)
    conv_low = mixed.astype(low)
    conv_blk, conv_five = conv_low[:, :bw], conv_low[:, bw:]
    conv_o = jnp.concatenate(
        [conv_blk, lax.dynamic_slice_in_dim(conv_five, (col // 2) * LANES, LANES, axis=1)], axis=1
    ).astype(f32)
    pre = [
        jnp.concatenate([dot(conv_blk, gates_blk[j]), dot(conv_five, gates_tile[j])], axis=1)
        + bias[j][None, :]
        for j in range(2)
    ]
    factor, inject = lru_coeffs(pre[0], pre[1], conv_o, decay_o, reset)
    local_state, since = scan_rows(factor, inject, False)
    state_in = neighbour(local_state[group - 8 :], "dp", 1)[7:]
    state = local_state + since * state_in
    branch = jnp.where(channel_ok, state * gelu(y_branch), 0.0).astype(low)
    out_one = scatter_rows(dot(branch, w_out))
    resid = inputs + out_one
    sumsq_two = jnp.sum(resid * resid, axis=-1, keepdims=True)
    scale_two = lax.rsqrt(sumsq_two / width + epsilon)
    normed_two = (resid * scale_two * gains_all[1]).astype(low)

    n2 = gather_rows(normed_two)
    gate_part = dot(n2, w_in[0])
    up_part = dot(n2, w_in[1])
    g_all = gather_rows(upstream_low)
    d_hidden = jnp.where(hidden_ok, dot(g_all, w_down, ((1,), (1,))), 0.0)
    hidden = jnp.where(hidden_ok, gelu(gate_part) * up_part, 0.0).astype(low)
    _, glu_back = jax.vjp(lambda gate_v, up_v: gelu(gate_v) * up_v, gate_part, up_part)
    d_gate, d_up = glu_back(d_hidden)
    d_glu = jnp.concatenate([d_gate.astype(low), d_up.astype(low)], axis=1)
    g_down = outer(g_all, hidden, n_dp, n_col, 512)
    g_in = outer(n2, d_glu, n_dp, n_col, 512)
    d_normed_two = scatter_rows(
        dot(d_glu[:, :span], w_in[0], ((1,), (1,))) + dot(d_glu[:, span:], w_in[1], ((1,), (1,)))
    )
    out_two = scatter_rows(dot(hidden, w_down))
    result = (resid + out_two).astype(low)

    gained_two = gains_all[1] * d_normed_two
    inner_two = jnp.sum(gained_two * resid, axis=-1, keepdims=True)
    grad_gain_two = jnp.sum(d_normed_two * resid * scale_two, axis=0)
    d_resid = upstream + scale_two * gained_two - resid * scale_two**3 * (inner_two / width)
    d_out = gather_rows(d_resid.astype(low))

    d_branch = jnp.where(channel_ok, dot(d_out, w_out, ((1,), (1,))), 0.0)
    g_out = outer(d_out, branch, n_dp, n_col, chans)
    _, mix_back = jax.vjp(lambda state_v, gate_v: state_v * gelu(gate_v), state, y_branch)
    d_state, d_y = mix_back(d_branch)
    message, until = scan_rows(factor, factor * d_state, True)
    message_in = neighbour(message[:8], "dp", -1)[:1]
    message = message + until * message_in
    grad_state = d_state + jnp.concatenate([message[1:], message_in], axis=0)
    state_prev = jnp.concatenate([state_in, state[:-1]], axis=0)
    _, coef_back = jax.vjp(
        lambda a, b, c, d: lru_coeffs(a, b, c, d, reset), pre[0], pre[1], conv_o, decay_o
    )
    d_pre_in, d_pre_rate, d_conv, g_decay = coef_back((grad_state * state_prev, grad_state))
    d_pre = [d_pre_in.astype(low), d_pre_rate.astype(low)]
    tiles_here = jnp.concatenate([d[:, bw:] for d in d_pre], axis=1)
    tiles_there = lax.ppermute(tiles_here, "col", [(i, i ^ 2) for i in range(n_col)])
    low_half = col // 2 == 0
    d_conv_parts = []
    d_five = []
    for j in range(2):
        here = d_pre[j][:, bw:]
        there = tiles_there[:, j * LANES : (j + 1) * LANES]
        d_five.append(
            jnp.where(
                low_half,
                jnp.concatenate([here, there], axis=1),
                jnp.concatenate([there, here], axis=1),
            )
        )
        d_conv_parts.append(
            jnp.concatenate(
                [
                    dot(d_pre[j][:, :bw], gates_blk[j], ((1,), (1,))),
                    dot(d_five[j], gates_rows[j], ((1,), (1,))),
                ],
                axis=1,
            )
        )
    d_conv = d_conv + d_conv_parts[0] + d_conv_parts[1]
    g_gates = jnp.stack(
        [
            jnp.concatenate(
                [
                    dot(conv_blk, d_pre[j][:, :bw], ((0,), (0,))),
                    dot(conv_five, d_pre[j][:, bw:], ((0,), (0,))),
                ],
                axis=1,
            )
            for j in range(2)
        ]
    )
    g_bias = [jnp.sum(d.astype(f32), axis=0) for d in d_pre]
    later = neighbour(d_conv[:8], "dp", -1)[: taps - 1]
    d_ext = jnp.concatenate([d_conv, later], axis=0)
    x_own = jnp.concatenate(
        [x_ext[:, :bw], lax.dynamic_slice_in_dim(x_ext, bw + (col // 2) * LANES, LANES, axis=1)],
        axis=1,
    )
    d_x = jnp.zeros_like(d_conv)
    g_taps = []
    for t in range(taps):
        ahead = d_ext[t : t + group]
        valid = (places_ext[t : t + group] >= t)[:, None]
        d_x = d_x + jnp.where(valid, conv_w_o[t][None, :] * ahead, 0.0)
        lagged = x_own[taps - 1 - t : taps - 1 - t + group]
        g_taps.append(jnp.sum(jnp.where((places >= t)[:, None], d_conv * lagged, 0.0), axis=0))
    g_conv_b = jnp.sum(d_conv, axis=0)
    d_x_low = jnp.where(channel_ok, d_x, 0.0).astype(low)
    d_y_low = jnp.where(channel_ok, d_y, 0.0).astype(low)
    d_rec = jnp.concatenate([d_x_low, d_y_low], axis=1)
    w_x_own = jnp.concatenate(
        [w_x[:, :bw], lax.dynamic_slice_in_dim(w_x, bw + (col // 2) * LANES, LANES, axis=1)], axis=1
    )
    d_normed_one = scatter_rows(
        dot(d_x_low, w_x_own, ((1,), (1,))) + dot(d_y_low, w_y, ((1,), (1,)))
    )
    g_rec = outer(n1, d_rec, n_dp, n_col, chans)
    gained_one = gains_all[0] * d_normed_one
    inner_one = jnp.sum(gained_one * inputs, axis=-1, keepdims=True)
    grad_gain_one = jnp.sum(d_normed_one * inputs * scale_one, axis=0)
    d_input = d_resid + scale_one * gained_one - inputs * scale_one**3 * (inner_one / width)

    result = home_rows(result)
    grad_input = home_rows(d_input.astype(low))

    def windows(got, first):
        return [
            got[c][..., first + (LANES if c > n_col - 1 - (wide * n_col - tiles) else 0) : first + span]
            for c in range(n_col)
        ]

    def channels_of(got, first):
        return [got[c][..., first : first + bw] for c in range(n_col)] + [
            got[c][..., first + bw : first + chans] for c in range(0, n_col, 2)
        ]

    down = deal_back(g_down, n_col)
    grad_mlp_out = jnp.concatenate(windows(down, 0), axis=-1).astype(f32).T
    into = deal_back(g_in, n_col)
    grad_mlp_in = jnp.stack(
        [jnp.concatenate(windows(into[..., j * span : (j + 1) * span], 0), axis=-1) for j in range(2)]
    ).astype(f32)
    outs = deal_back(g_out, n_col)
    grad_rec_out = jnp.concatenate(channels_of(outs, 0), axis=-1).astype(f32).T
    recs = deal_back(g_rec, n_col)
    grad_rec_in = jnp.stack(
        [jnp.concatenate(channels_of(recs, j * chans), axis=-1) for j in range(2)]
    ).astype(f32)

    gate_parts = lax.all_gather(lax.psum(g_gates.astype(low), "dp"), "col", axis=0).astype(f32)
    five = jnp.concatenate([gate_parts[c, :, :, bw:] for c in range(0, n_col, 2)], axis=-1)
    grad_gates = jnp.stack([gate_parts[c, :, :, :bw] for c in range(n_col)] + [five], axis=1)

    small = jnp.where(channel_ok, jnp.stack(g_bias + [g_decay] + g_taps + [g_conv_b]), 0.0)
    placed = jnp.zeros((small.shape[0], n_row * half), f32)
    placed = lax.dynamic_update_slice(placed, small[:, :bw], (0, row * half + col * bw))
    tile_spot = (0, row * half + tile_at)
    placed = lax.dynamic_update_slice(placed, small[:, bw:], tile_spot)
    square_sums = jnp.stack(
        [jnp.sum(sumsq_one), jnp.sum(out_one * out_one), jnp.sum(sumsq_two), jnp.sum(out_two * out_two)]
    )
    stat_row = jnp.pad(square_sums, (0, width - 4))[None, :]
    rows_all = jnp.concatenate(
        [placed, grad_gain_one[None, :], grad_gain_two[None, :], stat_row], axis=0
    )
    sums = lax.psum(rows_all, ("dp", "row", "col"))
    mine = lax.dynamic_slice_in_dim(sums[:8], row * half, half, axis=1)
    grad_gains = lax.dynamic_slice_in_dim(sums[8:10], col * part, part, axis=1)
    stats = jnp.sqrt(sums[10, :4] / (n_dp * group * width))
    return (
        result,
        grad_input,
        grad_rec_in,
        grad_rec_out,
        grad_gates,
        mine[0:2],
        mine[2],
        mine[3 : 3 + taps],
        mine[3 + taps],
        grad_gains,
        grad_mlp_in,
        grad_mlp_out,
        stats,
    )


def solution(mesh):
    placed = (
        P(("dp", "row"), "col"),
        P(("dp", "row"), "col"),
        P(None, "col", "row"),
        P("row", "col"),
        P(None, "row", None, None),
        P(None, "row"),
        P("row"),
        P(None, "row"),
        P("row"),
        P(None, "col"),
        P(None, "col", "row"),
        P("row", "col"),
        P(),
        P(),
    )
    return jax.shard_map(
        body,
        mesh=mesh,
        in_specs=placed,
        out_specs=(
            P(("dp", "row"), "col"),
            P(("dp", "row"), "col"),
            P(None, ("col", "dp"), "row"),
            P("row", ("col", "dp")),
            P(None, "row", None, None),
            P(None, "row"),
            P("row"),
            P(None, "row"),
            P("row"),
            P(None, "col"),
            P(None, ("col", "dp"), "row"),
            P("row", ("col", "dp")),
            P(),
        ),
        check_vma=False,
    )
```

```python
import functools

import jax
import jax.numpy as jnp
from jax import lax
from jax.experimental import pallas as pl
from jax.experimental.pallas import tpu as pltpu
from jax.sharding import PartitionSpec as P

epsilon = 1e-06
LANES = 128
ROWS = 16
MIB = 1024 * 1024
MESH = pl.DeviceIdType.MESH
low = jnp.bfloat16
f32 = jnp.float32
anywhere = pl.BlockSpec(memory_space=pl.ANY)
in_vmem = pl.BlockSpec(memory_space=pltpu.VMEM)


def gelu(values):
    return jax.nn.gelu(values, approximate=True)


def window_tile(col, tiles, n_col, wide):
    spare = wide * n_col - tiles
    return col * wide - jnp.maximum(col - (n_col - 1 - spare), 0)


def spare_window(col, tiles, n_col, wide):
    spare = wide * n_col - tiles
    return col > n_col - 1 - spare


class Place:
    def __init__(self):
        self.dp, self.row, self.col = (lax.axis_index(a) for a in ("dp", "row", "col"))

    def chip(self, k):
        return jnp.bitwise_xor(self.col, k)

    def device(self, name):
        if name == "core":
            return {"row": 1 - self.row}
        if name == "z":
            return {"dp": jnp.bitwise_xor(self.dp, 1)}
        if name in ("next", "prev"):
            n_dp = lax.axis_size("dp")
            return {"dp": lax.rem(self.dp + (1 if name == "next" else n_dp - 1), n_dp)}
        if name[0] == "d":
            return {"dp": jnp.bitwise_xor(self.dp, int(name[1:]))}
        return {"col": self.chip({"x": 1, "y": 2, "xy": 3}[name])}

    def meet(self, names):
        barrier = pltpu.get_barrier_semaphore()
        for name in names:
            pl.semaphore_signal(
                barrier, inc=1, device_id=self.device(name), device_id_type=MESH
            )
        pl.semaphore_wait(barrier, len(names))


class Copies:
    def __init__(self, place, send, recv):
        self.place, self.send, self.recv = place, send, recv
        self.made, self.landed, self.left, self.local = [], set(), set(), []

    def start(self, src, dst, to):
        i = len(self.made)
        copy = pltpu.make_async_remote_copy(
            src_ref=src,
            dst_ref=dst,
            send_sem=self.send.at[i],
            recv_sem=self.recv.at[i],
            device_id=self.place.device(to),
            device_id_type=MESH,
        )
        copy.start()
        self.made.append(copy)
        return i

    def land(self, *numbers):
        for i in numbers:
            if i not in self.landed:
                self.made[i].wait_recv()
                self.landed.add(i)

    def leave(self, *numbers):
        for i in numbers:
            if i not in self.left:
                self.made[i].wait_send()
                self.left.add(i)

    def keep(self, src, dst, sem):
        copy = pltpu.make_async_copy(src, dst, sem)
        copy.start()
        self.local.append(copy)
        return copy

    def finish(self):
        self.land(*range(len(self.made)))
        self.leave(*range(len(self.made)))


def share(rows):
    far = rows * 9 // 20 // ROWS * ROWS
    return rows - far, far


class Dealer:
    def __init__(self, copies):
        self.copies = copies
        self.waiting = []

    def deal(self, piece):
        place = self.copies.place
        odd = lax.rem(place.dp, 2)
        batch = []
        for name, k in (("x", 1), ("y", 2), ("xy", 3)):
            src, dst, rows = piece(place.chip(k), place.col)
            near, far = share(rows)
            start = pl.multiple_of(odd * far, ROWS)
            at = pl.ds(start, near)
            number = self.copies.start(src(at), dst(at), name)
            batch.append((k, number, piece))
        self.waiting.append(batch)

    def forward(self):
        place = self.copies.place
        odd = lax.rem(place.dp, 2)
        for k, number, piece in self.waiting.pop(0):
            self.copies.land(number)
            _, dst, rows = piece(place.col, place.chip(k))
            near, far = share(rows)
            at = pl.ds(pl.multiple_of(odd * near, ROWS), far)
            self.copies.start(dst(at), dst(at), "z")


def rows_of(ref, first, rows, lead=None, columns=None):
    def view(at):
        where = pl.ds(pl.multiple_of(first + at.start, ROWS), at.size)
        index = (where, columns if columns is not None else slice(None))
        return ref.at[index] if lead is None else ref.at[(lead,) + index]

    return view


def weight_pieces(geo, refs, outs):
    n_col, part, bw, tiles, wide = geo
    shared, span = n_col * bw, wide * LANES
    rec_in, rec_out, mlp_in, mlp_out = refs
    w_rec, w_out, w_in, w_down = outs

    def here(chip):
        return pl.multiple_of(chip * part, LANES)

    def blk(chip):
        return pl.multiple_of(chip * bw, LANES)

    def tile(chip):
        return pl.multiple_of(shared + lax.div(chip, 2) * LANES, LANES)

    def win(chip):
        return pl.multiple_of(window_tile(chip, tiles, n_col, wide) * LANES, LANES)

    def in_piece(ref, j, out, lead, source_at, size, column):
        def piece(dest, source):
            return (
                rows_of(ref, 0, part, j, pl.ds(pl.multiple_of(source_at(dest), LANES), size)),
                rows_of(out, here(source), part, lead, pl.ds(column, size)),
                part,
            )

        return piece

    def down_piece(ref, out, source_at, size, row):
        def piece(dest, source):
            return (
                rows_of(ref, source_at(dest), size),
                rows_of(out, row, size, None, pl.ds(here(source), part)),
                size,
            )

        return piece

    found = {}
    if rec_in is not None:
        found["rec_in"] = [
            in_piece(rec_in, 0, w_rec, None, blk, bw, 0),
            in_piece(rec_in, 0, w_rec, None, lambda chip: shared, bw, bw),
            in_piece(rec_in, 1, w_rec, None, blk, bw, 2 * bw),
            in_piece(rec_in, 1, w_rec, None, tile, LANES, 3 * bw),
        ]
    if rec_out is not None:
        found["rec_out"] = [
            down_piece(rec_out, w_out, blk, bw, 0),
            down_piece(rec_out, w_out, tile, LANES, bw),
        ]
    if mlp_in is not None:
        half = span // 2
        found["mlp_in"] = [
            in_piece(mlp_in, j, w_in, j, lambda chip, h=h: win(chip) + h * half, half, h * half)
            for j in range(2)
            for h in range(2)
        ]
    if mlp_out is not None:
        found["mlp_out"] = [down_piece(mlp_out, w_down, win, span, 0)]
    return found


def keep_own(copies, pieces, sems, first):
    col = copies.place.col
    for i, piece in enumerate(pieces):
        src, dst, rows = piece(col, col)
        copies.keep(src(pl.ds(0, rows)), dst(pl.ds(0, rows)), sems.at[first + i])


class Gather:
    def __init__(self, copies, mine, at):
        self.copies, self.at = copies, at
        place = copies.place
        row, col = place.row, place.col
        self.first = [
            copies.start(mine(half), at(row, col, half), name)
            for half in (0, 1)
            for name in ("x", "y")
        ]
        self.own = copies.start(mine(None), at(row, col, None), "core")

    def pass_on(self):
        copies, place = self.copies, self.copies.place
        row = place.row
        x, y = place.chip(1), place.chip(2)
        x0, y0, x1, y1 = self.first
        copies.land(x0)
        self.round0 = copies.start(self.at(row, x, 0), self.at(row, x, 0), "y")
        copies.land(y0, y1)
        self.round1 = copies.start(self.at(row, y, 1), self.at(row, y, 1), "x")
        self.core_y = copies.start(self.at(row, y, None), self.at(row, y, None), "core")
        copies.land(x1)
        self.core_x = copies.start(self.at(row, x, None), self.at(row, x, None), "core")

    def last(self):
        copies, place = self.copies, self.copies.place
        corner = self.at(place.row, place.chip(3), None)
        copies.land(self.round0, self.round1)
        self.core_xy = copies.start(corner, corner, "core")


def block_gather(copies, source, target, sem):
    rows, part = source.shape
    cut = rows // 2

    def at(row, col, half):
        first = row * rows + (0 if half is None else half * cut)
        size = rows if half is None else cut
        return target.at[
            pl.ds(pl.multiple_of(first, ROWS), size), pl.ds(pl.multiple_of(col * part, LANES), part)
        ]

    def mine(half):
        return source if half is None else source.at[pl.ds(half * cut, cut), :]

    place = copies.place
    copies.keep(source, at(place.row, place.col, None), sem)
    return Gather(copies, mine, at)


AROUND = ("x", "y", "xy", "core", "z")


def open_kernel(geo, tokens, rec_in, gains, x_all, w_rec, gains_all, send, recv, local):
    place = Place()
    place.meet(AROUND)
    copies = Copies(place, send, recv)
    pieces = weight_pieces(geo, (rec_in, None, None, None), (w_rec, None, None, None))["rec_in"]
    dealer = Dealer(copies)
    dealer.deal(pieces[0])
    dealer.deal(pieces[1])
    gather = block_gather(copies, tokens, x_all, local.at[0])
    dealer.deal(pieces[2])
    dealer.deal(pieces[3])
    mine = gains_all.at[place.col]
    for name in ("x", "y", "xy"):
        copies.start(gains, mine, name)
    copies.keep(gains, mine, local.at[5])
    keep_own(copies, pieces, local, 1)
    dealer.forward()
    dealer.forward()
    gather.pass_on()
    dealer.forward()
    dealer.forward()
    gather.last()
    copies.finish()
    for copy in copies.local:
        copy.wait()


def open_gather(tokens, rec_in, gains, geo):
    n_col, part, bw, tiles, wide = geo
    width = part * n_col
    return pl.pallas_call(
        functools.partial(open_kernel, geo),
        out_shape=(
            jax.ShapeDtypeStruct((2 * tokens.shape[0], width), low),
            jax.ShapeDtypeStruct((width, 3 * bw + LANES), low),
            jax.ShapeDtypeStruct((n_col,) + gains.shape, f32),
        ),
        in_specs=[anywhere] * 3,
        out_specs=(anywhere,) * 3,
        scratch_shapes=[
            pltpu.SemaphoreType.DMA((37,)),
            pltpu.SemaphoreType.DMA((37,)),
            pltpu.SemaphoreType.DMA((6,)),
        ],
        compiler_params=pltpu.CompilerParams(collective_id=1, has_side_effects=True),
        name="open_gather",
    )(tokens, rec_in, gains)


def slot_gather(copies, local_ref, buf, own):
    cut = own // 2
    n_col = buf.shape[0] // 2

    def at(row, col, half):
        slot = buf.at[row * n_col + col]
        return slot if half is None else slot.at[pl.ds(half * cut, cut), :]

    def mine(half):
        return local_ref if half is None else local_ref.at[pl.ds(half * cut, cut), :]

    return Gather(copies, mine, at)


def tanh_parts(x):
    k = 0.7978845608028654
    square = x * x
    t = jnp.tanh(k * x * (1.0 + 0.044715 * square))
    value = 0.5 * x * (1.0 + t)
    slope = 0.5 * (1.0 + t) + 0.5 * x * (1.0 - t * t) * k * (1.0 + 3 * 0.044715 * square)
    return value, slope


def glu_kernel(
    spare, n2, w_in, w_down, g_all, n2_all, hidden, d_glu, buf, wi, wd, g, hid, dgl, send, recv, local
):
    place = Place()
    place.meet(("x", "y", "core"))
    copies = Copies(place, send, recv)
    own, width = n2.shape
    n_col = buf.shape[0] // 2
    span = wd.shape[0]
    step = 256
    gather = slot_gather(copies, n2, buf, own)
    me = place.row * n_col + place.col
    loads = [
        copies.keep(n2, buf.at[me], local.at[0]),
        copies.keep(w_in, wi, local.at[1]),
        copies.keep(w_down, wd, local.at[2]),
        copies.keep(g_all, g, local.at[3]),
    ]
    for load in loads:
        load.wait()
    hide = spare(place.col)

    def work(chip):
        slots = (chip, n_col + chip)
        rows = [pl.ds(pl.multiple_of(s * own, ROWS), own) for s in slots]
        n2_here = jnp.concatenate([buf[s] for s in slots], axis=0)
        g_here = jnp.concatenate([g[r, :] for r in rows], axis=0)

        def columns(i, carry):
            at = pl.ds(pl.multiple_of(i * step, LANES), step)
            up_at = pl.ds(pl.multiple_of(span + i * step, LANES), step)
            gate = dot(n2_here, wi[0, :, at])
            up = dot(n2_here, wi[1, :, at])
            d_hid = dot(g_here, wd[at, :], ((1,), (1,)))
            lane = lax.broadcasted_iota(jnp.int32, gate.shape, 1) + i * step
            used = (lane >= LANES) | jnp.logical_not(hide)
            up = jnp.where(used, up, 0.0)
            d_hid = jnp.where(used, d_hid, 0.0)
            value, slope = tanh_parts(gate)
            h = (value * up).astype(low)
            dg = (d_hid * up * slope).astype(low)
            du = (d_hid * value).astype(low)
            for n, r in enumerate(rows):
                part = slice(n * own, (n + 1) * own)
                hid[r, at] = h[part]
                dgl[r, at] = dg[part]
                dgl[r, up_at] = du[part]
            return carry

        lax.fori_loop(0, span // step, columns, 0)

    copies.land(gather.own)
    work(place.col)
    gather.pass_on()
    copies.land(gather.core_y)
    work(place.chip(2))
    gather.last()
    copies.land(gather.core_x)
    work(place.chip(1))
    copies.land(gather.core_xy)
    out_n2 = copies.keep(buf, n2_all, local.at[4])
    work(place.chip(3))
    out_h = copies.keep(hid, hidden, local.at[5])
    out_d = copies.keep(dgl, d_glu, local.at[6])
    copies.finish()
    out_n2.wait()
    out_h.wait()
    out_d.wait()


def glu(n2, w_in, w_down, g_all, spare):
    own, width = n2.shape
    group = g_all.shape[0]
    span = w_down.shape[0]
    n_all, h, d = pl.pallas_call(
        functools.partial(glu_kernel, spare),
        out_shape=(
            jax.ShapeDtypeStruct((group // own, own, width), low),
            jax.ShapeDtypeStruct((group, span), low),
            jax.ShapeDtypeStruct((group, 2 * span), low),
        ),
        in_specs=[anywhere] * 4,
        out_specs=(anywhere,) * 3,
        scratch_shapes=[
            pltpu.VMEM((group // own, own, width), low),
            pltpu.VMEM(w_in.shape, low),
            pltpu.VMEM(w_down.shape, low),
            pltpu.VMEM((group, width), low),
            pltpu.VMEM((group, span), low),
            pltpu.VMEM((group, 2 * span), low),
            pltpu.SemaphoreType.DMA((10,)),
            pltpu.SemaphoreType.DMA((10,)),
            pltpu.SemaphoreType.DMA((7,)),
        ],
        compiler_params=pltpu.CompilerParams(
            collective_id=3, has_side_effects=True, vmem_limit_bytes=58 * MIB
        ),
        cost_estimate=pl.CostEstimate(
            flops=6 * group * width * span, bytes_accessed=60 * MIB, transcendentals=group * span
        ),
        name="glu",
    )(n2, w_in, w_down, g_all)
    return n_all.reshape(group, width), h, d


def branch_kernel(x, w, x_all, y, buf, wv, send, recv, local):
    place = Place()
    place.meet(("x", "y", "core"))
    copies = Copies(place, send, recv)
    own = x.shape[0]
    n_col = buf.shape[0] // 2
    gather = slot_gather(copies, x, buf, own)
    me = place.row * n_col + place.col
    load = copies.keep(w, wv, local.at[0])
    mine = copies.keep(x, buf.at[me], local.at[1])
    load.wait()
    mine.wait()

    def work(chip):
        slots = (chip, n_col + chip)
        value = dot(jnp.concatenate([buf[s] for s in slots], axis=0), wv[...], ((1,), (1,)))
        for n, s in enumerate(slots):
            y[pl.ds(pl.multiple_of(s * own, ROWS), own), :] = value[n * own : (n + 1) * own]

    copies.land(gather.own)
    work(place.col)
    gather.pass_on()
    copies.land(gather.core_y)
    work(place.chip(2))
    gather.last()
    copies.land(gather.core_x)
    work(place.chip(1))
    copies.land(gather.core_xy)
    out = copies.keep(buf, x_all, local.at[2])
    work(place.chip(3))
    copies.finish()
    out.wait()


def gather_branch(x, w):
    own, width = x.shape
    slots = 2 * lax.axis_size("col")
    x_all, y = pl.pallas_call(
        branch_kernel,
        out_shape=(
            jax.ShapeDtypeStruct((slots, own, width), low),
            jax.ShapeDtypeStruct((slots * own, w.shape[0]), f32),
        ),
        in_specs=[anywhere] * 2,
        out_specs=(anywhere, in_vmem),
        scratch_shapes=[
            pltpu.VMEM((slots, own, width), low),
            pltpu.VMEM(w.shape, low),
            pltpu.SemaphoreType.DMA((10,)),
            pltpu.SemaphoreType.DMA((10,)),
            pltpu.SemaphoreType.DMA((3,)),
        ],
        compiler_params=pltpu.CompilerParams(
            collective_id=4, has_side_effects=True, vmem_limit_bytes=48 * MIB
        ),
        name="gather_branch",
    )(x, w)
    return x_all.reshape(slots * own, width), y


def scatter_kernel(
    n_parts, across, act, w, out, actv, wv, other, mine, from_core, from_x, from_y, turn, send, recv, local
):
    place = Place()
    place.meet(("x", "y", "core"))
    copies = Copies(place, send, recv)
    own, width = out.shape
    cut = own // 2
    n_col = act.shape[0] // own // 2
    k = act.shape[1] // n_parts
    step = 256
    loads = [copies.keep(act, actv, local.at[0]), copies.keep(w, wv, local.at[1])]
    for load in loads:
        load.wait()
    top, bottom = pl.ds(0, cut), pl.ds(cut, cut)

    def work(j):
        chip = place.chip(j)
        slots = ((1 - place.row) * n_col + chip, place.row * n_col + chip)
        left = [
            jnp.concatenate(
                [
                    actv[pl.ds(pl.multiple_of(s * own, ROWS), own), n * k : (n + 1) * k]
                    for s in slots
                ],
                axis=0,
            )
            for n in range(n_parts)
        ]

        def columns(i, carry):
            at = pl.ds(pl.multiple_of(i * step, LANES), step)
            total = None
            for n in range(n_parts):
                if across:
                    right = wv[n, at, :] if n_parts > 1 else wv[at, :]
                    term = dot(left[n], right, ((1,), (1,)))
                else:
                    term = dot(left[n], wv[:, at])
                total = term if total is None else total + term
            other[j, :, at] = total[:own].astype(low)
            mine[j, :, at] = total[own:]
            return carry

        lax.fori_loop(0, width // step, columns, 0)
        return copies.start(other.at[j], from_core.at[j], "core")

    def add_core(j, number):
        copies.land(number)
        mine[j] = mine[j] + from_core[j].astype(f32)
        turn[j] = mine[j].astype(low)

    core3 = work(3)
    core1 = work(1)
    add_core(3, core3)
    x3 = copies.start(turn.at[3, top, :], from_x.at[0], "x")
    y3 = copies.start(turn.at[3, bottom, :], from_y.at[0], "y")
    core2 = work(2)
    add_core(1, core1)
    x1 = copies.start(turn.at[1, top, :], from_x.at[1], "x")
    core0 = work(0)
    add_core(2, core2)
    y2 = copies.start(turn.at[2, bottom, :], from_y.at[1], "y")
    copies.land(x3)
    turn[2, top, :] = (mine[2, top, :] + from_x[0].astype(f32)).astype(low)
    y_last = copies.start(turn.at[2, top, :], from_y.at[2], "y")
    copies.land(y3)
    turn[1, bottom, :] = (mine[1, bottom, :] + from_y[0].astype(f32)).astype(low)
    x_last = copies.start(turn.at[1, bottom, :], from_x.at[2], "x")
    add_core(0, core0)
    copies.land(x1, y2, y_last, x_last)
    out[top, :] = mine[0, top, :] + from_x[1].astype(f32) + from_y[2].astype(f32)
    out[bottom, :] = mine[0, bottom, :] + from_y[1].astype(f32) + from_x[2].astype(f32)
    copies.finish()


def multiply_scatter(act, w, across, number, name):
    n_parts = w.shape[0] if w.ndim == 3 else 1
    group = act.shape[0]
    slots = 2 * lax.axis_size("col")
    own = group // slots
    width = w.shape[-2] if across else w.shape[-1]
    return pl.pallas_call(
        functools.partial(scatter_kernel, n_parts, across),
        out_shape=jax.ShapeDtypeStruct((own, width), f32),
        in_specs=[anywhere] * 2,
        out_specs=in_vmem,
        scratch_shapes=[
            pltpu.VMEM(act.shape, low),
            pltpu.VMEM(w.shape, low),
            pltpu.VMEM((4, own, width), low),
            pltpu.VMEM((4, own, width), f32),
            pltpu.VMEM((4, own, width), low),
            pltpu.VMEM((3, own // 2, width), low),
            pltpu.VMEM((3, own // 2, width), low),
            pltpu.VMEM((4, own, width), low),
            pltpu.SemaphoreType.DMA((10,)),
            pltpu.SemaphoreType.DMA((10,)),
            pltpu.SemaphoreType.DMA((2,)),
        ],
        compiler_params=pltpu.CompilerParams(
            collective_id=number, has_side_effects=True, vmem_limit_bytes=58 * MIB
        ),
        cost_estimate=pl.CostEstimate(
            flops=2 * group * width * act.shape[1], bytes_accessed=40 * MIB, transcendentals=0
        ),
        name=name,
    )(act, w)


def sums_kernel(far, split, mixed, gate_part, sums_out, chans_out, gates_out, got, acc, ch, send, recv, local):
    place = Place()
    steps = [f"d{d}" for d in far if d & (d - 1) == 0]
    place.meet(("core", "x", "y") + tuple(f"d{d}" for d in far))
    copies = Copies(place, send, recv)
    dp, col = place.dp, place.col
    own_gates = gates_out.at[col]
    stay = copies.keep(gate_part, own_gates.at[dp], local)
    parts = [copies.start(gate_part, own_gates.at[dp], f"d{d}") for d in far]
    acc[0] = mixed[...]
    n = 0
    for name in steps:
        copies.land(copies.start(acc.at[n], got.at[n], name))
        acc[n + 1] = acc[n] + got[n]
        n += 1
    stay.wait()
    copies.land(*parts)
    half = gates_out.shape[1] // 2
    halves = (pl.ds(0, half), pl.ds(half, half))

    def gate_view(chip, h):
        return gates_out.at[chip, halves[h]]

    direct = {
        (name, h): copies.start(gate_view(col, h), gate_view(col, h), name)
        for h in (0, 1)
        for name in ("x", "y")
    }
    ch[col] = acc[n][:, :split]
    x_ch = copies.start(ch.at[col], ch.at[col], "x")
    rest = slice(split, None)
    for name in ("core", "x", "y"):
        number = copies.start(acc.at[n, :, rest], got.at[n, :, rest], name)
        if name == "y":
            copies.land(x_ch)
            pair = pl.ds(lax.div(col, 2) * 2, 2)
            y_ch = copies.start(ch.at[pair], ch.at[pair], "y")
        copies.land(number)
        acc[n + 1, :, rest] = acc[n, :, rest] + got[n, :, rest]
        n += 1
    copies.land(direct["x", 0])
    far_x = gate_view(place.chip(1), 0)
    copies.start(far_x, far_x, "y")
    copies.land(direct["y", 1])
    far_y = gate_view(place.chip(2), 1)
    copies.start(far_y, far_y, "x")
    sums_out[...] = acc[n, :, rest]
    copies.land(y_ch)
    chans_out[...] = ch[...]
    copies.finish()


def sum_everywhere(mixed, split, gate_part, n_dp, n_col):
    far = tuple(range(1, n_dp))
    stages = len([d for d in far if d & (d - 1) == 0]) + 3
    count = 2 * len(far) + stages + 8
    rows, columns = mixed.shape
    return pl.pallas_call(
        functools.partial(sums_kernel, far, split),
        out_shape=(
            jax.ShapeDtypeStruct((rows, columns - split), f32),
            jax.ShapeDtypeStruct((n_col, rows, split), f32),
            jax.ShapeDtypeStruct((n_col, n_dp) + gate_part.shape, gate_part.dtype),
        ),
        in_specs=[in_vmem, anywhere],
        out_specs=(in_vmem, in_vmem, anywhere),
        scratch_shapes=[
            pltpu.VMEM((stages, rows, columns), f32),
            pltpu.VMEM((stages + 1, rows, columns), f32),
            pltpu.VMEM((n_col, rows, split), f32),
            pltpu.SemaphoreType.DMA((count,)),
            pltpu.SemaphoreType.DMA((count,)),
            pltpu.SemaphoreType.DMA,
        ],
        compiler_params=pltpu.CompilerParams(collective_id=5, has_side_effects=True),
        name="small_sums",
    )(mixed, gate_part)


def one_less_exp(z):
    series = 1.0 + z / 6.0
    for n in (5.0, 4.0, 3.0, 2.0):
        series = 1.0 + z / n * series
    return jnp.where(z > -0.1, -z * series, 1.0 - jnp.exp(z))


def scan_tile(a, u, reverse):
    rows = a.shape[0]
    index = lax.broadcasted_iota(jnp.int32, a.shape, 0)
    by = 1
    while by < rows:
        turn = rows - by if reverse else by
        inside = index < rows - by if reverse else index >= by
        u = u + a * jnp.where(inside, pltpu.roll(u, turn, 0), 0.0)
        a = a * jnp.where(inside, pltpu.roll(a, turn, 0), 1.0)
        by *= 2
    return a, u


def forward_kernel(
    geo,
    x_all,
    w_rec,
    gain,
    gates_blk,
    gates_tile,
    bias,
    soft,
    conv_w,
    conv_b,
    places,
    cotangent,
    rec_out,
    mlp_in,
    mlp_out,
    n1_out,
    x_out,
    y_out,
    pre_out,
    c_out,
    state_out,
    branch_out,
    first_out,
    g_all,
    w_out,
    w_in,
    w_down,
    xv,
    wv,
    before,
    xb,
    yv,
    prev,
    cv,
    hv,
    pv,
    bv,
    carry,
    first,
    send,
    recv,
    local,
):
    place = Place()
    place.meet(AROUND + ("next", "prev"))
    copies = Copies(place, send, recv)
    n_col, part, bw, tiles, wide = geo
    chans = bw + LANES
    group, width = xv.shape
    tile = 256
    n_tiles = group // tile
    loads = [copies.keep(x_all, xv, local.at[0]), copies.keep(w_rec, wv, local.at[1])]
    halo = copies.start(x_all.at[pl.ds(group - ROWS, ROWS), :], before, "next")
    found = weight_pieces(geo, (None, rec_out, mlp_in, mlp_out), (None, w_out, w_in, w_down))
    pieces = found["rec_out"] + found["mlp_in"] + found["mlp_out"]
    dealer = Dealer(copies)
    dealer.deal(pieces[0])
    dealer.deal(pieces[1])
    dealer.deal(pieces[2])
    dealer.deal(pieces[3])
    keep_own(copies, pieces, local, 2)
    for load in loads:
        load.wait()
    high_tile = place.col >= 2
    idle_tile = lax.rem(place.col, 2) == 1

    def normed(x):
        x = x.astype(f32)
        scale = lax.rsqrt(jnp.sum(x * x, axis=-1, keepdims=True) / width + epsilon)
        return (x * scale * gain[...]).astype(low)

    copies.land(halo)
    xb[0:8, :] = dot(normed(before[...]), wv[:, : 2 * bw])[ROWS - 8 :]
    carry[0:1] = jnp.zeros_like(carry[0:1])
    carry[1:2] = jnp.ones_like(carry[1:2])

    def work(i, unused):
        r0 = pl.multiple_of(i * tile, tile)
        rows = pl.ds(r0, tile)
        n1 = normed(xv[rows, :])
        xv[rows, :] = n1
        both = dot(n1, wv[...])
        xb[pl.ds(pl.multiple_of(r0 + 8, 8), tile), :] = both[:, : 2 * bw]
        yv[rows, :] = both[:, 2 * bw :]
        spot = places[rows, :]
        reach = xb[pl.ds(r0, tile + 8), :]
        conv = []
        for lane in range(2 * bw // LANES):
            at = slice(lane * LANES, (lane + 1) * LANES)
            near = reach[:, at]
            total = conv_b[0:1, at] + conv_w[0:1, at] * near[8:]
            for t in range(1, conv_w.shape[0]):
                lagged = pltpu.roll(near, t, 0)[8:]
                total = total + jnp.where(spot >= t, conv_w[t : t + 1, at] * lagged, 0.0)
            conv.append(total.astype(low))
        c = jnp.concatenate(conv, axis=1)
        cv[rows, :] = c
        pre = [
            jnp.concatenate([dot(c[:, :bw], gates_blk[j]), dot(c[:, bw:], gates_tile[j])], axis=1)
            + bias[j : j + 1, :]
            for j in range(2)
        ]
        prev[rows, :chans] = pre[0]
        prev[rows, chans:] = pre[1]
        reset = spot == 0
        for lane in range(chans // LANES):
            at = slice(lane * LANES, (lane + 1) * LANES)
            if lane * LANES < bw:
                own_c = conv[lane].astype(f32)
            else:
                own_c = jnp.where(high_tile, conv[lane + 1].astype(f32), conv[lane].astype(f32))
            log_a = -8.0 * jax.nn.sigmoid(pre[1][:, at]) * soft[0:1, at]
            a = jnp.where(reset, 0.0, jnp.exp(log_a))
            m = jnp.where(reset, 1.0, jnp.sqrt(one_less_exp(2.0 * log_a)))
            u = own_c * jax.nn.sigmoid(pre[0][:, at]) * m
            a, u = scan_tile(a, u, False)
            h = u + a * carry[0:1, at]
            p = a * carry[1:2, at]
            hv[rows, at] = h
            pv[rows, at] = p
            carry[0:1, at] = h[tile - 1 :]
            carry[1:2, at] = p[tile - 1 :]
        return unused

    third = n_tiles // 3
    lax.fori_loop(0, third, work, 0)
    dealer.forward()
    dealer.forward()
    dealer.deal(pieces[4])
    dealer.forward()
    lax.fori_loop(third, 2 * third, work, 0)
    dealer.forward()
    gather = block_gather(copies, cotangent, g_all, local.at[9])
    dealer.deal(pieces[5])
    lax.fori_loop(2 * third, n_tiles, work, 0)
    state_in = copies.start(hv.at[pl.ds(group - 8, 8), :], first, "next")
    outs = [
        copies.keep(src, dst, local.at[10 + i])
        for i, (src, dst) in enumerate(
            ((xv, n1_out), (xb, x_out), (yv, y_out), (prev, pre_out), (cv, c_out))
        )
    ]
    dealer.forward()
    dealer.deal(pieces[6])
    copies.land(state_in)
    copies.leave(state_in)
    before_all = first[7:8, :]

    def finish(i, unused):
        rows = pl.ds(pl.multiple_of(i * tile, tile), tile)
        for lane in range(chans // LANES):
            at = slice(lane * LANES, (lane + 1) * LANES)
            state = hv[rows, at] + pv[rows, at] * before_all[:, at]
            hv[rows, at] = state
            value, _ = tanh_parts(yv[rows, at])
            b = state * value
            if lane * LANES >= bw:
                b = jnp.where(idle_tile, 0.0, b)
            bv[rows, at] = b.astype(low)
        return unused

    lax.fori_loop(0, n_tiles, finish, 0)
    outs += [
        copies.keep(hv, state_out, local.at[15]),
        copies.keep(bv, branch_out, local.at[16]),
        copies.keep(first, first_out, local.at[17]),
    ]
    dealer.forward()
    gather.pass_on()
    gather.last()
    dealer.forward()
    copies.finish()
    for copy in copies.local:
        if not any(copy is load for load in loads):
            copy.wait()


def rec_forward(x_all, w_rec, params, places, cotangent, rec_out, mlp_in, mlp_out, geo):
    n_col, part, bw, tiles, wide = geo
    width, span, chans = part * n_col, wide * LANES, bw + LANES
    group = x_all.shape[0]

    def of(shape, dtype):
        return jax.ShapeDtypeStruct(shape, dtype)

    kept = [
        ((group, width), low),
        ((group + 8, 2 * bw), f32),
        ((group, chans), f32),
        ((group, 2 * chans), f32),
        ((group, 2 * bw), low),
        ((group, chans), f32),
        ((group, chans), low),
        ((8, chans), f32),
    ]
    dealt = [((group, width), low), ((chans, width), low), ((2, width, span), low), ((span, width), low)]
    copy_count = 1 + 6 * 7 + 10 + 1
    return pl.pallas_call(
        functools.partial(forward_kernel, geo),
        out_shape=tuple(of(*s) for s in kept + dealt),
        in_specs=[anywhere] * 2 + [in_vmem] * 8 + [anywhere] * 4,
        out_specs=(anywhere,) * 12,
        scratch_shapes=[
            pltpu.VMEM((group, width), low),
            pltpu.VMEM(w_rec.shape, low),
            pltpu.VMEM((ROWS, width), low),
            pltpu.VMEM((group + 8, 2 * bw), f32),
            pltpu.VMEM((group, chans), f32),
            pltpu.VMEM((group, 2 * chans), f32),
            pltpu.VMEM((group, 2 * bw), low),
            pltpu.VMEM((group, chans), f32),
            pltpu.VMEM((group, chans), f32),
            pltpu.VMEM((group, chans), low),
            pltpu.VMEM((8, chans), f32),
            pltpu.VMEM((8, chans), f32),
            pltpu.SemaphoreType.DMA((copy_count,)),
            pltpu.SemaphoreType.DMA((copy_count,)),
            pltpu.SemaphoreType.DMA((18,)),
        ],
        compiler_params=pltpu.CompilerParams(
            collective_id=2, has_side_effects=True, vmem_limit_bytes=58 * MIB
        ),
        name="rec_forward",
    )(x_all, w_rec, *params, places, cotangent, rec_out, mlp_in, mlp_out)


def scan_kernel(reverse, a_ref, u_ref, h_ref, p_ref, carry):
    step = pl.program_id(0)
    rows = a_ref.shape[0]

    @pl.when(step == 0)
    def _():
        carry[0:1] = jnp.zeros_like(carry[0:1])
        carry[1:2] = jnp.ones_like(carry[1:2])

    for lane in range(a_ref.shape[1] // LANES):
        at = slice(lane * LANES, (lane + 1) * LANES)
        a = a_ref[:, at]
        u = u_ref[:, at]
        index = lax.broadcasted_iota(jnp.int32, a.shape, 0)
        by = 1
        while by < rows:
            turn = rows - by if reverse else by
            inside = index < rows - by if reverse else index >= by
            a_far = jnp.where(inside, pltpu.roll(a, turn, 0), 1.0)
            u_far = jnp.where(inside, pltpu.roll(u, turn, 0), 0.0)
            u = u + a * u_far
            a = a * a_far
            by *= 2
        h = u + a * carry[0:1, at]
        p = a * carry[1:2, at]
        h_ref[:, at] = h
        p_ref[:, at] = p
        edge = 0 if reverse else rows - 1
        carry[0:1, at] = h[edge : edge + 1]
        carry[1:2, at] = p[edge : edge + 1]


def scan_rows(decay, inject, reverse, rows=256):
    length, channels = decay.shape
    steps = length // rows
    block = pl.BlockSpec((rows, channels), lambda i: (steps - 1 - i if reverse else i, 0))
    shape = jax.ShapeDtypeStruct(decay.shape, f32)
    return pl.pallas_call(
        functools.partial(scan_kernel, reverse),
        grid=(steps,),
        out_shape=(shape, shape),
        in_specs=[block, block],
        out_specs=(block, block),
        scratch_shapes=[pltpu.VMEM((8, channels), f32)],
        name="scan_back" if reverse else "scan",
    )(decay, inject)


def outer_kernel(n_dp, first_steps, left1, right1, left2, right2, out_ref):
    def multiply(left, right):
        total = dot(left[...], right[...], ((0,), (0,)))
        rows = total.shape[0] // n_dp
        for k in range(n_dp):
            out_ref[k, 0] = total[k * rows : (k + 1) * rows].astype(out_ref.dtype)

    j = pl.program_id(1)

    @pl.when(j < first_steps)
    def _():
        multiply(left1, right1)

    @pl.when(j >= first_steps)
    def _():
        multiply(left2, right2)


def outer_pair(left1, right1, left2, right2, n_dp, n_col, columns, name):
    length, width = left1.shape
    part = width // n_col
    steps1, steps2 = right1.shape[1] // columns, right2.shape[1] // columns
    count = (steps1 + steps2) * columns
    left_block = pl.BlockSpec((length, part), lambda i, j: (0, i))
    return pl.pallas_call(
        functools.partial(outer_kernel, n_dp, steps1),
        grid=(n_col, steps1 + steps2),
        out_shape=jax.ShapeDtypeStruct((n_dp, n_col, part // n_dp, count), low),
        in_specs=[
            left_block,
            pl.BlockSpec((length, columns), lambda i, j: (0, jnp.minimum(j, steps1 - 1))),
            left_block,
            pl.BlockSpec((length, columns), lambda i, j: (0, jnp.maximum(j - steps1, 0))),
        ],
        out_specs=pl.BlockSpec((n_dp, 1, part // n_dp, columns), lambda i, j: (0, i, 0, j)),
        compiler_params=pltpu.CompilerParams(vmem_limit_bytes=48 * MIB),
        cost_estimate=pl.CostEstimate(
            flops=2 * length * width * count,
            bytes_accessed=2 * (2 * length * width + length * count + width * count),
            transcendentals=0,
        ),
        name=name,
    )(left1, right1, left2, right2)


def dot(a, b, dims=((1,), (0,))):
    return lax.dot_general(a, b, (dims, ((), ())), preferred_element_type=f32)


def neighbour(x, axis, by):
    length = lax.axis_size(axis)
    pairs = [(i, i + by) for i in range(length) if 0 <= i + by < length]
    return lax.ppermute(x, axis, pairs)


def places_of(rows, lengths):
    ends = jnp.cumsum(lengths)
    starts = ends - lengths
    inside = (rows[:, None] >= starts[None, :]) & (rows[:, None] < ends[None, :])
    return rows - jnp.sum(jnp.where(inside, starts[None, :], 0), axis=1)


def lru_coeffs(pre_in, pre_rate, inputs, decay, reset):
    input_gate = jax.nn.sigmoid(pre_in)
    rate_gate = jax.nn.sigmoid(pre_rate)
    log_decay = -8.0 * rate_gate * jax.nn.softplus(decay)
    decay_factor = jnp.where(reset, 0.0, jnp.exp(log_decay))
    scaling = jnp.where(reset, 1.0, jnp.sqrt(-jnp.expm1(2.0 * log_decay)))
    return (decay_factor, inputs * input_gate * scaling)


def body(
    tokens,
    cotangent,
    rec_in,
    rec_out,
    gates,
    gate_bias,
    decay,
    conv_w,
    conv_b,
    gains,
    mlp_in,
    mlp_out,
    lengths,
    order,
):
    n_dp, n_row, n_col = (lax.axis_size(a) for a in ("dp", "row", "col"))
    dp, row, col = (lax.axis_index(a) for a in ("dp", "row", "col"))
    given, part = tokens.shape
    own = given // n_col
    group = given * n_row
    width = part * n_col
    taps = conv_w.shape[0]
    blocks, bw = gates.shape[1], gates.shape[2]
    half = rec_out.shape[0]
    hidden_half = mlp_out.shape[0]
    tiles = hidden_half // LANES
    wide = -(-tiles // n_col)
    span = wide * LANES
    shared = n_col * bw
    chans = bw + LANES

    geo = (n_col, part, bw, tiles, wide)
    x_all, w_rec, gains_all = open_gather(tokens, rec_in, gains, geo)
    gains_all = gains_all.transpose(1, 0, 2).reshape(gains.shape[0], width)
    w_x, w_y = w_rec[:, : 2 * bw], w_rec[:, 2 * bw :]

    def own_rows(x):
        return lax.dynamic_slice_in_dim(x, (row * n_col + col) * own, own, axis=0)

    def home_rows(x):
        dealt = lax.all_to_all(x.reshape(own, n_col, part).transpose(1, 0, 2), "col", 0, 0)
        return dealt.reshape(given, part)

    tile_at = shared + (col // 2) * LANES
    tile_owner = col % 2 == 0

    def own_channels(x):
        blk = lax.dynamic_slice_in_dim(x, col * bw, bw, axis=-1)
        tile = lax.dynamic_slice_in_dim(x, tile_at, LANES, axis=-1)
        return jnp.concatenate([blk, tile], axis=-1)

    def block_channels(x):
        blk = lax.dynamic_slice_in_dim(x, col * bw, bw, axis=-1)
        return jnp.concatenate([blk, x[..., shared:]], axis=-1)

    bias = own_channels(gate_bias)
    decay_o = own_channels(decay)
    conv_w_c = block_channels(conv_w)
    conv_b_c = block_channels(conv_b)
    conv_w_o = own_channels(conv_w)
    gates_blk = lax.dynamic_index_in_dim(gates, col, axis=1, keepdims=False)
    gates_five = gates[:, n_col]
    gates_tile = lax.dynamic_slice_in_dim(gates_five, (col // 2) * LANES, LANES, axis=2)
    gates_rows = lax.dynamic_slice_in_dim(gates_five, (col // 2) * LANES, LANES, axis=1)
    channel_ok = (jnp.arange(chans) < bw) | tile_owner

    base = dp * group
    places_ext = places_of(base + jnp.arange(group + taps - 1, dtype=jnp.int32), lengths)
    places = places_ext[:group]
    reset = (places == 0)[:, None]

    n1, x_rows, y_branch, pre_both, conv_low, state, branch, first, g_all, w_out, w_in, w_down = rec_forward(
        x_all,
        w_rec,
        (
            gains_all[0:1],
            gates_blk,
            gates_tile,
            bias,
            jax.nn.softplus(decay_o)[None, :],
            conv_w_c,
            conv_b_c[None, :],
        ),
        jnp.broadcast_to(places[:, None], (group, LANES)),
        cotangent,
        rec_out,
        mlp_in,
        mlp_out,
        geo,
    )
    inputs = own_rows(x_all).astype(f32)
    upstream = own_rows(g_all).astype(f32)
    sumsq_one = jnp.sum(inputs * inputs, axis=-1, keepdims=True)
    scale_one = lax.rsqrt(sumsq_one / width + epsilon)
    x_ext = x_rows[8 - (taps - 1) :]
    conv_blk, conv_five = conv_low[:, :bw], conv_low[:, bw:]
    conv_o = jnp.concatenate(
        [conv_blk, lax.dynamic_slice_in_dim(conv_five, (col // 2) * LANES, LANES, axis=1)], axis=1
    ).astype(f32)
    pre = [pre_both[:, :chans], pre_both[:, chans:]]
    factor, _ = lru_coeffs(pre[0], pre[1], conv_o, decay_o, reset)
    state_in = first[7:]
    out_one = multiply_scatter(branch, w_out, False, 6, "out_one")
    resid = inputs + out_one
    sumsq_two = jnp.sum(resid * resid, axis=-1, keepdims=True)
    scale_two = lax.rsqrt(sumsq_two / width + epsilon)
    normed_two = (resid * scale_two * gains_all[1]).astype(low)

    def spare(at):
        return spare_window(at, tiles, n_col, wide)

    n2, hidden, d_glu = glu(normed_two, w_in, w_down, g_all, spare)
    g_mlp = outer_pair(n2, d_glu, g_all, hidden, n_dp, n_col, 512, "outer_mlp")
    d_glu, hidden, g_mlp = lax.optimization_barrier((d_glu, hidden, g_mlp))
    sum_mlp = lax.psum_scatter(g_mlp, "dp", scatter_dimension=0)
    d_normed_two = multiply_scatter(d_glu, w_in, True, 7, "d_normed_two")
    gained_two = gains_all[1] * d_normed_two
    inner_two = jnp.sum(gained_two * resid, axis=-1, keepdims=True)
    grad_gain_two = jnp.sum(d_normed_two * resid * scale_two, axis=0)
    d_resid = upstream + scale_two * gained_two - resid * scale_two**3 * (inner_two / width)
    d_out, d_branch = gather_branch(d_resid.astype(low), w_out)

    d_branch = jnp.where(channel_ok, d_branch, 0.0)
    _, mix_back = jax.vjp(lambda state_v, gate_v: state_v * gelu(gate_v), state, y_branch)
    d_state, d_y = mix_back(d_branch)
    message, until = scan_rows(factor, factor * d_state, True)
    message_in = neighbour(message[:8], "dp", -1)[:1]
    message = message + until * message_in
    grad_state = d_state + jnp.concatenate([message[1:], message_in], axis=0)
    state_prev = jnp.concatenate([state_in, state[:-1]], axis=0)
    _, coef_back = jax.vjp(
        lambda a, b, c, d: lru_coeffs(a, b, c, d, reset), pre[0], pre[1], conv_o, decay_o
    )
    d_pre_in, d_pre_rate, d_conv, g_decay = coef_back((grad_state * state_prev, grad_state))
    d_pre = [d_pre_in.astype(low), d_pre_rate.astype(low)]
    tiles_here = jnp.concatenate([d[:, bw:] for d in d_pre], axis=1)
    tiles_there = lax.ppermute(tiles_here, "col", [(i, i ^ 2) for i in range(n_col)])
    low_half = col // 2 == 0
    d_conv_parts = []
    d_five = []
    for j in range(2):
        here = d_pre[j][:, bw:]
        there = tiles_there[:, j * LANES : (j + 1) * LANES]
        d_five.append(
            jnp.where(
                low_half,
                jnp.concatenate([here, there], axis=1),
                jnp.concatenate([there, here], axis=1),
            )
        )
        d_conv_parts.append(
            jnp.concatenate(
                [
                    dot(d_pre[j][:, :bw], gates_blk[j], ((1,), (1,))),
                    dot(d_five[j], gates_rows[j], ((1,), (1,))),
                ],
                axis=1,
            )
        )
    d_conv = d_conv + d_conv_parts[0] + d_conv_parts[1]
    g_gates = jnp.stack(
        [
            jnp.concatenate(
                [
                    dot(conv_blk, d_pre[j][:, :bw], ((0,), (0,))),
                    dot(conv_five, d_pre[j][:, bw:], ((0,), (0,))),
                ],
                axis=1,
            )
            for j in range(2)
        ]
    )
    g_bias = [jnp.sum(d.astype(f32), axis=0) for d in d_pre]
    later = neighbour(d_conv[:8], "dp", -1)[: taps - 1]
    d_ext = jnp.concatenate([d_conv, later], axis=0)
    x_own = jnp.concatenate(
        [x_ext[:, :bw], lax.dynamic_slice_in_dim(x_ext, bw + (col // 2) * LANES, LANES, axis=1)],
        axis=1,
    )
    d_x = jnp.zeros_like(d_conv)
    g_taps = []
    for t in range(taps):
        ahead = d_ext[t : t + group]
        valid = (places_ext[t : t + group] >= t)[:, None]
        d_x = d_x + jnp.where(valid, conv_w_o[t][None, :] * ahead, 0.0)
        lagged = x_own[taps - 1 - t : taps - 1 - t + group]
        g_taps.append(jnp.sum(jnp.where((places >= t)[:, None], d_conv * lagged, 0.0), axis=0))
    g_conv_b = jnp.sum(d_conv, axis=0)
    d_x_low = jnp.where(channel_ok, d_x, 0.0).astype(low)
    d_y_low = jnp.where(channel_ok, d_y, 0.0).astype(low)
    d_rec = jnp.concatenate([d_x_low, d_y_low], axis=1)
    w_x_own = jnp.concatenate(
        [w_x[:, :bw], lax.dynamic_slice_in_dim(w_x, bw + (col // 2) * LANES, LANES, axis=1)], axis=1
    )
    w_back = jnp.concatenate([w_x_own, w_y], axis=1)
    g_rec = outer_pair(n1, d_rec, d_out, branch, n_dp, n_col, chans, "outer_rec")
    g_rec, d_rec = lax.optimization_barrier((g_rec, d_rec))
    d_normed_one = multiply_scatter(d_rec, w_back, True, 9, "d_normed_one")
    g_rec, g_gates, sum_mlp, d_normed_one, hidden = lax.optimization_barrier(
        (g_rec, g_gates, sum_mlp, d_normed_one, hidden)
    )
    gate_sums = lax.psum_scatter(
        g_gates.astype(low).reshape(n_dp, 2 * bw // n_dp, chans), "dp", scatter_dimension=0
    )
    g_rec, gate_sums = lax.optimization_barrier((g_rec, gate_sums))
    sum_rec = lax.psum_scatter(g_rec, "dp", scatter_dimension=0)
    out_two = multiply_scatter(hidden, w_down, False, 8, "out_two")
    result = (resid + out_two).astype(low)
    gained_one = gains_all[0] * d_normed_one
    inner_one = jnp.sum(gained_one * inputs, axis=-1, keepdims=True)
    grad_gain_one = jnp.sum(d_normed_one * inputs * scale_one, axis=0)
    d_input = d_resid + scale_one * gained_one - inputs * scale_one**3 * (inner_one / width)

    result = home_rows(result)
    grad_input = home_rows(d_input.astype(low))

    def windows(got, first):
        return [
            got[c][..., first + (LANES if c > n_col - 1 - (wide * n_col - tiles) else 0) : first + span]
            for c in range(n_col)
        ]

    def channels_of(got, first):
        return [got[c][..., first : first + bw] for c in range(n_col)] + [
            got[c][..., first + bw : first + chans] for c in range(0, n_col, 2)
        ]

    dealt = lax.all_to_all(sum_mlp, "col", 0, 0)
    grad_mlp_in = jnp.stack(
        [jnp.concatenate(windows(dealt[..., j * span : (j + 1) * span], 0), axis=-1) for j in range(2)]
    ).astype(f32)
    grad_mlp_out = jnp.concatenate(windows(dealt[..., 2 * span :], 0), axis=-1).astype(f32).T
    recs = lax.all_to_all(sum_rec, "col", 0, 0)
    grad_rec_in = jnp.stack(
        [jnp.concatenate(channels_of(recs, j * chans), axis=-1) for j in range(2)]
    ).astype(f32)
    grad_rec_out = jnp.concatenate(channels_of(recs, 2 * chans), axis=-1).astype(f32).T

    small = jnp.where(channel_ok, jnp.stack(g_bias + [g_decay] + g_taps + [g_conv_b]), 0.0)
    square_sums = jnp.stack(
        [jnp.sum(sumsq_one), jnp.sum(out_one * out_one), jnp.sum(sumsq_two), jnp.sum(out_two * out_two)]
    )
    lines = small.shape[0]
    gain_sums = jnp.stack([grad_gain_one, grad_gain_two]).reshape(lines, 2 * width // lines)
    stat_block = jnp.pad(square_sums[None, :], ((0, lines - 1), (0, LANES - 4)))
    mixed = jnp.concatenate([small, gain_sums, stat_block], axis=1)
    sums, chan_sums, gate_parts = sum_everywhere(mixed, chans, gate_sums, n_dp, n_col)
    mine = jnp.concatenate(channels_of(chan_sums, 0), axis=-1)
    gain_rows = sums[:, : 2 * width // lines].reshape(2, width)
    grad_gains = lax.dynamic_slice_in_dim(gain_rows, col * part, part, axis=1)
    stats = jnp.sqrt(sums[0, 2 * width // lines :][:4] / (n_dp * group * width))
    gate_parts = gate_parts.reshape(n_col, 2, bw, chans).astype(f32)
    five = jnp.concatenate([gate_parts[c, :, :, bw:] for c in range(0, n_col, 2)], axis=-1)
    grad_gates = jnp.stack([gate_parts[c, :, :, :bw] for c in range(n_col)] + [five], axis=1)
    return (
        result,
        grad_input,
        grad_rec_in,
        grad_rec_out,
        grad_gates,
        mine[0:2],
        mine[2],
        mine[3 : 3 + taps],
        mine[3 + taps],
        grad_gains,
        grad_mlp_in,
        grad_mlp_out,
        stats,
    )


def solution(mesh):
    placed = (
        P(("dp", "row"), "col"),
        P(("dp", "row"), "col"),
        P(None, "col", "row"),
        P("row", "col"),
        P(None, "row", None, None),
        P(None, "row"),
        P("row"),
        P(None, "row"),
        P("row"),
        P(None, "col"),
        P(None, "col", "row"),
        P("row", "col"),
        P(),
        P(),
    )
    return jax.shard_map(
        body,
        mesh=mesh,
        in_specs=placed,
        out_specs=(
            P(("dp", "row"), "col"),
            P(("dp", "row"), "col"),
            P(None, ("col", "dp"), "row"),
            P("row", ("col", "dp")),
            P(None, "row", None, None),
            P(None, "row"),
            P("row"),
            P(None, "row"),
            P("row"),
            P(None, "col"),
            P(None, ("col", "dp"), "row"),
            P("row", ("col", "dp")),
            P(),
        ),
        check_vma=False,
    )
```

```python
import functools

import jax
import jax.numpy as jnp
from jax import lax
from jax.experimental import pallas as pl
from jax.experimental.pallas import tpu as pltpu
from jax.sharding import PartitionSpec as P

epsilon = 1e-06
LANES = 128
ROWS = 16
MIB = 1024 * 1024
MESH = pl.DeviceIdType.MESH
low = jnp.bfloat16
f32 = jnp.float32
anywhere = pl.BlockSpec(memory_space=pl.ANY)
in_vmem = pl.BlockSpec(memory_space=pltpu.VMEM)


def window_tile(col, tiles, n_col, wide):
    spare = wide * n_col - tiles
    return col * wide - jnp.maximum(col - (n_col - 1 - spare), 0)


def spare_window(col, tiles, n_col, wide):
    spare = wide * n_col - tiles
    return col > n_col - 1 - spare


class Place:
    def __init__(self):
        self.dp, self.row, self.col = (lax.axis_index(a) for a in ("dp", "row", "col"))

    def chip(self, k):
        return jnp.bitwise_xor(self.col, k)

    def device(self, name):
        if name == "core":
            return {"row": 1 - self.row}
        if name == "z":
            return {"dp": jnp.bitwise_xor(self.dp, 1)}
        if name in ("next", "prev"):
            n_dp = lax.axis_size("dp")
            return {"dp": lax.rem(self.dp + (1 if name == "next" else n_dp - 1), n_dp)}
        if name[0] == "d":
            return {"dp": jnp.bitwise_xor(self.dp, int(name[1:]))}
        return {"col": self.chip({"x": 1, "y": 2, "xy": 3}[name])}

    def meet(self, names):
        barrier = pltpu.get_barrier_semaphore()
        for name in names:
            pl.semaphore_signal(
                barrier, inc=1, device_id=self.device(name), device_id_type=MESH
            )
        pl.semaphore_wait(barrier, len(names))


class Copies:
    def __init__(self, place, send, recv):
        self.place, self.send, self.recv = place, send, recv
        self.made, self.landed, self.left, self.local = [], set(), set(), []

    def start(self, src, dst, to):
        i = len(self.made)
        copy = pltpu.make_async_remote_copy(
            src_ref=src,
            dst_ref=dst,
            send_sem=self.send.at[i],
            recv_sem=self.recv.at[i],
            device_id=self.place.device(to),
            device_id_type=MESH,
        )
        copy.start()
        self.made.append(copy)
        return i

    def land(self, *numbers):
        for i in numbers:
            if i not in self.landed:
                self.made[i].wait_recv()
                self.landed.add(i)

    def leave(self, *numbers):
        for i in numbers:
            if i not in self.left:
                self.made[i].wait_send()
                self.left.add(i)

    def keep(self, src, dst, sem):
        copy = pltpu.make_async_copy(src, dst, sem)
        copy.start()
        self.local.append(copy)
        return copy

    def finish(self):
        self.land(*range(len(self.made)))
        self.leave(*range(len(self.made)))


def share(rows):
    far = rows * 2 // 5 // ROWS * ROWS
    return rows - far, far


class Dealer:
    def __init__(self, copies):
        self.copies = copies
        self.waiting = []

    def deal(self, piece):
        place = self.copies.place
        odd = lax.rem(place.dp, 2)
        batch = []
        for name, k in (("x", 1), ("y", 2), ("xy", 3)):
            src, dst, rows = piece(place.chip(k), place.col)
            near, far = share(rows)
            start = pl.multiple_of(odd * far, ROWS)
            at = pl.ds(start, near)
            number = self.copies.start(src(at), dst(at), name)
            batch.append((k, number, piece))
        self.waiting.append(batch)

    def forward(self):
        place = self.copies.place
        odd = lax.rem(place.dp, 2)
        for k, number, piece in self.waiting.pop(0):
            self.copies.land(number)
            _, dst, rows = piece(place.col, place.chip(k))
            near, far = share(rows)
            at = pl.ds(pl.multiple_of(odd * near, ROWS), far)
            self.copies.start(dst(at), dst(at), "z")


def rows_of(ref, first, rows, lead=None, columns=None):
    def view(at):
        where = pl.ds(pl.multiple_of(first + at.start, ROWS), at.size)
        index = (where, columns if columns is not None else slice(None))
        return ref.at[index] if lead is None else ref.at[(lead,) + index]

    return view


def weight_pieces(geo, refs, outs):
    n_col, part, bw, tiles, wide = geo
    shared, span = n_col * bw, wide * LANES
    rec_in, rec_out, mlp_in, mlp_out = refs
    w_rec, w_out, w_in, w_down = outs

    def here(chip):
        return pl.multiple_of(chip * part, LANES)

    def blk(chip):
        return pl.multiple_of(chip * bw, LANES)

    def tile(chip):
        return pl.multiple_of(shared + lax.div(chip, 2) * LANES, LANES)

    def win(chip):
        return pl.multiple_of(window_tile(chip, tiles, n_col, wide) * LANES, LANES)

    def in_piece(ref, j, out, lead, source_at, size, column):
        def piece(dest, source):
            return (
                rows_of(ref, 0, part, j, pl.ds(pl.multiple_of(source_at(dest), LANES), size)),
                rows_of(out, here(source), part, lead, pl.ds(column, size)),
                part,
            )

        return piece

    def down_piece(ref, out, source_at, size, row):
        def piece(dest, source):
            return (
                rows_of(ref, source_at(dest), size),
                rows_of(out, row, size, None, pl.ds(here(source), part)),
                size,
            )

        return piece

    found = {}
    if rec_in is not None:
        found["rec_in"] = [
            in_piece(rec_in, 0, w_rec, None, blk, bw, 0),
            in_piece(rec_in, 0, w_rec, None, lambda chip: shared, bw, bw),
            in_piece(rec_in, 1, w_rec, None, blk, bw, 2 * bw),
            in_piece(rec_in, 1, w_rec, None, tile, LANES, 3 * bw),
        ]
    if rec_out is not None:
        found["rec_out"] = [
            down_piece(rec_out, w_out, blk, bw, 0),
            down_piece(rec_out, w_out, tile, LANES, bw),
        ]
    if mlp_in is not None:
        half = span // 2
        found["mlp_in"] = [
            in_piece(mlp_in, j, w_in, j, lambda chip, h=h: win(chip) + h * half, half, h * half)
            for j in range(2)
            for h in range(2)
        ]
    if mlp_out is not None:
        half = span // 2
        found["mlp_out"] = [
            down_piece(mlp_out, w_down, lambda chip, h=h: win(chip) + h * half, half, h * half)
            for h in range(2)
        ]
    return found


def keep_own(copies, pieces, sems, first):
    col = copies.place.col
    for i, piece in enumerate(pieces):
        src, dst, rows = piece(col, col)
        copies.keep(src(pl.ds(0, rows)), dst(pl.ds(0, rows)), sems.at[first + i])


class Gather:
    def __init__(self, copies, mine, at):
        self.copies, self.at = copies, at
        place = copies.place
        row, col = place.row, place.col
        self.first = [
            copies.start(mine(half), at(row, col, half), name)
            for half in (0, 1)
            for name in ("x", "y")
        ]
        self.own = copies.start(mine(None), at(row, col, None), "core")

    def pass_on(self):
        copies, place = self.copies, self.copies.place
        row = place.row
        x, y = place.chip(1), place.chip(2)
        x0, y0, x1, y1 = self.first
        copies.land(x0)
        self.round0 = copies.start(self.at(row, x, 0), self.at(row, x, 0), "y")
        copies.land(y0, y1)
        self.round1 = copies.start(self.at(row, y, 1), self.at(row, y, 1), "x")
        self.core_y = copies.start(self.at(row, y, None), self.at(row, y, None), "core")
        copies.land(x1)
        self.core_x = copies.start(self.at(row, x, None), self.at(row, x, None), "core")

    def last(self):
        copies, place = self.copies, self.copies.place
        corner = self.at(place.row, place.chip(3), None)
        copies.land(self.round0, self.round1)
        self.core_xy = copies.start(corner, corner, "core")


def block_gather(copies, source, target, sem):
    rows, part = source.shape
    cut = rows // 2

    def at(row, col, half):
        first = row * rows + (0 if half is None else half * cut)
        size = rows if half is None else cut
        return target.at[
            pl.ds(pl.multiple_of(first, ROWS), size), pl.ds(pl.multiple_of(col * part, LANES), part)
        ]

    def mine(half):
        return source if half is None else source.at[pl.ds(half * cut, cut), :]

    place = copies.place
    copies.keep(source, at(place.row, place.col, None), sem)
    return Gather(copies, mine, at)


AROUND = ("x", "y", "xy", "core", "z")


def open_kernel(geo, tokens, rec_in, gains, x_all, w_rec, gains_all, send, recv, local):
    place = Place()
    place.meet(AROUND)
    copies = Copies(place, send, recv)
    pieces = weight_pieces(geo, (rec_in, None, None, None), (w_rec, None, None, None))["rec_in"]
    dealer = Dealer(copies)
    dealer.deal(pieces[0])
    dealer.deal(pieces[1])
    gather = block_gather(copies, tokens, x_all, local.at[0])
    dealer.deal(pieces[2])
    dealer.deal(pieces[3])
    mine = gains_all.at[place.col]
    for name in ("x", "y", "xy"):
        copies.start(gains, mine, name)
    copies.keep(gains, mine, local.at[5])
    keep_own(copies, pieces, local, 1)
    dealer.forward()
    dealer.forward()
    gather.pass_on()
    dealer.forward()
    dealer.forward()
    gather.last()
    copies.finish()
    for copy in copies.local:
        copy.wait()


def open_gather(tokens, rec_in, gains, geo):
    n_col, part, bw, tiles, wide = geo
    width = part * n_col
    return pl.pallas_call(
        functools.partial(open_kernel, geo),
        out_shape=(
            jax.ShapeDtypeStruct((2 * tokens.shape[0], width), low),
            jax.ShapeDtypeStruct((width, 3 * bw + LANES), low),
            jax.ShapeDtypeStruct((n_col,) + gains.shape, f32),
        ),
        in_specs=[anywhere] * 3,
        out_specs=(anywhere,) * 3,
        scratch_shapes=[
            pltpu.SemaphoreType.DMA((37,)),
            pltpu.SemaphoreType.DMA((37,)),
            pltpu.SemaphoreType.DMA((6,)),
        ],
        compiler_params=pltpu.CompilerParams(collective_id=1, has_side_effects=True),
        name="open_gather",
    )(tokens, rec_in, gains)


def slot_gather(copies, local_ref, buf, own):
    cut = own // 2
    n_col = buf.shape[0] // 2

    def at(row, col, half):
        slot = buf.at[row * n_col + col]
        return slot if half is None else slot.at[pl.ds(half * cut, cut), :]

    def mine(half):
        return local_ref if half is None else local_ref.at[pl.ds(half * cut, cut), :]

    return Gather(copies, mine, at)


def tanh_parts(x):
    k = 0.7978845608028654
    square = x * x
    t = jnp.tanh(k * x * (1.0 + 0.044715 * square))
    value = 0.5 * x * (1.0 + t)
    slope = 0.5 * (1.0 + t) + 0.5 * x * (1.0 - t * t) * k * (1.0 + 3 * 0.044715 * square)
    return value, slope


def glu_kernel(
    spare, n2, w_in, w_down, g_all, n2_all, hidden, d_glu, buf, wi, wd, g, hid, dgl, send, recv, local
):
    place = Place()
    place.meet(("x", "y", "core"))
    copies = Copies(place, send, recv)
    own, width = n2.shape
    n_col = buf.shape[0] // 2
    span = wd.shape[0]
    step = 256
    gather = slot_gather(copies, n2, buf, own)
    me = place.row * n_col + place.col
    loads = [
        copies.keep(n2, buf.at[me], local.at[0]),
        copies.keep(w_in, wi, local.at[1]),
        copies.keep(w_down, wd, local.at[2]),
        copies.keep(g_all, g, local.at[3]),
    ]
    for load in loads:
        load.wait()
    hide = spare(place.col)

    def work(chip):
        slots = (chip, n_col + chip)
        rows = [pl.ds(pl.multiple_of(s * own, ROWS), own) for s in slots]
        n2_here = jnp.concatenate([buf[s] for s in slots], axis=0)
        g_here = jnp.concatenate([g[r, :] for r in rows], axis=0)

        def columns(i, carry):
            at = pl.ds(pl.multiple_of(i * step, LANES), step)
            up_at = pl.ds(pl.multiple_of(span + i * step, LANES), step)
            gate = dot(n2_here, wi[0, :, at])
            up = dot(n2_here, wi[1, :, at])
            d_hid = dot(g_here, wd[at, :], ((1,), (1,)))
            lane = lax.broadcasted_iota(jnp.int32, gate.shape, 1) + i * step
            used = (lane >= LANES) | jnp.logical_not(hide)
            up = jnp.where(used, up, 0.0)
            d_hid = jnp.where(used, d_hid, 0.0)
            value, slope = tanh_parts(gate)
            h = (value * up).astype(low)
            dg = (d_hid * up * slope).astype(low)
            du = (d_hid * value).astype(low)
            for n, r in enumerate(rows):
                part = slice(n * own, (n + 1) * own)
                hid[r, at] = h[part]
                dgl[r, at] = dg[part]
                dgl[r, up_at] = du[part]
            return carry

        lax.fori_loop(0, span // step, columns, 0)

    copies.land(gather.own)
    work(place.col)
    gather.pass_on()
    copies.land(gather.core_y)
    work(place.chip(2))
    gather.last()
    copies.land(gather.core_x)
    work(place.chip(1))
    copies.land(gather.core_xy)
    out_n2 = copies.keep(buf, n2_all, local.at[4])
    work(place.chip(3))
    out_h = copies.keep(hid, hidden, local.at[5])
    out_d = copies.keep(dgl, d_glu, local.at[6])
    copies.finish()
    out_n2.wait()
    out_h.wait()
    out_d.wait()


def glu(n2, w_in, w_down, g_all, spare):
    own, width = n2.shape
    group = g_all.shape[0]
    span = w_down.shape[0]
    n_all, h, d = pl.pallas_call(
        functools.partial(glu_kernel, spare),
        out_shape=(
            jax.ShapeDtypeStruct((group // own, own, width), low),
            jax.ShapeDtypeStruct((group, span), low),
            jax.ShapeDtypeStruct((group, 2 * span), low),
        ),
        in_specs=[anywhere] * 4,
        out_specs=(anywhere,) * 3,
        scratch_shapes=[
            pltpu.VMEM((group // own, own, width), low),
            pltpu.VMEM(w_in.shape, low),
            pltpu.VMEM(w_down.shape, low),
            pltpu.VMEM((group, width), low),
            pltpu.VMEM((group, span), low),
            pltpu.VMEM((group, 2 * span), low),
            pltpu.SemaphoreType.DMA((10,)),
            pltpu.SemaphoreType.DMA((10,)),
            pltpu.SemaphoreType.DMA((7,)),
        ],
        compiler_params=pltpu.CompilerParams(
            collective_id=3, has_side_effects=True, vmem_limit_bytes=58 * MIB
        ),
        cost_estimate=pl.CostEstimate(
            flops=6 * group * width * span, bytes_accessed=60 * MIB, transcendentals=group * span
        ),
        name="glu",
    )(n2, w_in, w_down, g_all)
    return n_all.reshape(group, width), h, d


def scatter_kernel(shape, finish, n_more, n_outs, homes, act, w, *refs):
    n_parts, across, own, width = shape
    more, refs = refs[:n_more], refs[n_more:]
    outs, refs = refs[:n_outs], refs[n_outs:]
    actv, wv, other, mine, from_core, from_x, from_y, turn, fin, back, send, recv, local, home_sem = refs[:14]
    held = refs[14:]
    place = Place()
    place.meet(("x", "y", "xy", "core") if homes else ("x", "y", "core"))
    copies = Copies(place, send, recv)
    cut = own // 2
    n_col = act.shape[0] // own // 2
    k = act.shape[1] // n_parts
    step = 256
    loads = [copies.keep(act, actv, local.at[0]), copies.keep(w, wv, local.at[1])]
    my_rows = pl.ds(pl.multiple_of((place.row * n_col + place.col) * own, ROWS), own)
    extra = []
    for i, (ref, buf) in enumerate(zip(more, held)):
        src = ref.at[my_rows, :] if ref.shape[0] > own else ref
        extra.append(copies.keep(src, buf, local.at[2 + i]))
    for load in loads:
        load.wait()
    top, bottom = pl.ds(0, cut), pl.ds(cut, cut)

    def work(j):
        chip = place.chip(j)
        slots = ((1 - place.row) * n_col + chip, place.row * n_col + chip)
        left = [
            jnp.concatenate(
                [
                    actv[pl.ds(pl.multiple_of(s * own, ROWS), own), n * k : (n + 1) * k]
                    for s in slots
                ],
                axis=0,
            )
            for n in range(n_parts)
        ]

        def columns(i, carry):
            at = pl.ds(pl.multiple_of(i * step, LANES), step)
            total = None
            for n in range(n_parts):
                if across:
                    right = wv[n, at, :] if n_parts > 1 else wv[at, :]
                    term = dot(left[n], right, ((1,), (1,)))
                else:
                    term = dot(left[n], wv[:, at])
                total = term if total is None else total + term
            other[j, :, at] = total[:own].astype(low)
            mine[j, :, at] = total[own:]
            return carry

        lax.fori_loop(0, width // step, columns, 0)
        return copies.start(other.at[j], from_core.at[j], "core")

    def add_core(j, number):
        copies.land(number)
        mine[j] = mine[j] + from_core[j].astype(f32)
        turn[j] = mine[j].astype(low)

    core3 = work(3)
    core1 = work(1)
    add_core(3, core3)
    x3 = copies.start(turn.at[3, top, :], from_x.at[0], "x")
    y3 = copies.start(turn.at[3, bottom, :], from_y.at[0], "y")
    core2 = work(2)
    add_core(1, core1)
    x1 = copies.start(turn.at[1, top, :], from_x.at[1], "x")
    core0 = work(0)
    add_core(2, core2)
    y2 = copies.start(turn.at[2, bottom, :], from_y.at[1], "y")
    copies.land(x3)
    turn[2, top, :] = (mine[2, top, :] + from_x[0].astype(f32)).astype(low)
    y_last = copies.start(turn.at[2, top, :], from_y.at[2], "y")
    copies.land(y3)
    turn[1, bottom, :] = (mine[1, bottom, :] + from_y[0].astype(f32)).astype(low)
    x_last = copies.start(turn.at[1, bottom, :], from_x.at[2], "x")
    add_core(0, core0)
    copies.land(x1, y2, y_last, x_last)
    fin[top, :] = mine[0, top, :] + from_x[1].astype(f32) + from_y[2].astype(f32)
    fin[bottom, :] = mine[0, bottom, :] + from_y[1].astype(f32) + from_x[2].astype(f32)
    for load in extra:
        load.wait()
    for ref in outs[(1 if homes else 0) :]:
        if ref.shape[0] == 8:
            ref[...] = jnp.zeros_like(ref)
    rows_at_once = 64

    def rows_done(i, carry):
        rows = pl.ds(pl.multiple_of(i * rows_at_once, rows_at_once), rows_at_once)
        finish(rows, fin, held, back, outs[(1 if homes else 0) :])
        return carry

    lax.fori_loop(0, own // rows_at_once, rows_done, 0)
    if homes:
        home = outs[0]
        part = width // n_col

        def columns_of(chip):
            return back.at[:, pl.ds(pl.multiple_of(chip * part, LANES), part)]

        spot = home.at[pl.ds(pl.multiple_of(place.col * own, ROWS), own), :]
        for name, j in (("xy", 3), ("x", 1), ("y", 2)):
            copies.start(columns_of(place.chip(j)), spot, name)
        stay = copies.keep(columns_of(place.col), spot, home_sem)
        stay.wait()
    copies.finish()


def multiply_scatter(act, w, across, number, name, finish, more, outs, homes):
    n_parts = w.shape[0] if w.ndim == 3 else 1
    group = act.shape[0]
    n_col = lax.axis_size("col")
    own = group // (2 * n_col)
    width = w.shape[-2] if across else w.shape[-1]
    held = [((own, r.shape[1]) if r.shape[0] > own else r.shape, r.dtype) for r in more]
    return pl.pallas_call(
        functools.partial(
            scatter_kernel, (n_parts, across, own, width), finish, len(more), len(outs), homes
        ),
        out_shape=tuple(jax.ShapeDtypeStruct(*s) for s in outs),
        in_specs=[anywhere] * (2 + len(more)),
        out_specs=tuple(anywhere if homes and i == 0 else in_vmem for i in range(len(outs))),
        scratch_shapes=[
            pltpu.VMEM(act.shape, low),
            pltpu.VMEM(w.shape, low),
            pltpu.VMEM((4, own, width), low),
            pltpu.VMEM((4, own, width), f32),
            pltpu.VMEM((4, own, width), low),
            pltpu.VMEM((3, own // 2, width), low),
            pltpu.VMEM((3, own // 2, width), low),
            pltpu.VMEM((4, own, width), low),
            pltpu.VMEM((own, width), f32),
            pltpu.VMEM((own, width), low),
            pltpu.SemaphoreType.DMA((13,)),
            pltpu.SemaphoreType.DMA((13,)),
            pltpu.SemaphoreType.DMA((2 + len(more),)),
            pltpu.SemaphoreType.DMA,
        ]
        + [pltpu.VMEM(*h) for h in held],
        compiler_params=pltpu.CompilerParams(
            collective_id=number, has_side_effects=True, vmem_limit_bytes=60 * MIB
        ),
        cost_estimate=pl.CostEstimate(
            flops=2 * group * width * act.shape[1], bytes_accessed=40 * MIB, transcendentals=0
        ),
        name=name,
    )(act, w, *more)


def square_sum(ref, row, x):
    ref[row : row + 1, :] += jnp.broadcast_to(jnp.sum(x * x, keepdims=True), (1, LANES))


def norm_scale(x):
    return lax.rsqrt(jnp.mean(x * x, axis=-1, keepdims=True) + epsilon)


def after_out_one(rows, fin, held, back, outs):
    x, gain = held
    resid_out, n2_out, squares = outs
    out_one = fin[rows, :]
    resid = x[rows, :].astype(f32) + out_one
    resid_out[rows, :] = resid
    n2_out[rows, :] = (resid * norm_scale(resid) * gain[1:2, :]).astype(low)
    square_sum(squares, 0, out_one)
    square_sum(squares, 1, resid)


def norm_back(d_normed, x, gain, grad_gain):
    scale = norm_scale(x)
    gained = gain * d_normed
    inner = jnp.mean(gained * x, axis=-1, keepdims=True)
    grad_gain[0:1, :] += jnp.sum(d_normed * x * scale, axis=0, keepdims=True)
    return scale * gained - x * (scale * scale * scale * inner)


def after_normed_two(rows, fin, held, back, outs):
    resid, upstream, gain = held
    d_resid_out, d_out, grad_gain = outs
    d_resid = upstream[rows, :].astype(f32) + norm_back(
        fin[rows, :], resid[rows, :], gain[1:2, :], grad_gain
    )
    d_resid_out[rows, :] = d_resid
    d_out[rows, :] = d_resid.astype(low)


def after_normed_one(rows, fin, held, back, outs):
    x, d_resid, gain = held
    grad_gain, squares = outs
    x_here = x[rows, :].astype(f32)
    passed = norm_back(fin[rows, :], x_here, gain[0:1, :], grad_gain)
    back[rows, :] = (d_resid[rows, :] + passed).astype(low)
    square_sum(squares, 0, x_here)


def after_out_two(rows, fin, held, back, outs):
    (resid,) = held
    (squares,) = outs
    out_two = fin[rows, :]
    back[rows, :] = (resid[rows, :] + out_two).astype(low)
    square_sum(squares, 0, out_two)


def start_deal(copies, source, target):
    col = copies.place.col
    for name, j in (("xy", 3), ("x", 1), ("y", 2)):
        copies.start(source.at[copies.place.chip(j)], target.at[col], name)


def deal_kernel(source, target, send, recv, local):
    place = Place()
    place.meet(("x", "y", "xy"))
    copies = Copies(place, send, recv)
    start_deal(copies, source, target)
    stay = copies.keep(source.at[place.col], target.at[place.col], local)
    copies.finish()
    stay.wait()


def deal_back(x, number, name):
    return pl.pallas_call(
        deal_kernel,
        out_shape=jax.ShapeDtypeStruct(x.shape, x.dtype),
        in_specs=[anywhere],
        out_specs=anywhere,
        scratch_shapes=[
            pltpu.SemaphoreType.DMA((3,)),
            pltpu.SemaphoreType.DMA((3,)),
            pltpu.SemaphoreType.DMA,
        ],
        compiler_params=pltpu.CompilerParams(collective_id=number, has_side_effects=True),
        name=name,
    )(x)


def sums_kernel(
    far,
    split,
    mixed,
    gate_part,
    grads_a,
    grads_b,
    sums_out,
    chans_out,
    gates_out,
    out_a,
    out_b,
    got,
    acc,
    ch,
    send,
    recv,
    local,
):
    place = Place()
    steps = [f"d{d}" for d in far if d & (d - 1) == 0]
    place.meet(("core", "x", "y", "xy") + tuple(f"d{d}" for d in far))
    copies = Copies(place, send, recv)
    dp, col = place.dp, place.col
    start_deal(copies, grads_a, out_a)
    start_deal(copies, grads_b, out_b)
    keeps = [
        copies.keep(grads_a.at[col], out_a.at[col], local.at[1]),
        copies.keep(grads_b.at[col], out_b.at[col], local.at[2]),
    ]
    own_gates = gates_out.at[col]
    stay = copies.keep(gate_part, own_gates.at[dp], local.at[0])
    parts = [copies.start(gate_part, own_gates.at[dp], f"d{d}") for d in far]
    acc[0] = mixed[...]
    n = 0
    for name in steps:
        copies.land(copies.start(acc.at[n], got.at[n], name))
        acc[n + 1] = acc[n] + got[n]
        n += 1
    stay.wait()
    copies.land(*parts)
    half = gates_out.shape[1] // 2
    halves = (pl.ds(0, half), pl.ds(half, half))

    def gate_view(chip, h):
        return gates_out.at[chip, halves[h]]

    direct = {
        (name, h): copies.start(gate_view(col, h), gate_view(col, h), name)
        for h in (0, 1)
        for name in ("x", "y")
    }
    ch[col] = acc[n][:, :split]
    x_ch = copies.start(ch.at[col], ch.at[col], "x")
    rest = slice(split, None)
    for name in ("core", "x", "y"):
        number = copies.start(acc.at[n, :, rest], got.at[n, :, rest], name)
        if name == "y":
            copies.land(x_ch)
            pair = pl.ds(lax.div(col, 2) * 2, 2)
            y_ch = copies.start(ch.at[pair], ch.at[pair], "y")
        copies.land(number)
        acc[n + 1, :, rest] = acc[n, :, rest] + got[n, :, rest]
        n += 1
    copies.land(direct["x", 0])
    far_x = gate_view(place.chip(1), 0)
    copies.start(far_x, far_x, "y")
    copies.land(direct["y", 1])
    far_y = gate_view(place.chip(2), 1)
    copies.start(far_y, far_y, "x")
    sums_out[...] = acc[n, :, rest]
    copies.land(y_ch)
    chans_out[...] = ch[...]
    copies.finish()
    for copy in keeps:
        copy.wait()


def sum_everywhere(mixed, split, gate_part, grads_a, grads_b, n_dp, n_col):
    far = tuple(range(1, n_dp))
    stages = len([d for d in far if d & (d - 1) == 0]) + 3
    count = 2 * len(far) + stages + 14
    rows, columns = mixed.shape
    return pl.pallas_call(
        functools.partial(sums_kernel, far, split),
        out_shape=(
            jax.ShapeDtypeStruct((rows, columns - split), f32),
            jax.ShapeDtypeStruct((n_col, rows, split), f32),
            jax.ShapeDtypeStruct((n_col, n_dp) + gate_part.shape, gate_part.dtype),
            jax.ShapeDtypeStruct(grads_a.shape, grads_a.dtype),
            jax.ShapeDtypeStruct(grads_b.shape, grads_b.dtype),
        ),
        in_specs=[in_vmem] + [anywhere] * 3,
        out_specs=(in_vmem, in_vmem) + (anywhere,) * 3,
        scratch_shapes=[
            pltpu.VMEM((stages, rows, columns), f32),
            pltpu.VMEM((stages + 1, rows, columns), f32),
            pltpu.VMEM((n_col, rows, split), f32),
            pltpu.SemaphoreType.DMA((count,)),
            pltpu.SemaphoreType.DMA((count,)),
            pltpu.SemaphoreType.DMA((3,)),
        ],
        compiler_params=pltpu.CompilerParams(collective_id=5, has_side_effects=True),
        name="small_sums",
    )(mixed, gate_part, grads_a, grads_b)


def one_less_exp(z):
    series = 1.0 + z / 6.0
    for n in (5.0, 4.0, 3.0, 2.0):
        series = 1.0 + z / n * series
    return jnp.where(z > -0.1, -z * series, 1.0 - jnp.exp(z))


def scan_tile(a, u, reverse):
    rows = a.shape[0]
    index = lax.broadcasted_iota(jnp.int32, a.shape, 0)
    by = 1
    while by < rows:
        turn = rows - by if reverse else by
        inside = index < rows - by if reverse else index >= by
        u = u + a * jnp.where(inside, pltpu.roll(u, turn, 0), 0.0)
        a = a * jnp.where(inside, pltpu.roll(a, turn, 0), 1.0)
        by *= 2
    return a, u


def forward_kernel(
    geo,
    x_all,
    w_rec,
    gain,
    gates_blk,
    gates_tile,
    bias,
    soft,
    conv_w,
    conv_b,
    places,
    cotangent,
    rec_out,
    mlp_in,
    mlp_out,
    n1_out,
    x_out,
    y_out,
    pre_out,
    c_out,
    state_out,
    branch_out,
    first_out,
    g_all,
    w_out,
    w_in,
    w_down,
    xv,
    wv,
    before,
    xb,
    yv,
    prev,
    cv,
    hv,
    pv,
    bv,
    carry,
    first,
    send,
    recv,
    local,
):
    place = Place()
    place.meet(AROUND + ("next", "prev"))
    copies = Copies(place, send, recv)
    n_col, part, bw, tiles, wide = geo
    chans = bw + LANES
    group, width = xv.shape
    tile = 256
    n_tiles = group // tile
    loads = [copies.keep(x_all, xv, local.at[0]), copies.keep(w_rec, wv, local.at[1])]
    halo = copies.start(x_all.at[pl.ds(group - ROWS, ROWS), :], before, "next")
    found = weight_pieces(geo, (None, rec_out, mlp_in, mlp_out), (None, w_out, w_in, w_down))
    pieces = found["rec_out"] + found["mlp_in"] + found["mlp_out"]
    dealer = Dealer(copies)
    for piece in pieces[:5]:
        dealer.deal(piece)
    keep_own(copies, pieces, local, 2)
    for load in loads:
        load.wait()
    high_tile = place.col >= 2
    idle_tile = lax.rem(place.col, 2) == 1

    def normed(x):
        x = x.astype(f32)
        scale = lax.rsqrt(jnp.sum(x * x, axis=-1, keepdims=True) / width + epsilon)
        return (x * scale * gain[...]).astype(low)

    copies.land(halo)
    xb[0:8, :] = dot(normed(before[...]), wv[:, : 2 * bw])[ROWS - 8 :]
    carry[0:1] = jnp.zeros_like(carry[0:1])
    carry[1:2] = jnp.ones_like(carry[1:2])

    def work(i, unused):
        r0 = pl.multiple_of(i * tile, tile)
        rows = pl.ds(r0, tile)
        n1 = normed(xv[rows, :])
        xv[rows, :] = n1
        both = dot(n1, wv[...])
        xb[pl.ds(pl.multiple_of(r0 + 8, 8), tile), :] = both[:, : 2 * bw]
        yv[rows, :] = both[:, 2 * bw :]
        spot = places[rows, :]
        reach = xb[pl.ds(r0, tile + 8), :]
        conv = []
        for lane in range(2 * bw // LANES):
            at = slice(lane * LANES, (lane + 1) * LANES)
            near = reach[:, at]
            total = conv_b[0:1, at] + conv_w[0:1, at] * near[8:]
            for t in range(1, conv_w.shape[0]):
                lagged = pltpu.roll(near, t, 0)[8:]
                total = total + jnp.where(spot >= t, conv_w[t : t + 1, at] * lagged, 0.0)
            conv.append(total.astype(low))
        c = jnp.concatenate(conv, axis=1)
        cv[rows, :] = c
        pre = [
            jnp.concatenate([dot(c[:, :bw], gates_blk[j]), dot(c[:, bw:], gates_tile[j])], axis=1)
            + bias[j : j + 1, :]
            for j in range(2)
        ]
        prev[rows, :chans] = pre[0]
        prev[rows, chans:] = pre[1]
        reset = spot == 0
        for lane in range(chans // LANES):
            at = slice(lane * LANES, (lane + 1) * LANES)
            if lane * LANES < bw:
                own_c = conv[lane].astype(f32)
            else:
                own_c = jnp.where(high_tile, conv[lane + 1].astype(f32), conv[lane].astype(f32))
            log_a = -8.0 * jax.nn.sigmoid(pre[1][:, at]) * soft[0:1, at]
            a = jnp.where(reset, 0.0, jnp.exp(log_a))
            m = jnp.where(reset, 1.0, jnp.sqrt(one_less_exp(2.0 * log_a)))
            u = own_c * jax.nn.sigmoid(pre[0][:, at]) * m
            a, u = scan_tile(a, u, False)
            h = u + a * carry[0:1, at]
            p = a * carry[1:2, at]
            hv[rows, at] = h
            pv[rows, at] = p
            carry[0:1, at] = h[tile - 1 :]
            carry[1:2, at] = p[tile - 1 :]
        return unused

    third = n_tiles // 3
    lax.fori_loop(0, third, work, 0)
    dealer.forward()
    dealer.forward()
    dealer.deal(pieces[5])
    dealer.forward()
    lax.fori_loop(third, 2 * third, work, 0)
    dealer.forward()
    dealer.deal(pieces[6])
    lax.fori_loop(2 * third, n_tiles, work, 0)
    dealer.forward()
    dealer.deal(pieces[7])
    state_in = copies.start(hv.at[pl.ds(group - 8, 8), :], first, "next")
    outs = [
        copies.keep(src, dst, local.at[10 + i])
        for i, (src, dst) in enumerate(
            ((xv, n1_out), (xb, x_out), (yv, y_out), (prev, pre_out), (cv, c_out))
        )
    ]
    copies.land(state_in)
    copies.leave(state_in)
    before_all = first[7:8, :]

    def finish(i, unused):
        rows = pl.ds(pl.multiple_of(i * tile, tile), tile)
        for lane in range(chans // LANES):
            at = slice(lane * LANES, (lane + 1) * LANES)
            state = hv[rows, at] + pv[rows, at] * before_all[:, at]
            hv[rows, at] = state
            value, _ = tanh_parts(yv[rows, at])
            b = state * value
            if lane * LANES >= bw:
                b = jnp.where(idle_tile, 0.0, b)
            bv[rows, at] = b.astype(low)
        return unused

    lax.fori_loop(0, n_tiles, finish, 0)
    outs += [
        copies.keep(hv, state_out, local.at[15]),
        copies.keep(bv, branch_out, local.at[16]),
        copies.keep(first, first_out, local.at[17]),
    ]
    dealer.forward()
    gather = block_gather(copies, cotangent, g_all, local.at[18])
    dealer.forward()
    dealer.forward()
    gather.pass_on()
    gather.last()
    copies.finish()
    for copy in copies.local:
        if not any(copy is load for load in loads):
            copy.wait()


def rec_forward(x_all, w_rec, params, places, cotangent, rec_out, mlp_in, mlp_out, geo):
    n_col, part, bw, tiles, wide = geo
    width, span, chans = part * n_col, wide * LANES, bw + LANES
    group = x_all.shape[0]

    def of(shape, dtype):
        return jax.ShapeDtypeStruct(shape, dtype)

    kept = [
        ((group, width), low),
        ((group + 8, 2 * bw), f32),
        ((group, chans), f32),
        ((group, 2 * chans), f32),
        ((group, 2 * bw), low),
        ((group, chans), f32),
        ((group, chans), low),
        ((8, chans), f32),
    ]
    dealt = [((group, width), low), ((chans, width), low), ((2, width, span), low), ((span, width), low)]
    copy_count = 1 + 6 * 8 + 10 + 1
    return pl.pallas_call(
        functools.partial(forward_kernel, geo),
        out_shape=tuple(of(*s) for s in kept + dealt),
        in_specs=[anywhere] * 2 + [in_vmem] * 8 + [anywhere] * 4,
        out_specs=(anywhere,) * 12,
        scratch_shapes=[
            pltpu.VMEM((group, width), low),
            pltpu.VMEM(w_rec.shape, low),
            pltpu.VMEM((ROWS, width), low),
            pltpu.VMEM((group + 8, 2 * bw), f32),
            pltpu.VMEM((group, chans), f32),
            pltpu.VMEM((group, 2 * chans), f32),
            pltpu.VMEM((group, 2 * bw), low),
            pltpu.VMEM((group, chans), f32),
            pltpu.VMEM((group, chans), f32),
            pltpu.VMEM((group, chans), low),
            pltpu.VMEM((8, chans), f32),
            pltpu.VMEM((8, chans), f32),
            pltpu.SemaphoreType.DMA((copy_count,)),
            pltpu.SemaphoreType.DMA((copy_count,)),
            pltpu.SemaphoreType.DMA((19,)),
        ],
        compiler_params=pltpu.CompilerParams(
            collective_id=2, has_side_effects=True, vmem_limit_bytes=58 * MIB
        ),
        name="rec_forward",
    )(x_all, w_rec, *params, places, cotangent, rec_out, mlp_in, mlp_out)


def backward_kernel(
    geo,
    d_out,
    w_out,
    y_in,
    state_in,
    first_in,
    pre_in,
    c_in,
    x_in,
    gates_blk,
    gates_rows,
    soft,
    conv_w,
    places,
    d_all,
    d_rec_out,
    gate_out,
    sums,
    buf,
    wv,
    dbv,
    yv,
    hs,
    prev,
    cv,
    xb,
    ghv,
    qv,
    dpv,
    there,
    dcv,
    drv,
    gg,
    glo,
    gfar,
    carry,
    message,
    send,
    recv,
    local,
):
    place = Place()
    n_dp = glo.shape[0]
    far = [f"d{d}" for d in range(1, n_dp)]
    place.meet(["x", "y", "core", "next", "prev"] + far)
    copies = Copies(place, send, recv)
    n_col, part, bw, tiles, wide = geo
    chans = bw + LANES
    own = d_out.shape[0]
    group = yv.shape[0]
    tile = 256
    n_tiles = group // tile
    lanes = [slice(k * LANES, (k + 1) * LANES) for k in range(chans // LANES)]
    gather = slot_gather(copies, d_out, buf, own)
    me = place.row * n_col + place.col
    load = copies.keep(w_out, wv, local.at[0])
    mine = copies.keep(d_out, buf.at[me], local.at[1])
    loads = [
        copies.keep(src, dst, local.at[2 + i])
        for i, (src, dst) in enumerate(
            (
                (y_in, yv),
                (state_in, hs.at[pl.ds(8, group), :]),
                (first_in, hs.at[pl.ds(0, 8), :]),
                (pre_in, prev),
                (c_in, cv),
                (x_in, xb),
            )
        )
    ]
    load.wait()
    mine.wait()
    high_tile = place.col >= 2
    idle_tile = lax.rem(place.col, 2) == 1

    def work(chip):
        slots = (chip, n_col + chip)
        value = dot(jnp.concatenate([buf[s] for s in slots], axis=0), wv[...], ((1,), (1,)))
        for n, s in enumerate(slots):
            rows = pl.ds(pl.multiple_of(s * own, ROWS), own)
            dbv[rows, :] = value[n * own : (n + 1) * own]

    copies.land(gather.own)
    work(place.col)
    gather.pass_on()
    copies.land(gather.core_y)
    work(place.chip(2))
    gather.last()
    copies.land(gather.core_x)
    work(place.chip(1))
    copies.land(gather.core_xy)
    out = copies.keep(buf, d_all, local.at[8])
    work(place.chip(3))
    for each in loads:
        each.wait()

    def coeffs(rows, at, spot):
        rate = jax.nn.sigmoid(prev[rows, slice(chans + at.start, chans + at.stop)])
        log_a = -8.0 * rate * soft[0:1, at]
        return rate, log_a, jnp.where(spot == 0, 0.0, jnp.exp(log_a))

    carry[0:1] = jnp.zeros_like(carry[0:1])
    carry[1:2] = jnp.ones_like(carry[1:2])

    def scan_back(k, unused):
        r0 = pl.multiple_of((n_tiles - 1 - k) * tile, tile)
        rows = pl.ds(r0, tile)
        spot = places[rows, :]
        last = lax.broadcasted_iota(jnp.int32, spot.shape, 0) == tile - 1
        for at in lanes:
            d_branch = dbv[rows, at]
            if at.start >= bw:
                d_branch = jnp.where(idle_tile, 0.0, d_branch)
            value, slope = tanh_parts(yv[rows, at])
            state = hs[pl.ds(pl.multiple_of(r0 + 8, 8), tile), at]
            d_state = d_branch * value
            drv[rows, slice(chans + at.start, chans + at.stop)] = (d_branch * state * slope).astype(low)
            _, _, a = coeffs(rows, at, spot)
            a, u = scan_tile(a, a * d_state, True)
            m = u + a * carry[0:1, at]
            q = a * carry[1:2, at]
            ghv[rows, at] = d_state + jnp.where(last, carry[0:1, at], pltpu.roll(m, tile - 1, 0))
            qv[rows, at] = jnp.where(last, carry[1:2, at], pltpu.roll(q, tile - 1, 0))
            carry[0:1, at] = m[0:1]
            carry[1:2, at] = q[0:1]
        return unused

    lax.fori_loop(0, n_tiles, scan_back, 0)
    arriving = copies.start(carry, message, "prev")
    copies.land(arriving)
    sums[...] = jnp.zeros_like(sums)
    gg[...] = jnp.zeros_like(gg)

    def through_gates(k, unused):
        r0 = pl.multiple_of(k * tile, tile)
        rows = pl.ds(r0, tile)
        spot = places[rows, :]
        reset = spot == 0
        for n, at in enumerate(lanes):
            g = ghv[rows, at] + qv[rows, at] * message[0:1, at]
            before = pltpu.roll(hs[pl.ds(r0, tile + 8), at], 1, 0)[8:]
            if at.start < bw:
                c = cv[rows, at].astype(f32)
            else:
                c = jnp.where(
                    high_tile,
                    cv[rows, slice(at.start + LANES, at.stop + LANES)].astype(f32),
                    cv[rows, at].astype(f32),
                )
            gate = jax.nn.sigmoid(prev[rows, at])
            rate, log_a, a = coeffs(rows, at, spot)
            m = jnp.where(reset, 1.0, jnp.sqrt(one_less_exp(2.0 * log_a)))
            gated = gate * m
            d_log = jnp.where(reset, 0.0, g * before * a - g * c * gate * a * a / m)
            d_pre_in = (g * c * gated * (1.0 - gate)).astype(low)
            d_pre_rate = (d_log * (-8.0 * soft[0:1, at]) * rate * (1.0 - rate)).astype(low)
            dpv[rows, at] = d_pre_in
            dpv[rows, slice(chans + at.start, chans + at.stop)] = d_pre_rate
            dcv[rows, at] = g * gated
            sums[0:1, at] += jnp.sum(d_pre_in.astype(f32), axis=0, keepdims=True)
            sums[1:2, at] += jnp.sum(d_pre_rate.astype(f32), axis=0, keepdims=True)
            sums[2:3, at] += jnp.sum(d_log * (-8.0 * rate), axis=0, keepdims=True)
        return unused

    swaps = []
    for h in range(2):
        lax.fori_loop(h * n_tiles // 2, (h + 1) * n_tiles // 2, through_gates, 0)
        rows = pl.ds(h * group // 2, group // 2)
        for j in range(2):
            swaps.append(
                copies.start(
                    dpv.at[rows, pl.ds(j * chans + bw, LANES)],
                    there.at[rows, pl.ds(j * LANES, LANES)],
                    "y",
                )
            )

    def through_blocks(k, unused):
        rows = pl.ds(pl.multiple_of(k * tile, tile), tile)
        c = cv[rows, :]
        d_blk = dcv[rows, :bw]
        d_tile = dcv[rows, bw:]
        for j in range(2):
            p_blk = dpv[rows, slice(j * chans, j * chans + bw)]
            here = dpv[rows, slice(j * chans + bw, (j + 1) * chans)]
            far = there[rows, slice(j * LANES, (j + 1) * LANES)]
            five = jnp.concatenate(
                [jnp.where(high_tile, far, here), jnp.where(high_tile, here, far)], axis=1
            )
            d_blk = d_blk + dot(p_blk, gates_blk[j], ((1,), (1,)))
            d_tile = d_tile + dot(five, gates_rows[j], ((1,), (1,)))
            gg[j, :, :bw] += dot(c[:, :bw], p_blk, ((0,), (0,)))
            gg[j, :, bw:] += dot(c[:, bw:], here, ((0,), (0,)))
        dcv[rows, :bw] = d_blk
        dcv[rows, bw:] = d_tile
        return unused

    copies.land(swaps[0], swaps[1])
    lax.fori_loop(0, 1, through_blocks, 0)
    later = copies.start(dcv.at[pl.ds(0, 8), :], dcv.at[pl.ds(group, 8), :], "prev")
    lax.fori_loop(1, n_tiles // 2, through_blocks, 0)
    copies.land(swaps[2], swaps[3])
    lax.fori_loop(n_tiles // 2, n_tiles, through_blocks, 0)
    part_rows = gate_out.shape[0]
    for p in range(n_dp):
        j, first_row = divmod(p * part_rows, bw)
        glo[p] = gg[j, first_row : first_row + part_rows].astype(low)
    parts = [
        copies.start(glo.at[jnp.bitwise_xor(place.dp, d + 1)], gfar.at[d], name)
        for d, name in enumerate(far)
    ]
    copies.land(later)

    def through_conv(k, unused):
        r0 = pl.multiple_of(k * tile, tile)
        rows = pl.ds(r0, tile)
        ext = pl.ds(r0, tile + 8)
        spot = places[ext, :]
        for at in lanes:
            reach = dcv[ext, at]
            if at.start < bw:
                x = xb[ext, at]
            else:
                x = jnp.where(high_tile, xb[ext, slice(at.start + LANES, at.stop + LANES)], xb[ext, at])
            d_c = reach[:tile]
            d_x = conv_w[0:1, at] * d_c
            sums[3:4, at] += jnp.sum(d_c * x[8:], axis=0, keepdims=True)
            for t in range(1, conv_w.shape[0]):
                term = jnp.where(spot >= t, conv_w[t : t + 1, at] * reach, 0.0)
                d_x = d_x + pltpu.roll(term, tile + 8 - t, 0)[:tile]
                lagged = pltpu.roll(x, t, 0)[8:]
                here = jnp.where(spot[:tile] >= t, d_c * lagged, 0.0)
                sums[3 + t : 4 + t, at] += jnp.sum(here, axis=0, keepdims=True)
            sums[7:8, at] += jnp.sum(d_c, axis=0, keepdims=True)
            drv[rows, at] = d_x.astype(low)
        return unused

    lax.fori_loop(0, n_tiles, through_conv, 0)
    out_rec = copies.keep(drv, d_rec_out, local.at[9])
    copies.land(*parts)
    total = glo[place.dp].astype(f32)
    for d in range(n_dp - 1):
        total = total + gfar[d].astype(f32)
    gate_out[...] = total.astype(low)
    copies.finish()
    out.wait()
    out_rec.wait()


def rec_backward(d_out, w_out, kept, gates_blk, gates_rows, soft, conv_w, places, geo, n_dp):
    n_col, part, bw, tiles, wide = geo
    own, width = d_out.shape
    slots = 2 * n_col
    group, chans = slots * own, bw + LANES
    part_rows = 2 * bw // n_dp
    d_all, d_rec, gate_grads, sums = pl.pallas_call(
        functools.partial(backward_kernel, geo),
        out_shape=(
            jax.ShapeDtypeStruct((slots, own, width), low),
            jax.ShapeDtypeStruct((group, 2 * chans), low),
            jax.ShapeDtypeStruct((part_rows, chans), low),
            jax.ShapeDtypeStruct((8, chans), f32),
        ),
        in_specs=[anywhere] * 8 + [in_vmem] * 5,
        out_specs=(anywhere, anywhere, in_vmem, in_vmem),
        scratch_shapes=[
            pltpu.VMEM((slots, own, width), low),
            pltpu.VMEM(w_out.shape, low),
            pltpu.VMEM((group, chans), f32),
            pltpu.VMEM((group, chans), f32),
            pltpu.VMEM((group + 8, chans), f32),
            pltpu.VMEM((group, 2 * chans), f32),
            pltpu.VMEM((group, 2 * bw), low),
            pltpu.VMEM((group + 8, 2 * bw), f32),
            pltpu.VMEM((group, chans), f32),
            pltpu.VMEM((group, chans), f32),
            pltpu.VMEM((group, 2 * chans), low),
            pltpu.VMEM((group, 2 * LANES), low),
            pltpu.VMEM((group + 8, chans), f32),
            pltpu.VMEM((group, 2 * chans), low),
            pltpu.VMEM((2, bw, chans), f32),
            pltpu.VMEM((n_dp, part_rows, chans), low),
            pltpu.VMEM((n_dp - 1, part_rows, chans), low),
            pltpu.VMEM((8, chans), f32),
            pltpu.VMEM((8, chans), f32),
            pltpu.SemaphoreType.DMA((15 + n_dp,)),
            pltpu.SemaphoreType.DMA((15 + n_dp,)),
            pltpu.SemaphoreType.DMA((10,)),
        ],
        compiler_params=pltpu.CompilerParams(
            collective_id=4, has_side_effects=True, vmem_limit_bytes=60 * MIB
        ),
        name="rec_backward",
    )(d_out, w_out, *kept, gates_blk, gates_rows, soft, conv_w, places)
    return d_all.reshape(group, width), d_rec, gate_grads, sums


def outer_kernel(n_dp, first_steps, left1, right1, left2, right2, out_ref):
    def multiply(left, right):
        total = dot(left[...], right[...], ((0,), (0,)))
        rows = total.shape[0] // n_dp
        for k in range(n_dp):
            out_ref[k, 0] = total[k * rows : (k + 1) * rows].astype(out_ref.dtype)

    j = pl.program_id(1)

    @pl.when(j < first_steps)
    def _():
        multiply(left1, right1)

    @pl.when(j >= first_steps)
    def _():
        multiply(left2, right2)


def outer_one_kernel(n_dp, left, right, out_ref):
    total = dot(left[...], right[...], ((0,), (0,)))
    rows = total.shape[0] // n_dp
    for k in range(n_dp):
        out_ref[k, 0] = total[k * rows : (k + 1) * rows].astype(out_ref.dtype)


def outer(left, right, n_dp, n_col, columns, name):
    length, width = left.shape
    part = width // n_col
    count = right.shape[1]
    return pl.pallas_call(
        functools.partial(outer_one_kernel, n_dp),
        grid=(n_col, count // columns),
        out_shape=jax.ShapeDtypeStruct((n_dp, n_col, part // n_dp, count), low),
        in_specs=[
            pl.BlockSpec((length, part), lambda i, j: (0, i)),
            pl.BlockSpec((length, columns), lambda i, j: (0, j)),
        ],
        out_specs=pl.BlockSpec((n_dp, 1, part // n_dp, columns), lambda i, j: (0, i, 0, j)),
        compiler_params=pltpu.CompilerParams(vmem_limit_bytes=48 * MIB),
        cost_estimate=pl.CostEstimate(
            flops=2 * length * width * count,
            bytes_accessed=2 * (length * width + length * count + width * count),
            transcendentals=0,
        ),
        name=name,
    )(left, right)


def outer_pair(left1, right1, left2, right2, n_dp, n_col, columns, name):
    length, width = left1.shape
    part = width // n_col
    steps1, steps2 = right1.shape[1] // columns, right2.shape[1] // columns
    count = (steps1 + steps2) * columns
    left_block = pl.BlockSpec((length, part), lambda i, j: (0, i))
    return pl.pallas_call(
        functools.partial(outer_kernel, n_dp, steps1),
        grid=(n_col, steps1 + steps2),
        out_shape=jax.ShapeDtypeStruct((n_dp, n_col, part // n_dp, count), low),
        in_specs=[
            left_block,
            pl.BlockSpec((length, columns), lambda i, j: (0, jnp.minimum(j, steps1 - 1))),
            left_block,
            pl.BlockSpec((length, columns), lambda i, j: (0, jnp.maximum(j - steps1, 0))),
        ],
        out_specs=pl.BlockSpec((n_dp, 1, part // n_dp, columns), lambda i, j: (0, i, 0, j)),
        compiler_params=pltpu.CompilerParams(vmem_limit_bytes=48 * MIB),
        cost_estimate=pl.CostEstimate(
            flops=2 * length * width * count,
            bytes_accessed=2 * (2 * length * width + length * count + width * count),
            transcendentals=0,
        ),
        name=name,
    )(left1, right1, left2, right2)


def dot(a, b, dims=((1,), (0,))):
    return lax.dot_general(a, b, (dims, ((), ())), preferred_element_type=f32)


def places_of(rows, lengths):
    ends = jnp.cumsum(lengths)
    starts = ends - lengths
    inside = (rows[:, None] >= starts[None, :]) & (rows[:, None] < ends[None, :])
    places = rows - jnp.sum(jnp.where(inside, starts[None, :], 0), axis=1)
    return jnp.where(jnp.any(inside, axis=1), places, 0)


def body(
    tokens,
    cotangent,
    rec_in,
    rec_out,
    gates,
    gate_bias,
    decay,
    conv_w,
    conv_b,
    gains,
    mlp_in,
    mlp_out,
    lengths,
    order,
):
    n_dp, n_row, n_col = (lax.axis_size(a) for a in ("dp", "row", "col"))
    dp, row, col = (lax.axis_index(a) for a in ("dp", "row", "col"))
    given, part = tokens.shape
    own = given // n_col
    group = given * n_row
    width = part * n_col
    taps = conv_w.shape[0]
    blocks, bw = gates.shape[1], gates.shape[2]
    half = rec_out.shape[0]
    hidden_half = mlp_out.shape[0]
    tiles = hidden_half // LANES
    wide = -(-tiles // n_col)
    span = wide * LANES
    shared = n_col * bw
    chans = bw + LANES

    geo = (n_col, part, bw, tiles, wide)
    x_all, w_rec, gains_all = open_gather(tokens, rec_in, gains, geo)
    gains_all = gains_all.transpose(1, 0, 2).reshape(gains.shape[0], width)
    w_x, w_y = w_rec[:, : 2 * bw], w_rec[:, 2 * bw :]

    tile_at = shared + (col // 2) * LANES

    def own_channels(x):
        blk = lax.dynamic_slice_in_dim(x, col * bw, bw, axis=-1)
        tile = lax.dynamic_slice_in_dim(x, tile_at, LANES, axis=-1)
        return jnp.concatenate([blk, tile], axis=-1)

    def block_channels(x):
        blk = lax.dynamic_slice_in_dim(x, col * bw, bw, axis=-1)
        return jnp.concatenate([blk, x[..., shared:]], axis=-1)

    bias = own_channels(gate_bias)
    decay_o = own_channels(decay)
    conv_w_c = block_channels(conv_w)
    conv_b_c = block_channels(conv_b)
    conv_w_o = own_channels(conv_w)
    gates_blk = lax.dynamic_index_in_dim(gates, col, axis=1, keepdims=False)
    gates_five = gates[:, n_col]
    gates_tile = lax.dynamic_slice_in_dim(gates_five, (col // 2) * LANES, LANES, axis=2)
    gates_rows = lax.dynamic_slice_in_dim(gates_five, (col // 2) * LANES, LANES, axis=1)

    base = dp * group
    places = places_of(base + jnp.arange(group + 8, dtype=jnp.int32), lengths)
    places = jnp.broadcast_to(places[:, None], (group + 8, LANES))
    soft = jax.nn.softplus(decay_o)[None, :]

    n1, x_rows, y_branch, pre_both, conv_low, state, branch, first, g_all, w_out, w_in, w_down = rec_forward(
        x_all,
        w_rec,
        (
            gains_all[0:1],
            gates_blk,
            gates_tile,
            bias,
            soft,
            conv_w_c,
            conv_b_c[None, :],
        ),
        places,
        cotangent,
        rec_out,
        mlp_in,
        mlp_out,
        geo,
    )
    rows_f, rows_b = ((own, width), f32), ((own, width), low)
    line, squares, home = ((8, width), f32), ((8, LANES), f32), ((given, part), low)
    resid, normed_two, squares_one = multiply_scatter(
        branch, w_out, False, 6, "out_one", after_out_one, (x_all, gains_all), (rows_f, rows_b, squares), False
    )

    def spare(at):
        return spare_window(at, tiles, n_col, wide)

    n2, hidden, d_glu = glu(normed_two, w_in, w_down, g_all, spare)
    g_down = outer(g_all, hidden, n_dp, n_col, 512, "outer_down")
    d_glu, hidden, g_down = lax.optimization_barrier((d_glu, hidden, g_down))
    sum_down = lax.psum_scatter(g_down, "dp", scatter_dimension=0)
    g_in = outer(n2, d_glu, n_dp, n_col, 512, "outer_in")
    d_glu, g_in = lax.optimization_barrier((d_glu, g_in))
    d_resid, d_out, gain_two = multiply_scatter(
        d_glu,
        w_in,
        True,
        7,
        "d_normed_two",
        after_normed_two,
        (resid, g_all, gains_all),
        (rows_f, rows_b, line),
        False,
    )
    g_in, sum_down, d_out = lax.optimization_barrier((g_in, sum_down, d_out))
    sum_in = lax.psum_scatter(g_in, "dp", scatter_dimension=0)

    d_out_all, d_rec, gate_sums, small = rec_backward(
        d_out,
        w_out,
        (y_branch, state, first, pre_both, conv_low, x_rows),
        gates_blk,
        gates_rows,
        soft,
        conv_w_o,
        places,
        geo,
        n_dp,
    )
    small = small.at[2].multiply(jax.nn.sigmoid(decay_o))
    w_x_own = jnp.concatenate(
        [w_x[:, :bw], lax.dynamic_slice_in_dim(w_x, bw + (col // 2) * LANES, LANES, axis=1)], axis=1
    )
    w_back = jnp.concatenate([w_x_own, w_y], axis=1)
    g_rec = outer_pair(n1, d_rec, d_out_all, branch, n_dp, n_col, chans, "outer_rec")
    g_rec, d_rec = lax.optimization_barrier((g_rec, d_rec))
    grad_input, gain_one, squares_x = multiply_scatter(
        d_rec,
        w_back,
        True,
        9,
        "d_normed_one",
        after_normed_one,
        (x_all, d_resid, gains_all),
        (home, line, squares),
        True,
    )
    g_rec, sum_in, grad_input, hidden = lax.optimization_barrier((g_rec, sum_in, grad_input, hidden))
    sum_rec = lax.psum_scatter(g_rec, "dp", scatter_dimension=0)
    result, squares_two = multiply_scatter(
        hidden, w_down, False, 8, "out_two", after_out_two, (resid,), (home, squares), True
    )

    def windows(got, first):
        return [
            got[c][..., first + (LANES if c > n_col - 1 - (wide * n_col - tiles) else 0) : first + span]
            for c in range(n_col)
        ]

    def channels_of(got, first):
        return [got[c][..., first : first + bw] for c in range(n_col)] + [
            got[c][..., first + bw : first + chans] for c in range(0, n_col, 2)
        ]

    square_sums = jnp.stack([squares_x[0, 0], squares_one[0, 0], squares_one[1, 0], squares_two[0, 0]])
    lines = small.shape[0]
    gain_sums = jnp.concatenate([gain_one[:1], gain_two[:1]]).reshape(lines, 2 * width // lines)
    stat_block = jnp.pad(square_sums[None, :], ((0, lines - 1), (0, LANES - 4)))
    mixed = jnp.concatenate([small, gain_sums, stat_block], axis=1)
    sums, chan_sums, gate_parts, into, down = sum_everywhere(
        mixed, chans, gate_sums, sum_in, sum_down, n_dp, n_col
    )
    sum_rec, into = lax.optimization_barrier((sum_rec, into))
    recs = deal_back(sum_rec, 10, "deal_rec")
    grad_mlp_in = jnp.stack(
        [jnp.concatenate(windows(into[..., j * span : (j + 1) * span], 0), axis=-1) for j in range(2)]
    ).astype(f32)
    grad_mlp_out = jnp.concatenate(windows(down, 0), axis=-1).astype(f32).T
    grad_rec_in = jnp.stack(
        [jnp.concatenate(channels_of(recs, j * chans), axis=-1) for j in range(2)]
    ).astype(f32)
    grad_rec_out = jnp.concatenate(channels_of(recs, 2 * chans), axis=-1).astype(f32).T
    mine = jnp.concatenate(channels_of(chan_sums, 0), axis=-1)
    gain_rows = sums[:, : 2 * width // lines].reshape(2, width)
    grad_gains = lax.dynamic_slice_in_dim(gain_rows, col * part, part, axis=1)
    stats = jnp.sqrt(sums[0, 2 * width // lines :][:4] / (n_dp * group * width))
    gate_parts = gate_parts.reshape(n_col, 2, bw, chans).astype(f32)
    five = jnp.concatenate([gate_parts[c, :, :, bw:] for c in range(0, n_col, 2)], axis=-1)
    grad_gates = jnp.stack([gate_parts[c, :, :, :bw] for c in range(n_col)] + [five], axis=1)
    return (
        result,
        grad_input,
        grad_rec_in,
        grad_rec_out,
        grad_gates,
        mine[0:2],
        mine[2],
        mine[3 : 3 + taps],
        mine[3 + taps],
        grad_gains,
        grad_mlp_in,
        grad_mlp_out,
        stats,
    )


def solution(mesh):
    placed = (
        P(("dp", "row"), "col"),
        P(("dp", "row"), "col"),
        P(None, "col", "row"),
        P("row", "col"),
        P(None, "row", None, None),
        P(None, "row"),
        P("row"),
        P(None, "row"),
        P("row"),
        P(None, "col"),
        P(None, "col", "row"),
        P("row", "col"),
        P(),
        P(),
    )
    return jax.shard_map(
        body,
        mesh=mesh,
        in_specs=placed,
        out_specs=(
            P(("dp", "row"), "col"),
            P(("dp", "row"), "col"),
            P(None, ("col", "dp"), "row"),
            P("row", ("col", "dp")),
            P(None, "row", None, None),
            P(None, "row"),
            P("row"),
            P(None, "row"),
            P("row"),
            P(None, "col"),
            P(None, ("col", "dp"), "row"),
            P("row", ("col", "dp")),
            P(),
        ),
        check_vma=False,
    )
```

```python
import functools

import jax
import jax.numpy as jnp
from jax import lax
from jax.experimental import pallas as pl
from jax.experimental.pallas import tpu as pltpu
from jax.sharding import PartitionSpec as P

epsilon = 1e-06
LANES = 128
ROWS = 16
MIB = 1024 * 1024
MESH = pl.DeviceIdType.MESH
low = jnp.bfloat16
f32 = jnp.float32
anywhere = pl.BlockSpec(memory_space=pl.ANY)
in_vmem = pl.BlockSpec(memory_space=pltpu.VMEM)


def window_tile(col, tiles, n_col, wide):
    spare = wide * n_col - tiles
    return col * wide - jnp.maximum(col - (n_col - 1 - spare), 0)


def spare_window(col, tiles, n_col, wide):
    spare = wide * n_col - tiles
    return col > n_col - 1 - spare


class Place:
    def __init__(self):
        self.dp, self.row, self.col = (lax.axis_index(a) for a in ("dp", "row", "col"))

    def chip(self, k):
        return jnp.bitwise_xor(self.col, k)

    def device(self, name):
        if name == "core":
            return {"row": 1 - self.row}
        if name == "z":
            return {"dp": jnp.bitwise_xor(self.dp, 1)}
        if name in ("next", "prev"):
            n_dp = lax.axis_size("dp")
            return {"dp": lax.rem(self.dp + (1 if name == "next" else n_dp - 1), n_dp)}
        if name[0] == "d":
            return {"dp": jnp.bitwise_xor(self.dp, int(name[1:]))}
        if name[0] == "c":
            return {"row": 1 - self.row, "col": self.chip({"x": 1, "y": 2, "xy": 3}[name[1:]])}
        return {"col": self.chip({"x": 1, "y": 2, "xy": 3}[name])}

    def meet(self, names):
        barrier = pltpu.get_barrier_semaphore()
        for name in names:
            pl.semaphore_signal(
                barrier, inc=1, device_id=self.device(name), device_id_type=MESH
            )
        pl.semaphore_wait(barrier, len(names))


class Copies:
    def __init__(self, place, send, recv):
        self.place, self.send, self.recv = place, send, recv
        self.made, self.landed, self.left, self.local = [], set(), set(), []

    def start(self, src, dst, to):
        i = len(self.made)
        copy = pltpu.make_async_remote_copy(
            src_ref=src,
            dst_ref=dst,
            send_sem=self.send.at[i],
            recv_sem=self.recv.at[i],
            device_id=self.place.device(to),
            device_id_type=MESH,
        )
        copy.start()
        self.made.append(copy)
        return i

    def land(self, *numbers):
        for i in numbers:
            if i not in self.landed:
                self.made[i].wait_recv()
                self.landed.add(i)

    def leave(self, *numbers):
        for i in numbers:
            if i not in self.left:
                self.made[i].wait_send()
                self.left.add(i)

    def keep(self, src, dst, sem):
        copy = pltpu.make_async_copy(src, dst, sem)
        copy.start()
        self.local.append(copy)
        return copy

    def finish(self):
        self.land(*range(len(self.made)))
        self.leave(*range(len(self.made)))


def share(rows, far_part):
    far = rows * far_part // 20 // ROWS * ROWS
    return rows - far, far


class Dealer:
    def __init__(self, copies, far_part):
        self.copies, self.far_part = copies, far_part
        self.waiting = []

    def deal(self, piece):
        place = self.copies.place
        odd = lax.rem(place.dp, 2)
        batch = []
        for name, k in (("x", 1), ("y", 2), ("xy", 3)):
            src, dst, rows = piece(place.chip(k), place.col)
            near, far = share(rows, self.far_part)
            start = pl.multiple_of(odd * far, ROWS)
            at = pl.ds(start, near)
            number = self.copies.start(src(at), dst(at), name)
            batch.append((k, number, piece))
        self.waiting.append(batch)

    def forward(self):
        place = self.copies.place
        odd = lax.rem(place.dp, 2)
        for k, number, piece in self.waiting.pop(0):
            self.copies.land(number)
            _, dst, rows = piece(place.col, place.chip(k))
            near, far = share(rows, self.far_part)
            at = pl.ds(pl.multiple_of(odd * near, ROWS), far)
            self.copies.start(dst(at), dst(at), "z")


def rows_of(ref, first, rows, lead=None, columns=None):
    def view(at):
        where = pl.ds(pl.multiple_of(first + at.start, ROWS), at.size)
        index = (where, columns if columns is not None else slice(None))
        return ref.at[index] if lead is None else ref.at[(lead,) + index]

    return view


def weight_pieces(geo, refs, outs):
    n_col, part, bw, tiles, wide = geo
    shared, span = n_col * bw, wide * LANES
    rec_in, rec_out, mlp_in, mlp_out = refs
    w_rec, w_out, w_in, w_down = outs

    def here(chip):
        return pl.multiple_of(chip * part, LANES)

    def blk(chip):
        return pl.multiple_of(chip * bw, LANES)

    def tile(chip):
        return pl.multiple_of(shared + lax.div(chip, 2) * LANES, LANES)

    def win(chip):
        return pl.multiple_of(window_tile(chip, tiles, n_col, wide) * LANES, LANES)

    def in_piece(ref, j, out, lead, source_at, size, column):
        def piece(dest, source):
            return (
                rows_of(ref, 0, part, j, pl.ds(pl.multiple_of(source_at(dest), LANES), size)),
                rows_of(out, here(source), part, lead, pl.ds(column, size)),
                part,
            )

        return piece

    def down_piece(ref, out, source_at, size, row):
        def piece(dest, source):
            return (
                rows_of(ref, source_at(dest), size),
                rows_of(out, row, size, None, pl.ds(here(source), part)),
                size,
            )

        return piece

    found = {}
    if rec_in is not None:
        found["rec_in"] = [
            in_piece(rec_in, 0, w_rec, None, blk, bw, 0),
            in_piece(rec_in, 0, w_rec, None, lambda chip: shared, bw, bw),
            in_piece(rec_in, 1, w_rec, None, blk, bw, 2 * bw),
            in_piece(rec_in, 1, w_rec, None, tile, LANES, 3 * bw),
        ]
    if rec_out is not None:
        found["rec_out"] = [
            down_piece(rec_out, w_out, blk, bw, 0),
            down_piece(rec_out, w_out, tile, LANES, bw),
        ]
    if mlp_in is not None:
        half = span // 2
        found["mlp_in"] = [
            in_piece(mlp_in, j, w_in, j, lambda chip, h=h: win(chip) + h * half, half, h * half)
            for j in range(2)
            for h in range(2)
        ]
    if mlp_out is not None:
        half = span // 2
        found["mlp_out"] = [
            down_piece(mlp_out, w_down, lambda chip, h=h: win(chip) + h * half, half, h * half)
            for h in range(2)
        ]
    return found


def own_pieces(place, pieces):
    pairs = []
    for piece in pieces:
        src, dst, rows = piece(place.col, place.col)
        pairs.append((src(pl.ds(0, rows)), dst(pl.ds(0, rows))))
    return pairs


class Stay:
    def __init__(self, pairs, bufs, sems):
        self.pairs, self.bufs, self.sems = pairs, bufs, sems
        self.loads = [
            pltpu.make_async_copy(src, buf, sems.at[i])
            for i, ((src, _), buf) in enumerate(zip(pairs, bufs))
        ]
        for load in self.loads:
            load.start()

    def turn(self):
        for load in self.loads:
            load.wait()
        self.stores = [
            pltpu.make_async_copy(buf, dst, self.sems.at[i])
            for i, ((_, dst), buf) in enumerate(zip(self.pairs, self.bufs))
        ]
        for store in self.stores:
            store.start()

    def finish(self):
        for store in self.stores:
            store.wait()


class Gather:
    def __init__(self, copies, mine, at):
        self.copies, self.at = copies, at
        place = copies.place
        row, col = place.row, place.col
        self.first = [
            copies.start(mine(half), at(row, col, half), name)
            for half in (0, 1)
            for name in ("x", "y")
        ]
        self.own = copies.start(mine(None), at(row, col, None), "core")
        self.rounds = []

    def pass_half(self, half):
        copies, place = self.copies, self.copies.place
        views = [self.at(place.row, place.chip(k), half) for k in (1, 2)]
        x, y = self.first[2 * half], self.first[2 * half + 1]
        if half == 0:
            copies.land(x)
            round_ = copies.start(views[0], views[0], "y")
            core_x = copies.start(views[0], views[0], "core")
            copies.land(y)
            core_y = copies.start(views[1], views[1], "core")
        else:
            copies.land(y)
            round_ = copies.start(views[1], views[1], "x")
            core_y = copies.start(views[1], views[1], "core")
            copies.land(x)
            core_x = copies.start(views[0], views[0], "core")
        self.rounds.append(round_)
        return core_x, core_y

    def pass_on(self):
        return self.pass_half(0) + self.pass_half(1)

    def last(self):
        copies, place = self.copies, self.copies.place
        corner = self.at(place.row, place.chip(3), None)
        copies.land(*self.rounds)
        return copies.start(corner, corner, "core")


def block_view(source, target, row, col, half):
    rows, part = source.shape
    cut = rows // 2
    first = row * rows + (0 if half is None else half * cut)
    size = rows if half is None else cut
    return target.at[
        pl.ds(pl.multiple_of(first, ROWS), size), pl.ds(pl.multiple_of(col * part, LANES), part)
    ]


def block_gather(copies, source, target):
    cut = source.shape[0] // 2

    def mine(half):
        return source if half is None else source.at[pl.ds(half * cut, cut), :]

    return Gather(copies, mine, functools.partial(block_view, source, target))


AROUND = ("x", "y", "xy", "core", "z")


def open_kernel(geo, tokens, rec_in, gains, x_all, w_rec, gains_all, send, recv, local, *bufs):
    place = Place()
    place.meet(AROUND)
    copies = Copies(place, send, recv)
    pieces = weight_pieces(geo, (rec_in, None, None, None), (w_rec, None, None, None))["rec_in"]
    dealer = Dealer(copies, 10)
    dealer.deal(pieces[0])
    dealer.deal(pieces[1])
    gather = block_gather(copies, tokens, x_all)
    own_block = (tokens, block_view(tokens, x_all, place.row, place.col, None))
    dealer.deal(pieces[2])
    dealer.deal(pieces[3])
    mine = gains_all.at[place.col]
    for name in ("x", "y", "xy"):
        copies.start(gains, mine, name)
    stay = Stay([own_block] + own_pieces(place, pieces) + [(gains, mine)], bufs, local)
    stay.turn()
    dealer.forward()
    dealer.forward()
    gather.pass_on()
    dealer.forward()
    dealer.forward()
    gather.last()
    copies.finish()
    stay.finish()


def open_gather(tokens, rec_in, gains, geo):
    n_col, part, bw, tiles, wide = geo
    width = part * n_col
    return pl.pallas_call(
        functools.partial(open_kernel, geo),
        out_shape=(
            jax.ShapeDtypeStruct((2 * tokens.shape[0], width), low),
            jax.ShapeDtypeStruct((width, 3 * bw + LANES), low),
            jax.ShapeDtypeStruct((n_col,) + gains.shape, f32),
        ),
        in_specs=[anywhere] * 3,
        out_specs=(anywhere,) * 3,
        scratch_shapes=[
            pltpu.SemaphoreType.DMA((39,)),
            pltpu.SemaphoreType.DMA((39,)),
            pltpu.SemaphoreType.DMA((6,)),
            pltpu.VMEM(tokens.shape, low),
            pltpu.VMEM((part, bw), low),
            pltpu.VMEM((part, bw), low),
            pltpu.VMEM((part, bw), low),
            pltpu.VMEM((part, LANES), low),
            pltpu.VMEM(gains.shape, f32),
        ],
        compiler_params=pltpu.CompilerParams(collective_id=1, has_side_effects=True),
        name="open_gather",
    )(tokens, rec_in, gains)


def slot_gather(copies, local_ref, buf, own):
    cut = own // 2
    n_col = buf.shape[0] // 2

    def at(row, col, half):
        slot = buf.at[row * n_col + col]
        return slot if half is None else slot.at[pl.ds(half * cut, cut), :]

    def mine(half):
        return local_ref if half is None else local_ref.at[pl.ds(half * cut, cut), :]

    return Gather(copies, mine, at)


def tanh_parts(x):
    k = 0.7978845608028654
    square = x * x
    t = jnp.tanh(k * x * (1.0 + 0.044715 * square))
    value = 0.5 * x * (1.0 + t)
    slope = 0.5 * (1.0 + t) + 0.5 * x * (1.0 - t * t) * k * (1.0 + 3 * 0.044715 * square)
    return value, slope


def glu_kernel(
    spare, n2, w_in, w_down, g_all, n2_all, hidden, d_glu, buf, wi, wd, g, hid, dgl, send, recv, local
):
    place = Place()
    place.meet(("x", "y", "core"))
    copies = Copies(place, send, recv)
    own, width = n2.shape
    n_col = buf.shape[0] // 2
    span = wd.shape[0]
    step = 256
    gather = slot_gather(copies, n2, buf, own)
    me = place.row * n_col + place.col
    loads = [
        copies.keep(n2, buf.at[me], local.at[0]),
        copies.keep(w_in, wi, local.at[1]),
        copies.keep(w_down, wd, local.at[2]),
        copies.keep(g_all, g, local.at[3]),
    ]
    for load in loads:
        load.wait()
    hide = spare(place.col)

    n_steps = span // step

    def work(slots, first, size, lo, hi):
        rows = [pl.ds(pl.multiple_of(s * own + first, ROWS), size) for s in slots]
        n2_here = jnp.concatenate([buf[s, first : first + size, :] for s in slots], axis=0)
        g_here = jnp.concatenate([g[r, :] for r in rows], axis=0)

        def columns(i, carry):
            at = pl.ds(pl.multiple_of(i * step, LANES), step)
            up_at = pl.ds(pl.multiple_of(span + i * step, LANES), step)
            gate = dot(n2_here, wi[0, :, at])
            up = dot(n2_here, wi[1, :, at])
            d_hid = dot(g_here, wd[at, :], ((1,), (1,)))
            lane = lax.broadcasted_iota(jnp.int32, gate.shape, 1) + i * step
            used = (lane >= LANES) | jnp.logical_not(hide)
            up = jnp.where(used, up, 0.0)
            d_hid = jnp.where(used, d_hid, 0.0)
            value, slope = tanh_parts(gate)
            h = (value * up).astype(low)
            dg = (d_hid * up * slope).astype(low)
            du = (d_hid * value).astype(low)
            for n, r in enumerate(rows):
                part = slice(n * size, (n + 1) * size)
                hid[r, at] = h[part]
                dgl[r, at] = dg[part]
                dgl[r, up_at] = du[part]
            return carry

        lax.fori_loop(lo, hi, columns, 0)

    def both_cores(*chips):
        return [s for chip in chips for s in (chip, n_col + chip)]

    half = own // 2
    near = both_cores(place.chip(1), place.chip(2))
    copies.land(gather.own)
    work(both_cores(place.col), 0, own, 0, n_steps)
    core0 = gather.pass_half(0)
    copies.land(*core0)
    work(near, 0, half, 0, n_steps // 2)
    core1 = gather.pass_half(1)
    work(near, 0, half, n_steps // 2, n_steps)
    copies.land(*core1)
    work(near, half, half, 0, n_steps // 2)
    corner = gather.last()
    work(near, half, half, n_steps // 2, n_steps)
    copies.land(corner)
    out_n2 = copies.keep(buf, n2_all, local.at[4])
    work(both_cores(place.chip(3)), 0, own, 0, n_steps)
    out_h = copies.keep(hid, hidden, local.at[5])
    out_d = copies.keep(dgl, d_glu, local.at[6])
    copies.finish()
    out_n2.wait()
    out_h.wait()
    out_d.wait()


def glu(n2, w_in, w_down, g_all, spare):
    own, width = n2.shape
    group = g_all.shape[0]
    span = w_down.shape[0]
    n_all, h, d = pl.pallas_call(
        functools.partial(glu_kernel, spare),
        out_shape=(
            jax.ShapeDtypeStruct((group // own, own, width), low),
            jax.ShapeDtypeStruct((group, span), low),
            jax.ShapeDtypeStruct((group, 2 * span), low),
        ),
        in_specs=[anywhere] * 4,
        out_specs=(anywhere,) * 3,
        scratch_shapes=[
            pltpu.VMEM((group // own, own, width), low),
            pltpu.VMEM(w_in.shape, low),
            pltpu.VMEM(w_down.shape, low),
            pltpu.VMEM((group, width), low),
            pltpu.VMEM((group, span), low),
            pltpu.VMEM((group, 2 * span), low),
            pltpu.SemaphoreType.DMA((12,)),
            pltpu.SemaphoreType.DMA((12,)),
            pltpu.SemaphoreType.DMA((7,)),
        ],
        compiler_params=pltpu.CompilerParams(
            collective_id=3, has_side_effects=True, vmem_limit_bytes=58 * MIB
        ),
        cost_estimate=pl.CostEstimate(
            flops=6 * group * width * span, bytes_accessed=60 * MIB, transcendentals=group * span
        ),
        name="glu",
    )(n2, w_in, w_down, g_all)
    return n_all.reshape(group, width), h, d


def scatter_kernel(shape, finish, n_more, n_outs, homes, act, w, *refs):
    n_parts, across, own, width = shape
    more, refs = refs[:n_more], refs[n_more:]
    outs, refs = refs[:n_outs], refs[n_outs:]
    actv, wv, other, mine, from_core, from_x, from_y, turn, fin, back, send, recv, local, home_sem = refs[:14]
    held = refs[14:]
    place = Place()
    place.meet(("x", "y", "xy", "core") if homes else ("x", "y", "core"))
    copies = Copies(place, send, recv)
    cut = own // 2
    n_col = act.shape[0] // own // 2
    k = act.shape[1] // n_parts
    step = 256
    loads = [copies.keep(act, actv, local.at[0]), copies.keep(w, wv, local.at[1])]
    my_rows = pl.ds(pl.multiple_of((place.row * n_col + place.col) * own, ROWS), own)
    extra = []
    for i, (ref, buf) in enumerate(zip(more, held)):
        src = ref.at[my_rows, :] if ref.shape[0] > own else ref
        extra.append(copies.keep(src, buf, local.at[2 + i]))
    for load in loads:
        load.wait()
    top, bottom = pl.ds(0, cut), pl.ds(cut, cut)

    def work(j):
        chip = place.chip(j)
        slots = ((1 - place.row) * n_col + chip, place.row * n_col + chip)
        left = [
            jnp.concatenate(
                [
                    actv[pl.ds(pl.multiple_of(s * own, ROWS), own), n * k : (n + 1) * k]
                    for s in slots
                ],
                axis=0,
            )
            for n in range(n_parts)
        ]

        def columns(i, carry):
            at = pl.ds(pl.multiple_of(i * step, LANES), step)
            total = None
            for n in range(n_parts):
                if across:
                    right = wv[n, at, :] if n_parts > 1 else wv[at, :]
                    term = dot(left[n], right, ((1,), (1,)))
                else:
                    term = dot(left[n], wv[:, at])
                total = term if total is None else total + term
            other[j, :, at] = total[:own].astype(low)
            mine[j, :, at] = total[own:]
            return carry

        lax.fori_loop(0, width // step, columns, 0)
        return copies.start(other.at[j], from_core.at[j], "core")

    def add_core(j, number):
        copies.land(number)
        mine[j] = mine[j] + from_core[j].astype(f32)
        turn[j] = mine[j].astype(low)

    core3 = work(3)
    core1 = work(1)
    add_core(3, core3)
    x3 = copies.start(turn.at[3, top, :], from_x.at[0], "x")
    y3 = copies.start(turn.at[3, bottom, :], from_y.at[0], "y")
    core2 = work(2)
    add_core(1, core1)
    x1 = copies.start(turn.at[1, top, :], from_x.at[1], "x")
    core0 = work(0)
    add_core(2, core2)
    y2 = copies.start(turn.at[2, bottom, :], from_y.at[1], "y")
    copies.land(x3)
    turn[2, top, :] = (mine[2, top, :] + from_x[0].astype(f32)).astype(low)
    y_last = copies.start(turn.at[2, top, :], from_y.at[2], "y")
    copies.land(y3)
    turn[1, bottom, :] = (mine[1, bottom, :] + from_y[0].astype(f32)).astype(low)
    x_last = copies.start(turn.at[1, bottom, :], from_x.at[2], "x")
    add_core(0, core0)
    copies.land(x1, y2, y_last, x_last)
    fin[top, :] = mine[0, top, :] + from_x[1].astype(f32) + from_y[2].astype(f32)
    fin[bottom, :] = mine[0, bottom, :] + from_y[1].astype(f32) + from_x[2].astype(f32)
    for load in extra:
        load.wait()
    for ref in outs[(1 if homes else 0) :]:
        if ref.shape[0] == 8:
            ref[...] = jnp.zeros_like(ref)
    rows_at_once = 64

    def rows_done(i, carry):
        rows = pl.ds(pl.multiple_of(i * rows_at_once, rows_at_once), rows_at_once)
        finish(rows, fin, held, back, outs[(1 if homes else 0) :])
        return carry

    lax.fori_loop(0, own // rows_at_once, rows_done, 0)
    if homes:
        home = outs[0]
        part = width // n_col

        def columns_of(chip):
            return back.at[:, pl.ds(pl.multiple_of(chip * part, LANES), part)]

        spot = home.at[pl.ds(pl.multiple_of(place.col * own, ROWS), own), :]
        for name, j in (("xy", 3), ("x", 1), ("y", 2)):
            copies.start(columns_of(place.chip(j)), spot, name)
        stay = copies.keep(columns_of(place.col), spot, home_sem)
        stay.wait()
    copies.finish()


def multiply_scatter(act, w, across, number, name, finish, more, outs, homes):
    n_parts = w.shape[0] if w.ndim == 3 else 1
    group = act.shape[0]
    n_col = lax.axis_size("col")
    own = group // (2 * n_col)
    width = w.shape[-2] if across else w.shape[-1]
    held = [((own, r.shape[1]) if r.shape[0] > own else r.shape, r.dtype) for r in more]
    return pl.pallas_call(
        functools.partial(
            scatter_kernel, (n_parts, across, own, width), finish, len(more), len(outs), homes
        ),
        out_shape=tuple(jax.ShapeDtypeStruct(*s) for s in outs),
        in_specs=[anywhere] * (2 + len(more)),
        out_specs=tuple(anywhere if homes and i == 0 else in_vmem for i in range(len(outs))),
        scratch_shapes=[
            pltpu.VMEM(act.shape, low),
            pltpu.VMEM(w.shape, low),
            pltpu.VMEM((4, own, width), low),
            pltpu.VMEM((4, own, width), f32),
            pltpu.VMEM((4, own, width), low),
            pltpu.VMEM((3, own // 2, width), low),
            pltpu.VMEM((3, own // 2, width), low),
            pltpu.VMEM((4, own, width), low),
            pltpu.VMEM((own, width), f32),
            pltpu.VMEM((own, width), low),
            pltpu.SemaphoreType.DMA((13,)),
            pltpu.SemaphoreType.DMA((13,)),
            pltpu.SemaphoreType.DMA((2 + len(more),)),
            pltpu.SemaphoreType.DMA,
        ]
        + [pltpu.VMEM(*h) for h in held],
        compiler_params=pltpu.CompilerParams(
            collective_id=number, has_side_effects=True, vmem_limit_bytes=60 * MIB
        ),
        cost_estimate=pl.CostEstimate(
            flops=2 * group * width * act.shape[1], bytes_accessed=40 * MIB, transcendentals=0
        ),
        name=name,
    )(act, w, *more)


def square_sum(ref, row, x):
    ref[row : row + 1, :] += jnp.broadcast_to(jnp.sum(x * x, keepdims=True), (1, LANES))


def norm_scale(x):
    return lax.rsqrt(jnp.mean(x * x, axis=-1, keepdims=True) + epsilon)


def after_out_one(rows, fin, held, back, outs):
    x, gain = held
    resid_out, n2_out, squares = outs
    out_one = fin[rows, :]
    resid = x[rows, :].astype(f32) + out_one
    resid_out[rows, :] = resid
    n2_out[rows, :] = (resid * norm_scale(resid) * gain[1:2, :]).astype(low)
    square_sum(squares, 0, out_one)
    square_sum(squares, 1, resid)


def norm_back(d_normed, x, gain, grad_gain):
    scale = norm_scale(x)
    gained = gain * d_normed
    inner = jnp.mean(gained * x, axis=-1, keepdims=True)
    grad_gain[0:1, :] += jnp.sum(d_normed * x * scale, axis=0, keepdims=True)
    return scale * gained - x * (scale * scale * scale * inner)


def after_normed_two(rows, fin, held, back, outs):
    resid, upstream, gain = held
    d_resid_out, d_out, grad_gain = outs
    d_resid = upstream[rows, :].astype(f32) + norm_back(
        fin[rows, :], resid[rows, :], gain[1:2, :], grad_gain
    )
    d_resid_out[rows, :] = d_resid
    d_out[rows, :] = d_resid.astype(low)


def after_normed_one(rows, fin, held, back, outs):
    x, d_resid, gain = held
    grad_gain, squares = outs
    x_here = x[rows, :].astype(f32)
    passed = norm_back(fin[rows, :], x_here, gain[0:1, :], grad_gain)
    back[rows, :] = (d_resid[rows, :] + passed).astype(low)
    square_sum(squares, 0, x_here)


def after_out_two(rows, fin, held, back, outs):
    (resid,) = held
    (squares,) = outs
    out_two = fin[rows, :]
    back[rows, :] = (resid[rows, :] + out_two).astype(low)
    square_sum(squares, 0, out_two)


def start_deal(copies, source, target):
    col = copies.place.col
    for name, j in (("xy", 3), ("x", 1), ("y", 2)):
        copies.start(source.at[copies.place.chip(j)], target.at[col], name)


def deal_kernel(source, target, send, recv, local, buf):
    place = Place()
    place.meet(("x", "y", "xy"))
    copies = Copies(place, send, recv)
    start_deal(copies, source, target)
    stay = Stay([(source.at[place.col], target.at[place.col])], [buf], local)
    stay.turn()
    copies.finish()
    stay.finish()


def deal_back(x, number, name):
    return pl.pallas_call(
        deal_kernel,
        out_shape=jax.ShapeDtypeStruct(x.shape, x.dtype),
        in_specs=[anywhere],
        out_specs=anywhere,
        scratch_shapes=[
            pltpu.SemaphoreType.DMA((3,)),
            pltpu.SemaphoreType.DMA((3,)),
            pltpu.SemaphoreType.DMA((1,)),
            pltpu.VMEM(x.shape[1:], x.dtype),
        ],
        compiler_params=pltpu.CompilerParams(
            collective_id=number, has_side_effects=True, vmem_limit_bytes=16 * MIB
        ),
        name=name,
    )(x)


PLANE = ("x", "y", "xy", "core", "cx", "cy", "cxy")


def sums_kernel(
    n_dp,
    split,
    mixed,
    gate_part,
    grads,
    sums_out,
    chans_out,
    gates_out,
    grads_out,
    got,
    total,
    ch,
    shared,
    send,
    recv,
    local,
    *bufs,
):
    place = Place()
    far = [f"d{d}" for d in range(1, n_dp)]
    place.meet(list(PLANE) + far)
    copies = Copies(place, send, recv)
    dp, col = place.dp, place.col
    own_gates = gates_out.at[col]
    parts = [copies.start(gate_part, own_gates.at[dp], name) for name in far]
    planes = [copies.start(mixed, got.at[i], name) for i, name in enumerate(far)]
    start_deal(copies, grads, grads_out)
    stay = Stay(
        [(gate_part, own_gates.at[dp]), (grads.at[col], grads_out.at[col])], bufs, local
    )
    stay.turn()
    copies.land(*planes)
    value = mixed[...]
    for i in range(n_dp - 1):
        value = value + got[i]
    total[...] = value
    ch[col] = value[:, :split]
    for name in ("x", "y", "xy"):
        copies.start(ch.at[col], ch.at[col], name)
    rest = slice(split, None)
    others = [
        copies.start(total.at[:, rest], shared.at[i], name) for i, name in enumerate(PLANE)
    ]
    stay.finish()
    copies.land(*parts)
    half = n_dp // 2
    halves = (pl.ds(0, half), pl.ds(half, half))

    def gate_view(chip, h):
        return gates_out.at[chip, halves[h]]

    direct = {
        (name, h): copies.start(gate_view(col, h), gate_view(col, h), name)
        for h in (0, 1)
        for name in ("x", "y")
    }
    copies.land(*others)
    value = total[:, rest]
    for i in range(len(PLANE)):
        value = value + shared[i]
    sums_out[...] = value
    copies.land(direct["x", 0])
    far_x = gate_view(place.chip(1), 0)
    copies.start(far_x, far_x, "y")
    copies.land(direct["y", 1])
    far_y = gate_view(place.chip(2), 1)
    copies.start(far_y, far_y, "x")
    copies.finish()
    chans_out[...] = ch[...]


def sum_everywhere(mixed, split, gate_part, grads, n_dp, n_col):
    count = 2 * n_dp + 20
    rows, columns = mixed.shape
    rest = columns - split
    return pl.pallas_call(
        functools.partial(sums_kernel, n_dp, split),
        out_shape=(
            jax.ShapeDtypeStruct((rows, rest), f32),
            jax.ShapeDtypeStruct((n_col, rows, split), f32),
            jax.ShapeDtypeStruct((n_col, n_dp) + gate_part.shape, gate_part.dtype),
            jax.ShapeDtypeStruct(grads.shape, grads.dtype),
        ),
        in_specs=[in_vmem] + [anywhere] * 2,
        out_specs=(in_vmem, in_vmem) + (anywhere,) * 2,
        scratch_shapes=[
            pltpu.VMEM((n_dp - 1, rows, columns), f32),
            pltpu.VMEM((rows, columns), f32),
            pltpu.VMEM((n_col, rows, split), f32),
            pltpu.VMEM((len(PLANE), rows, rest), f32),
            pltpu.SemaphoreType.DMA((count,)),
            pltpu.SemaphoreType.DMA((count,)),
            pltpu.SemaphoreType.DMA((2,)),
            pltpu.VMEM(gate_part.shape, gate_part.dtype),
            pltpu.VMEM(grads.shape[1:], grads.dtype),
        ],
        compiler_params=pltpu.CompilerParams(
            collective_id=5, has_side_effects=True, vmem_limit_bytes=24 * MIB
        ),
        name="small_sums",
    )(mixed, gate_part, grads)


def one_less_exp(z):
    series = 1.0 + z / 6.0
    for n in (5.0, 4.0, 3.0, 2.0):
        series = 1.0 + z / n * series
    return jnp.where(z > -0.1, -z * series, 1.0 - jnp.exp(z))


def scan_tile(a, u, reverse):
    rows = a.shape[0]
    index = lax.broadcasted_iota(jnp.int32, a.shape, 0)
    by = 1
    while by < rows:
        turn = rows - by if reverse else by
        inside = index < rows - by if reverse else index >= by
        u = u + a * jnp.where(inside, pltpu.roll(u, turn, 0), 0.0)
        a = a * jnp.where(inside, pltpu.roll(a, turn, 0), 1.0)
        by *= 2
    return a, u


def forward_kernel(
    geo,
    x_all,
    w_rec,
    gain,
    gates_blk,
    gates_tile,
    bias,
    soft,
    conv_w,
    conv_b,
    places,
    cotangent,
    rec_out,
    mlp_in,
    mlp_out,
    n1_out,
    x_out,
    y_out,
    pre_out,
    c_out,
    state_out,
    branch_out,
    first_out,
    g_all,
    w_out,
    w_in,
    w_down,
    xv,
    wv,
    before,
    xb,
    yv,
    prev,
    cv,
    hv,
    pv,
    bv,
    carry,
    first,
    send,
    recv,
    local,
    stay_sems,
    *bufs,
):
    place = Place()
    place.meet(AROUND + ("next", "prev"))
    copies = Copies(place, send, recv)
    n_col, part, bw, tiles, wide = geo
    chans = bw + LANES
    group, width = xv.shape
    tile = 256
    n_tiles = group // tile
    loads = [copies.keep(x_all, xv, local.at[0]), copies.keep(w_rec, wv, local.at[1])]
    halo = copies.start(x_all.at[pl.ds(group - ROWS, ROWS), :], before, "next")
    found = weight_pieces(geo, (None, rec_out, mlp_in, mlp_out), (None, w_out, w_in, w_down))
    pieces = found["rec_out"] + found["mlp_in"] + found["mlp_out"]
    dealer = Dealer(copies, 9)
    for piece in pieces[:5]:
        dealer.deal(piece)
    for load in loads:
        load.wait()
    own_block = (cotangent, block_view(cotangent, g_all, place.row, place.col, None))
    stay = Stay([own_block] + own_pieces(place, pieces), bufs, stay_sems)
    high_tile = place.col >= 2
    idle_tile = lax.rem(place.col, 2) == 1

    def normed(x):
        x = x.astype(f32)
        scale = lax.rsqrt(jnp.sum(x * x, axis=-1, keepdims=True) / width + epsilon)
        return (x * scale * gain[...]).astype(low)

    copies.land(halo)
    xb[0:8, :] = dot(normed(before[...]), wv[:, : 2 * bw])[ROWS - 8 :]
    carry[0:1] = jnp.zeros_like(carry[0:1])
    carry[1:2] = jnp.ones_like(carry[1:2])

    def work(i, unused):
        r0 = pl.multiple_of(i * tile, tile)
        rows = pl.ds(r0, tile)
        n1 = normed(xv[rows, :])
        xv[rows, :] = n1
        both = dot(n1, wv[...])
        xb[pl.ds(pl.multiple_of(r0 + 8, 8), tile), :] = both[:, : 2 * bw]
        yv[rows, :] = both[:, 2 * bw :]
        spot = places[rows, :]
        reach = xb[pl.ds(r0, tile + 8), :]
        conv = []
        for lane in range(2 * bw // LANES):
            at = slice(lane * LANES, (lane + 1) * LANES)
            near = reach[:, at]
            total = conv_b[0:1, at] + conv_w[0:1, at] * near[8:]
            for t in range(1, conv_w.shape[0]):
                lagged = pltpu.roll(near, t, 0)[8:]
                total = total + jnp.where(spot >= t, conv_w[t : t + 1, at] * lagged, 0.0)
            conv.append(total.astype(low))
        c = jnp.concatenate(conv, axis=1)
        cv[rows, :] = c
        pre = [
            jnp.concatenate([dot(c[:, :bw], gates_blk[j]), dot(c[:, bw:], gates_tile[j])], axis=1)
            + bias[j : j + 1, :]
            for j in range(2)
        ]
        prev[rows, :chans] = pre[0]
        prev[rows, chans:] = pre[1]
        reset = spot == 0
        for lane in range(chans // LANES):
            at = slice(lane * LANES, (lane + 1) * LANES)
            if lane * LANES < bw:
                own_c = conv[lane].astype(f32)
            else:
                own_c = jnp.where(high_tile, conv[lane + 1].astype(f32), conv[lane].astype(f32))
            log_a = -8.0 * jax.nn.sigmoid(pre[1][:, at]) * soft[0:1, at]
            a = jnp.where(reset, 0.0, jnp.exp(log_a))
            m = jnp.where(reset, 1.0, jnp.sqrt(one_less_exp(2.0 * log_a)))
            u = own_c * jax.nn.sigmoid(pre[0][:, at]) * m
            a, u = scan_tile(a, u, False)
            h = u + a * carry[0:1, at]
            p = a * carry[1:2, at]
            hv[rows, at] = h
            pv[rows, at] = p
            carry[0:1, at] = h[tile - 1 :]
            carry[1:2, at] = p[tile - 1 :]
        return unused

    third = n_tiles // 3
    lax.fori_loop(0, third, work, 0)
    stay.turn()
    dealer.forward()
    dealer.forward()
    dealer.deal(pieces[5])
    dealer.forward()
    lax.fori_loop(third, 2 * third, work, 0)
    dealer.forward()
    dealer.deal(pieces[6])
    lax.fori_loop(2 * third, n_tiles, work, 0)
    dealer.forward()
    dealer.deal(pieces[7])
    state_in = copies.start(hv.at[pl.ds(group - 8, 8), :], first, "next")
    outs = [
        copies.keep(src, dst, local.at[10 + i])
        for i, (src, dst) in enumerate(
            ((xv, n1_out), (xb, x_out), (yv, y_out), (prev, pre_out), (cv, c_out))
        )
    ]
    copies.land(state_in)
    copies.leave(state_in)
    before_all = first[7:8, :]

    def finish(i, unused):
        rows = pl.ds(pl.multiple_of(i * tile, tile), tile)
        for lane in range(chans // LANES):
            at = slice(lane * LANES, (lane + 1) * LANES)
            state = hv[rows, at] + pv[rows, at] * before_all[:, at]
            hv[rows, at] = state
            value, _ = tanh_parts(yv[rows, at])
            b = state * value
            if lane * LANES >= bw:
                b = jnp.where(idle_tile, 0.0, b)
            bv[rows, at] = b.astype(low)
        return unused

    lax.fori_loop(0, n_tiles, finish, 0)
    outs += [
        copies.keep(hv, state_out, local.at[15]),
        copies.keep(bv, branch_out, local.at[16]),
        copies.keep(first, first_out, local.at[17]),
    ]
    dealer.forward()
    gather = block_gather(copies, cotangent, g_all)
    dealer.forward()
    dealer.forward()
    gather.pass_on()
    gather.last()
    copies.finish()
    for copy in outs:
        copy.wait()
    stay.finish()


def rec_forward(x_all, w_rec, params, places, cotangent, rec_out, mlp_in, mlp_out, geo):
    n_col, part, bw, tiles, wide = geo
    width, span, chans = part * n_col, wide * LANES, bw + LANES
    group = x_all.shape[0]

    def of(shape, dtype):
        return jax.ShapeDtypeStruct(shape, dtype)

    kept = [
        ((group, width), low),
        ((group + 8, 2 * bw), f32),
        ((group, chans), f32),
        ((group, 2 * chans), f32),
        ((group, 2 * bw), low),
        ((group, chans), f32),
        ((group, chans), low),
        ((8, chans), f32),
    ]
    dealt = [((group, width), low), ((chans, width), low), ((2, width, span), low), ((span, width), low)]
    copy_count = 1 + 6 * 8 + 12 + 1
    return pl.pallas_call(
        functools.partial(forward_kernel, geo),
        out_shape=tuple(of(*s) for s in kept + dealt),
        in_specs=[anywhere] * 2 + [in_vmem] * 8 + [anywhere] * 4,
        out_specs=(anywhere,) * 12,
        scratch_shapes=[
            pltpu.VMEM((group, width), low),
            pltpu.VMEM(w_rec.shape, low),
            pltpu.VMEM((ROWS, width), low),
            pltpu.VMEM((group + 8, 2 * bw), f32),
            pltpu.VMEM((group, chans), f32),
            pltpu.VMEM((group, 2 * chans), f32),
            pltpu.VMEM((group, 2 * bw), low),
            pltpu.VMEM((group, chans), f32),
            pltpu.VMEM((group, chans), f32),
            pltpu.VMEM((group, chans), low),
            pltpu.VMEM((8, chans), f32),
            pltpu.VMEM((8, chans), f32),
            pltpu.SemaphoreType.DMA((copy_count,)),
            pltpu.SemaphoreType.DMA((copy_count,)),
            pltpu.SemaphoreType.DMA((18,)),
            pltpu.SemaphoreType.DMA((9,)),
            pltpu.VMEM(cotangent.shape, low),
            pltpu.VMEM((bw, part), low),
            pltpu.VMEM((LANES, part), low),
        ]
        + [pltpu.VMEM((part, span // 2), low)] * 4
        + [pltpu.VMEM((span // 2, part), low)] * 2,
        compiler_params=pltpu.CompilerParams(
            collective_id=2, has_side_effects=True, vmem_limit_bytes=58 * MIB
        ),
        name="rec_forward",
    )(x_all, w_rec, *params, places, cotangent, rec_out, mlp_in, mlp_out)


def backward_kernel(
    geo,
    d_out,
    w_out,
    y_in,
    state_in,
    first_in,
    pre_in,
    c_in,
    x_in,
    gates_blk,
    gates_rows,
    soft,
    conv_w,
    places,
    down,
    d_all,
    d_rec_out,
    gate_out,
    sums,
    down_out,
    buf,
    wv,
    dbv,
    yv,
    hs,
    prev,
    cv,
    xb,
    ghv,
    qv,
    dpv,
    there,
    dcv,
    drv,
    gg,
    glo,
    gfar,
    carry,
    message,
    down_buf,
    send,
    recv,
    local,
    stay_sem,
):
    place = Place()
    n_dp = glo.shape[0]
    far = [f"d{d}" for d in range(1, n_dp)]
    place.meet(["x", "y", "xy", "core", "next", "prev"] + far)
    copies = Copies(place, send, recv)
    n_col, part, bw, tiles, wide = geo
    chans = bw + LANES
    own = d_out.shape[0]
    group = yv.shape[0]
    tile = 256
    n_tiles = group // tile
    lanes = [slice(k * LANES, (k + 1) * LANES) for k in range(chans // LANES)]
    gather = slot_gather(copies, d_out, buf, own)
    me = place.row * n_col + place.col
    load = copies.keep(w_out, wv, local.at[0])
    mine = copies.keep(d_out, buf.at[me], local.at[1])
    loads = [
        copies.keep(src, dst, local.at[2 + i])
        for i, (src, dst) in enumerate(
            (
                (y_in, yv),
                (state_in, hs.at[pl.ds(8, group), :]),
                (first_in, hs.at[pl.ds(0, 8), :]),
                (pre_in, prev),
                (c_in, cv),
                (x_in, xb),
            )
        )
    ]
    load.wait()
    mine.wait()
    high_tile = place.col >= 2
    idle_tile = lax.rem(place.col, 2) == 1

    def work(chip):
        slots = (chip, n_col + chip)
        value = dot(jnp.concatenate([buf[s] for s in slots], axis=0), wv[...], ((1,), (1,)))
        for n, s in enumerate(slots):
            rows = pl.ds(pl.multiple_of(s * own, ROWS), own)
            dbv[rows, :] = value[n * own : (n + 1) * own]

    copies.land(gather.own)
    work(place.col)
    x0, y0, x1, y1 = gather.pass_on()
    start_deal(copies, down, down_out)
    stay = Stay([(down.at[place.col], down_out.at[place.col])], [down_buf], stay_sem)
    stay.turn()
    copies.land(y0, y1)
    work(place.chip(2))
    corner = gather.last()
    copies.land(x0, x1)
    work(place.chip(1))
    copies.land(corner)
    out = copies.keep(buf, d_all, local.at[8])
    work(place.chip(3))
    for each in loads:
        each.wait()

    def coeffs(rows, at, spot):
        rate = jax.nn.sigmoid(prev[rows, slice(chans + at.start, chans + at.stop)])
        log_a = -8.0 * rate * soft[0:1, at]
        return rate, log_a, jnp.where(spot == 0, 0.0, jnp.exp(log_a))

    carry[0:1] = jnp.zeros_like(carry[0:1])
    carry[1:2] = jnp.ones_like(carry[1:2])

    def scan_back(k, unused):
        r0 = pl.multiple_of((n_tiles - 1 - k) * tile, tile)
        rows = pl.ds(r0, tile)
        spot = places[rows, :]
        last = lax.broadcasted_iota(jnp.int32, spot.shape, 0) == tile - 1
        for at in lanes:
            d_branch = dbv[rows, at]
            if at.start >= bw:
                d_branch = jnp.where(idle_tile, 0.0, d_branch)
            value, slope = tanh_parts(yv[rows, at])
            state = hs[pl.ds(pl.multiple_of(r0 + 8, 8), tile), at]
            d_state = d_branch * value
            drv[rows, slice(chans + at.start, chans + at.stop)] = (d_branch * state * slope).astype(low)
            _, _, a = coeffs(rows, at, spot)
            a, u = scan_tile(a, a * d_state, True)
            m = u + a * carry[0:1, at]
            q = a * carry[1:2, at]
            ghv[rows, at] = d_state + jnp.where(last, carry[0:1, at], pltpu.roll(m, tile - 1, 0))
            qv[rows, at] = jnp.where(last, carry[1:2, at], pltpu.roll(q, tile - 1, 0))
            carry[0:1, at] = m[0:1]
            carry[1:2, at] = q[0:1]
        return unused

    lax.fori_loop(0, n_tiles, scan_back, 0)
    arriving = copies.start(carry, message, "prev")
    copies.land(arriving)
    sums[...] = jnp.zeros_like(sums)
    gg[...] = jnp.zeros_like(gg)

    def through_gates(k, unused):
        r0 = pl.multiple_of(k * tile, tile)
        rows = pl.ds(r0, tile)
        spot = places[rows, :]
        reset = spot == 0
        for n, at in enumerate(lanes):
            g = ghv[rows, at] + qv[rows, at] * message[0:1, at]
            before = pltpu.roll(hs[pl.ds(r0, tile + 8), at], 1, 0)[8:]
            if at.start < bw:
                c = cv[rows, at].astype(f32)
            else:
                c = jnp.where(
                    high_tile,
                    cv[rows, slice(at.start + LANES, at.stop + LANES)].astype(f32),
                    cv[rows, at].astype(f32),
                )
            gate = jax.nn.sigmoid(prev[rows, at])
            rate, log_a, a = coeffs(rows, at, spot)
            m = jnp.where(reset, 1.0, jnp.sqrt(one_less_exp(2.0 * log_a)))
            gated = gate * m
            d_log = jnp.where(reset, 0.0, g * before * a - g * c * gate * a * a / m)
            d_pre_in = (g * c * gated * (1.0 - gate)).astype(low)
            d_pre_rate = (d_log * (-8.0 * soft[0:1, at]) * rate * (1.0 - rate)).astype(low)
            dpv[rows, at] = d_pre_in
            dpv[rows, slice(chans + at.start, chans + at.stop)] = d_pre_rate
            dcv[rows, at] = g * gated
            sums[0:1, at] += jnp.sum(d_pre_in.astype(f32), axis=0, keepdims=True)
            sums[1:2, at] += jnp.sum(d_pre_rate.astype(f32), axis=0, keepdims=True)
            sums[2:3, at] += jnp.sum(d_log * (-8.0 * rate), axis=0, keepdims=True)
        return unused

    swaps = []
    for h in range(2):
        lax.fori_loop(h * n_tiles // 2, (h + 1) * n_tiles // 2, through_gates, 0)
        rows = pl.ds(h * group // 2, group // 2)
        for j in range(2):
            swaps.append(
                copies.start(
                    dpv.at[rows, pl.ds(j * chans + bw, LANES)],
                    there.at[rows, pl.ds(j * LANES, LANES)],
                    "y",
                )
            )

    def through_blocks(k, unused):
        rows = pl.ds(pl.multiple_of(k * tile, tile), tile)
        c = cv[rows, :]
        d_blk = dcv[rows, :bw]
        d_tile = dcv[rows, bw:]
        for j in range(2):
            p_blk = dpv[rows, slice(j * chans, j * chans + bw)]
            here = dpv[rows, slice(j * chans + bw, (j + 1) * chans)]
            far = there[rows, slice(j * LANES, (j + 1) * LANES)]
            five = jnp.concatenate(
                [jnp.where(high_tile, far, here), jnp.where(high_tile, here, far)], axis=1
            )
            d_blk = d_blk + dot(p_blk, gates_blk[j], ((1,), (1,)))
            d_tile = d_tile + dot(five, gates_rows[j], ((1,), (1,)))
            gg[j, :, :bw] += dot(c[:, :bw], p_blk, ((0,), (0,)))
            gg[j, :, bw:] += dot(c[:, bw:], here, ((0,), (0,)))
        dcv[rows, :bw] = d_blk
        dcv[rows, bw:] = d_tile
        return unused

    copies.land(swaps[0], swaps[1])
    lax.fori_loop(0, 1, through_blocks, 0)
    later = copies.start(dcv.at[pl.ds(0, 8), :], dcv.at[pl.ds(group, 8), :], "prev")
    lax.fori_loop(1, n_tiles // 2, through_blocks, 0)
    copies.land(swaps[2], swaps[3])
    lax.fori_loop(n_tiles // 2, n_tiles, through_blocks, 0)
    part_rows = gate_out.shape[0]
    for p in range(n_dp):
        j, first_row = divmod(p * part_rows, bw)
        glo[p] = gg[j, first_row : first_row + part_rows].astype(low)
    parts = [
        copies.start(glo.at[jnp.bitwise_xor(place.dp, d + 1)], gfar.at[d], name)
        for d, name in enumerate(far)
    ]
    copies.land(later)

    def through_conv(k, unused):
        r0 = pl.multiple_of(k * tile, tile)
        rows = pl.ds(r0, tile)
        ext = pl.ds(r0, tile + 8)
        spot = places[ext, :]
        for at in lanes:
            reach = dcv[ext, at]
            if at.start < bw:
                x = xb[ext, at]
            else:
                x = jnp.where(high_tile, xb[ext, slice(at.start + LANES, at.stop + LANES)], xb[ext, at])
            d_c = reach[:tile]
            d_x = conv_w[0:1, at] * d_c
            sums[3:4, at] += jnp.sum(d_c * x[8:], axis=0, keepdims=True)
            for t in range(1, conv_w.shape[0]):
                term = jnp.where(spot >= t, conv_w[t : t + 1, at] * reach, 0.0)
                d_x = d_x + pltpu.roll(term, tile + 8 - t, 0)[:tile]
                lagged = pltpu.roll(x, t, 0)[8:]
                here = jnp.where(spot[:tile] >= t, d_c * lagged, 0.0)
                sums[3 + t : 4 + t, at] += jnp.sum(here, axis=0, keepdims=True)
            sums[7:8, at] += jnp.sum(d_c, axis=0, keepdims=True)
            drv[rows, at] = d_x.astype(low)
        return unused

    lax.fori_loop(0, n_tiles, through_conv, 0)
    out_rec = copies.keep(drv, d_rec_out, local.at[9])
    copies.land(*parts)
    total = glo[place.dp].astype(f32)
    for d in range(n_dp - 1):
        total = total + gfar[d].astype(f32)
    gate_out[...] = total.astype(low)
    copies.finish()
    out.wait()
    out_rec.wait()
    stay.finish()


def rec_backward(d_out, w_out, kept, gates_blk, gates_rows, soft, conv_w, places, down, geo, n_dp):
    n_col, part, bw, tiles, wide = geo
    own, width = d_out.shape
    slots = 2 * n_col
    group, chans = slots * own, bw + LANES
    part_rows = 2 * bw // n_dp
    d_all, d_rec, gate_grads, sums, down_dealt = pl.pallas_call(
        functools.partial(backward_kernel, geo),
        out_shape=(
            jax.ShapeDtypeStruct((slots, own, width), low),
            jax.ShapeDtypeStruct((group, 2 * chans), low),
            jax.ShapeDtypeStruct((part_rows, chans), low),
            jax.ShapeDtypeStruct((8, chans), f32),
            jax.ShapeDtypeStruct(down.shape, low),
        ),
        in_specs=[anywhere] * 8 + [in_vmem] * 5 + [anywhere],
        out_specs=(anywhere, anywhere, in_vmem, in_vmem, anywhere),
        scratch_shapes=[
            pltpu.VMEM((slots, own, width), low),
            pltpu.VMEM(w_out.shape, low),
            pltpu.VMEM((group, chans), f32),
            pltpu.VMEM((group, chans), f32),
            pltpu.VMEM((group + 8, chans), f32),
            pltpu.VMEM((group, 2 * chans), f32),
            pltpu.VMEM((group, 2 * bw), low),
            pltpu.VMEM((group + 8, 2 * bw), f32),
            pltpu.VMEM((group, chans), f32),
            pltpu.VMEM((group, chans), f32),
            pltpu.VMEM((group, 2 * chans), low),
            pltpu.VMEM((group, 2 * LANES), low),
            pltpu.VMEM((group + 8, chans), f32),
            pltpu.VMEM((group, 2 * chans), low),
            pltpu.VMEM((2, bw, chans), f32),
            pltpu.VMEM((n_dp, part_rows, chans), low),
            pltpu.VMEM((n_dp - 1, part_rows, chans), low),
            pltpu.VMEM((8, chans), f32),
            pltpu.VMEM((8, chans), f32),
            pltpu.VMEM(down.shape[1:], low),
            pltpu.SemaphoreType.DMA((20 + n_dp,)),
            pltpu.SemaphoreType.DMA((20 + n_dp,)),
            pltpu.SemaphoreType.DMA((10,)),
            pltpu.SemaphoreType.DMA((1,)),
        ],
        compiler_params=pltpu.CompilerParams(
            collective_id=4, has_side_effects=True, vmem_limit_bytes=60 * MIB
        ),
        name="rec_backward",
    )(d_out, w_out, *kept, gates_blk, gates_rows, soft, conv_w, places, down)
    return d_all.reshape(group, width), d_rec, gate_grads, sums, down_dealt


def outer_kernel(n_dp, first_steps, left1, right1, left2, right2, out_ref):
    def multiply(left, right):
        total = dot(left[...], right[...], ((0,), (0,)))
        rows = total.shape[0] // n_dp
        for k in range(n_dp):
            out_ref[k, 0] = total[k * rows : (k + 1) * rows].astype(out_ref.dtype)

    j = pl.program_id(1)

    @pl.when(j < first_steps)
    def _():
        multiply(left1, right1)

    @pl.when(j >= first_steps)
    def _():
        multiply(left2, right2)


def outer_one_kernel(n_dp, left, right, out_ref):
    total = dot(left[...], right[...], ((0,), (0,)))
    rows = total.shape[0] // n_dp
    for k in range(n_dp):
        out_ref[k, 0] = total[k * rows : (k + 1) * rows].astype(out_ref.dtype)


def outer(left, right, n_dp, n_col, columns, name):
    length, width = left.shape
    part = width // n_col
    count = right.shape[1]
    return pl.pallas_call(
        functools.partial(outer_one_kernel, n_dp),
        grid=(n_col, count // columns),
        out_shape=jax.ShapeDtypeStruct((n_dp, n_col, part // n_dp, count), low),
        in_specs=[
            pl.BlockSpec((length, part), lambda i, j: (0, i)),
            pl.BlockSpec((length, columns), lambda i, j: (0, j)),
        ],
        out_specs=pl.BlockSpec((n_dp, 1, part // n_dp, columns), lambda i, j: (0, i, 0, j)),
        compiler_params=pltpu.CompilerParams(vmem_limit_bytes=48 * MIB),
        cost_estimate=pl.CostEstimate(
            flops=2 * length * width * count,
            bytes_accessed=2 * (length * width + length * count + width * count),
            transcendentals=0,
        ),
        name=name,
    )(left, right)


def outer_pair(left1, right1, left2, right2, n_dp, n_col, columns, name):
    length, width = left1.shape
    part = width // n_col
    steps1, steps2 = right1.shape[1] // columns, right2.shape[1] // columns
    count = (steps1 + steps2) * columns
    left_block = pl.BlockSpec((length, part), lambda i, j: (0, i))
    return pl.pallas_call(
        functools.partial(outer_kernel, n_dp, steps1),
        grid=(n_col, steps1 + steps2),
        out_shape=jax.ShapeDtypeStruct((n_dp, n_col, part // n_dp, count), low),
        in_specs=[
            left_block,
            pl.BlockSpec((length, columns), lambda i, j: (0, jnp.minimum(j, steps1 - 1))),
            left_block,
            pl.BlockSpec((length, columns), lambda i, j: (0, jnp.maximum(j - steps1, 0))),
        ],
        out_specs=pl.BlockSpec((n_dp, 1, part // n_dp, columns), lambda i, j: (0, i, 0, j)),
        compiler_params=pltpu.CompilerParams(vmem_limit_bytes=48 * MIB),
        cost_estimate=pl.CostEstimate(
            flops=2 * length * width * count,
            bytes_accessed=2 * (2 * length * width + length * count + width * count),
            transcendentals=0,
        ),
        name=name,
    )(left1, right1, left2, right2)


def dot(a, b, dims=((1,), (0,))):
    return lax.dot_general(a, b, (dims, ((), ())), preferred_element_type=f32)


def places_of(rows, lengths):
    ends = jnp.cumsum(lengths)
    starts = ends - lengths
    inside = (rows[:, None] >= starts[None, :]) & (rows[:, None] < ends[None, :])
    places = rows - jnp.sum(jnp.where(inside, starts[None, :], 0), axis=1)
    return jnp.where(jnp.any(inside, axis=1), places, 0)


def body(
    tokens,
    cotangent,
    rec_in,
    rec_out,
    gates,
    gate_bias,
    decay,
    conv_w,
    conv_b,
    gains,
    mlp_in,
    mlp_out,
    lengths,
    order,
):
    n_dp, n_row, n_col = (lax.axis_size(a) for a in ("dp", "row", "col"))
    dp, row, col = (lax.axis_index(a) for a in ("dp", "row", "col"))
    given, part = tokens.shape
    own = given // n_col
    group = given * n_row
    width = part * n_col
    taps = conv_w.shape[0]
    blocks, bw = gates.shape[1], gates.shape[2]
    half = rec_out.shape[0]
    hidden_half = mlp_out.shape[0]
    tiles = hidden_half // LANES
    wide = -(-tiles // n_col)
    span = wide * LANES
    shared = n_col * bw
    chans = bw + LANES

    geo = (n_col, part, bw, tiles, wide)
    x_all, w_rec, gains_all = open_gather(tokens, rec_in, gains, geo)
    gains_all = gains_all.transpose(1, 0, 2).reshape(gains.shape[0], width)
    w_x, w_y = w_rec[:, : 2 * bw], w_rec[:, 2 * bw :]

    tile_at = shared + (col // 2) * LANES

    def own_channels(x):
        blk = lax.dynamic_slice_in_dim(x, col * bw, bw, axis=-1)
        tile = lax.dynamic_slice_in_dim(x, tile_at, LANES, axis=-1)
        return jnp.concatenate([blk, tile], axis=-1)

    def block_channels(x):
        blk = lax.dynamic_slice_in_dim(x, col * bw, bw, axis=-1)
        return jnp.concatenate([blk, x[..., shared:]], axis=-1)

    bias = own_channels(gate_bias)
    decay_o = own_channels(decay)
    conv_w_c = block_channels(conv_w)
    conv_b_c = block_channels(conv_b)
    conv_w_o = own_channels(conv_w)
    gates_blk = lax.dynamic_index_in_dim(gates, col, axis=1, keepdims=False)
    gates_five = gates[:, n_col]
    gates_tile = lax.dynamic_slice_in_dim(gates_five, (col // 2) * LANES, LANES, axis=2)
    gates_rows = lax.dynamic_slice_in_dim(gates_five, (col // 2) * LANES, LANES, axis=1)

    base = dp * group
    places = places_of(base + jnp.arange(group + 8, dtype=jnp.int32), lengths)
    places = jnp.broadcast_to(places[:, None], (group + 8, LANES))
    soft = jax.nn.softplus(decay_o)[None, :]

    n1, x_rows, y_branch, pre_both, conv_low, state, branch, first, g_all, w_out, w_in, w_down = rec_forward(
        x_all,
        w_rec,
        (
            gains_all[0:1],
            gates_blk,
            gates_tile,
            bias,
            soft,
            conv_w_c,
            conv_b_c[None, :],
        ),
        places,
        cotangent,
        rec_out,
        mlp_in,
        mlp_out,
        geo,
    )
    rows_f, rows_b = ((own, width), f32), ((own, width), low)
    line, squares, home = ((8, width), f32), ((8, LANES), f32), ((given, part), low)
    resid, normed_two, squares_one = multiply_scatter(
        branch, w_out, False, 6, "out_one", after_out_one, (x_all, gains_all), (rows_f, rows_b, squares), False
    )

    def spare(at):
        return spare_window(at, tiles, n_col, wide)

    n2, hidden, d_glu = glu(normed_two, w_in, w_down, g_all, spare)
    g_down = outer(g_all, hidden, n_dp, n_col, 512, "outer_down")
    d_glu, hidden, g_down = lax.optimization_barrier((d_glu, hidden, g_down))
    sum_down = lax.psum_scatter(g_down, "dp", scatter_dimension=0)
    g_in = outer(n2, d_glu, n_dp, n_col, 512, "outer_in")
    d_glu, g_in = lax.optimization_barrier((d_glu, g_in))
    d_resid, d_out, gain_two = multiply_scatter(
        d_glu,
        w_in,
        True,
        7,
        "d_normed_two",
        after_normed_two,
        (resid, g_all, gains_all),
        (rows_f, rows_b, line),
        False,
    )
    g_in, sum_down, d_out = lax.optimization_barrier((g_in, sum_down, d_out))
    sum_in = lax.psum_scatter(g_in, "dp", scatter_dimension=0)

    d_out_all, d_rec, gate_sums, small, down = rec_backward(
        d_out,
        w_out,
        (y_branch, state, first, pre_both, conv_low, x_rows),
        gates_blk,
        gates_rows,
        soft,
        conv_w_o,
        places,
        sum_down,
        geo,
        n_dp,
    )
    small = small.at[2].multiply(jax.nn.sigmoid(decay_o))
    w_x_own = jnp.concatenate(
        [w_x[:, :bw], lax.dynamic_slice_in_dim(w_x, bw + (col // 2) * LANES, LANES, axis=1)], axis=1
    )
    w_back = jnp.concatenate([w_x_own, w_y], axis=1)
    g_rec = outer_pair(n1, d_rec, d_out_all, branch, n_dp, n_col, chans, "outer_rec")
    g_rec, d_rec = lax.optimization_barrier((g_rec, d_rec))
    grad_input, gain_one, squares_x = multiply_scatter(
        d_rec,
        w_back,
        True,
        9,
        "d_normed_one",
        after_normed_one,
        (x_all, d_resid, gains_all),
        (home, line, squares),
        True,
    )
    g_rec, sum_in, grad_input, hidden = lax.optimization_barrier((g_rec, sum_in, grad_input, hidden))
    sum_rec = lax.psum_scatter(g_rec, "dp", scatter_dimension=0)
    result, squares_two = multiply_scatter(
        hidden, w_down, False, 8, "out_two", after_out_two, (resid,), (home, squares), True
    )

    def windows(got, first):
        return [
            got[c][..., first + (LANES if c > n_col - 1 - (wide * n_col - tiles) else 0) : first + span]
            for c in range(n_col)
        ]

    def channels_of(got, first):
        return [got[c][..., first : first + bw] for c in range(n_col)] + [
            got[c][..., first + bw : first + chans] for c in range(0, n_col, 2)
        ]

    square_sums = jnp.stack([squares_x[0, 0], squares_one[0, 0], squares_one[1, 0], squares_two[0, 0]])
    lines = small.shape[0]
    gain_sums = jnp.concatenate([gain_one[:1], gain_two[:1]]).reshape(lines, 2 * width // lines)
    stat_block = jnp.pad(square_sums[None, :], ((0, lines - 1), (0, LANES - 4)))
    mixed = jnp.concatenate([small, gain_sums, stat_block], axis=1)
    sums, chan_sums, gate_parts, into = sum_everywhere(
        mixed, chans, gate_sums, sum_in, n_dp, n_col
    )
    sum_rec, into = lax.optimization_barrier((sum_rec, into))
    recs = deal_back(sum_rec, 10, "deal_rec")
    grad_mlp_in = jnp.stack(
        [jnp.concatenate(windows(into[..., j * span : (j + 1) * span], 0), axis=-1) for j in range(2)]
    ).astype(f32)
    grad_mlp_out = jnp.concatenate(windows(down, 0), axis=-1).astype(f32).T
    grad_rec_in = jnp.stack(
        [jnp.concatenate(channels_of(recs, j * chans), axis=-1) for j in range(2)]
    ).astype(f32)
    grad_rec_out = jnp.concatenate(channels_of(recs, 2 * chans), axis=-1).astype(f32).T
    mine = jnp.concatenate(channels_of(chan_sums, 0), axis=-1)
    gain_rows = sums[:, : 2 * width // lines].reshape(2, width)
    grad_gains = lax.dynamic_slice_in_dim(gain_rows, col * part, part, axis=1)
    stats = jnp.sqrt(sums[0, 2 * width // lines :][:4] / (n_dp * group * width))
    gate_parts = gate_parts.reshape(n_col, 2, bw, chans).astype(f32)
    five = jnp.concatenate([gate_parts[c, :, :, bw:] for c in range(0, n_col, 2)], axis=-1)
    grad_gates = jnp.stack([gate_parts[c, :, :, :bw] for c in range(n_col)] + [five], axis=1)
    return (
        result,
        grad_input,
        grad_rec_in,
        grad_rec_out,
        grad_gates,
        mine[0:2],
        mine[2],
        mine[3 : 3 + taps],
        mine[3 + taps],
        grad_gains,
        grad_mlp_in,
        grad_mlp_out,
        stats,
    )


def solution(mesh):
    placed = (
        P(("dp", "row"), "col"),
        P(("dp", "row"), "col"),
        P(None, "col", "row"),
        P("row", "col"),
        P(None, "row", None, None),
        P(None, "row"),
        P("row"),
        P(None, "row"),
        P("row"),
        P(None, "col"),
        P(None, "col", "row"),
        P("row", "col"),
        P(),
        P(),
    )
    return jax.shard_map(
        body,
        mesh=mesh,
        in_specs=placed,
        out_specs=(
            P(("dp", "row"), "col"),
            P(("dp", "row"), "col"),
            P(None, ("col", "dp"), "row"),
            P("row", ("col", "dp")),
            P(None, "row", None, None),
            P(None, "row"),
            P("row"),
            P(None, "row"),
            P("row"),
            P(None, "col"),
            P(None, ("col", "dp"), "row"),
            P("row", ("col", "dp")),
            P(),
        ),
        check_vma=False,
    )
```

```python
import functools

import jax
import jax.numpy as jnp
from jax import lax
from jax.experimental import pallas as pl
from jax.experimental.pallas import tpu as pltpu
from jax.sharding import PartitionSpec as P

epsilon = 1e-06
LANES = 128
ROWS = 16
MIB = 1024 * 1024
MESH = pl.DeviceIdType.MESH
low = jnp.bfloat16
f32 = jnp.float32
anywhere = pl.BlockSpec(memory_space=pl.ANY)
in_vmem = pl.BlockSpec(memory_space=pltpu.VMEM)


def window_tile(col, tiles, n_col, wide):
    spare = wide * n_col - tiles
    return col * wide - jnp.maximum(col - (n_col - 1 - spare), 0)


def spare_window(col, tiles, n_col, wide):
    spare = wide * n_col - tiles
    return col > n_col - 1 - spare


class Place:
    def __init__(self):
        self.dp, self.row, self.col = (lax.axis_index(a) for a in ("dp", "row", "col"))

    def chip(self, k):
        return jnp.bitwise_xor(self.col, k)

    def device(self, name):
        if name == "core":
            return {"row": 1 - self.row}
        if name == "z":
            return {"dp": jnp.bitwise_xor(self.dp, 1)}
        if name in ("next", "prev"):
            n_dp = lax.axis_size("dp")
            return {"dp": lax.rem(self.dp + (1 if name == "next" else n_dp - 1), n_dp)}
        if name[0] == "d":
            return {"dp": jnp.bitwise_xor(self.dp, int(name[1:]))}
        if name[0] == "c":
            return {"row": 1 - self.row, "col": self.chip({"x": 1, "y": 2, "xy": 3}[name[1:]])}
        return {"col": self.chip({"x": 1, "y": 2, "xy": 3}[name])}

    def meet(self, names):
        barrier = pltpu.get_barrier_semaphore()
        for name in names:
            pl.semaphore_signal(
                barrier, inc=1, device_id=self.device(name), device_id_type=MESH
            )
        pl.semaphore_wait(barrier, len(names))


class Copies:
    def __init__(self, place, send, recv):
        self.place, self.send, self.recv = place, send, recv
        self.made, self.landed, self.left, self.local = [], set(), set(), []

    def start(self, src, dst, to):
        i = len(self.made)
        copy = pltpu.make_async_remote_copy(
            src_ref=src,
            dst_ref=dst,
            send_sem=self.send.at[i],
            recv_sem=self.recv.at[i],
            device_id=self.place.device(to),
            device_id_type=MESH,
        )
        copy.start()
        self.made.append(copy)
        return i

    def land(self, *numbers):
        for i in numbers:
            if i not in self.landed:
                self.made[i].wait_recv()
                self.landed.add(i)

    def leave(self, *numbers):
        for i in numbers:
            if i not in self.left:
                self.made[i].wait_send()
                self.left.add(i)

    def keep(self, src, dst, sem):
        copy = pltpu.make_async_copy(src, dst, sem)
        copy.start()
        self.local.append(copy)
        return copy

    def finish(self):
        self.land(*range(len(self.made)))
        self.leave(*range(len(self.made)))


def share(rows, far_part):
    far = rows * far_part // 20 // ROWS * ROWS
    return rows - far, far


class Dealer:
    def __init__(self, copies, far_part):
        self.copies, self.far_part = copies, far_part
        self.waiting = []

    def deal(self, piece):
        place = self.copies.place
        odd = lax.rem(place.dp, 2)
        batch = []
        for name, k in (("x", 1), ("y", 2), ("xy", 3)):
            src, dst, rows = piece(place.chip(k), place.col)
            near, far = share(rows, self.far_part)
            start = pl.multiple_of(odd * far, ROWS)
            at = pl.ds(start, near)
            number = self.copies.start(src(at), dst(at), name)
            batch.append((k, number, piece))
        self.waiting.append(batch)

    def forward(self):
        place = self.copies.place
        odd = lax.rem(place.dp, 2)
        for k, number, piece in self.waiting.pop(0):
            self.copies.land(number)
            _, dst, rows = piece(place.col, place.chip(k))
            near, far = share(rows, self.far_part)
            at = pl.ds(pl.multiple_of(odd * near, ROWS), far)
            self.copies.start(dst(at), dst(at), "z")


def rows_of(ref, first, rows, lead=None, columns=None):
    def view(at):
        where = pl.ds(pl.multiple_of(first + at.start, ROWS), at.size)
        index = (where, columns if columns is not None else slice(None))
        return ref.at[index] if lead is None else ref.at[(lead,) + index]

    return view


def weight_pieces(geo, refs, outs):
    n_col, part, bw, tiles, wide = geo
    shared, span = n_col * bw, wide * LANES
    rec_in, rec_out, mlp_in, mlp_out = refs
    w_rec, w_out, w_in, w_down = outs

    def here(chip):
        return pl.multiple_of(chip * part, LANES)

    def blk(chip):
        return pl.multiple_of(chip * bw, LANES)

    def tile(chip):
        return pl.multiple_of(shared + lax.div(chip, 2) * LANES, LANES)

    def win(chip):
        return pl.multiple_of(window_tile(chip, tiles, n_col, wide) * LANES, LANES)

    def in_piece(ref, j, out, lead, source_at, size, column):
        def piece(dest, source):
            return (
                rows_of(ref, 0, part, j, pl.ds(pl.multiple_of(source_at(dest), LANES), size)),
                rows_of(out, here(source), part, lead, pl.ds(column, size)),
                part,
            )

        return piece

    def down_piece(ref, out, source_at, size, row):
        def piece(dest, source):
            return (
                rows_of(ref, source_at(dest), size),
                rows_of(out, row, size, None, pl.ds(here(source), part)),
                size,
            )

        return piece

    found = {}
    if rec_in is not None:
        found["rec_in"] = [
            in_piece(rec_in, 0, w_rec, None, blk, bw, 0),
            in_piece(rec_in, 0, w_rec, None, lambda chip: shared, bw, bw),
            in_piece(rec_in, 1, w_rec, None, blk, bw, 2 * bw),
            in_piece(rec_in, 1, w_rec, None, tile, LANES, 3 * bw),
        ]
    if rec_out is not None:
        found["rec_out"] = [
            down_piece(rec_out, w_out, blk, bw, 0),
            down_piece(rec_out, w_out, tile, LANES, bw),
        ]
    if mlp_in is not None:
        half = span // 2
        found["mlp_in"] = [
            in_piece(mlp_in, j, w_in, j, lambda chip, h=h: win(chip) + h * half, half, h * half)
            for j in range(2)
            for h in range(2)
        ]
    if mlp_out is not None:
        half = span // 2
        found["mlp_out"] = [
            down_piece(mlp_out, w_down, lambda chip, h=h: win(chip) + h * half, half, h * half)
            for h in range(2)
        ]
    return found


def own_pieces(place, pieces):
    pairs = []
    for piece in pieces:
        src, dst, rows = piece(place.col, place.col)
        pairs.append((src(pl.ds(0, rows)), dst(pl.ds(0, rows))))
    return pairs


class Stay:
    def __init__(self, pairs, bufs, sems):
        self.pairs, self.bufs, self.sems = pairs, bufs, sems
        self.loads = [
            pltpu.make_async_copy(src, buf, sems.at[i])
            for i, ((src, _), buf) in enumerate(zip(pairs, bufs))
        ]
        for load in self.loads:
            load.start()

    def turn(self):
        for load in self.loads:
            load.wait()
        self.stores = [
            pltpu.make_async_copy(buf, dst, self.sems.at[i])
            for i, ((_, dst), buf) in enumerate(zip(self.pairs, self.bufs))
        ]
        for store in self.stores:
            store.start()

    def finish(self):
        for store in self.stores:
            store.wait()


class Gather:
    def __init__(self, copies, mine, at):
        self.copies, self.at = copies, at
        place = copies.place
        row, col = place.row, place.col
        self.first = [
            copies.start(mine(half), at(row, col, half), name)
            for half in (0, 1)
            for name in ("x", "y")
        ]
        self.own = copies.start(mine(None), at(row, col, None), "core")
        self.rounds = []

    def pass_half(self, half):
        copies, place = self.copies, self.copies.place
        views = [self.at(place.row, place.chip(k), half) for k in (1, 2)]
        x, y = self.first[2 * half], self.first[2 * half + 1]
        if half == 0:
            copies.land(x)
            round_ = copies.start(views[0], views[0], "y")
            core_x = copies.start(views[0], views[0], "core")
            copies.land(y)
            core_y = copies.start(views[1], views[1], "core")
        else:
            copies.land(y)
            round_ = copies.start(views[1], views[1], "x")
            core_y = copies.start(views[1], views[1], "core")
            copies.land(x)
            core_x = copies.start(views[0], views[0], "core")
        self.rounds.append(round_)
        return core_x, core_y

    def pass_on(self):
        return self.pass_half(0) + self.pass_half(1)

    def last(self):
        copies, place = self.copies, self.copies.place
        corner = self.at(place.row, place.chip(3), None)
        copies.land(*self.rounds)
        return copies.start(corner, corner, "core")


def block_view(source, target, row, col, half):
    rows, part = source.shape
    cut = rows // 2
    first = row * rows + (0 if half is None else half * cut)
    size = rows if half is None else cut
    return target.at[
        pl.ds(pl.multiple_of(first, ROWS), size), pl.ds(pl.multiple_of(col * part, LANES), part)
    ]


def block_gather(copies, source, target):
    cut = source.shape[0] // 2

    def mine(half):
        return source if half is None else source.at[pl.ds(half * cut, cut), :]

    return Gather(copies, mine, functools.partial(block_view, source, target))


AROUND = ("x", "y", "xy", "core", "z")


def open_kernel(geo, tokens, rec_in, gains, x_all, w_rec, gains_all, send, recv, local, *bufs):
    place = Place()
    place.meet(AROUND)
    copies = Copies(place, send, recv)
    pieces = weight_pieces(geo, (rec_in, None, None, None), (w_rec, None, None, None))["rec_in"]
    dealer = Dealer(copies, 10)
    dealer.deal(pieces[0])
    dealer.deal(pieces[1])
    gather = block_gather(copies, tokens, x_all)
    own_block = (tokens, block_view(tokens, x_all, place.row, place.col, None))
    dealer.deal(pieces[2])
    dealer.deal(pieces[3])
    mine = gains_all.at[:, pl.ds(pl.multiple_of(place.col * geo[1], LANES), geo[1])]
    for name in ("x", "y", "xy"):
        copies.start(gains, mine, name)
    stay = Stay([own_block] + own_pieces(place, pieces) + [(gains, mine)], bufs, local)
    stay.turn()
    dealer.forward()
    dealer.forward()
    gather.pass_on()
    dealer.forward()
    dealer.forward()
    gather.last()
    copies.finish()
    stay.finish()


def open_gather(tokens, rec_in, gains, geo):
    n_col, part, bw, tiles, wide = geo
    width = part * n_col
    return pl.pallas_call(
        functools.partial(open_kernel, geo),
        out_shape=(
            jax.ShapeDtypeStruct((2 * tokens.shape[0], width), low),
            jax.ShapeDtypeStruct((width, 3 * bw + LANES), low),
            jax.ShapeDtypeStruct((gains.shape[0], width), f32),
        ),
        in_specs=[anywhere] * 3,
        out_specs=(anywhere,) * 3,
        scratch_shapes=[
            pltpu.SemaphoreType.DMA((39,)),
            pltpu.SemaphoreType.DMA((39,)),
            pltpu.SemaphoreType.DMA((6,)),
            pltpu.VMEM(tokens.shape, low),
            pltpu.VMEM((part, bw), low),
            pltpu.VMEM((part, bw), low),
            pltpu.VMEM((part, bw), low),
            pltpu.VMEM((part, LANES), low),
            pltpu.VMEM(gains.shape, f32),
        ],
        compiler_params=pltpu.CompilerParams(collective_id=1, has_side_effects=True),
        name="open_gather",
    )(tokens, rec_in, gains)


def slot_gather(copies, local_ref, buf, own):
    cut = own // 2
    n_col = buf.shape[0] // 2

    def at(row, col, half):
        slot = buf.at[row * n_col + col]
        return slot if half is None else slot.at[pl.ds(half * cut, cut), :]

    def mine(half):
        return local_ref if half is None else local_ref.at[pl.ds(half * cut, cut), :]

    return Gather(copies, mine, at)


def tanh_parts(x):
    k = 0.7978845608028654
    square = x * x
    t = jnp.tanh(k * x * (1.0 + 0.044715 * square))
    value = 0.5 * x * (1.0 + t)
    slope = 0.5 * (1.0 + t) + 0.5 * x * (1.0 - t * t) * k * (1.0 + 3 * 0.044715 * square)
    return value, slope


def glu_kernel(
    spare, n2, w_in, w_down, g_all, n2_all, hidden, d_glu, buf, wi, wd, g, hid, dgl, send, recv, local
):
    place = Place()
    place.meet(("x", "y", "core"))
    copies = Copies(place, send, recv)
    own, width = n2.shape
    n_col = buf.shape[0] // 2
    span = wd.shape[0]
    step = 512
    gather = slot_gather(copies, n2, buf, own)
    me = place.row * n_col + place.col
    n_steps = span // step
    near_slots = [place.col, n_col + place.col]
    far_slots = [r * n_col + place.chip(k) for k in (1, 2, 3) for r in (0, 1)]

    def load_rows(slot, i):
        rows = pl.ds(pl.multiple_of(slot * own, ROWS), own)
        return copies.keep(g_all.at[rows, :], g.at[rows, :], local.at[i])

    first = [copies.keep(n2, buf.at[me], local.at[3])]
    first += [load_rows(slot, 4 + i) for i, slot in enumerate(near_slots)]
    weights = []
    for i in range(n_steps):
        at = pl.ds(i * step, step)
        weights.append(
            (
                copies.keep(w_in.at[:, :, at], wi.at[:, :, at], local.at[12 + 2 * i]),
                copies.keep(w_down.at[at, :], wd.at[at, :], local.at[13 + 2 * i]),
            )
        )
    others = [load_rows(slot, 6 + i) for i, slot in enumerate(far_slots)]
    for load in first:
        load.wait()
    hide = spare(place.col)

    def work(slots, first, size, lo, hi):
        rows = [pl.ds(pl.multiple_of(s * own + first, ROWS), size) for s in slots]
        n2_here = jnp.concatenate([buf[s, first : first + size, :] for s in slots], axis=0)
        g_here = jnp.concatenate([g[r, :] for r in rows], axis=0)

        def columns(i, carry):
            at = pl.ds(pl.multiple_of(i * step, LANES), step)
            up_at = pl.ds(pl.multiple_of(span + i * step, LANES), step)
            gate = dot(n2_here, wi[0, :, at])
            up = dot(n2_here, wi[1, :, at])
            d_hid = dot(g_here, wd[at, :], ((1,), (1,)))
            lane = lax.broadcasted_iota(jnp.int32, gate.shape, 1) + i * step
            used = (lane >= LANES) | jnp.logical_not(hide)
            up = jnp.where(used, up, 0.0)
            d_hid = jnp.where(used, d_hid, 0.0)
            value, slope = tanh_parts(gate)
            h = (value * up).astype(low)
            dg = (d_hid * up * slope).astype(low)
            du = (d_hid * value).astype(low)
            for n, r in enumerate(rows):
                part = slice(n * size, (n + 1) * size)
                hid[r, at] = h[part]
                dgl[r, at] = dg[part]
                dgl[r, up_at] = du[part]
            return carry

        lax.fori_loop(lo, hi, columns, 0)

    def both_cores(*chips):
        return [s for chip in chips for s in (chip, n_col + chip)]

    half = own // 2
    near = both_cores(place.chip(1), place.chip(2))
    copies.land(gather.own)
    for i in range(n_steps):
        for load in weights[i]:
            load.wait()
        work(both_cores(place.col), 0, own, i, i + 1)
    for load in others:
        load.wait()
    core0 = gather.pass_half(0)
    copies.land(*core0)
    work(near, 0, half, 0, n_steps // 2)
    core1 = gather.pass_half(1)
    work(near, 0, half, n_steps // 2, n_steps)
    copies.land(*core1)
    work(near, half, half, 0, n_steps // 2)
    corner = gather.last()
    work(near, half, half, n_steps // 2, n_steps)
    copies.land(corner)
    out_n2 = copies.keep(buf, n2_all, local.at[0])
    work(both_cores(place.chip(3)), 0, own, 0, n_steps)
    out_h = copies.keep(hid, hidden, local.at[1])
    out_d = copies.keep(dgl, d_glu, local.at[2])
    copies.finish()
    out_n2.wait()
    out_h.wait()
    out_d.wait()


def glu(n2, w_in, w_down, g_all, spare):
    own, width = n2.shape
    group = g_all.shape[0]
    span = w_down.shape[0]
    n_all, h, d = pl.pallas_call(
        functools.partial(glu_kernel, spare),
        out_shape=(
            jax.ShapeDtypeStruct((group // own, own, width), low),
            jax.ShapeDtypeStruct((group, span), low),
            jax.ShapeDtypeStruct((group, 2 * span), low),
        ),
        in_specs=[anywhere] * 4,
        out_specs=(anywhere,) * 3,
        scratch_shapes=[
            pltpu.VMEM((group // own, own, width), low),
            pltpu.VMEM(w_in.shape, low),
            pltpu.VMEM(w_down.shape, low),
            pltpu.VMEM((group, width), low),
            pltpu.VMEM((group, span), low),
            pltpu.VMEM((group, 2 * span), low),
            pltpu.SemaphoreType.DMA((12,)),
            pltpu.SemaphoreType.DMA((12,)),
            pltpu.SemaphoreType.DMA((12 + 2 * (span // 256),)),
        ],
        compiler_params=pltpu.CompilerParams(
            collective_id=3, has_side_effects=True, vmem_limit_bytes=58 * MIB
        ),
        cost_estimate=pl.CostEstimate(
            flops=6 * group * width * span, bytes_accessed=60 * MIB, transcendentals=group * span
        ),
        name="glu",
    )(n2, w_in, w_down, g_all)
    return n_all.reshape(group, width), h, d


def start_home(copies, source, home, buf, sem):
    place = copies.place
    own, part = source.shape[0], home.shape[1]
    spot = home.at[pl.ds(pl.multiple_of(place.col * own, ROWS), own), :]

    def columns_of(chip):
        return source.at[:, pl.ds(pl.multiple_of(chip * part, LANES), part)]

    for name, j in (("xy", 3), ("x", 1), ("y", 2)):
        copies.start(columns_of(place.chip(j)), spot, name)
    return Stay([(columns_of(place.col), spot)], [buf], sem)


def scatter_kernel(shape, finish, n_more, n_outs, pick, beside, act, w, *refs):
    n_parts, across, own, width = shape
    side = []
    if beside is not None:
        n_in, n_out, n_hold = beside.counts
        side, refs = list(refs[:n_in]), refs[n_in:]
    more, refs = refs[:n_more], refs[n_more:]
    outs, refs = refs[:n_outs], refs[n_outs:]
    if beside is not None:
        side += refs[:n_out]
        side += refs[len(refs) - n_hold :]
        refs = refs[n_out : len(refs) - n_hold]
    actv, wv, other, mine, from_core, from_x, from_y, turn, fin, send, recv, local = refs[:12]
    held = refs[12 : 12 + n_more]
    place = Place()
    place.meet(["x", "y", "core"] + ([] if beside is None else beside.names()))
    copies = Copies(place, send, recv)
    if beside is not None:
        beside.start(copies, *side)
    cut = own // 2
    n_col = act.shape[0] // own // 2
    k = act.shape[1] // n_parts
    step = 512
    loads = [copies.keep(act, actv, local.at[0])]
    if pick is None:
        loads.append(copies.keep(w, wv, local.at[1]))
    else:
        for i, (src, dst, size) in enumerate(pick(place.col)):
            loads.append(
                copies.keep(w.at[:, pl.ds(src, size)], wv.at[:, pl.ds(dst, size)], local.at[1 + i])
            )
    my_rows = pl.ds(pl.multiple_of((place.row * n_col + place.col) * own, ROWS), own)
    extra = []
    for i, (ref, buf) in enumerate(zip(more, held)):
        src = ref.at[my_rows, :] if ref.shape[0] > own else ref
        extra.append(copies.keep(src, buf, local.at[4 + i]))
    for load in loads:
        load.wait()
    top, bottom = pl.ds(0, cut), pl.ds(cut, cut)

    def work(j):
        chip = place.chip(j)
        slots = ((1 - place.row) * n_col + chip, place.row * n_col + chip)
        left = [
            jnp.concatenate(
                [
                    actv[pl.ds(pl.multiple_of(s * own, ROWS), own), n * k : (n + 1) * k]
                    for s in slots
                ],
                axis=0,
            )
            for n in range(n_parts)
        ]

        def columns(i, carry):
            at = pl.ds(pl.multiple_of(i * step, LANES), step)
            total = None
            for n in range(n_parts):
                if across:
                    right = wv[n, at, :] if n_parts > 1 else wv[at, :]
                    term = dot(left[n], right, ((1,), (1,)))
                else:
                    term = dot(left[n], wv[:, at])
                total = term if total is None else total + term
            other[j, :, at] = total[:own].astype(low)
            mine[j, :, at] = total[own:]
            return carry

        lax.fori_loop(0, width // step, columns, 0)
        return copies.start(other.at[j], from_core.at[j], "core")

    def add_core(j, number):
        copies.land(number)
        mine[j] = mine[j] + from_core[j].astype(f32)
        turn[j] = mine[j].astype(low)

    if beside is not None:
        beside.turn()
    core3 = work(3)
    core1 = work(1)
    add_core(3, core3)
    x3 = copies.start(turn.at[3, top, :], from_x.at[0], "x")
    y3 = copies.start(turn.at[3, bottom, :], from_y.at[0], "y")
    core2 = work(2)
    add_core(1, core1)
    x1 = copies.start(turn.at[1, top, :], from_x.at[1], "x")
    core0 = work(0)
    add_core(2, core2)
    y2 = copies.start(turn.at[2, bottom, :], from_y.at[1], "y")
    copies.land(x3)
    turn[2, top, :] = (mine[2, top, :] + from_x[0].astype(f32)).astype(low)
    y_last = copies.start(turn.at[2, top, :], from_y.at[2], "y")
    copies.land(y3)
    turn[1, bottom, :] = (mine[1, bottom, :] + from_y[0].astype(f32)).astype(low)
    x_last = copies.start(turn.at[1, bottom, :], from_x.at[2], "x")
    add_core(0, core0)
    copies.land(x1, y2, y_last, x_last)
    fin[top, :] = mine[0, top, :] + from_x[1].astype(f32) + from_y[2].astype(f32)
    fin[bottom, :] = mine[0, bottom, :] + from_y[1].astype(f32) + from_x[2].astype(f32)
    for load in extra:
        load.wait()
    for ref in outs:
        if ref.shape[0] == 8:
            ref[...] = jnp.zeros_like(ref)
    rows_at_once = 64

    def rows_done(i, carry):
        rows = pl.ds(pl.multiple_of(i * rows_at_once, rows_at_once), rows_at_once)
        finish(rows, fin, held, outs)
        return carry

    lax.fori_loop(0, own // rows_at_once, rows_done, 0)
    if beside is not None:
        beside.finish(copies, *side)
    copies.finish()


def multiply_scatter(act, w, across, number, name, finish, more, outs, pick=None, beside=None):
    n_parts = w.shape[0] if w.ndim == 3 else 1
    group = act.shape[0]
    n_col = lax.axis_size("col")
    own = group // (2 * n_col)
    width = w.shape[-2] if across else w.shape[-1]
    held = [((own, r.shape[1]) if r.shape[0] > own else r.shape, r.dtype) for r in more]
    out_specs = [in_vmem] * len(outs)
    scratch = [pltpu.VMEM(*h) for h in held]
    n_outs, side_in, copy_count = len(outs), (), 13
    in_specs = [anywhere] * (2 + len(more))
    if beside is not None:
        side_in, side_out, side_scratch = beside.inputs, beside.outputs, beside.scratch
        in_specs = in_specs[:2] + beside.in_specs + in_specs[2:]
        outs += side_out
        out_specs += beside.out_specs
        scratch += side_scratch
        copy_count += beside.copy_count
    return pl.pallas_call(
        functools.partial(
            scatter_kernel,
            (n_parts, across, own, width),
            finish,
            len(more),
            n_outs,
            pick,
            beside,
        ),
        out_shape=tuple(jax.ShapeDtypeStruct(*s) for s in outs),
        in_specs=in_specs,
        out_specs=tuple(out_specs),
        scratch_shapes=[
            pltpu.VMEM(act.shape, low),
            pltpu.VMEM(w.shape if pick is None else (width, act.shape[1]), low),
            pltpu.VMEM((4, own, width), low),
            pltpu.VMEM((4, own, width), f32),
            pltpu.VMEM((4, own, width), low),
            pltpu.VMEM((3, own // 2, width), low),
            pltpu.VMEM((3, own // 2, width), low),
            pltpu.VMEM((4, own, width), low),
            pltpu.VMEM((own, width), f32),
            pltpu.SemaphoreType.DMA((copy_count,)),
            pltpu.SemaphoreType.DMA((copy_count,)),
            pltpu.SemaphoreType.DMA((4 + len(held),)),
        ]
        + scratch,
        compiler_params=pltpu.CompilerParams(
            collective_id=number, has_side_effects=True, vmem_limit_bytes=60 * MIB
        ),
        cost_estimate=pl.CostEstimate(
            flops=2 * group * width * act.shape[1], bytes_accessed=40 * MIB, transcendentals=0
        ),
        name=name,
    )(act, w, *side_in, *more)


def home_kernel(rows, home, send, recv, buf, sem):
    place = Place()
    place.meet(("x", "y", "xy"))
    copies = Copies(place, send, recv)
    stay = start_home(copies, rows, home, buf, sem)
    stay.turn()
    copies.finish()
    stay.finish()


def take_home(rows, n_col):
    own, width = rows.shape
    home = (n_col * own, width // n_col)
    return pl.pallas_call(
        home_kernel,
        out_shape=jax.ShapeDtypeStruct(home, low),
        in_specs=[anywhere],
        out_specs=anywhere,
        scratch_shapes=[
            pltpu.SemaphoreType.DMA((3,)),
            pltpu.SemaphoreType.DMA((3,)),
            pltpu.VMEM((own, home[1]), low),
            pltpu.SemaphoreType.DMA((1,)),
        ],
        compiler_params=pltpu.CompilerParams(collective_id=11, has_side_effects=True),
        name="take_home",
    )(rows)


class GateReduce:
    counts = (2, 2, 3)

    def __init__(self, gates, small):
        self.n_dp = gates.shape[0]
        part = gates.shape[1:]
        self.inputs = (gates, small)
        self.outputs = ((part, low), (small.shape, f32))
        self.copy_count = 2 * (self.n_dp - 1)
        self.scratch = [
            pltpu.VMEM(gates.shape, low),
            pltpu.VMEM((self.n_dp - 1,) + part, low),
            pltpu.VMEM((self.n_dp - 1,) + small.shape, f32),
        ]

    in_specs, out_specs = [in_vmem] * 2, [in_vmem] * 2

    def turn(self):
        pass

    def names(self):
        return [f"d{d}" for d in range(1, self.n_dp)]

    def start(self, copies, gates, small, part_out, small_out, held, far, far_small):
        dp = copies.place.dp
        held[...] = gates[...]
        self.numbers = []
        for i, name in enumerate(self.names()):
            other = jnp.bitwise_xor(dp, i + 1)
            self.numbers.append(copies.start(held.at[other], far.at[i], name))
            self.numbers.append(copies.start(small, far_small.at[i], name))

    def finish(self, copies, gates, small, part_out, small_out, held, far, far_small):
        copies.land(*self.numbers)
        total = held[copies.place.dp].astype(f32)
        value = small[...]
        for i in range(self.n_dp - 1):
            total = total + far[i].astype(f32)
            value = value + far_small[i]
        part_out[...] = total.astype(low)
        small_out[...] = value


class GateGather:
    counts = (2, 2, 3)
    in_specs, out_specs = [in_vmem, anywhere], [in_vmem, anywhere]

    def __init__(self, part, grads, n_dp):
        self.n_dp = n_dp
        self.inputs = (part, grads)
        self.outputs = (((n_dp,) + part.shape, low), (grads.shape, grads.dtype))
        self.copy_count = n_dp + 2
        self.scratch = [
            pltpu.VMEM((n_dp,) + part.shape, low),
            pltpu.VMEM(grads.shape[1:], grads.dtype),
            pltpu.SemaphoreType.DMA((1,)),
        ]

    def names(self):
        return ["xy"] + [f"d{d}" for d in range(1, self.n_dp)]

    def start(self, copies, part, grads, all_out, grads_out, held, buf, sem):
        col = copies.place.col
        mine = held.at[copies.place.dp]
        self.numbers = [copies.start(part, mine, name) for name in self.names()[1:]]
        start_deal(copies, grads, grads_out)
        self.stay = Stay([(grads.at[col], grads_out.at[col])], [buf], sem)

    def turn(self):
        self.stay.turn()

    def finish(self, copies, part, grads, all_out, grads_out, held, buf, sem):
        held[copies.place.dp] = part[...]
        copies.land(*self.numbers)
        all_out[...] = held[...]
        self.stay.finish()


def square_sum(ref, row, x):
    ref[row : row + 1, :] += jnp.broadcast_to(jnp.sum(x * x, keepdims=True), (1, LANES))


def norm_scale(x):
    return lax.rsqrt(jnp.mean(x * x, axis=-1, keepdims=True) + epsilon)


def after_out_one(rows, fin, held, outs):
    x, gain = held
    resid_out, n2_out, squares = outs
    out_one = fin[rows, :]
    resid = x[rows, :].astype(f32) + out_one
    resid_out[rows, :] = resid
    n2_out[rows, :] = (resid * norm_scale(resid) * gain[1:2, :]).astype(low)
    square_sum(squares, 0, out_one)
    square_sum(squares, 1, resid)


def norm_back(d_normed, x, gain, grad_gain):
    scale = norm_scale(x)
    gained = gain * d_normed
    inner = jnp.mean(gained * x, axis=-1, keepdims=True)
    grad_gain[0:1, :] += jnp.sum(d_normed * x * scale, axis=0, keepdims=True)
    return scale * gained - x * (scale * scale * scale * inner)


def after_normed_two(rows, fin, held, outs):
    resid, upstream, gain = held
    d_resid_out, d_out, grad_gain = outs
    d_resid = upstream[rows, :].astype(f32) + norm_back(
        fin[rows, :], resid[rows, :], gain[1:2, :], grad_gain
    )
    d_resid_out[rows, :] = d_resid
    d_out[rows, :] = d_resid.astype(low)


def after_normed_one(rows, fin, held, outs):
    x, d_resid, gain = held
    back, grad_gain, squares = outs
    x_here = x[rows, :].astype(f32)
    passed = norm_back(fin[rows, :], x_here, gain[0:1, :], grad_gain)
    back[rows, :] = (d_resid[rows, :] + passed).astype(low)
    square_sum(squares, 0, x_here)


def after_out_two(rows, fin, held, outs):
    (resid,) = held
    back, squares = outs
    out_two = fin[rows, :]
    back[rows, :] = (resid[rows, :] + out_two).astype(low)
    square_sum(squares, 0, out_two)


def start_deal(copies, source, target):
    col = copies.place.col
    for name, j in (("xy", 3), ("x", 1), ("y", 2)):
        copies.start(source.at[copies.place.chip(j)], target.at[col], name)


def deal_kernel(source, target, send, recv, local, buf):
    place = Place()
    place.meet(("x", "y", "xy"))
    copies = Copies(place, send, recv)
    start_deal(copies, source, target)
    stay = Stay([(source.at[place.col], target.at[place.col])], [buf], local)
    stay.turn()
    copies.finish()
    stay.finish()


def deal_back(x, number, name):
    return pl.pallas_call(
        deal_kernel,
        out_shape=jax.ShapeDtypeStruct(x.shape, x.dtype),
        in_specs=[anywhere],
        out_specs=anywhere,
        scratch_shapes=[
            pltpu.SemaphoreType.DMA((3,)),
            pltpu.SemaphoreType.DMA((3,)),
            pltpu.SemaphoreType.DMA((1,)),
            pltpu.VMEM(x.shape[1:], x.dtype),
        ],
        compiler_params=pltpu.CompilerParams(
            collective_id=number, has_side_effects=True, vmem_limit_bytes=16 * MIB
        ),
        name=name,
    )(x)


PLANE = ("x", "y", "xy", "core", "cx", "cy", "cxy")


def sums_kernel(
    n_dp,
    mixed,
    small,
    gates,
    rows,
    sums_out,
    chans_out,
    gates_out,
    home,
    got,
    total,
    shared,
    ch,
    gv,
    send,
    recv,
    *bufs,
):
    place = Place()
    far = [f"d{d}" for d in range(1, n_dp)]
    place.meet(list(PLANE) + far)
    copies = Copies(place, send, recv)
    planes = [copies.start(mixed, got.at[i], name) for i, name in enumerate(far)]
    col = place.col
    ch[col] = small[...]
    gv[col] = gates[...]
    for name in ("x", "y", "xy"):
        copies.start(ch.at[col], ch.at[col], name)
    half = n_dp // 2
    halves = (pl.ds(0, half), pl.ds(half, half))

    def gate_view(chip, h):
        return gv.at[chip, halves[h]]

    direct = {
        (name, h): copies.start(gate_view(col, h), gate_view(col, h), name)
        for h in (0, 1)
        for name in ("x", "y")
    }
    stay_home = start_home(copies, rows, home, bufs[0], bufs[1])
    stay_home.turn()
    copies.land(direct["x", 0])
    far_x = gate_view(place.chip(1), 0)
    copies.start(far_x, far_x, "y")
    copies.land(direct["y", 1])
    far_y = gate_view(place.chip(2), 1)
    copies.start(far_y, far_y, "x")
    copies.land(*planes)
    value = mixed[...]
    for i in range(n_dp - 1):
        value = value + got[i]
    total[...] = value
    others = [copies.start(total, shared.at[i], name) for i, name in enumerate(PLANE)]
    copies.land(*others)
    for i in range(len(PLANE)):
        value = value + shared[i]
    sums_out[...] = value
    copies.finish()
    chans_out[...] = ch[...]
    gates_out[...] = gv[...]
    stay_home.finish()


def sum_everywhere(mixed, small, gates, rows_low, n_dp, n_col):
    count = n_dp + 22
    home = (n_col * rows_low.shape[0], rows_low.shape[1] // n_col)
    return pl.pallas_call(
        functools.partial(sums_kernel, n_dp),
        out_shape=(
            jax.ShapeDtypeStruct(mixed.shape, f32),
            jax.ShapeDtypeStruct((n_col,) + small.shape, f32),
            jax.ShapeDtypeStruct((n_col,) + gates.shape, low),
            jax.ShapeDtypeStruct(home, low),
        ),
        in_specs=[in_vmem] * 3 + [anywhere],
        out_specs=(in_vmem,) * 3 + (anywhere,),
        scratch_shapes=[
            pltpu.VMEM((n_dp - 1,) + mixed.shape, f32),
            pltpu.VMEM(mixed.shape, f32),
            pltpu.VMEM((len(PLANE),) + mixed.shape, f32),
            pltpu.VMEM((n_col,) + small.shape, f32),
            pltpu.VMEM((n_col,) + gates.shape, low),
            pltpu.SemaphoreType.DMA((count,)),
            pltpu.SemaphoreType.DMA((count,)),
            pltpu.VMEM((rows_low.shape[0], home[1]), low),
            pltpu.SemaphoreType.DMA((1,)),
        ],
        compiler_params=pltpu.CompilerParams(
            collective_id=5, has_side_effects=True, vmem_limit_bytes=24 * MIB
        ),
        name="small_sums",
    )(mixed, small, gates, rows_low)


def own_lanes(place, geo):
    n_col, part, bw, tiles, wide = geo
    found = [
        pl.ds(pl.multiple_of(place.col * bw + k * LANES, LANES), LANES) for k in range(bw // LANES)
    ]
    shared_tile = n_col * bw + lax.div(place.col, 2) * LANES
    return found + [pl.ds(pl.multiple_of(shared_tile, LANES), LANES)]


def one_less_exp(z):
    series = 1.0 + z / 6.0
    for n in (5.0, 4.0, 3.0, 2.0):
        series = 1.0 + z / n * series
    return jnp.where(z > -0.1, -z * series, 1.0 - jnp.exp(z))


def scan_tile(a, u, reverse):
    rows = a.shape[0]
    index = lax.broadcasted_iota(jnp.int32, a.shape, 0)
    by = 1
    while by < rows:
        turn = rows - by if reverse else by
        inside = index < rows - by if reverse else index >= by
        u = u + a * jnp.where(inside, pltpu.roll(u, turn, 0), 0.0)
        a = a * jnp.where(inside, pltpu.roll(a, turn, 0), 1.0)
        by *= 2
    return a, u


def forward_kernel(
    geo,
    x_all,
    w_rec,
    gain,
    gates,
    bias,
    soft,
    conv_w,
    conv_b,
    places,
    cotangent,
    rec_out,
    mlp_in,
    mlp_out,
    n1_out,
    x_out,
    y_out,
    pre_out,
    c_out,
    state_out,
    branch_out,
    first_out,
    g_all,
    w_out,
    w_in,
    w_down,
    xv,
    wv,
    before,
    xb,
    yv,
    prev,
    cv,
    hv,
    pv,
    bv,
    carry,
    first,
    send,
    recv,
    local,
    stay_sems,
    *bufs,
):
    place = Place()
    place.meet(AROUND + ("next", "prev"))
    copies = Copies(place, send, recv)
    n_col, part, bw, tiles, wide = geo
    chans = bw + LANES
    group, width = xv.shape
    tile = 256
    n_tiles = group // tile
    loads = [copies.keep(x_all, xv, local.at[0]), copies.keep(w_rec, wv, local.at[1])]
    halo = copies.start(x_all.at[pl.ds(group - ROWS, ROWS), :], before, "next")
    found = weight_pieces(geo, (None, rec_out, mlp_in, mlp_out), (None, w_out, w_in, w_down))
    pieces = found["rec_out"] + found["mlp_in"] + found["mlp_out"]
    dealer = Dealer(copies, 9)
    for piece in pieces[:5]:
        dealer.deal(piece)
    for load in loads:
        load.wait()
    own_block = (cotangent, block_view(cotangent, g_all, place.row, place.col, None))
    stay = Stay([own_block] + own_pieces(place, pieces), bufs, stay_sems)
    high_tile = place.col >= 2
    mine = own_lanes(place, geo)
    conv_lanes = mine[:-1] + [
        slice(n_col * bw + k * LANES, n_col * bw + (k + 1) * LANES) for k in range(bw // LANES)
    ]
    tile_cols = pl.ds(pl.multiple_of(lax.div(place.col, 2) * LANES, LANES), LANES)
    idle_tile = lax.rem(place.col, 2) == 1

    def normed(x):
        x = x.astype(f32)
        scale = lax.rsqrt(jnp.sum(x * x, axis=-1, keepdims=True) / width + epsilon)
        return (x * scale * gain[0:1, :]).astype(low)

    copies.land(halo)
    xb[0:8, :] = dot(normed(before[...]), wv[:, : 2 * bw])[ROWS - 8 :]
    carry[0:1] = jnp.zeros_like(carry[0:1])
    carry[1:2] = jnp.ones_like(carry[1:2])

    def work(i, unused):
        r0 = pl.multiple_of(i * tile, tile)
        rows = pl.ds(r0, tile)
        n1 = normed(xv[rows, :])
        xv[rows, :] = n1
        both = dot(n1, wv[...])
        xb[pl.ds(pl.multiple_of(r0 + 8, 8), tile), :] = both[:, : 2 * bw]
        yv[rows, :] = both[:, 2 * bw :]
        spot = places[rows, :]
        reach = xb[pl.ds(r0, tile + 8), :]
        conv = []
        for lane in range(2 * bw // LANES):
            at = slice(lane * LANES, (lane + 1) * LANES)
            near = reach[:, at]
            tap = conv_lanes[lane]
            total = conv_b[0:1, tap] + conv_w[0:1, tap] * near[8:]
            for t in range(1, conv_w.shape[0]):
                lagged = pltpu.roll(near, t, 0)[8:]
                total = total + jnp.where(spot >= t, conv_w[t : t + 1, tap] * lagged, 0.0)
            conv.append(total.astype(low))
        c = jnp.concatenate(conv, axis=1)
        cv[rows, :] = c
        pre = [
            jnp.concatenate(
                [dot(c[:, :bw], gates[j, place.col]), dot(c[:, bw:], gates[j, n_col, :, tile_cols])],
                axis=1,
            )
            + jnp.concatenate([bias[j : j + 1, at] for at in mine], axis=1)
            for j in range(2)
        ]
        prev[rows, :chans] = pre[0]
        prev[rows, chans:] = pre[1]
        reset = spot == 0
        for lane in range(chans // LANES):
            at = slice(lane * LANES, (lane + 1) * LANES)
            if lane * LANES < bw:
                own_c = conv[lane].astype(f32)
            else:
                own_c = jnp.where(high_tile, conv[lane + 1].astype(f32), conv[lane].astype(f32))
            log_a = -8.0 * jax.nn.sigmoid(pre[1][:, at]) * soft[0:1, mine[lane]]
            a = jnp.where(reset, 0.0, jnp.exp(log_a))
            m = jnp.where(reset, 1.0, jnp.sqrt(one_less_exp(2.0 * log_a)))
            u = own_c * jax.nn.sigmoid(pre[0][:, at]) * m
            a, u = scan_tile(a, u, False)
            h = u + a * carry[0:1, at]
            p = a * carry[1:2, at]
            hv[rows, at] = h
            pv[rows, at] = p
            carry[0:1, at] = h[tile - 1 :]
            carry[1:2, at] = p[tile - 1 :]
        return unused

    third = n_tiles // 3
    lax.fori_loop(0, third, work, 0)
    stay.turn()
    dealer.forward()
    dealer.forward()
    dealer.deal(pieces[5])
    dealer.forward()
    lax.fori_loop(third, 2 * third, work, 0)
    dealer.forward()
    dealer.deal(pieces[6])
    lax.fori_loop(2 * third, n_tiles, work, 0)
    dealer.forward()
    dealer.deal(pieces[7])
    state_in = copies.start(hv.at[pl.ds(group - 8, 8), :], first, "next")
    outs = [
        copies.keep(src, dst, local.at[10 + i])
        for i, (src, dst) in enumerate(
            ((xv, n1_out), (xb, x_out), (yv, y_out), (prev, pre_out), (cv, c_out))
        )
    ]
    copies.land(state_in)
    copies.leave(state_in)
    before_all = first[7:8, :]

    def finish(i, unused):
        rows = pl.ds(pl.multiple_of(i * tile, tile), tile)
        for lane in range(chans // LANES):
            at = slice(lane * LANES, (lane + 1) * LANES)
            state = hv[rows, at] + pv[rows, at] * before_all[:, at]
            hv[rows, at] = state
            value, _ = tanh_parts(yv[rows, at])
            b = state * value
            if lane * LANES >= bw:
                b = jnp.where(idle_tile, 0.0, b)
            bv[rows, at] = b.astype(low)
        return unused

    lax.fori_loop(0, n_tiles, finish, 0)
    outs += [
        copies.keep(hv, state_out, local.at[15]),
        copies.keep(bv, branch_out, local.at[16]),
        copies.keep(first, first_out, local.at[17]),
    ]
    dealer.forward()
    gather = block_gather(copies, cotangent, g_all)
    dealer.forward()
    dealer.forward()
    gather.pass_on()
    gather.last()
    copies.finish()
    for copy in outs:
        copy.wait()
    stay.finish()


def rec_forward(x_all, w_rec, params, places, cotangent, rec_out, mlp_in, mlp_out, geo):
    n_col, part, bw, tiles, wide = geo
    width, span, chans = part * n_col, wide * LANES, bw + LANES
    group = x_all.shape[0]

    def of(shape, dtype):
        return jax.ShapeDtypeStruct(shape, dtype)

    kept = [
        ((group, width), low),
        ((group + 8, 2 * bw), f32),
        ((group, chans), f32),
        ((group, 2 * chans), f32),
        ((group, 2 * bw), low),
        ((group, chans), f32),
        ((group, chans), low),
        ((8, chans), f32),
    ]
    dealt = [((group, width), low), ((chans, width), low), ((2, width, span), low), ((span, width), low)]
    copy_count = 1 + 6 * 8 + 12 + 1
    return pl.pallas_call(
        functools.partial(forward_kernel, geo),
        out_shape=tuple(of(*s) for s in kept + dealt),
        in_specs=[anywhere] * 2 + [in_vmem] * 7 + [anywhere] * 4,
        out_specs=(anywhere,) * 12,
        scratch_shapes=[
            pltpu.VMEM((group, width), low),
            pltpu.VMEM(w_rec.shape, low),
            pltpu.VMEM((ROWS, width), low),
            pltpu.VMEM((group + 8, 2 * bw), f32),
            pltpu.VMEM((group, chans), f32),
            pltpu.VMEM((group, 2 * chans), f32),
            pltpu.VMEM((group, 2 * bw), low),
            pltpu.VMEM((group, chans), f32),
            pltpu.VMEM((group, chans), f32),
            pltpu.VMEM((group, chans), low),
            pltpu.VMEM((8, chans), f32),
            pltpu.VMEM((8, chans), f32),
            pltpu.SemaphoreType.DMA((copy_count,)),
            pltpu.SemaphoreType.DMA((copy_count,)),
            pltpu.SemaphoreType.DMA((18,)),
            pltpu.SemaphoreType.DMA((9,)),
            pltpu.VMEM(cotangent.shape, low),
            pltpu.VMEM((bw, part), low),
            pltpu.VMEM((LANES, part), low),
        ]
        + [pltpu.VMEM((part, span // 2), low)] * 4
        + [pltpu.VMEM((span // 2, part), low)] * 2,
        compiler_params=pltpu.CompilerParams(
            collective_id=2, has_side_effects=True, vmem_limit_bytes=58 * MIB
        ),
        name="rec_forward",
    )(x_all, w_rec, *params, places, cotangent, rec_out, mlp_in, mlp_out)


def backward_kernel(
    geo,
    d_out,
    w_out,
    y_in,
    state_in,
    first_in,
    pre_in,
    c_in,
    x_in,
    gates,
    soft,
    conv_w,
    places,
    down,
    d_all,
    d_rec_out,
    gate_out,
    sums,
    down_out,
    buf,
    wv,
    dbv,
    yv,
    slv,
    hs,
    prev,
    cv,
    xb,
    ghv,
    qv,
    dpv,
    there,
    dcv,
    drv,
    gg,
    carry,
    message,
    down_buf,
    send,
    recv,
    local,
    stay_sem,
):
    place = Place()
    place.meet(["x", "y", "xy", "core", "next", "prev"])
    copies = Copies(place, send, recv)
    n_col, part, bw, tiles, wide = geo
    chans = bw + LANES
    own_rows = d_out.shape[0]
    group = yv.shape[0]
    tile = 256
    n_tiles = group // tile
    lanes = [slice(k * LANES, (k + 1) * LANES) for k in range(chans // LANES)]
    gather = slot_gather(copies, d_out, buf, own_rows)
    me = place.row * n_col + place.col
    load = copies.keep(w_out, wv, local.at[0])
    mine = copies.keep(d_out, buf.at[me], local.at[1])
    loads = [
        copies.keep(src, dst, local.at[2 + i])
        for i, (src, dst) in enumerate(
            (
                (y_in, yv),
                (state_in, hs.at[pl.ds(8, group), :]),
                (first_in, hs.at[pl.ds(0, 8), :]),
                (pre_in, prev),
                (c_in, cv),
                (x_in, xb),
            )
        )
    ]
    load.wait()
    mine.wait()
    high_tile = place.col >= 2
    idle_tile = lax.rem(place.col, 2) == 1
    mine_at = own_lanes(place, geo)
    tile_rows = pl.ds(pl.multiple_of(lax.div(place.col, 2) * LANES, LANES), LANES)

    def work(chip):
        slots = (chip, n_col + chip)
        value = dot(jnp.concatenate([buf[s] for s in slots], axis=0), wv[...], ((1,), (1,)))
        for n, s in enumerate(slots):
            rows = pl.ds(pl.multiple_of(s * own_rows, ROWS), own_rows)
            dbv[rows, :] = value[n * own_rows : (n + 1) * own_rows]

    def before_rows(k, unused):
        rows = pl.ds(pl.multiple_of(k * tile, tile), tile)
        for at in lanes:
            value, slope = tanh_parts(yv[rows, at])
            yv[rows, at] = value
            slv[rows, at] = slope
        prev[rows, :] = jax.nn.sigmoid(prev[rows, :])
        return unused

    copies.land(gather.own)
    work(place.col)
    for each in loads:
        each.wait()
    third = n_tiles // 3
    lax.fori_loop(0, third, before_rows, 0)
    x0, y0 = gather.pass_half(0)
    lax.fori_loop(third, 2 * third, before_rows, 0)
    x1, y1 = gather.pass_half(1)
    start_deal(copies, down, down_out)
    stay = Stay([(down.at[place.col], down_out.at[place.col])], [down_buf], stay_sem)
    stay.turn()
    copies.land(y0, y1)
    work(place.chip(2))
    corner = gather.last()
    copies.land(x0, x1)
    work(place.chip(1))
    lax.fori_loop(2 * third, n_tiles, before_rows, 0)
    copies.land(corner)
    out = copies.keep(buf, d_all, local.at[8])
    work(place.chip(3))

    def own(at):
        return mine_at[at.start // LANES]

    def coeffs(rows, at, spot):
        rate = prev[rows, slice(chans + at.start, chans + at.stop)]
        log_a = -8.0 * rate * soft[0:1, own(at)]
        return rate, log_a, jnp.where(spot == 0, 0.0, jnp.exp(log_a))

    carry[0:1] = jnp.zeros_like(carry[0:1])
    carry[1:2] = jnp.ones_like(carry[1:2])

    def scan_back(k, unused):
        r0 = pl.multiple_of((n_tiles - 1 - k) * tile, tile)
        rows = pl.ds(r0, tile)
        spot = places[rows, :]
        last = lax.broadcasted_iota(jnp.int32, spot.shape, 0) == tile - 1
        for at in lanes:
            d_branch = dbv[rows, at]
            if at.start >= bw:
                d_branch = jnp.where(idle_tile, 0.0, d_branch)
            value, slope = yv[rows, at], slv[rows, at]
            state = hs[pl.ds(pl.multiple_of(r0 + 8, 8), tile), at]
            d_state = d_branch * value
            drv[rows, slice(chans + at.start, chans + at.stop)] = (d_branch * state * slope).astype(low)
            _, _, a = coeffs(rows, at, spot)
            a, u = scan_tile(a, a * d_state, True)
            m = u + a * carry[0:1, at]
            q = a * carry[1:2, at]
            ghv[rows, at] = d_state + jnp.where(last, carry[0:1, at], pltpu.roll(m, tile - 1, 0))
            qv[rows, at] = jnp.where(last, carry[1:2, at], pltpu.roll(q, tile - 1, 0))
            carry[0:1, at] = m[0:1]
            carry[1:2, at] = q[0:1]
        return unused

    lax.fori_loop(0, n_tiles, scan_back, 0)
    arriving = copies.start(carry, message, "prev")
    copies.land(arriving)
    sums[...] = jnp.zeros_like(sums)
    gg[...] = jnp.zeros_like(gg)

    def through_gates(k, unused):
        r0 = pl.multiple_of(k * tile, tile)
        rows = pl.ds(r0, tile)
        spot = places[rows, :]
        reset = spot == 0
        for n, at in enumerate(lanes):
            g = ghv[rows, at] + qv[rows, at] * message[0:1, at]
            before = pltpu.roll(hs[pl.ds(r0, tile + 8), at], 1, 0)[8:]
            if at.start < bw:
                c = cv[rows, at].astype(f32)
            else:
                c = jnp.where(
                    high_tile,
                    cv[rows, slice(at.start + LANES, at.stop + LANES)].astype(f32),
                    cv[rows, at].astype(f32),
                )
            gate = prev[rows, at]
            rate, log_a, a = coeffs(rows, at, spot)
            m = jnp.where(reset, 1.0, jnp.sqrt(one_less_exp(2.0 * log_a)))
            gated = gate * m
            d_log = jnp.where(reset, 0.0, g * before * a - g * c * gate * a * a / m)
            d_pre_in = (g * c * gated * (1.0 - gate)).astype(low)
            d_pre_rate = (d_log * (-8.0 * soft[0:1, own(at)]) * rate * (1.0 - rate)).astype(low)
            dpv[rows, at] = d_pre_in
            dpv[rows, slice(chans + at.start, chans + at.stop)] = d_pre_rate
            dcv[rows, at] = g * gated
            sums[0:1, at] += jnp.sum(d_pre_in.astype(f32), axis=0, keepdims=True)
            sums[1:2, at] += jnp.sum(d_pre_rate.astype(f32), axis=0, keepdims=True)
            sums[2:3, at] += jnp.sum(d_log * (-8.0 * rate), axis=0, keepdims=True)
        return unused

    swaps = []
    for h in range(2):
        lax.fori_loop(h * n_tiles // 2, (h + 1) * n_tiles // 2, through_gates, 0)
        rows = pl.ds(h * group // 2, group // 2)
        for j in range(2):
            swaps.append(
                copies.start(
                    dpv.at[rows, pl.ds(j * chans + bw, LANES)],
                    there.at[rows, pl.ds(j * LANES, LANES)],
                    "y",
                )
            )

    def through_blocks(k, unused):
        rows = pl.ds(pl.multiple_of(k * tile, tile), tile)
        c = cv[rows, :]
        d_blk = dcv[rows, :bw]
        d_tile = dcv[rows, bw:]
        for j in range(2):
            p_blk = dpv[rows, slice(j * chans, j * chans + bw)]
            here = dpv[rows, slice(j * chans + bw, (j + 1) * chans)]
            far = there[rows, slice(j * LANES, (j + 1) * LANES)]
            five = jnp.concatenate(
                [jnp.where(high_tile, far, here), jnp.where(high_tile, here, far)], axis=1
            )
            d_blk = d_blk + dot(p_blk, gates[j, place.col], ((1,), (1,)))
            d_tile = d_tile + dot(five, gates[j, n_col, tile_rows, :], ((1,), (1,)))
            gg[j, :, :bw] += dot(c[:, :bw], p_blk, ((0,), (0,)))
            gg[j, :, bw:] += dot(c[:, bw:], here, ((0,), (0,)))
        dcv[rows, :bw] = d_blk
        dcv[rows, bw:] = d_tile
        return unused

    copies.land(swaps[0], swaps[1])
    lax.fori_loop(0, 1, through_blocks, 0)
    later = copies.start(dcv.at[pl.ds(0, 8), :], dcv.at[pl.ds(group, 8), :], "prev")
    lax.fori_loop(1, n_tiles // 2, through_blocks, 0)
    copies.land(swaps[2], swaps[3])
    lax.fori_loop(n_tiles // 2, n_tiles, through_blocks, 0)
    part_rows = gate_out.shape[1]
    for p in range(gate_out.shape[0]):
        j, first_row = divmod(p * part_rows, bw)
        gate_out[p] = gg[j, first_row : first_row + part_rows].astype(low)
    copies.land(later)

    def through_conv(k, unused):
        r0 = pl.multiple_of(k * tile, tile)
        rows = pl.ds(r0, tile)
        ext = pl.ds(r0, tile + 8)
        spot = places[ext, :]
        for at in lanes:
            reach = dcv[ext, at]
            if at.start < bw:
                x = xb[ext, at]
            else:
                x = jnp.where(high_tile, xb[ext, slice(at.start + LANES, at.stop + LANES)], xb[ext, at])
            d_c = reach[:tile]
            d_x = conv_w[0:1, own(at)] * d_c
            sums[3:4, at] += jnp.sum(d_c * x[8:], axis=0, keepdims=True)
            for t in range(1, conv_w.shape[0]):
                term = jnp.where(spot >= t, conv_w[t : t + 1, own(at)] * reach, 0.0)
                d_x = d_x + pltpu.roll(term, tile + 8 - t, 0)[:tile]
                lagged = pltpu.roll(x, t, 0)[8:]
                here = jnp.where(spot[:tile] >= t, d_c * lagged, 0.0)
                sums[3 + t : 4 + t, at] += jnp.sum(here, axis=0, keepdims=True)
            sums[7:8, at] += jnp.sum(d_c, axis=0, keepdims=True)
            drv[rows, at] = d_x.astype(low)
        return unused

    lax.fori_loop(0, n_tiles, through_conv, 0)
    for at in lanes:
        sums[2:3, at] = sums[2:3, at] * soft[1:2, own(at)]
    out_rec = copies.keep(drv, d_rec_out, local.at[9])
    copies.finish()
    out.wait()
    out_rec.wait()
    stay.finish()


def rec_backward(d_out, w_out, kept, gates, soft, conv_w, places, down, geo, n_dp):
    n_col, part, bw, tiles, wide = geo
    own, width = d_out.shape
    slots = 2 * n_col
    group, chans = slots * own, bw + LANES
    part_rows = 2 * bw // n_dp
    d_all, d_rec, gate_grads, sums, down_dealt = pl.pallas_call(
        functools.partial(backward_kernel, geo),
        out_shape=(
            jax.ShapeDtypeStruct((slots, own, width), low),
            jax.ShapeDtypeStruct((group, 2 * chans), low),
            jax.ShapeDtypeStruct((n_dp, part_rows, chans), low),
            jax.ShapeDtypeStruct((8, chans), f32),
            jax.ShapeDtypeStruct(down.shape, low),
        ),
        in_specs=[anywhere] * 8 + [in_vmem] * 4 + [anywhere],
        out_specs=(anywhere, anywhere, in_vmem, in_vmem, anywhere),
        scratch_shapes=[
            pltpu.VMEM((slots, own, width), low),
            pltpu.VMEM(w_out.shape, low),
            pltpu.VMEM((group, chans), f32),
            pltpu.VMEM((group, chans), f32),
            pltpu.VMEM((group, chans), f32),
            pltpu.VMEM((group + 8, chans), f32),
            pltpu.VMEM((group, 2 * chans), f32),
            pltpu.VMEM((group, 2 * bw), low),
            pltpu.VMEM((group + 8, 2 * bw), f32),
            pltpu.VMEM((group, chans), f32),
            pltpu.VMEM((group, chans), f32),
            pltpu.VMEM((group, 2 * chans), low),
            pltpu.VMEM((group, 2 * LANES), low),
            pltpu.VMEM((group + 8, chans), f32),
            pltpu.VMEM((group, 2 * chans), low),
            pltpu.VMEM((2, bw, chans), f32),
            pltpu.VMEM((8, chans), f32),
            pltpu.VMEM((8, chans), f32),
            pltpu.VMEM(down.shape[1:], low),
            pltpu.SemaphoreType.DMA((22,)),
            pltpu.SemaphoreType.DMA((22,)),
            pltpu.SemaphoreType.DMA((10,)),
            pltpu.SemaphoreType.DMA((1,)),
        ],
        compiler_params=pltpu.CompilerParams(
            collective_id=4, has_side_effects=True, vmem_limit_bytes=60 * MIB
        ),
        name="rec_backward",
    )(d_out, w_out, *kept, gates, soft, conv_w, places, down)
    return d_all.reshape(group, width), d_rec, gate_grads, sums, down_dealt


def outer_kernel(n_dp, first_steps, left1, right1, left2, right2, out_ref):
    def multiply(left, right):
        total = dot(left[...], right[...], ((0,), (0,)))
        rows = total.shape[0] // n_dp
        for k in range(n_dp):
            out_ref[k, 0] = total[k * rows : (k + 1) * rows].astype(out_ref.dtype)

    j = pl.program_id(1)

    @pl.when(j < first_steps)
    def _():
        multiply(left1, right1)

    @pl.when(j >= first_steps)
    def _():
        multiply(left2, right2)


def outer_one_kernel(n_dp, left, right, out_ref):
    total = dot(left[...], right[...], ((0,), (0,)))
    rows = total.shape[0] // n_dp
    for k in range(n_dp):
        out_ref[k, 0] = total[k * rows : (k + 1) * rows].astype(out_ref.dtype)


def outer(left, right, n_dp, n_col, columns, name):
    length, width = left.shape
    part = width // n_col
    count = right.shape[1]
    return pl.pallas_call(
        functools.partial(outer_one_kernel, n_dp),
        grid=(n_col, count // columns),
        out_shape=jax.ShapeDtypeStruct((n_dp, n_col, part // n_dp, count), low),
        in_specs=[
            pl.BlockSpec((length, part), lambda i, j: (0, i)),
            pl.BlockSpec((length, columns), lambda i, j: (0, j)),
        ],
        out_specs=pl.BlockSpec((n_dp, 1, part // n_dp, columns), lambda i, j: (0, i, 0, j)),
        compiler_params=pltpu.CompilerParams(vmem_limit_bytes=48 * MIB),
        cost_estimate=pl.CostEstimate(
            flops=2 * length * width * count,
            bytes_accessed=2 * (length * width + length * count + width * count),
            transcendentals=0,
        ),
        name=name,
    )(left, right)


def outer_pair(left1, right1, left2, right2, n_dp, n_col, columns, name):
    length, width = left1.shape
    part = width // n_col
    steps1, steps2 = right1.shape[1] // columns, right2.shape[1] // columns
    count = (steps1 + steps2) * columns
    left_block = pl.BlockSpec((length, part), lambda i, j: (0, i))
    return pl.pallas_call(
        functools.partial(outer_kernel, n_dp, steps1),
        grid=(n_col, steps1 + steps2),
        out_shape=jax.ShapeDtypeStruct((n_dp, n_col, part // n_dp, count), low),
        in_specs=[
            left_block,
            pl.BlockSpec((length, columns), lambda i, j: (0, jnp.minimum(j, steps1 - 1))),
            left_block,
            pl.BlockSpec((length, columns), lambda i, j: (0, jnp.maximum(j - steps1, 0))),
        ],
        out_specs=pl.BlockSpec((n_dp, 1, part // n_dp, columns), lambda i, j: (0, i, 0, j)),
        compiler_params=pltpu.CompilerParams(vmem_limit_bytes=48 * MIB),
        cost_estimate=pl.CostEstimate(
            flops=2 * length * width * count,
            bytes_accessed=2 * (2 * length * width + length * count + width * count),
            transcendentals=0,
        ),
        name=name,
    )(left1, right1, left2, right2)


def dot(a, b, dims=((1,), (0,))):
    return lax.dot_general(a, b, (dims, ((), ())), preferred_element_type=f32)


def places_of(rows, lengths):
    ends = jnp.cumsum(lengths)
    starts = ends - lengths
    inside = (rows[:, None] >= starts[None, :]) & (rows[:, None] < ends[None, :])
    places = rows - jnp.sum(jnp.where(inside, starts[None, :], 0), axis=1)
    return jnp.where(jnp.any(inside, axis=1), places, 0)


def body(
    tokens,
    cotangent,
    rec_in,
    rec_out,
    gates,
    gate_bias,
    decay,
    conv_w,
    conv_b,
    gains,
    mlp_in,
    mlp_out,
    lengths,
    order,
):
    n_dp, n_row, n_col = (lax.axis_size(a) for a in ("dp", "row", "col"))
    dp, row, col = (lax.axis_index(a) for a in ("dp", "row", "col"))
    given, part = tokens.shape
    own = given // n_col
    group = given * n_row
    width = part * n_col
    taps = conv_w.shape[0]
    blocks, bw = gates.shape[1], gates.shape[2]
    half = rec_out.shape[0]
    hidden_half = mlp_out.shape[0]
    tiles = hidden_half // LANES
    wide = -(-tiles // n_col)
    span = wide * LANES
    shared = n_col * bw
    chans = bw + LANES

    geo = (n_col, part, bw, tiles, wide)
    x_all, w_rec, gains_all = open_gather(tokens, rec_in, gains, geo)
    base = dp * group
    places = places_of(base + jnp.arange(group + 8, dtype=jnp.int32), lengths)
    places = jnp.broadcast_to(places[:, None], (group + 8, LANES))
    soft = jnp.stack([jax.nn.softplus(decay), jax.nn.sigmoid(decay)])

    n1, x_rows, y_branch, pre_both, conv_low, state, branch, first, g_all, w_out, w_in, w_down = rec_forward(
        x_all,
        w_rec,
        (gains_all, gates, gate_bias, soft, conv_w, conv_b[None, :]),
        places,
        cotangent,
        rec_out,
        mlp_in,
        mlp_out,
        geo,
    )
    rows_f, rows_b = ((own, width), f32), ((own, width), low)
    line, squares = ((8, width), f32), ((8, LANES), f32)
    resid, normed_two, squares_one = multiply_scatter(
        branch, w_out, False, 6, "out_one", after_out_one, (x_all, gains_all), (rows_f, rows_b, squares)
    )

    def spare(at):
        return spare_window(at, tiles, n_col, wide)

    n2, hidden, d_glu = glu(normed_two, w_in, w_down, g_all, spare)
    g_down = outer(g_all, hidden, n_dp, n_col, span, "outer_down")
    d_glu, hidden, g_down = lax.optimization_barrier((d_glu, hidden, g_down))
    sum_down = lax.psum_scatter(g_down, "dp", scatter_dimension=0)
    g_in = outer(n2, d_glu, n_dp, n_col, span, "outer_in")
    d_glu, g_in = lax.optimization_barrier((d_glu, g_in))
    d_resid, d_out, gain_two = multiply_scatter(
        d_glu,
        w_in,
        True,
        7,
        "d_normed_two",
        after_normed_two,
        (resid, g_all, gains_all),
        (rows_f, rows_b, line),
    )
    g_in, sum_down, d_out = lax.optimization_barrier((g_in, sum_down, d_out))
    sum_in = lax.psum_scatter(g_in, "dp", scatter_dimension=0)

    d_out_all, d_rec, gate_grads, small, down = rec_backward(
        d_out,
        w_out,
        (y_branch, state, first, pre_both, conv_low, x_rows),
        gates,
        soft,
        conv_w,
        places,
        sum_down,
        geo,
        n_dp,
    )

    def pick(at):
        tile = pl.multiple_of(bw + lax.div(at, 2) * LANES, LANES)
        return ((0, 0, bw), (tile, bw, LANES), (2 * bw, chans, chans))

    g_rec = outer_pair(n1, d_rec, d_out_all, branch, n_dp, n_col, chans, "outer_rec")
    g_rec, d_rec = lax.optimization_barrier((g_rec, d_rec))
    grad_rows, gain_one, squares_x, gate_part, small = multiply_scatter(
        d_rec,
        w_rec,
        True,
        9,
        "d_normed_one",
        after_normed_one,
        (x_all, d_resid, gains_all),
        (rows_b, line, squares),
        pick=pick,
        beside=GateReduce(gate_grads, small),
    )
    grad_input = take_home(grad_rows, n_col)
    g_rec, sum_in, grad_input, hidden = lax.optimization_barrier((g_rec, sum_in, grad_input, hidden))
    sum_rec = lax.psum_scatter(g_rec, "dp", scatter_dimension=0)
    result_rows, squares_two, gate_planes, into = multiply_scatter(
        hidden,
        w_down,
        False,
        8,
        "out_two",
        after_out_two,
        (resid,),
        (rows_b, squares),
        beside=GateGather(gate_part, sum_in, n_dp),
    )

    def windows(got, first):
        return [
            got[c][..., first + (LANES if c > n_col - 1 - (wide * n_col - tiles) else 0) : first + span]
            for c in range(n_col)
        ]

    def channels_of(got, first):
        return [got[c][..., first : first + bw] for c in range(n_col)] + [
            got[c][..., first + bw : first + chans] for c in range(0, n_col, 2)
        ]

    square_sums = jnp.stack([squares_x[0, 0], squares_one[0, 0], squares_one[1, 0], squares_two[0, 0]])
    lines = small.shape[0]
    gain_sums = jnp.concatenate([gain_one[:1], gain_two[:1]]).reshape(lines, 2 * width // lines)
    stat_block = jnp.pad(square_sums[None, :], ((0, lines - 1), (0, LANES - 4)))
    mixed = jnp.concatenate([gain_sums, stat_block], axis=1)
    sums, chan_sums, gate_parts, result = sum_everywhere(
        mixed, small, gate_planes, result_rows, n_dp, n_col
    )
    grad_mlp_in = jnp.stack(
        [jnp.concatenate(windows(into[..., j * span : (j + 1) * span], 0), axis=-1) for j in range(2)]
    ).astype(f32)
    grad_mlp_out = jnp.concatenate(windows(down, 0), axis=-1).astype(f32).T
    sum_rec, grad_mlp_in, grad_mlp_out = lax.optimization_barrier((sum_rec, grad_mlp_in, grad_mlp_out))
    recs = deal_back(sum_rec, 10, "deal_rec")
    grad_rec_in = jnp.stack(
        [jnp.concatenate(channels_of(recs, j * chans), axis=-1) for j in range(2)]
    ).astype(f32)
    grad_rec_out = jnp.concatenate(channels_of(recs, 2 * chans), axis=-1).astype(f32).T
    mine = jnp.concatenate(channels_of(chan_sums, 0), axis=-1)
    gain_rows = sums[:, : 2 * width // lines].reshape(2, width)
    grad_gains = lax.dynamic_slice_in_dim(gain_rows, col * part, part, axis=1)
    stats = jnp.sqrt(sums[0, 2 * width // lines :][:4] / (n_dp * group * width))
    gate_parts = gate_parts.reshape(n_col, 2, bw, chans).astype(f32)
    five = jnp.concatenate([gate_parts[c, :, :, bw:] for c in range(0, n_col, 2)], axis=-1)
    grad_gates = jnp.stack([gate_parts[c, :, :, :bw] for c in range(n_col)] + [five], axis=1)
    return (
        result,
        grad_input,
        grad_rec_in,
        grad_rec_out,
        grad_gates,
        mine[0:2],
        mine[2],
        mine[3 : 3 + taps],
        mine[3 + taps],
        grad_gains,
        grad_mlp_in,
        grad_mlp_out,
        stats,
    )


def solution(mesh):
    placed = (
        P(("dp", "row"), "col"),
        P(("dp", "row"), "col"),
        P(None, "col", "row"),
        P("row", "col"),
        P(None, "row", None, None),
        P(None, "row"),
        P("row"),
        P(None, "row"),
        P("row"),
        P(None, "col"),
        P(None, "col", "row"),
        P("row", "col"),
        P(),
        P(),
    )
    return jax.shard_map(
        body,
        mesh=mesh,
        in_specs=placed,
        out_specs=(
            P(("dp", "row"), "col"),
            P(("dp", "row"), "col"),
            P(None, ("col", "dp"), "row"),
            P("row", ("col", "dp")),
            P(None, "row", None, None),
            P(None, "row"),
            P("row"),
            P(None, "row"),
            P("row"),
            P(None, "col"),
            P(None, ("col", "dp"), "row"),
            P("row", ("col", "dp")),
            P(),
        ),
        check_vma=False,
    )
```

```python
import functools

import jax
import jax.numpy as jnp
from jax import lax
from jax.experimental import pallas as pl
from jax.experimental.pallas import tpu as pltpu
from jax.sharding import PartitionSpec as P

epsilon = 1e-06
LANES = 128
ROWS = 16
MIB = 1024 * 1024
MESH = pl.DeviceIdType.MESH
low = jnp.bfloat16
f32 = jnp.float32
anywhere = pl.BlockSpec(memory_space=pl.ANY)
in_vmem = pl.BlockSpec(memory_space=pltpu.VMEM)


def window_tile(col, tiles, n_col, wide):
    spare = wide * n_col - tiles
    return col * wide - jnp.maximum(col - (n_col - 1 - spare), 0)


def spare_window(col, tiles, n_col, wide):
    spare = wide * n_col - tiles
    return col > n_col - 1 - spare


class Place:
    def __init__(self):
        self.dp, self.row, self.col = (lax.axis_index(a) for a in ("dp", "row", "col"))

    def chip(self, k):
        return jnp.bitwise_xor(self.col, k)

    def device(self, name):
        if name == "core":
            return {"row": 1 - self.row}
        if name == "z":
            return {"dp": jnp.bitwise_xor(self.dp, 1)}
        if name in ("next", "prev"):
            n_dp = lax.axis_size("dp")
            return {"dp": lax.rem(self.dp + (1 if name == "next" else n_dp - 1), n_dp)}
        if name[0] == "d":
            return {"dp": jnp.bitwise_xor(self.dp, int(name[1:]))}
        if name[0] == "c":
            return {"row": 1 - self.row, "col": self.chip({"x": 1, "y": 2, "xy": 3}[name[1:]])}
        return {"col": self.chip({"x": 1, "y": 2, "xy": 3}[name])}

    def meet(self, names):
        barrier = pltpu.get_barrier_semaphore()
        for name in names:
            pl.semaphore_signal(
                barrier, inc=1, device_id=self.device(name), device_id_type=MESH
            )
        pl.semaphore_wait(barrier, len(names))


class Copies:
    def __init__(self, place, send, recv):
        self.place, self.send, self.recv = place, send, recv
        self.made, self.landed, self.left, self.local = [], set(), set(), []

    def start(self, src, dst, to):
        i = len(self.made)
        copy = pltpu.make_async_remote_copy(
            src_ref=src,
            dst_ref=dst,
            send_sem=self.send.at[i],
            recv_sem=self.recv.at[i],
            device_id=self.place.device(to),
            device_id_type=MESH,
        )
        copy.start()
        self.made.append(copy)
        return i

    def land(self, *numbers):
        for i in numbers:
            if i not in self.landed:
                self.made[i].wait_recv()
                self.landed.add(i)

    def leave(self, *numbers):
        for i in numbers:
            if i not in self.left:
                self.made[i].wait_send()
                self.left.add(i)

    def keep(self, src, dst, sem):
        copy = pltpu.make_async_copy(src, dst, sem)
        copy.start()
        self.local.append(copy)
        return copy

    def finish(self):
        self.land(*range(len(self.made)))
        self.leave(*range(len(self.made)))


def share(rows, far_part):
    far = rows * far_part // 20 // ROWS * ROWS
    return rows - far, far


class Dealer:
    def __init__(self, copies, far_part):
        self.copies, self.far_part = copies, far_part
        self.waiting = []

    def deal(self, piece):
        place = self.copies.place
        odd = lax.rem(place.dp, 2)
        batch = []
        for name, k in (("x", 1), ("y", 2), ("xy", 3)):
            src, dst, rows = piece(place.chip(k), place.col)
            near, far = share(rows, self.far_part)
            start = pl.multiple_of(odd * far, ROWS)
            at = pl.ds(start, near)
            number = self.copies.start(src(at), dst(at), name)
            batch.append((k, number, piece))
        self.waiting.append(batch)

    def forward(self):
        place = self.copies.place
        odd = lax.rem(place.dp, 2)
        for k, number, piece in self.waiting.pop(0):
            self.copies.land(number)
            _, dst, rows = piece(place.col, place.chip(k))
            near, far = share(rows, self.far_part)
            at = pl.ds(pl.multiple_of(odd * near, ROWS), far)
            self.copies.start(dst(at), dst(at), "z")


def rows_of(ref, first, rows, lead=None, columns=None):
    def view(at):
        where = pl.ds(pl.multiple_of(first + at.start, ROWS), at.size)
        index = (where, columns if columns is not None else slice(None))
        return ref.at[index] if lead is None else ref.at[(lead,) + index]

    return view


def weight_pieces(geo, refs, outs):
    n_col, part, bw, tiles, wide = geo
    shared, span = n_col * bw, wide * LANES
    rec_in, rec_out, mlp_in, mlp_out = refs
    w_rec, w_out, w_in, w_down = outs

    def here(chip):
        return pl.multiple_of(chip * part, LANES)

    def blk(chip):
        return pl.multiple_of(chip * bw, LANES)

    def tile(chip):
        return pl.multiple_of(shared + lax.div(chip, 2) * LANES, LANES)

    def win(chip):
        return pl.multiple_of(window_tile(chip, tiles, n_col, wide) * LANES, LANES)

    def in_piece(ref, j, out, lead, source_at, size, column):
        def piece(dest, source):
            return (
                rows_of(ref, 0, part, j, pl.ds(pl.multiple_of(source_at(dest), LANES), size)),
                rows_of(out, here(source), part, lead, pl.ds(column, size)),
                part,
            )

        return piece

    def down_piece(ref, out, source_at, size, row):
        def piece(dest, source):
            return (
                rows_of(ref, source_at(dest), size),
                rows_of(out, row, size, None, pl.ds(here(source), part)),
                size,
            )

        return piece

    found = {}
    if rec_in is not None:
        found["rec_in"] = [
            in_piece(rec_in, 0, w_rec, None, blk, bw, 0),
            in_piece(rec_in, 0, w_rec, None, lambda chip: shared, bw, bw),
            in_piece(rec_in, 1, w_rec, None, blk, bw, 2 * bw),
            in_piece(rec_in, 1, w_rec, None, tile, LANES, 3 * bw),
        ]
    if rec_out is not None:
        found["rec_out"] = [
            down_piece(rec_out, w_out, blk, bw, 0),
            down_piece(rec_out, w_out, tile, LANES, bw),
        ]
    if mlp_in is not None:
        half = span // 2
        found["mlp_in"] = [
            in_piece(mlp_in, j, w_in, j, lambda chip, h=h: win(chip) + h * half, half, h * half)
            for j in range(2)
            for h in range(2)
        ]
    if mlp_out is not None:
        half = span // 2
        found["mlp_out"] = [
            down_piece(mlp_out, w_down, lambda chip, h=h: win(chip) + h * half, half, h * half)
            for h in range(2)
        ]
    return found


def own_pieces(place, pieces):
    pairs = []
    for piece in pieces:
        src, dst, rows = piece(place.col, place.col)
        pairs.append((src(pl.ds(0, rows)), dst(pl.ds(0, rows))))
    return pairs


class Stay:
    def __init__(self, pairs, bufs, sems):
        self.pairs, self.bufs, self.sems = pairs, bufs, sems
        self.loads = [
            pltpu.make_async_copy(src, buf, sems.at[i])
            for i, ((src, _), buf) in enumerate(zip(pairs, bufs))
        ]
        for load in self.loads:
            load.start()

    def turn(self):
        for load in self.loads:
            load.wait()
        self.stores = [
            pltpu.make_async_copy(buf, dst, self.sems.at[i])
            for i, ((_, dst), buf) in enumerate(zip(self.pairs, self.bufs))
        ]
        for store in self.stores:
            store.start()

    def finish(self):
        for store in self.stores:
            store.wait()


class Gather:
    def __init__(self, copies, mine, at):
        self.copies, self.at = copies, at
        place = copies.place
        row, col = place.row, place.col
        self.first = [
            copies.start(mine(half), at(row, col, half), name)
            for half in (0, 1)
            for name in ("x", "y")
        ]
        self.own = copies.start(mine(None), at(row, col, None), "core")
        self.rounds = []

    def pass_half(self, half):
        copies, place = self.copies, self.copies.place
        views = [self.at(place.row, place.chip(k), half) for k in (1, 2)]
        x, y = self.first[2 * half], self.first[2 * half + 1]
        if half == 0:
            copies.land(x)
            round_ = copies.start(views[0], views[0], "y")
            core_x = copies.start(views[0], views[0], "core")
            copies.land(y)
            core_y = copies.start(views[1], views[1], "core")
        else:
            copies.land(y)
            round_ = copies.start(views[1], views[1], "x")
            core_y = copies.start(views[1], views[1], "core")
            copies.land(x)
            core_x = copies.start(views[0], views[0], "core")
        self.rounds.append(round_)
        return core_x, core_y

    def pass_on(self):
        return self.pass_half(0) + self.pass_half(1)

    def last(self):
        copies, place = self.copies, self.copies.place
        corner = self.at(place.row, place.chip(3), None)
        copies.land(*self.rounds)
        return copies.start(corner, corner, "core")


def block_view(source, target, row, col, half):
    rows, part = source.shape
    cut = rows // 2
    first = row * rows + (0 if half is None else half * cut)
    size = rows if half is None else cut
    return target.at[
        pl.ds(pl.multiple_of(first, ROWS), size), pl.ds(pl.multiple_of(col * part, LANES), part)
    ]


def block_gather(copies, source, target):
    cut = source.shape[0] // 2

    def mine(half):
        return source if half is None else source.at[pl.ds(half * cut, cut), :]

    return Gather(copies, mine, functools.partial(block_view, source, target))


AROUND = ("x", "y", "xy", "core", "z")


def open_kernel(geo, tokens, rec_in, gains, x_all, w_rec, gains_all, send, recv, local, *bufs):
    place = Place()
    place.meet(AROUND)
    copies = Copies(place, send, recv)
    pieces = weight_pieces(geo, (rec_in, None, None, None), (w_rec, None, None, None))["rec_in"]
    dealer = Dealer(copies, 10)
    dealer.deal(pieces[0])
    dealer.deal(pieces[1])
    gather = block_gather(copies, tokens, x_all)
    own_block = (tokens, block_view(tokens, x_all, place.row, place.col, None))
    dealer.deal(pieces[2])
    dealer.deal(pieces[3])
    mine = gains_all.at[:, pl.ds(pl.multiple_of(place.col * geo[1], LANES), geo[1])]
    for name in ("x", "y", "xy"):
        copies.start(gains, mine, name)
    stay = Stay([own_block] + own_pieces(place, pieces) + [(gains, mine)], bufs, local)
    stay.turn()
    dealer.forward()
    dealer.forward()
    gather.pass_on()
    dealer.forward()
    dealer.forward()
    gather.last()
    copies.finish()
    stay.finish()


def open_gather(tokens, rec_in, gains, geo):
    n_col, part, bw, tiles, wide = geo
    width = part * n_col
    return pl.pallas_call(
        functools.partial(open_kernel, geo),
        out_shape=(
            jax.ShapeDtypeStruct((2 * tokens.shape[0], width), low),
            jax.ShapeDtypeStruct((width, 3 * bw + LANES), low),
            jax.ShapeDtypeStruct((gains.shape[0], width), f32),
        ),
        in_specs=[anywhere] * 3,
        out_specs=(anywhere,) * 3,
        scratch_shapes=[
            pltpu.SemaphoreType.DMA((39,)),
            pltpu.SemaphoreType.DMA((39,)),
            pltpu.SemaphoreType.DMA((6,)),
            pltpu.VMEM(tokens.shape, low),
            pltpu.VMEM((part, bw), low),
            pltpu.VMEM((part, bw), low),
            pltpu.VMEM((part, bw), low),
            pltpu.VMEM((part, LANES), low),
            pltpu.VMEM(gains.shape, f32),
        ],
        compiler_params=pltpu.CompilerParams(collective_id=1, has_side_effects=True),
        name="open_gather",
    )(tokens, rec_in, gains)


def slot_gather(copies, local_ref, buf, own):
    cut = own // 2
    n_col = buf.shape[0] // 2

    def at(row, col, half):
        slot = buf.at[row * n_col + col]
        return slot if half is None else slot.at[pl.ds(half * cut, cut), :]

    def mine(half):
        return local_ref if half is None else local_ref.at[pl.ds(half * cut, cut), :]

    return Gather(copies, mine, at)


def tanh_parts(x):
    k = 0.7978845608028654
    square = x * x
    t = jnp.tanh(k * x * (1.0 + 0.044715 * square))
    value = 0.5 * x * (1.0 + t)
    slope = 0.5 * (1.0 + t) + 0.5 * x * (1.0 - t * t) * k * (1.0 + 3 * 0.044715 * square)
    return value, slope


def glu_kernel(
    spare, n2, w_in, w_down, g_all, n2_all, hidden, d_glu, buf, wi, wd, g, hid, dgl, send, recv, local
):
    place = Place()
    place.meet(("x", "y", "core"))
    copies = Copies(place, send, recv)
    own, width = n2.shape
    n_col = buf.shape[0] // 2
    span = wd.shape[0]
    step = 512
    gather = slot_gather(copies, n2, buf, own)
    me = place.row * n_col + place.col
    n_steps = span // step
    near_slots = [place.col, n_col + place.col]
    far_slots = [r * n_col + place.chip(k) for k in (1, 2, 3) for r in (0, 1)]

    def load_rows(slot, i):
        rows = pl.ds(pl.multiple_of(slot * own, ROWS), own)
        return copies.keep(g_all.at[rows, :], g.at[rows, :], local.at[i])

    first = [copies.keep(n2, buf.at[me], local.at[3])]
    first += [load_rows(slot, 4 + i) for i, slot in enumerate(near_slots)]
    weights = []
    for i in range(n_steps):
        at = pl.ds(i * step, step)
        weights.append(
            (
                copies.keep(w_in.at[:, :, at], wi.at[:, :, at], local.at[12 + 2 * i]),
                copies.keep(w_down.at[at, :], wd.at[at, :], local.at[13 + 2 * i]),
            )
        )
    others = [load_rows(slot, 6 + i) for i, slot in enumerate(far_slots)]
    for load in first:
        load.wait()
    hide = spare(place.col)

    def work(slots, first, size, lo, hi):
        rows = [pl.ds(pl.multiple_of(s * own + first, ROWS), size) for s in slots]
        n2_here = jnp.concatenate([buf[s, first : first + size, :] for s in slots], axis=0)
        g_here = jnp.concatenate([g[r, :] for r in rows], axis=0)

        def columns(i, carry):
            at = pl.ds(pl.multiple_of(i * step, LANES), step)
            up_at = pl.ds(pl.multiple_of(span + i * step, LANES), step)
            gate = dot(n2_here, wi[0, :, at])
            up = dot(n2_here, wi[1, :, at])
            d_hid = dot(g_here, wd[at, :], ((1,), (1,)))
            lane = lax.broadcasted_iota(jnp.int32, gate.shape, 1) + i * step
            used = (lane >= LANES) | jnp.logical_not(hide)
            up = jnp.where(used, up, 0.0)
            d_hid = jnp.where(used, d_hid, 0.0)
            value, slope = tanh_parts(gate)
            h = (value * up).astype(low)
            dg = (d_hid * up * slope).astype(low)
            du = (d_hid * value).astype(low)
            for n, r in enumerate(rows):
                part = slice(n * size, (n + 1) * size)
                hid[r, at] = h[part]
                dgl[r, at] = dg[part]
                dgl[r, up_at] = du[part]
            return carry

        lax.fori_loop(lo, hi, columns, 0)

    def both_cores(*chips):
        return [s for chip in chips for s in (chip, n_col + chip)]

    half = own // 2
    near = both_cores(place.chip(1), place.chip(2))
    copies.land(gather.own)
    for i in range(n_steps):
        for load in weights[i]:
            load.wait()
        work(both_cores(place.col), 0, own, i, i + 1)
    for load in others:
        load.wait()
    core0 = gather.pass_half(0)
    copies.land(*core0)
    work(near, 0, half, 0, n_steps // 2)
    core1 = gather.pass_half(1)
    work(near, 0, half, n_steps // 2, n_steps)
    copies.land(*core1)
    work(near, half, half, 0, n_steps // 2)
    corner = gather.last()
    work(near, half, half, n_steps // 2, n_steps)
    copies.land(corner)
    out_n2 = copies.keep(buf, n2_all, local.at[0])
    work(both_cores(place.chip(3)), 0, own, 0, n_steps)
    out_h = copies.keep(hid, hidden, local.at[1])
    out_d = copies.keep(dgl, d_glu, local.at[2])
    copies.finish()
    out_n2.wait()
    out_h.wait()
    out_d.wait()


def glu(n2, w_in, w_down, g_all, spare):
    own, width = n2.shape
    group = g_all.shape[0]
    span = w_down.shape[0]
    n_all, h, d = pl.pallas_call(
        functools.partial(glu_kernel, spare),
        out_shape=(
            jax.ShapeDtypeStruct((group // own, own, width), low),
            jax.ShapeDtypeStruct((group, span), low),
            jax.ShapeDtypeStruct((group, 2 * span), low),
        ),
        in_specs=[anywhere] * 4,
        out_specs=(anywhere,) * 3,
        scratch_shapes=[
            pltpu.VMEM((group // own, own, width), low),
            pltpu.VMEM(w_in.shape, low),
            pltpu.VMEM(w_down.shape, low),
            pltpu.VMEM((group, width), low),
            pltpu.VMEM((group, span), low),
            pltpu.VMEM((group, 2 * span), low),
            pltpu.SemaphoreType.DMA((12,)),
            pltpu.SemaphoreType.DMA((12,)),
            pltpu.SemaphoreType.DMA((12 + 2 * (span // 256),)),
        ],
        compiler_params=pltpu.CompilerParams(
            collective_id=3, has_side_effects=True, vmem_limit_bytes=58 * MIB
        ),
        cost_estimate=pl.CostEstimate(
            flops=6 * group * width * span, bytes_accessed=60 * MIB, transcendentals=group * span
        ),
        name="glu",
    )(n2, w_in, w_down, g_all)
    return n_all.reshape(group, width), h, d


def start_home(copies, source, home, buf, sem):
    place = copies.place
    own, part = source.shape[0], home.shape[1]
    spot = home.at[pl.ds(pl.multiple_of(place.col * own, ROWS), own), :]

    def columns_of(chip):
        return source.at[:, pl.ds(pl.multiple_of(chip * part, LANES), part)]

    for name, j in (("xy", 3), ("x", 1), ("y", 2)):
        copies.start(columns_of(place.chip(j)), spot, name)
    return Stay([(columns_of(place.col), spot)], [buf], sem)


def scatter_kernel(shape, finish, n_more, n_outs, pick, beside, act, w, *refs):
    n_parts, across, own, width = shape
    side = []
    if beside is not None:
        n_in, n_out, n_hold = beside.counts
        side, refs = list(refs[:n_in]), refs[n_in:]
    more, refs = refs[:n_more], refs[n_more:]
    outs, refs = refs[:n_outs], refs[n_outs:]
    if beside is not None:
        side += refs[:n_out]
        side += refs[len(refs) - n_hold :]
        refs = refs[n_out : len(refs) - n_hold]
    actv, wv, other, mine, from_core, from_x, from_y, turn, fin, send, recv, local = refs[:12]
    held = refs[12 : 12 + n_more]
    place = Place()
    place.meet(["x", "y", "core"] + ([] if beside is None else beside.names()))
    copies = Copies(place, send, recv)
    if beside is not None:
        beside.start(copies, *side)
    cut = own // 2
    n_col = act.shape[0] // own // 2
    k = act.shape[1] // n_parts
    step = 512
    loads = [copies.keep(act, actv, local.at[0])]
    if pick is None:
        loads.append(copies.keep(w, wv, local.at[1]))
    else:
        for i, (src, dst, size) in enumerate(pick(place.col)):
            loads.append(
                copies.keep(w.at[:, pl.ds(src, size)], wv.at[:, pl.ds(dst, size)], local.at[1 + i])
            )
    my_rows = pl.ds(pl.multiple_of((place.row * n_col + place.col) * own, ROWS), own)
    extra = []
    for i, (ref, buf) in enumerate(zip(more, held)):
        src = ref.at[my_rows, :] if ref.shape[0] > own else ref
        extra.append(copies.keep(src, buf, local.at[4 + i]))
    for load in loads:
        load.wait()
    top, bottom = pl.ds(0, cut), pl.ds(cut, cut)

    def work(j):
        chip = place.chip(j)
        slots = ((1 - place.row) * n_col + chip, place.row * n_col + chip)
        left = [
            jnp.concatenate(
                [
                    actv[pl.ds(pl.multiple_of(s * own, ROWS), own), n * k : (n + 1) * k]
                    for s in slots
                ],
                axis=0,
            )
            for n in range(n_parts)
        ]

        def columns(i, carry):
            at = pl.ds(pl.multiple_of(i * step, LANES), step)
            total = None
            for n in range(n_parts):
                if across:
                    right = wv[n, at, :] if n_parts > 1 else wv[at, :]
                    term = dot(left[n], right, ((1,), (1,)))
                else:
                    term = dot(left[n], wv[:, at])
                total = term if total is None else total + term
            other[j, :, at] = total[:own].astype(low)
            mine[j, :, at] = total[own:]
            return carry

        lax.fori_loop(0, width // step, columns, 0)
        return copies.start(other.at[j], from_core.at[j], "core")

    def add_core(j, number):
        copies.land(number)
        mine[j] = mine[j] + from_core[j].astype(f32)
        turn[j] = mine[j].astype(low)

    if beside is not None:
        beside.turn()
    core3 = work(3)
    core1 = work(1)
    add_core(3, core3)
    x3 = copies.start(turn.at[3, top, :], from_x.at[0], "x")
    y3 = copies.start(turn.at[3, bottom, :], from_y.at[0], "y")
    core2 = work(2)
    add_core(1, core1)
    x1 = copies.start(turn.at[1, top, :], from_x.at[1], "x")
    core0 = work(0)
    add_core(2, core2)
    y2 = copies.start(turn.at[2, bottom, :], from_y.at[1], "y")
    copies.land(x3)
    turn[2, top, :] = (mine[2, top, :] + from_x[0].astype(f32)).astype(low)
    y_last = copies.start(turn.at[2, top, :], from_y.at[2], "y")
    copies.land(y3)
    turn[1, bottom, :] = (mine[1, bottom, :] + from_y[0].astype(f32)).astype(low)
    x_last = copies.start(turn.at[1, bottom, :], from_x.at[2], "x")
    add_core(0, core0)
    copies.land(x1, y2, y_last, x_last)
    fin[top, :] = mine[0, top, :] + from_x[1].astype(f32) + from_y[2].astype(f32)
    fin[bottom, :] = mine[0, bottom, :] + from_y[1].astype(f32) + from_x[2].astype(f32)
    for load in extra:
        load.wait()
    for ref in outs:
        if ref.shape[0] == 8:
            ref[...] = jnp.zeros_like(ref)
    rows_at_once = 64

    def rows_done(i, carry):
        rows = pl.ds(pl.multiple_of(i * rows_at_once, rows_at_once), rows_at_once)
        finish(rows, fin, held, outs)
        return carry

    lax.fori_loop(0, own // rows_at_once, rows_done, 0)
    if beside is not None:
        beside.finish(copies, *side)
    copies.finish()


def multiply_scatter(act, w, across, number, name, finish, more, outs, pick=None, beside=None):
    n_parts = w.shape[0] if w.ndim == 3 else 1
    group = act.shape[0]
    n_col = lax.axis_size("col")
    own = group // (2 * n_col)
    width = w.shape[-2] if across else w.shape[-1]
    held = [((own, r.shape[1]) if r.shape[0] > own else r.shape, r.dtype) for r in more]
    out_specs = [in_vmem] * len(outs)
    scratch = [pltpu.VMEM(*h) for h in held]
    n_outs, side_in, copy_count = len(outs), (), 13
    in_specs = [anywhere] * (2 + len(more))
    if beside is not None:
        side_in, side_out, side_scratch = beside.inputs, beside.outputs, beside.scratch
        in_specs = in_specs[:2] + beside.in_specs + in_specs[2:]
        outs += side_out
        out_specs += beside.out_specs
        scratch += side_scratch
        copy_count += beside.copy_count
    return pl.pallas_call(
        functools.partial(
            scatter_kernel,
            (n_parts, across, own, width),
            finish,
            len(more),
            n_outs,
            pick,
            beside,
        ),
        out_shape=tuple(jax.ShapeDtypeStruct(*s) for s in outs),
        in_specs=in_specs,
        out_specs=tuple(out_specs),
        scratch_shapes=[
            pltpu.VMEM(act.shape, low),
            pltpu.VMEM(w.shape if pick is None else (width, act.shape[1]), low),
            pltpu.VMEM((4, own, width), low),
            pltpu.VMEM((4, own, width), f32),
            pltpu.VMEM((4, own, width), low),
            pltpu.VMEM((3, own // 2, width), low),
            pltpu.VMEM((3, own // 2, width), low),
            pltpu.VMEM((4, own, width), low),
            pltpu.VMEM((own, width), f32),
            pltpu.SemaphoreType.DMA((copy_count,)),
            pltpu.SemaphoreType.DMA((copy_count,)),
            pltpu.SemaphoreType.DMA((4 + len(held),)),
        ]
        + scratch,
        compiler_params=pltpu.CompilerParams(
            collective_id=number, has_side_effects=True, vmem_limit_bytes=60 * MIB
        ),
        cost_estimate=pl.CostEstimate(
            flops=2 * group * width * act.shape[1], bytes_accessed=40 * MIB, transcendentals=0
        ),
        name=name,
    )(act, w, *side_in, *more)


def home_kernel(rows, home, send, recv, buf, sem):
    place = Place()
    place.meet(("x", "y", "xy"))
    copies = Copies(place, send, recv)
    stay = start_home(copies, rows, home, buf, sem)
    stay.turn()
    copies.finish()
    stay.finish()


def take_home(rows, n_col):
    own, width = rows.shape
    home = (n_col * own, width // n_col)
    return pl.pallas_call(
        home_kernel,
        out_shape=jax.ShapeDtypeStruct(home, low),
        in_specs=[anywhere],
        out_specs=anywhere,
        scratch_shapes=[
            pltpu.SemaphoreType.DMA((3,)),
            pltpu.SemaphoreType.DMA((3,)),
            pltpu.VMEM((own, home[1]), low),
            pltpu.SemaphoreType.DMA((1,)),
        ],
        compiler_params=pltpu.CompilerParams(collective_id=11, has_side_effects=True),
        name="take_home",
    )(rows)


class GateReduce:
    counts = (2, 2, 3)

    def __init__(self, gates, small):
        self.n_dp = gates.shape[0]
        part = gates.shape[1:]
        self.inputs = (gates, small)
        self.outputs = ((part, low), (small.shape, f32))
        self.copy_count = 2 * (self.n_dp - 1)
        self.scratch = [
            pltpu.VMEM(gates.shape, low),
            pltpu.VMEM((self.n_dp - 1,) + part, low),
            pltpu.VMEM((self.n_dp - 1,) + small.shape, f32),
        ]

    in_specs, out_specs = [in_vmem] * 2, [in_vmem] * 2

    def turn(self):
        pass

    def names(self):
        return [f"d{d}" for d in range(1, self.n_dp)]

    def start(self, copies, gates, small, part_out, small_out, held, far, far_small):
        dp = copies.place.dp
        held[...] = gates[...]
        self.numbers = []
        for i, name in enumerate(self.names()):
            other = jnp.bitwise_xor(dp, i + 1)
            self.numbers.append(copies.start(held.at[other], far.at[i], name))
            self.numbers.append(copies.start(small, far_small.at[i], name))

    def finish(self, copies, gates, small, part_out, small_out, held, far, far_small):
        copies.land(*self.numbers)
        total = held[copies.place.dp].astype(f32)
        value = small[...]
        for i in range(self.n_dp - 1):
            total = total + far[i].astype(f32)
            value = value + far_small[i]
        part_out[...] = total.astype(low)
        small_out[...] = value


class GateGather:
    counts = (2, 2, 3)
    in_specs, out_specs = [in_vmem, anywhere], [in_vmem, anywhere]

    def __init__(self, part, grads, n_dp):
        self.n_dp = n_dp
        self.inputs = (part, grads)
        self.outputs = (((n_dp,) + part.shape, low), (grads.shape, grads.dtype))
        self.copy_count = n_dp + 2
        self.scratch = [
            pltpu.VMEM((n_dp,) + part.shape, low),
            pltpu.VMEM(grads.shape[1:], grads.dtype),
            pltpu.SemaphoreType.DMA((1,)),
        ]

    def names(self):
        return ["xy"] + [f"d{d}" for d in range(1, self.n_dp)]

    def start(self, copies, part, grads, all_out, grads_out, held, buf, sem):
        col = copies.place.col
        mine = held.at[copies.place.dp]
        self.numbers = [copies.start(part, mine, name) for name in self.names()[1:]]
        start_deal(copies, grads, grads_out)
        self.stay = Stay([(grads.at[col], grads_out.at[col])], [buf], sem)

    def turn(self):
        self.stay.turn()

    def finish(self, copies, part, grads, all_out, grads_out, held, buf, sem):
        held[copies.place.dp] = part[...]
        copies.land(*self.numbers)
        all_out[...] = held[...]
        self.stay.finish()


def square_sum(ref, row, x):
    ref[row : row + 1, :] += jnp.broadcast_to(jnp.sum(x * x, keepdims=True), (1, LANES))


def norm_scale(x):
    return lax.rsqrt(jnp.mean(x * x, axis=-1, keepdims=True) + epsilon)


def after_out_one(rows, fin, held, outs):
    x, gain = held
    resid_out, n2_out, squares = outs
    out_one = fin[rows, :]
    resid = x[rows, :].astype(f32) + out_one
    resid_out[rows, :] = resid
    n2_out[rows, :] = (resid * norm_scale(resid) * gain[1:2, :]).astype(low)
    square_sum(squares, 0, out_one)
    square_sum(squares, 1, resid)


def norm_back(d_normed, x, gain, grad_gain):
    scale = norm_scale(x)
    gained = gain * d_normed
    inner = jnp.mean(gained * x, axis=-1, keepdims=True)
    grad_gain[0:1, :] += jnp.sum(d_normed * x * scale, axis=0, keepdims=True)
    return scale * gained - x * (scale * scale * scale * inner)


def after_normed_two(rows, fin, held, outs):
    resid, upstream, gain = held
    d_resid_out, d_out, grad_gain = outs
    d_resid = upstream[rows, :].astype(f32) + norm_back(
        fin[rows, :], resid[rows, :], gain[1:2, :], grad_gain
    )
    d_resid_out[rows, :] = d_resid
    d_out[rows, :] = d_resid.astype(low)


def after_normed_one(rows, fin, held, outs):
    x, d_resid, gain = held
    back, grad_gain, squares = outs
    x_here = x[rows, :].astype(f32)
    passed = norm_back(fin[rows, :], x_here, gain[0:1, :], grad_gain)
    back[rows, :] = (d_resid[rows, :] + passed).astype(low)
    square_sum(squares, 0, x_here)


def after_out_two(rows, fin, held, outs):
    (resid,) = held
    back, squares = outs
    out_two = fin[rows, :]
    back[rows, :] = (resid[rows, :] + out_two).astype(low)
    square_sum(squares, 0, out_two)


def start_deal(copies, source, target):
    col = copies.place.col
    for name, j in (("xy", 3), ("x", 1), ("y", 2)):
        copies.start(source.at[copies.place.chip(j)], target.at[col], name)


def deal_kernel(source, target, send, recv, local, buf):
    place = Place()
    place.meet(("x", "y", "xy"))
    copies = Copies(place, send, recv)
    start_deal(copies, source, target)
    stay = Stay([(source.at[place.col], target.at[place.col])], [buf], local)
    stay.turn()
    copies.finish()
    stay.finish()


def deal_back(x, number, name):
    return pl.pallas_call(
        deal_kernel,
        out_shape=jax.ShapeDtypeStruct(x.shape, x.dtype),
        in_specs=[anywhere],
        out_specs=anywhere,
        scratch_shapes=[
            pltpu.SemaphoreType.DMA((3,)),
            pltpu.SemaphoreType.DMA((3,)),
            pltpu.SemaphoreType.DMA((1,)),
            pltpu.VMEM(x.shape[1:], x.dtype),
        ],
        compiler_params=pltpu.CompilerParams(
            collective_id=number, has_side_effects=True, vmem_limit_bytes=16 * MIB
        ),
        name=name,
    )(x)


PLANE = ("x", "y", "xy", "core", "cx", "cy", "cxy")


def sums_kernel(
    n_dp,
    gain_one,
    gain_two,
    squares_x,
    squares_one,
    squares_two,
    small,
    gates,
    rows,
    gains_out,
    squares_out,
    chans_out,
    gates_out,
    home,
    mixed,
    got,
    total,
    shared,
    ch,
    gv,
    send,
    recv,
    *bufs,
):
    place = Place()
    far = [f"d{d}" for d in range(1, n_dp)]
    place.meet(list(PLANE) + far)
    copies = Copies(place, send, recv)
    n_col, part = ch.shape[0], gains_out.shape[1]
    mixed[...] = jnp.zeros_like(mixed)
    for c in range(n_col):
        mixed[c : c + 1, :part] = gain_one[0:1, c * part : (c + 1) * part]
        mixed[n_col + c : n_col + c + 1, :part] = gain_two[0:1, c * part : (c + 1) * part]
    mixed[0:1, part:] = squares_x[0:1, :]
    mixed[1:3, part:] = squares_one[0:2, :]
    mixed[3:4, part:] = squares_two[0:1, :]
    planes = [copies.start(mixed, got.at[i], name) for i, name in enumerate(far)]
    col = place.col
    ch[col] = small[...]
    gv[col] = gates[...]
    for name in ("x", "y", "xy"):
        copies.start(ch.at[col], ch.at[col], name)
    half = n_dp // 2
    halves = (pl.ds(0, half), pl.ds(half, half))

    def gate_view(chip, h):
        return gv.at[chip, halves[h]]

    direct = {
        (name, h): copies.start(gate_view(col, h), gate_view(col, h), name)
        for h in (0, 1)
        for name in ("x", "y")
    }
    stay_home = start_home(copies, rows, home, bufs[0], bufs[1])
    stay_home.turn()
    copies.land(direct["x", 0])
    far_x = gate_view(place.chip(1), 0)
    copies.start(far_x, far_x, "y")
    copies.land(direct["y", 1])
    far_y = gate_view(place.chip(2), 1)
    copies.start(far_y, far_y, "x")
    copies.land(*planes)
    value = mixed[...]
    for i in range(n_dp - 1):
        value = value + got[i]
    total[...] = value
    others = [copies.start(total, shared.at[i], name) for i, name in enumerate(PLANE)]
    copies.land(*others)
    for i in range(len(PLANE)):
        value = value + shared[i]
    got[0] = value
    gains_out[0:1, :] = got[0, pl.ds(col, 1), :part]
    gains_out[1:2, :] = got[0, pl.ds(n_col + col, 1), :part]
    squares_out[...] = value[:, part:]
    copies.finish()
    chans_out[...] = ch[...]
    gates_out[...] = gv[...]
    stay_home.finish()


def sum_everywhere(gain_one, gain_two, squares, small, gates, rows_low, n_dp, n_col):
    count = n_dp + 22
    part = rows_low.shape[1] // n_col
    mixed = (2 * n_col, part + LANES)
    home = (n_col * rows_low.shape[0], rows_low.shape[1] // n_col)
    return pl.pallas_call(
        functools.partial(sums_kernel, n_dp),
        out_shape=(
            jax.ShapeDtypeStruct((2, part), f32),
            jax.ShapeDtypeStruct((2 * n_col, LANES), f32),
            jax.ShapeDtypeStruct((n_col,) + small.shape, f32),
            jax.ShapeDtypeStruct((n_col,) + gates.shape, low),
            jax.ShapeDtypeStruct(home, low),
        ),
        in_specs=[in_vmem] * 7 + [anywhere],
        out_specs=(in_vmem,) * 4 + (anywhere,),
        scratch_shapes=[
            pltpu.VMEM(mixed, f32),
            pltpu.VMEM((n_dp - 1,) + mixed, f32),
            pltpu.VMEM(mixed, f32),
            pltpu.VMEM((len(PLANE),) + mixed, f32),
            pltpu.VMEM((n_col,) + small.shape, f32),
            pltpu.VMEM((n_col,) + gates.shape, low),
            pltpu.SemaphoreType.DMA((count,)),
            pltpu.SemaphoreType.DMA((count,)),
            pltpu.VMEM((rows_low.shape[0], home[1]), low),
            pltpu.SemaphoreType.DMA((1,)),
        ],
        compiler_params=pltpu.CompilerParams(
            collective_id=5, has_side_effects=True, vmem_limit_bytes=24 * MIB
        ),
        name="small_sums",
    )(gain_one, gain_two, *squares, small, gates, rows_low)


def own_lanes(place, geo):
    n_col, part, bw, tiles, wide = geo
    found = [
        pl.ds(pl.multiple_of(place.col * bw + k * LANES, LANES), LANES) for k in range(bw // LANES)
    ]
    shared_tile = n_col * bw + lax.div(place.col, 2) * LANES
    return found + [pl.ds(pl.multiple_of(shared_tile, LANES), LANES)]


def one_less_exp(z):
    series = 1.0 + z / 6.0
    for n in (5.0, 4.0, 3.0, 2.0):
        series = 1.0 + z / n * series
    return jnp.where(z > -0.1, -z * series, 1.0 - jnp.exp(z))


def scan_tile(a, u, reverse):
    rows = a.shape[0]
    index = lax.broadcasted_iota(jnp.int32, a.shape, 0)
    by = 1
    while by < rows:
        turn = rows - by if reverse else by
        inside = index < rows - by if reverse else index >= by
        u = u + a * jnp.where(inside, pltpu.roll(u, turn, 0), 0.0)
        a = a * jnp.where(inside, pltpu.roll(a, turn, 0), 1.0)
        by *= 2
    return a, u


def forward_kernel(
    geo,
    x_all,
    w_rec,
    gain,
    gates,
    bias,
    soft,
    conv_w,
    conv_b,
    places,
    cotangent,
    rec_out,
    mlp_in,
    mlp_out,
    n1_out,
    x_out,
    y_out,
    pre_out,
    c_out,
    state_out,
    branch_out,
    first_out,
    g_all,
    w_out,
    w_in,
    w_down,
    xv,
    wv,
    before,
    xb,
    yv,
    prev,
    cv,
    hv,
    pv,
    bv,
    carry,
    first,
    send,
    recv,
    local,
    stay_sems,
    *bufs,
):
    place = Place()
    place.meet(AROUND + ("next", "prev"))
    copies = Copies(place, send, recv)
    n_col, part, bw, tiles, wide = geo
    chans = bw + LANES
    group, width = xv.shape
    tile = 256
    n_tiles = group // tile
    loads = [copies.keep(x_all, xv, local.at[0]), copies.keep(w_rec, wv, local.at[1])]
    halo = copies.start(x_all.at[pl.ds(group - ROWS, ROWS), :], before, "next")
    found = weight_pieces(geo, (None, rec_out, mlp_in, mlp_out), (None, w_out, w_in, w_down))
    pieces = found["rec_out"] + found["mlp_in"] + found["mlp_out"]
    dealer = Dealer(copies, 9)
    for piece in pieces[:5]:
        dealer.deal(piece)
    for load in loads:
        load.wait()
    own_block = (cotangent, block_view(cotangent, g_all, place.row, place.col, None))
    stay = Stay([own_block] + own_pieces(place, pieces), bufs, stay_sems)
    high_tile = place.col >= 2
    mine = own_lanes(place, geo)
    conv_lanes = mine[:-1] + [
        slice(n_col * bw + k * LANES, n_col * bw + (k + 1) * LANES) for k in range(bw // LANES)
    ]
    tile_cols = pl.ds(pl.multiple_of(lax.div(place.col, 2) * LANES, LANES), LANES)
    idle_tile = lax.rem(place.col, 2) == 1

    def normed(x):
        x = x.astype(f32)
        scale = lax.rsqrt(jnp.sum(x * x, axis=-1, keepdims=True) / width + epsilon)
        return (x * scale * gain[0:1, :]).astype(low)

    copies.land(halo)
    xb[0:8, :] = dot(normed(before[...]), wv[:, : 2 * bw])[ROWS - 8 :]
    carry[0:1] = jnp.zeros_like(carry[0:1])
    carry[1:2] = jnp.ones_like(carry[1:2])

    def work(i, unused):
        r0 = pl.multiple_of(i * tile, tile)
        rows = pl.ds(r0, tile)
        n1 = normed(xv[rows, :])
        xv[rows, :] = n1
        both = dot(n1, wv[...])
        xb[pl.ds(pl.multiple_of(r0 + 8, 8), tile), :] = both[:, : 2 * bw]
        yv[rows, :] = both[:, 2 * bw :]
        spot = places[rows, :]
        reach = xb[pl.ds(r0, tile + 8), :]
        conv = []
        for lane in range(2 * bw // LANES):
            at = slice(lane * LANES, (lane + 1) * LANES)
            near = reach[:, at]
            tap = conv_lanes[lane]
            total = conv_b[0:1, tap] + conv_w[0:1, tap] * near[8:]
            for t in range(1, conv_w.shape[0]):
                lagged = pltpu.roll(near, t, 0)[8:]
                total = total + jnp.where(spot >= t, conv_w[t : t + 1, tap] * lagged, 0.0)
            conv.append(total.astype(low))
        c = jnp.concatenate(conv, axis=1)
        cv[rows, :] = c
        pre = [
            jnp.concatenate(
                [dot(c[:, :bw], gates[j, place.col]), dot(c[:, bw:], gates[j, n_col, :, tile_cols])],
                axis=1,
            )
            + jnp.concatenate([bias[j : j + 1, at] for at in mine], axis=1)
            for j in range(2)
        ]
        prev[rows, :chans] = pre[0]
        prev[rows, chans:] = pre[1]
        reset = spot == 0
        for lane in range(chans // LANES):
            at = slice(lane * LANES, (lane + 1) * LANES)
            if lane * LANES < bw:
                own_c = conv[lane].astype(f32)
            else:
                own_c = jnp.where(high_tile, conv[lane + 1].astype(f32), conv[lane].astype(f32))
            log_a = -8.0 * jax.nn.sigmoid(pre[1][:, at]) * soft[0:1, mine[lane]]
            a = jnp.where(reset, 0.0, jnp.exp(log_a))
            m = jnp.where(reset, 1.0, jnp.sqrt(one_less_exp(2.0 * log_a)))
            u = own_c * jax.nn.sigmoid(pre[0][:, at]) * m
            a, u = scan_tile(a, u, False)
            h = u + a * carry[0:1, at]
            p = a * carry[1:2, at]
            hv[rows, at] = h
            pv[rows, at] = p
            carry[0:1, at] = h[tile - 1 :]
            carry[1:2, at] = p[tile - 1 :]
        return unused

    third = n_tiles // 3
    lax.fori_loop(0, third, work, 0)
    stay.turn()
    dealer.forward()
    dealer.forward()
    dealer.deal(pieces[5])
    dealer.forward()
    lax.fori_loop(third, 2 * third, work, 0)
    dealer.forward()
    dealer.deal(pieces[6])
    lax.fori_loop(2 * third, n_tiles, work, 0)
    dealer.forward()
    dealer.deal(pieces[7])
    state_in = copies.start(hv.at[pl.ds(group - 8, 8), :], first, "next")
    outs = [
        copies.keep(src, dst, local.at[10 + i])
        for i, (src, dst) in enumerate(
            ((xv, n1_out), (xb, x_out), (yv, y_out), (prev, pre_out), (cv, c_out))
        )
    ]
    copies.land(state_in)
    copies.leave(state_in)
    before_all = first[7:8, :]

    def finish(i, unused):
        rows = pl.ds(pl.multiple_of(i * tile, tile), tile)
        for lane in range(chans // LANES):
            at = slice(lane * LANES, (lane + 1) * LANES)
            state = hv[rows, at] + pv[rows, at] * before_all[:, at]
            hv[rows, at] = state
            value, _ = tanh_parts(yv[rows, at])
            b = state * value
            if lane * LANES >= bw:
                b = jnp.where(idle_tile, 0.0, b)
            bv[rows, at] = b.astype(low)
        return unused

    lax.fori_loop(0, n_tiles, finish, 0)
    outs += [
        copies.keep(hv, state_out, local.at[15]),
        copies.keep(bv, branch_out, local.at[16]),
        copies.keep(first, first_out, local.at[17]),
    ]
    dealer.forward()
    gather = block_gather(copies, cotangent, g_all)
    dealer.forward()
    dealer.forward()
    gather.pass_on()
    gather.last()
    copies.finish()
    for copy in outs:
        copy.wait()
    stay.finish()


def rec_forward(x_all, w_rec, params, places, cotangent, rec_out, mlp_in, mlp_out, geo):
    n_col, part, bw, tiles, wide = geo
    width, span, chans = part * n_col, wide * LANES, bw + LANES
    group = x_all.shape[0]

    def of(shape, dtype):
        return jax.ShapeDtypeStruct(shape, dtype)

    kept = [
        ((group, width), low),
        ((group + 8, 2 * bw), f32),
        ((group, chans), f32),
        ((group, 2 * chans), f32),
        ((group, 2 * bw), low),
        ((group, chans), f32),
        ((group, chans), low),
        ((8, chans), f32),
    ]
    dealt = [((group, width), low), ((chans, width), low), ((2, width, span), low), ((span, width), low)]
    copy_count = 1 + 6 * 8 + 12 + 1
    return pl.pallas_call(
        functools.partial(forward_kernel, geo),
        out_shape=tuple(of(*s) for s in kept + dealt),
        in_specs=[anywhere] * 2 + [in_vmem] * 7 + [anywhere] * 4,
        out_specs=(anywhere,) * 12,
        scratch_shapes=[
            pltpu.VMEM((group, width), low),
            pltpu.VMEM(w_rec.shape, low),
            pltpu.VMEM((ROWS, width), low),
            pltpu.VMEM((group + 8, 2 * bw), f32),
            pltpu.VMEM((group, chans), f32),
            pltpu.VMEM((group, 2 * chans), f32),
            pltpu.VMEM((group, 2 * bw), low),
            pltpu.VMEM((group, chans), f32),
            pltpu.VMEM((group, chans), f32),
            pltpu.VMEM((group, chans), low),
            pltpu.VMEM((8, chans), f32),
            pltpu.VMEM((8, chans), f32),
            pltpu.SemaphoreType.DMA((copy_count,)),
            pltpu.SemaphoreType.DMA((copy_count,)),
            pltpu.SemaphoreType.DMA((18,)),
            pltpu.SemaphoreType.DMA((9,)),
            pltpu.VMEM(cotangent.shape, low),
            pltpu.VMEM((bw, part), low),
            pltpu.VMEM((LANES, part), low),
        ]
        + [pltpu.VMEM((part, span // 2), low)] * 4
        + [pltpu.VMEM((span // 2, part), low)] * 2,
        compiler_params=pltpu.CompilerParams(
            collective_id=2, has_side_effects=True, vmem_limit_bytes=58 * MIB
        ),
        name="rec_forward",
    )(x_all, w_rec, *params, places, cotangent, rec_out, mlp_in, mlp_out)


def backward_kernel(
    geo,
    d_out,
    w_out,
    y_in,
    state_in,
    first_in,
    pre_in,
    c_in,
    x_in,
    gates,
    soft,
    conv_w,
    places,
    down,
    d_all,
    d_rec_out,
    gate_out,
    sums,
    down_out,
    buf,
    wv,
    dbv,
    yv,
    slv,
    hs,
    prev,
    cv,
    xb,
    ghv,
    qv,
    dpv,
    there,
    dcv,
    drv,
    gg,
    carry,
    message,
    down_buf,
    send,
    recv,
    local,
    stay_sem,
):
    place = Place()
    place.meet(["x", "y", "xy", "core", "next", "prev"])
    copies = Copies(place, send, recv)
    n_col, part, bw, tiles, wide = geo
    chans = bw + LANES
    own_rows = d_out.shape[0]
    group = yv.shape[0]
    tile = 256
    n_tiles = group // tile
    lanes = [slice(k * LANES, (k + 1) * LANES) for k in range(chans // LANES)]
    gather = slot_gather(copies, d_out, buf, own_rows)
    me = place.row * n_col + place.col
    load = copies.keep(w_out, wv, local.at[0])
    mine = copies.keep(d_out, buf.at[me], local.at[1])
    loads = [
        copies.keep(src, dst, local.at[2 + i])
        for i, (src, dst) in enumerate(
            (
                (y_in, yv),
                (state_in, hs.at[pl.ds(8, group), :]),
                (first_in, hs.at[pl.ds(0, 8), :]),
                (pre_in, prev),
                (c_in, cv),
                (x_in, xb),
            )
        )
    ]
    load.wait()
    mine.wait()
    high_tile = place.col >= 2
    idle_tile = lax.rem(place.col, 2) == 1
    mine_at = own_lanes(place, geo)
    tile_rows = pl.ds(pl.multiple_of(lax.div(place.col, 2) * LANES, LANES), LANES)

    def work(chip):
        slots = (chip, n_col + chip)
        value = dot(jnp.concatenate([buf[s] for s in slots], axis=0), wv[...], ((1,), (1,)))
        for n, s in enumerate(slots):
            rows = pl.ds(pl.multiple_of(s * own_rows, ROWS), own_rows)
            dbv[rows, :] = value[n * own_rows : (n + 1) * own_rows]

    def before_rows(k, unused):
        rows = pl.ds(pl.multiple_of(k * tile, tile), tile)
        for at in lanes:
            value, slope = tanh_parts(yv[rows, at])
            yv[rows, at] = value
            slv[rows, at] = slope
        prev[rows, :] = jax.nn.sigmoid(prev[rows, :])
        return unused

    copies.land(gather.own)
    work(place.col)
    for each in loads:
        each.wait()
    third = n_tiles // 3
    lax.fori_loop(0, third, before_rows, 0)
    x0, y0 = gather.pass_half(0)
    lax.fori_loop(third, 2 * third, before_rows, 0)
    x1, y1 = gather.pass_half(1)
    start_deal(copies, down, down_out)
    stay = Stay([(down.at[place.col], down_out.at[place.col])], [down_buf], stay_sem)
    stay.turn()
    copies.land(y0, y1)
    work(place.chip(2))
    corner = gather.last()
    copies.land(x0, x1)
    work(place.chip(1))
    lax.fori_loop(2 * third, n_tiles, before_rows, 0)
    copies.land(corner)
    out = copies.keep(buf, d_all, local.at[8])
    work(place.chip(3))

    def own(at):
        return mine_at[at.start // LANES]

    def coeffs(rows, at, spot):
        rate = prev[rows, slice(chans + at.start, chans + at.stop)]
        log_a = -8.0 * rate * soft[0:1, own(at)]
        return rate, log_a, jnp.where(spot == 0, 0.0, jnp.exp(log_a))

    carry[0:1] = jnp.zeros_like(carry[0:1])
    carry[1:2] = jnp.ones_like(carry[1:2])

    def scan_back(k, unused):
        r0 = pl.multiple_of((n_tiles - 1 - k) * tile, tile)
        rows = pl.ds(r0, tile)
        spot = places[rows, :]
        last = lax.broadcasted_iota(jnp.int32, spot.shape, 0) == tile - 1
        for at in lanes:
            d_branch = dbv[rows, at]
            if at.start >= bw:
                d_branch = jnp.where(idle_tile, 0.0, d_branch)
            value, slope = yv[rows, at], slv[rows, at]
            state = hs[pl.ds(pl.multiple_of(r0 + 8, 8), tile), at]
            d_state = d_branch * value
            drv[rows, slice(chans + at.start, chans + at.stop)] = (d_branch * state * slope).astype(low)
            _, _, a = coeffs(rows, at, spot)
            a, u = scan_tile(a, a * d_state, True)
            m = u + a * carry[0:1, at]
            q = a * carry[1:2, at]
            ghv[rows, at] = d_state + jnp.where(last, carry[0:1, at], pltpu.roll(m, tile - 1, 0))
            qv[rows, at] = jnp.where(last, carry[1:2, at], pltpu.roll(q, tile - 1, 0))
            carry[0:1, at] = m[0:1]
            carry[1:2, at] = q[0:1]
        return unused

    lax.fori_loop(0, n_tiles, scan_back, 0)
    arriving = copies.start(carry, message, "prev")
    copies.land(arriving)
    sums[...] = jnp.zeros_like(sums)
    gg[...] = jnp.zeros_like(gg)

    def through_gates(k, unused):
        r0 = pl.multiple_of(k * tile, tile)
        rows = pl.ds(r0, tile)
        spot = places[rows, :]
        reset = spot == 0
        for n, at in enumerate(lanes):
            g = ghv[rows, at] + qv[rows, at] * message[0:1, at]
            before = pltpu.roll(hs[pl.ds(r0, tile + 8), at], 1, 0)[8:]
            if at.start < bw:
                c = cv[rows, at].astype(f32)
            else:
                c = jnp.where(
                    high_tile,
                    cv[rows, slice(at.start + LANES, at.stop + LANES)].astype(f32),
                    cv[rows, at].astype(f32),
                )
            gate = prev[rows, at]
            rate, log_a, a = coeffs(rows, at, spot)
            m = jnp.where(reset, 1.0, jnp.sqrt(one_less_exp(2.0 * log_a)))
            gated = gate * m
            d_log = jnp.where(reset, 0.0, g * before * a - g * c * gate * a * a / m)
            d_pre_in = (g * c * gated * (1.0 - gate)).astype(low)
            d_pre_rate = (d_log * (-8.0 * soft[0:1, own(at)]) * rate * (1.0 - rate)).astype(low)
            dpv[rows, at] = d_pre_in
            dpv[rows, slice(chans + at.start, chans + at.stop)] = d_pre_rate
            dcv[rows, at] = g * gated
            sums[0:1, at] += jnp.sum(d_pre_in.astype(f32), axis=0, keepdims=True)
            sums[1:2, at] += jnp.sum(d_pre_rate.astype(f32), axis=0, keepdims=True)
            sums[2:3, at] += jnp.sum(d_log * (-8.0 * rate), axis=0, keepdims=True)
        return unused

    swaps = []
    for h in range(2):
        lax.fori_loop(h * n_tiles // 2, (h + 1) * n_tiles // 2, through_gates, 0)
        rows = pl.ds(h * group // 2, group // 2)
        for j in range(2):
            swaps.append(
                copies.start(
                    dpv.at[rows, pl.ds(j * chans + bw, LANES)],
                    there.at[rows, pl.ds(j * LANES, LANES)],
                    "y",
                )
            )

    def through_blocks(k, unused):
        rows = pl.ds(pl.multiple_of(k * tile, tile), tile)
        c = cv[rows, :]
        d_blk = dcv[rows, :bw]
        d_tile = dcv[rows, bw:]
        for j in range(2):
            p_blk = dpv[rows, slice(j * chans, j * chans + bw)]
            here = dpv[rows, slice(j * chans + bw, (j + 1) * chans)]
            far = there[rows, slice(j * LANES, (j + 1) * LANES)]
            five = jnp.concatenate(
                [jnp.where(high_tile, far, here), jnp.where(high_tile, here, far)], axis=1
            )
            d_blk = d_blk + dot(p_blk, gates[j, place.col], ((1,), (1,)))
            d_tile = d_tile + dot(five, gates[j, n_col, tile_rows, :], ((1,), (1,)))
            gg[j, :, :bw] += dot(c[:, :bw], p_blk, ((0,), (0,)))
            gg[j, :, bw:] += dot(c[:, bw:], here, ((0,), (0,)))
        dcv[rows, :bw] = d_blk
        dcv[rows, bw:] = d_tile
        return unused

    copies.land(swaps[0], swaps[1])
    lax.fori_loop(0, 1, through_blocks, 0)
    later = copies.start(dcv.at[pl.ds(0, 8), :], dcv.at[pl.ds(group, 8), :], "prev")
    lax.fori_loop(1, n_tiles // 2, through_blocks, 0)
    copies.land(swaps[2], swaps[3])
    lax.fori_loop(n_tiles // 2, n_tiles, through_blocks, 0)
    part_rows = gate_out.shape[1]
    for p in range(gate_out.shape[0]):
        j, first_row = divmod(p * part_rows, bw)
        gate_out[p] = gg[j, first_row : first_row + part_rows].astype(low)
    copies.land(later)

    def through_conv(k, unused):
        r0 = pl.multiple_of(k * tile, tile)
        rows = pl.ds(r0, tile)
        ext = pl.ds(r0, tile + 8)
        spot = places[ext, :]
        for at in lanes:
            reach = dcv[ext, at]
            if at.start < bw:
                x = xb[ext, at]
            else:
                x = jnp.where(high_tile, xb[ext, slice(at.start + LANES, at.stop + LANES)], xb[ext, at])
            d_c = reach[:tile]
            d_x = conv_w[0:1, own(at)] * d_c
            sums[3:4, at] += jnp.sum(d_c * x[8:], axis=0, keepdims=True)
            for t in range(1, conv_w.shape[0]):
                term = jnp.where(spot >= t, conv_w[t : t + 1, own(at)] * reach, 0.0)
                d_x = d_x + pltpu.roll(term, tile + 8 - t, 0)[:tile]
                lagged = pltpu.roll(x, t, 0)[8:]
                here = jnp.where(spot[:tile] >= t, d_c * lagged, 0.0)
                sums[3 + t : 4 + t, at] += jnp.sum(here, axis=0, keepdims=True)
            sums[7:8, at] += jnp.sum(d_c, axis=0, keepdims=True)
            drv[rows, at] = d_x.astype(low)
        return unused

    lax.fori_loop(0, n_tiles, through_conv, 0)
    for at in lanes:
        sums[2:3, at] = sums[2:3, at] * soft[1:2, own(at)]
    out_rec = copies.keep(drv, d_rec_out, local.at[9])
    copies.finish()
    out.wait()
    out_rec.wait()
    stay.finish()


def rec_backward(d_out, w_out, kept, gates, soft, conv_w, places, down, geo, n_dp):
    n_col, part, bw, tiles, wide = geo
    own, width = d_out.shape
    slots = 2 * n_col
    group, chans = slots * own, bw + LANES
    part_rows = 2 * bw // n_dp
    d_all, d_rec, gate_grads, sums, down_dealt = pl.pallas_call(
        functools.partial(backward_kernel, geo),
        out_shape=(
            jax.ShapeDtypeStruct((slots, own, width), low),
            jax.ShapeDtypeStruct((group, 2 * chans), low),
            jax.ShapeDtypeStruct((n_dp, part_rows, chans), low),
            jax.ShapeDtypeStruct((8, chans), f32),
            jax.ShapeDtypeStruct(down.shape, low),
        ),
        in_specs=[anywhere] * 8 + [in_vmem] * 4 + [anywhere],
        out_specs=(anywhere, anywhere, in_vmem, in_vmem, anywhere),
        scratch_shapes=[
            pltpu.VMEM((slots, own, width), low),
            pltpu.VMEM(w_out.shape, low),
            pltpu.VMEM((group, chans), f32),
            pltpu.VMEM((group, chans), f32),
            pltpu.VMEM((group, chans), f32),
            pltpu.VMEM((group + 8, chans), f32),
            pltpu.VMEM((group, 2 * chans), f32),
            pltpu.VMEM((group, 2 * bw), low),
            pltpu.VMEM((group + 8, 2 * bw), f32),
            pltpu.VMEM((group, chans), f32),
            pltpu.VMEM((group, chans), f32),
            pltpu.VMEM((group, 2 * chans), low),
            pltpu.VMEM((group, 2 * LANES), low),
            pltpu.VMEM((group + 8, chans), f32),
            pltpu.VMEM((group, 2 * chans), low),
            pltpu.VMEM((2, bw, chans), f32),
            pltpu.VMEM((8, chans), f32),
            pltpu.VMEM((8, chans), f32),
            pltpu.VMEM(down.shape[1:], low),
            pltpu.SemaphoreType.DMA((22,)),
            pltpu.SemaphoreType.DMA((22,)),
            pltpu.SemaphoreType.DMA((10,)),
            pltpu.SemaphoreType.DMA((1,)),
        ],
        compiler_params=pltpu.CompilerParams(
            collective_id=4, has_side_effects=True, vmem_limit_bytes=60 * MIB
        ),
        name="rec_backward",
    )(d_out, w_out, *kept, gates, soft, conv_w, places, down)
    return d_all.reshape(group, width), d_rec, gate_grads, sums, down_dealt


def outer_kernel(n_dp, first_steps, left1, right1, left2, right2, out_ref):
    def multiply(left, right):
        total = dot(left[...], right[...], ((0,), (0,)))
        rows = total.shape[0] // n_dp
        for k in range(n_dp):
            out_ref[k, 0] = total[k * rows : (k + 1) * rows].astype(out_ref.dtype)

    j = pl.program_id(1)

    @pl.when(j < first_steps)
    def _():
        multiply(left1, right1)

    @pl.when(j >= first_steps)
    def _():
        multiply(left2, right2)


def outer_one_kernel(n_dp, left, right, out_ref):
    total = dot(left[...], right[...], ((0,), (0,)))
    rows = total.shape[0] // n_dp
    for k in range(n_dp):
        out_ref[k, 0] = total[k * rows : (k + 1) * rows].astype(out_ref.dtype)


def outer(left, right, n_dp, n_col, columns, name):
    length, width = left.shape
    part = width // n_col
    count = right.shape[1]
    return pl.pallas_call(
        functools.partial(outer_one_kernel, n_dp),
        grid=(n_col, count // columns),
        out_shape=jax.ShapeDtypeStruct((n_dp, n_col, part // n_dp, count), low),
        in_specs=[
            pl.BlockSpec((length, part), lambda i, j: (0, i)),
            pl.BlockSpec((length, columns), lambda i, j: (0, j)),
        ],
        out_specs=pl.BlockSpec((n_dp, 1, part // n_dp, columns), lambda i, j: (0, i, 0, j)),
        compiler_params=pltpu.CompilerParams(vmem_limit_bytes=48 * MIB),
        cost_estimate=pl.CostEstimate(
            flops=2 * length * width * count,
            bytes_accessed=2 * (length * width + length * count + width * count),
            transcendentals=0,
        ),
        name=name,
    )(left, right)


def outer_pair(left1, right1, left2, right2, n_dp, n_col, columns, name):
    length, width = left1.shape
    part = width // n_col
    steps1, steps2 = right1.shape[1] // columns, right2.shape[1] // columns
    count = (steps1 + steps2) * columns
    left_block = pl.BlockSpec((length, part), lambda i, j: (0, i))
    return pl.pallas_call(
        functools.partial(outer_kernel, n_dp, steps1),
        grid=(n_col, steps1 + steps2),
        out_shape=jax.ShapeDtypeStruct((n_dp, n_col, part // n_dp, count), low),
        in_specs=[
            left_block,
            pl.BlockSpec((length, columns), lambda i, j: (0, jnp.minimum(j, steps1 - 1))),
            left_block,
            pl.BlockSpec((length, columns), lambda i, j: (0, jnp.maximum(j - steps1, 0))),
        ],
        out_specs=pl.BlockSpec((n_dp, 1, part // n_dp, columns), lambda i, j: (0, i, 0, j)),
        compiler_params=pltpu.CompilerParams(vmem_limit_bytes=48 * MIB),
        cost_estimate=pl.CostEstimate(
            flops=2 * length * width * count,
            bytes_accessed=2 * (2 * length * width + length * count + width * count),
            transcendentals=0,
        ),
        name=name,
    )(left1, right1, left2, right2)


def dot(a, b, dims=((1,), (0,))):
    return lax.dot_general(a, b, (dims, ((), ())), preferred_element_type=f32)


def places_of(rows, lengths):
    ends = jnp.cumsum(lengths)
    starts = ends - lengths
    inside = (rows[:, None] >= starts[None, :]) & (rows[:, None] < ends[None, :])
    places = rows - jnp.sum(jnp.where(inside, starts[None, :], 0), axis=1)
    return jnp.where(jnp.any(inside, axis=1), places, 0)


def body(
    tokens,
    cotangent,
    rec_in,
    rec_out,
    gates,
    gate_bias,
    decay,
    conv_w,
    conv_b,
    gains,
    mlp_in,
    mlp_out,
    lengths,
    order,
):
    n_dp, n_row, n_col = (lax.axis_size(a) for a in ("dp", "row", "col"))
    dp, row, col = (lax.axis_index(a) for a in ("dp", "row", "col"))
    given, part = tokens.shape
    own = given // n_col
    group = given * n_row
    width = part * n_col
    taps = conv_w.shape[0]
    blocks, bw = gates.shape[1], gates.shape[2]
    half = rec_out.shape[0]
    hidden_half = mlp_out.shape[0]
    tiles = hidden_half // LANES
    wide = -(-tiles // n_col)
    span = wide * LANES
    shared = n_col * bw
    chans = bw + LANES

    geo = (n_col, part, bw, tiles, wide)
    x_all, w_rec, gains_all = open_gather(tokens, rec_in, gains, geo)
    base = dp * group
    places = places_of(base + jnp.arange(group + 8, dtype=jnp.int32), lengths)
    places = jnp.broadcast_to(places[:, None], (group + 8, LANES))
    soft = jnp.stack([jax.nn.softplus(decay), jax.nn.sigmoid(decay)])

    n1, x_rows, y_branch, pre_both, conv_low, state, branch, first, g_all, w_out, w_in, w_down = rec_forward(
        x_all,
        w_rec,
        (gains_all, gates, gate_bias, soft, conv_w, conv_b[None, :]),
        places,
        cotangent,
        rec_out,
        mlp_in,
        mlp_out,
        geo,
    )
    rows_f, rows_b = ((own, width), f32), ((own, width), low)
    line, squares = ((8, width), f32), ((8, LANES), f32)
    resid, normed_two, squares_one = multiply_scatter(
        branch, w_out, False, 6, "out_one", after_out_one, (x_all, gains_all), (rows_f, rows_b, squares)
    )

    def spare(at):
        return spare_window(at, tiles, n_col, wide)

    n2, hidden, d_glu = glu(normed_two, w_in, w_down, g_all, spare)
    g_down = outer(g_all, hidden, n_dp, n_col, span, "outer_down")
    d_glu, hidden, g_down = lax.optimization_barrier((d_glu, hidden, g_down))
    sum_down = lax.psum_scatter(g_down, "dp", scatter_dimension=0)
    g_in = outer(n2, d_glu, n_dp, n_col, span, "outer_in")
    d_glu, g_in = lax.optimization_barrier((d_glu, g_in))
    d_resid, d_out, gain_two = multiply_scatter(
        d_glu,
        w_in,
        True,
        7,
        "d_normed_two",
        after_normed_two,
        (resid, g_all, gains_all),
        (rows_f, rows_b, line),
    )
    g_in, sum_down, d_out = lax.optimization_barrier((g_in, sum_down, d_out))
    sum_in = lax.psum_scatter(g_in, "dp", scatter_dimension=0)

    d_out_all, d_rec, gate_grads, small, down = rec_backward(
        d_out,
        w_out,
        (y_branch, state, first, pre_both, conv_low, x_rows),
        gates,
        soft,
        conv_w,
        places,
        sum_down,
        geo,
        n_dp,
    )

    def pick(at):
        tile = pl.multiple_of(bw + lax.div(at, 2) * LANES, LANES)
        return ((0, 0, bw), (tile, bw, LANES), (2 * bw, chans, chans))

    g_rec = outer_pair(n1, d_rec, d_out_all, branch, n_dp, n_col, chans, "outer_rec")
    g_rec, d_rec = lax.optimization_barrier((g_rec, d_rec))
    grad_rows, gain_one, squares_x, gate_part, small = multiply_scatter(
        d_rec,
        w_rec,
        True,
        9,
        "d_normed_one",
        after_normed_one,
        (x_all, d_resid, gains_all),
        (rows_b, line, squares),
        pick=pick,
        beside=GateReduce(gate_grads, small),
    )
    grad_input = take_home(grad_rows, n_col)
    g_rec, sum_in, grad_input, hidden = lax.optimization_barrier((g_rec, sum_in, grad_input, hidden))
    sum_rec = lax.psum_scatter(g_rec, "dp", scatter_dimension=0)
    result_rows, squares_two, gate_planes, into = multiply_scatter(
        hidden,
        w_down,
        False,
        8,
        "out_two",
        after_out_two,
        (resid,),
        (rows_b, squares),
        beside=GateGather(gate_part, sum_in, n_dp),
    )

    def windows(got, first):
        return [
            got[c][..., first + (LANES if c > n_col - 1 - (wide * n_col - tiles) else 0) : first + span]
            for c in range(n_col)
        ]

    def channels_of(got, first):
        return [got[c][..., first : first + bw] for c in range(n_col)] + [
            got[c][..., first + bw : first + chans] for c in range(0, n_col, 2)
        ]

    grad_gains, square_sums, chan_sums, gate_parts, result = sum_everywhere(
        gain_one,
        gain_two,
        (squares_x, squares_one, squares_two),
        small,
        gate_planes,
        result_rows,
        n_dp,
        n_col,
    )
    grad_mlp_in = jnp.stack(
        [jnp.concatenate(windows(into[..., j * span : (j + 1) * span], 0), axis=-1) for j in range(2)]
    ).astype(f32)
    grad_mlp_out = jnp.concatenate(windows(down, 0), axis=-1).astype(f32).T
    sum_rec, grad_mlp_in, grad_mlp_out = lax.optimization_barrier((sum_rec, grad_mlp_in, grad_mlp_out))
    recs = deal_back(sum_rec, 10, "deal_rec")
    grad_rec_in = jnp.stack(
        [jnp.concatenate(channels_of(recs, j * chans), axis=-1) for j in range(2)]
    ).astype(f32)
    grad_rec_out = jnp.concatenate(channels_of(recs, 2 * chans), axis=-1).astype(f32).T
    mine = jnp.concatenate(channels_of(chan_sums, 0), axis=-1)
    stats = jnp.sqrt(square_sums[:4, 0] / (n_dp * group * width))
    gate_parts = gate_parts.reshape(n_col, 2, bw, chans).astype(f32)
    five = jnp.concatenate([gate_parts[c, :, :, bw:] for c in range(0, n_col, 2)], axis=-1)
    grad_gates = jnp.stack([gate_parts[c, :, :, :bw] for c in range(n_col)] + [five], axis=1)
    return (
        result,
        grad_input,
        grad_rec_in,
        grad_rec_out,
        grad_gates,
        mine[0:2],
        mine[2],
        mine[3 : 3 + taps],
        mine[3 + taps],
        grad_gains,
        grad_mlp_in,
        grad_mlp_out,
        stats,
    )


def solution(mesh):
    placed = (
        P(("dp", "row"), "col"),
        P(("dp", "row"), "col"),
        P(None, "col", "row"),
        P("row", "col"),
        P(None, "row", None, None),
        P(None, "row"),
        P("row"),
        P(None, "row"),
        P("row"),
        P(None, "col"),
        P(None, "col", "row"),
        P("row", "col"),
        P(),
        P(),
    )
    return jax.shard_map(
        body,
        mesh=mesh,
        in_specs=placed,
        out_specs=(
            P(("dp", "row"), "col"),
            P(("dp", "row"), "col"),
            P(None, ("col", "dp"), "row"),
            P("row", ("col", "dp")),
            P(None, "row", None, None),
            P(None, "row"),
            P("row"),
            P(None, "row"),
            P("row"),
            P(None, "col"),
            P(None, ("col", "dp"), "row"),
            P("row", ("col", "dp")),
            P(),
        ),
        check_vma=False,
    )
```

```python
import functools

import jax
import jax.numpy as jnp
from jax import lax
from jax.experimental import pallas as pl
from jax.experimental.pallas import tpu as pltpu
from jax.sharding import PartitionSpec as P

epsilon = 1e-06
LANES = 128
ROWS = 16
MIB = 1024 * 1024
MESH = pl.DeviceIdType.MESH
low = jnp.bfloat16
f32 = jnp.float32
anywhere = pl.BlockSpec(memory_space=pl.ANY)
in_vmem = pl.BlockSpec(memory_space=pltpu.VMEM)


def window_tile(col, tiles, n_col, wide):
    spare = wide * n_col - tiles
    return col * wide - jnp.maximum(col - (n_col - 1 - spare), 0)


def spare_window(col, tiles, n_col, wide):
    spare = wide * n_col - tiles
    return col > n_col - 1 - spare


class Place:
    def __init__(self):
        self.dp, self.row, self.col = (lax.axis_index(a) for a in ("dp", "row", "col"))

    def chip(self, k):
        return jnp.bitwise_xor(self.col, k)

    def device(self, name):
        if name == "core":
            return {"row": 1 - self.row}
        if name == "z":
            return {"dp": jnp.bitwise_xor(self.dp, 1)}
        if name in ("next", "prev"):
            n_dp = lax.axis_size("dp")
            return {"dp": lax.rem(self.dp + (1 if name == "next" else n_dp - 1), n_dp)}
        if name[0] == "d":
            return {"dp": jnp.bitwise_xor(self.dp, int(name[1:]))}
        if name[0] == "c":
            return {"row": 1 - self.row, "col": self.chip({"x": 1, "y": 2, "xy": 3}[name[1:]])}
        return {"col": self.chip({"x": 1, "y": 2, "xy": 3}[name])}

    def meet(self, names):
        barrier = pltpu.get_barrier_semaphore()
        for name in names:
            pl.semaphore_signal(
                barrier, inc=1, device_id=self.device(name), device_id_type=MESH
            )
        pl.semaphore_wait(barrier, len(names))


class Copies:
    def __init__(self, place, send, recv):
        self.place, self.send, self.recv = place, send, recv
        self.made, self.landed, self.left, self.local = [], set(), set(), []

    def start(self, src, dst, to):
        i = len(self.made)
        copy = pltpu.make_async_remote_copy(
            src_ref=src,
            dst_ref=dst,
            send_sem=self.send.at[i],
            recv_sem=self.recv.at[i],
            device_id=self.place.device(to),
            device_id_type=MESH,
        )
        copy.start()
        self.made.append(copy)
        return i

    def land(self, *numbers):
        for i in numbers:
            if i not in self.landed:
                self.made[i].wait_recv()
                self.landed.add(i)

    def leave(self, *numbers):
        for i in numbers:
            if i not in self.left:
                self.made[i].wait_send()
                self.left.add(i)

    def keep(self, src, dst, sem):
        copy = pltpu.make_async_copy(src, dst, sem)
        copy.start()
        self.local.append(copy)
        return copy

    def finish(self):
        self.land(*range(len(self.made)))
        self.leave(*range(len(self.made)))


def share(rows, far_part):
    far = rows * far_part // 20 // ROWS * ROWS
    return rows - far, far


class Dealer:
    def __init__(self, copies, far_part):
        self.copies, self.far_part = copies, far_part
        self.waiting = []

    def deal(self, piece):
        place = self.copies.place
        odd = lax.rem(place.dp, 2)
        batch = []
        for name, k in (("x", 1), ("y", 2), ("xy", 3)):
            src, dst, rows = piece(place.chip(k), place.col)
            near, far = share(rows, self.far_part)
            start = pl.multiple_of(odd * far, ROWS)
            at = pl.ds(start, near)
            number = self.copies.start(src(at), dst(at), name)
            batch.append((k, number, piece))
        self.waiting.append(batch)

    def forward(self):
        place = self.copies.place
        odd = lax.rem(place.dp, 2)
        for k, number, piece in self.waiting.pop(0):
            self.copies.land(number)
            _, dst, rows = piece(place.col, place.chip(k))
            near, far = share(rows, self.far_part)
            at = pl.ds(pl.multiple_of(odd * near, ROWS), far)
            self.copies.start(dst(at), dst(at), "z")


def rows_of(ref, first, rows, lead=None, columns=None):
    def view(at):
        where = pl.ds(pl.multiple_of(first + at.start, ROWS), at.size)
        index = (where, columns if columns is not None else slice(None))
        return ref.at[index] if lead is None else ref.at[(lead,) + index]

    return view


def weight_pieces(geo, refs, outs):
    n_col, part, bw, tiles, wide = geo
    shared, span = n_col * bw, wide * LANES
    rec_in, rec_out, mlp_in, mlp_out = refs
    w_rec, w_out, w_in, w_down = outs

    def here(chip):
        return pl.multiple_of(chip * part, LANES)

    def blk(chip):
        return pl.multiple_of(chip * bw, LANES)

    def tile(chip):
        return pl.multiple_of(shared + lax.div(chip, 2) * LANES, LANES)

    def win(chip):
        return pl.multiple_of(window_tile(chip, tiles, n_col, wide) * LANES, LANES)

    def in_piece(ref, j, out, lead, source_at, size, column):
        def piece(dest, source):
            return (
                rows_of(ref, 0, part, j, pl.ds(pl.multiple_of(source_at(dest), LANES), size)),
                rows_of(out, here(source), part, lead, pl.ds(column, size)),
                part,
            )

        return piece

    def down_piece(ref, out, source_at, size, row):
        def piece(dest, source):
            return (
                rows_of(ref, source_at(dest), size),
                rows_of(out, row, size, None, pl.ds(here(source), part)),
                size,
            )

        return piece

    found = {}
    if rec_in is not None:
        found["rec_in"] = [
            in_piece(rec_in, 0, w_rec, None, blk, bw, 0),
            in_piece(rec_in, 0, w_rec, None, lambda chip: shared, bw, bw),
            in_piece(rec_in, 1, w_rec, None, blk, bw, 2 * bw),
            in_piece(rec_in, 1, w_rec, None, tile, LANES, 3 * bw),
        ]
    if rec_out is not None:
        found["rec_out"] = [
            down_piece(rec_out, w_out, blk, bw, 0),
            down_piece(rec_out, w_out, tile, LANES, bw),
        ]
    if mlp_in is not None:
        half = span // 2
        found["mlp_in"] = [
            in_piece(mlp_in, j, w_in, j, lambda chip, h=h: win(chip) + h * half, half, h * half)
            for j in range(2)
            for h in range(2)
        ]
    if mlp_out is not None:
        half = span // 2
        found["mlp_out"] = [
            down_piece(mlp_out, w_down, lambda chip, h=h: win(chip) + h * half, half, h * half)
            for h in range(2)
        ]
    return found


def own_pieces(place, pieces):
    pairs = []
    for piece in pieces:
        src, dst, rows = piece(place.col, place.col)
        pairs.append((src(pl.ds(0, rows)), dst(pl.ds(0, rows))))
    return pairs


class Stay:
    def __init__(self, pairs, bufs, sems):
        self.pairs, self.bufs, self.sems = pairs, bufs, sems
        self.loads = [
            pltpu.make_async_copy(src, buf, sems.at[i])
            for i, ((src, _), buf) in enumerate(zip(pairs, bufs))
        ]
        for load in self.loads:
            load.start()

    def turn(self):
        for load in self.loads:
            load.wait()
        self.stores = [
            pltpu.make_async_copy(buf, dst, self.sems.at[i])
            for i, ((_, dst), buf) in enumerate(zip(self.pairs, self.bufs))
        ]
        for store in self.stores:
            store.start()

    def finish(self):
        for store in self.stores:
            store.wait()


class Gather:
    def __init__(self, copies, mine, at):
        self.copies, self.at = copies, at
        place = copies.place
        row, col = place.row, place.col
        self.first = [
            copies.start(mine(half), at(row, col, half), name)
            for half in (0, 1)
            for name in ("x", "y")
        ]
        self.own = copies.start(mine(None), at(row, col, None), "core")
        self.rounds = []

    def pass_half(self, half):
        copies, place = self.copies, self.copies.place
        views = [self.at(place.row, place.chip(k), half) for k in (1, 2)]
        x, y = self.first[2 * half], self.first[2 * half + 1]
        if half == 0:
            copies.land(x)
            round_ = copies.start(views[0], views[0], "y")
            core_x = copies.start(views[0], views[0], "core")
            copies.land(y)
            core_y = copies.start(views[1], views[1], "core")
        else:
            copies.land(y)
            round_ = copies.start(views[1], views[1], "x")
            core_y = copies.start(views[1], views[1], "core")
            copies.land(x)
            core_x = copies.start(views[0], views[0], "core")
        self.rounds.append(round_)
        return core_x, core_y

    def pass_on(self):
        return self.pass_half(0) + self.pass_half(1)

    def last(self):
        copies, place = self.copies, self.copies.place
        corner = self.at(place.row, place.chip(3), None)
        copies.land(*self.rounds)
        return copies.start(corner, corner, "core")


def block_view(source, target, row, col, half):
    rows, part = source.shape
    cut = rows // 2
    first = row * rows + (0 if half is None else half * cut)
    size = rows if half is None else cut
    return target.at[
        pl.ds(pl.multiple_of(first, ROWS), size), pl.ds(pl.multiple_of(col * part, LANES), part)
    ]


def block_gather(copies, source, target):
    cut = source.shape[0] // 2

    def mine(half):
        return source if half is None else source.at[pl.ds(half * cut, cut), :]

    return Gather(copies, mine, functools.partial(block_view, source, target))


AROUND = ("x", "y", "xy", "core", "z")


def open_kernel(geo, tokens, rec_in, gains, x_all, w_rec, gains_all, send, recv, local, *bufs):
    place = Place()
    place.meet(AROUND)
    copies = Copies(place, send, recv)
    pieces = weight_pieces(geo, (rec_in, None, None, None), (w_rec, None, None, None))["rec_in"]
    dealer = Dealer(copies, 10)
    dealer.deal(pieces[0])
    dealer.deal(pieces[1])
    gather = block_gather(copies, tokens, x_all)
    own_block = (tokens, block_view(tokens, x_all, place.row, place.col, None))
    dealer.deal(pieces[2])
    dealer.deal(pieces[3])
    mine = gains_all.at[:, pl.ds(pl.multiple_of(place.col * geo[1], LANES), geo[1])]
    for name in ("x", "y", "xy"):
        copies.start(gains, mine, name)
    stay = Stay([own_block] + own_pieces(place, pieces) + [(gains, mine)], bufs, local)
    stay.turn()
    dealer.forward()
    dealer.forward()
    gather.pass_on()
    dealer.forward()
    dealer.forward()
    gather.last()
    copies.finish()
    stay.finish()


def open_gather(tokens, rec_in, gains, geo):
    n_col, part, bw, tiles, wide = geo
    width = part * n_col
    return pl.pallas_call(
        functools.partial(open_kernel, geo),
        out_shape=(
            jax.ShapeDtypeStruct((2 * tokens.shape[0], width), low),
            jax.ShapeDtypeStruct((width, 3 * bw + LANES), low),
            jax.ShapeDtypeStruct((gains.shape[0], width), f32),
        ),
        in_specs=[anywhere] * 3,
        out_specs=(anywhere,) * 3,
        scratch_shapes=[
            pltpu.SemaphoreType.DMA((39,)),
            pltpu.SemaphoreType.DMA((39,)),
            pltpu.SemaphoreType.DMA((6,)),
            pltpu.VMEM(tokens.shape, low),
            pltpu.VMEM((part, bw), low),
            pltpu.VMEM((part, bw), low),
            pltpu.VMEM((part, bw), low),
            pltpu.VMEM((part, LANES), low),
            pltpu.VMEM(gains.shape, f32),
        ],
        compiler_params=pltpu.CompilerParams(collective_id=1, has_side_effects=True),
        name="open_gather",
    )(tokens, rec_in, gains)


def slot_gather(copies, local_ref, buf, own):
    cut = own // 2
    n_col = buf.shape[0] // 2

    def at(row, col, half):
        slot = buf.at[row * n_col + col]
        return slot if half is None else slot.at[pl.ds(half * cut, cut), :]

    def mine(half):
        return local_ref if half is None else local_ref.at[pl.ds(half * cut, cut), :]

    return Gather(copies, mine, at)


def tanh_parts(x):
    k = 0.7978845608028654
    square = x * x
    t = jnp.tanh(k * x * (1.0 + 0.044715 * square))
    value = 0.5 * x * (1.0 + t)
    slope = 0.5 * (1.0 + t) + 0.5 * x * (1.0 - t * t) * k * (1.0 + 3 * 0.044715 * square)
    return value, slope


def glu_kernel(
    spare, n2, w_in, w_down, g_all, n2_all, hidden, d_glu, buf, wi, wd, g, hid, dgl, send, recv, local, out_sems
):
    place = Place()
    place.meet(("x", "y", "core"))
    copies = Copies(place, send, recv)
    own, width = n2.shape
    n_col = buf.shape[0] // 2
    span = wd.shape[0]
    step = 512
    gather = slot_gather(copies, n2, buf, own)
    me = place.row * n_col + place.col
    n_steps = span // step
    near_slots = [place.col, n_col + place.col]
    far_slots = [r * n_col + place.chip(k) for k in (1, 2, 3) for r in (0, 1)]

    def load_rows(slot, i):
        rows = pl.ds(pl.multiple_of(slot * own, ROWS), own)
        return copies.keep(g_all.at[rows, :], g.at[rows, :], local.at[i])

    first = [copies.keep(n2, buf.at[me], local.at[3])]
    first += [load_rows(slot, 4 + i) for i, slot in enumerate(near_slots)]
    weights = []
    for i in range(n_steps):
        at = pl.ds(i * step, step)
        weights.append(
            (
                copies.keep(w_in.at[:, :, at], wi.at[:, :, at], local.at[12 + 2 * i]),
                copies.keep(w_down.at[at, :], wd.at[at, :], local.at[13 + 2 * i]),
            )
        )
    others = [load_rows(slot, 6 + i) for i, slot in enumerate(far_slots)]
    for load in first:
        load.wait()
    hide = spare(place.col)

    def work(slots, first, size, lo, hi):
        rows = [pl.ds(pl.multiple_of(s * own + first, ROWS), size) for s in slots]
        n2_here = jnp.concatenate([buf[s, first : first + size, :] for s in slots], axis=0)
        g_here = jnp.concatenate([g[r, :] for r in rows], axis=0)

        def columns(i, carry):
            at = pl.ds(pl.multiple_of(i * step, LANES), step)
            up_at = pl.ds(pl.multiple_of(span + i * step, LANES), step)
            gate = dot(n2_here, wi[0, :, at])
            up = dot(n2_here, wi[1, :, at])
            d_hid = dot(g_here, wd[at, :], ((1,), (1,)))
            lane = lax.broadcasted_iota(jnp.int32, gate.shape, 1) + i * step
            used = (lane >= LANES) | jnp.logical_not(hide)
            up = jnp.where(used, up, 0.0)
            d_hid = jnp.where(used, d_hid, 0.0)
            value, slope = tanh_parts(gate)
            h = (value * up).astype(low)
            dg = (d_hid * up * slope).astype(low)
            du = (d_hid * value).astype(low)
            for n, r in enumerate(rows):
                part = slice(n * size, (n + 1) * size)
                hid[r, at] = h[part]
                dgl[r, at] = dg[part]
                dgl[r, up_at] = du[part]
            return carry

        lax.fori_loop(lo, hi, columns, 0)

    def both_cores(*chips):
        return [s for chip in chips for s in (chip, n_col + chip)]

    half = own // 2
    near = both_cores(place.chip(1), place.chip(2))
    copies.land(gather.own)
    for i in range(n_steps):
        for load in weights[i]:
            load.wait()
        work(both_cores(place.col), 0, own, i, i + 1)
    for load in others:
        load.wait()
    core0 = gather.pass_half(0)
    copies.land(*core0)
    work(near, 0, half, 0, n_steps // 2)
    core1 = gather.pass_half(1)
    work(near, 0, half, n_steps // 2, n_steps)
    copies.land(*core1)
    work(near, half, half, 0, n_steps // 2)
    corner = gather.last()
    work(near, half, half, n_steps // 2, n_steps)
    copies.land(corner)
    out_n2 = copies.keep(buf, n2_all, local.at[0])
    written = [out_n2]

    def write(slots):
        for slot in slots:
            rows = pl.ds(pl.multiple_of(slot * own, ROWS), own)
            for src, dst in ((hid, hidden), (dgl, d_glu)):
                written.append(copies.keep(src.at[rows, :], dst.at[rows, :], out_sems.at[len(written) - 1]))

    write(both_cores(place.col) + near)
    work(both_cores(place.chip(3)), 0, own, 0, n_steps)
    write(both_cores(place.chip(3)))
    copies.finish()
    for copy in written:
        copy.wait()


def glu(n2, w_in, w_down, g_all, spare):
    own, width = n2.shape
    group = g_all.shape[0]
    span = w_down.shape[0]
    n_all, h, d = pl.pallas_call(
        functools.partial(glu_kernel, spare),
        out_shape=(
            jax.ShapeDtypeStruct((group // own, own, width), low),
            jax.ShapeDtypeStruct((group, span), low),
            jax.ShapeDtypeStruct((group, 2 * span), low),
        ),
        in_specs=[anywhere] * 4,
        out_specs=(anywhere,) * 3,
        scratch_shapes=[
            pltpu.VMEM((group // own, own, width), low),
            pltpu.VMEM(w_in.shape, low),
            pltpu.VMEM(w_down.shape, low),
            pltpu.VMEM((group, width), low),
            pltpu.VMEM((group, span), low),
            pltpu.VMEM((group, 2 * span), low),
            pltpu.SemaphoreType.DMA((12,)),
            pltpu.SemaphoreType.DMA((12,)),
            pltpu.SemaphoreType.DMA((12 + 2 * (span // 256),)),
            pltpu.SemaphoreType.DMA((2 * (group // own),)),
        ],
        compiler_params=pltpu.CompilerParams(
            collective_id=3, has_side_effects=True, vmem_limit_bytes=58 * MIB
        ),
        cost_estimate=pl.CostEstimate(
            flops=6 * group * width * span, bytes_accessed=60 * MIB, transcendentals=group * span
        ),
        name="glu",
    )(n2, w_in, w_down, g_all)
    return n_all.reshape(group, width), h, d


def start_home(copies, source, home, buf, sem):
    place = copies.place
    own, part = source.shape[0], home.shape[1]
    spot = home.at[pl.ds(pl.multiple_of(place.col * own, ROWS), own), :]

    def columns_of(chip):
        return source.at[:, pl.ds(pl.multiple_of(chip * part, LANES), part)]

    for name, j in (("xy", 3), ("x", 1), ("y", 2)):
        copies.start(columns_of(place.chip(j)), spot, name)
    return Stay([(columns_of(place.col), spot)], [buf], sem)


def scatter_kernel(shape, finish, n_more, n_outs, pick, beside, act, w, *refs):
    n_parts, across, own, width = shape
    side = []
    if beside is not None:
        n_in, n_out, n_hold = beside.counts
        side, refs = list(refs[:n_in]), refs[n_in:]
    more, refs = refs[:n_more], refs[n_more:]
    outs, refs = refs[:n_outs], refs[n_outs:]
    if beside is not None:
        side += refs[:n_out]
        side += refs[len(refs) - n_hold :]
        refs = refs[n_out : len(refs) - n_hold]
    actv, wv, other, mine, from_core, from_x, from_y, turn, fin, send, recv, local = refs[:12]
    held = refs[12 : 12 + n_more]
    place = Place()
    place.meet(["x", "y", "core"] + ([] if beside is None else beside.names()))
    copies = Copies(place, send, recv)
    if beside is not None:
        beside.start(copies, *side)
    cut = own // 2
    n_col = act.shape[0] // own // 2
    k = act.shape[1] // n_parts
    step = 512
    loads = [copies.keep(act, actv, local.at[0])]
    if pick is None:
        loads.append(copies.keep(w, wv, local.at[1]))
    else:
        for i, (src, dst, size) in enumerate(pick(place.col)):
            loads.append(
                copies.keep(w.at[:, pl.ds(src, size)], wv.at[:, pl.ds(dst, size)], local.at[1 + i])
            )
    my_rows = pl.ds(pl.multiple_of((place.row * n_col + place.col) * own, ROWS), own)
    extra = []
    for i, (ref, buf) in enumerate(zip(more, held)):
        src = ref.at[my_rows, :] if ref.shape[0] > own else ref
        extra.append(copies.keep(src, buf, local.at[4 + i]))
    for load in loads:
        load.wait()
    top, bottom = pl.ds(0, cut), pl.ds(cut, cut)

    def work(j):
        chip = place.chip(j)
        slots = ((1 - place.row) * n_col + chip, place.row * n_col + chip)
        left = [
            jnp.concatenate(
                [
                    actv[pl.ds(pl.multiple_of(s * own, ROWS), own), n * k : (n + 1) * k]
                    for s in slots
                ],
                axis=0,
            )
            for n in range(n_parts)
        ]

        def columns(i, carry):
            at = pl.ds(pl.multiple_of(i * step, LANES), step)
            total = None
            for n in range(n_parts):
                if across:
                    right = wv[n, at, :] if n_parts > 1 else wv[at, :]
                    term = dot(left[n], right, ((1,), (1,)))
                else:
                    term = dot(left[n], wv[:, at])
                total = term if total is None else total + term
            other[j, :, at] = total[:own].astype(low)
            mine[j, :, at] = total[own:]
            return carry

        lax.fori_loop(0, width // step, columns, 0)
        return copies.start(other.at[j], from_core.at[j], "core")

    def add_core(j, number):
        copies.land(number)
        mine[j] = mine[j] + from_core[j].astype(f32)
        turn[j] = mine[j].astype(low)

    if beside is not None:
        beside.turn()
    core3 = work(3)
    core1 = work(1)
    add_core(3, core3)
    x3 = copies.start(turn.at[3, top, :], from_x.at[0], "x")
    y3 = copies.start(turn.at[3, bottom, :], from_y.at[0], "y")
    core2 = work(2)
    add_core(1, core1)
    x1 = copies.start(turn.at[1, top, :], from_x.at[1], "x")
    core0 = work(0)
    add_core(2, core2)
    y2 = copies.start(turn.at[2, bottom, :], from_y.at[1], "y")
    copies.land(x3)
    turn[2, top, :] = (mine[2, top, :] + from_x[0].astype(f32)).astype(low)
    y_last = copies.start(turn.at[2, top, :], from_y.at[2], "y")
    copies.land(y3)
    turn[1, bottom, :] = (mine[1, bottom, :] + from_y[0].astype(f32)).astype(low)
    x_last = copies.start(turn.at[1, bottom, :], from_x.at[2], "x")
    add_core(0, core0)
    copies.land(x1, y2, y_last, x_last)
    fin[top, :] = mine[0, top, :] + from_x[1].astype(f32) + from_y[2].astype(f32)
    fin[bottom, :] = mine[0, bottom, :] + from_y[1].astype(f32) + from_x[2].astype(f32)
    for load in extra:
        load.wait()
    for ref in outs:
        if ref.shape[0] == 8:
            ref[...] = jnp.zeros_like(ref)
    rows_at_once = 64

    def rows_done(i, carry):
        rows = pl.ds(pl.multiple_of(i * rows_at_once, rows_at_once), rows_at_once)
        finish(rows, fin, held, outs)
        return carry

    lax.fori_loop(0, own // rows_at_once, rows_done, 0)
    if beside is not None:
        beside.finish(copies, *side)
    copies.finish()


def multiply_scatter(act, w, across, number, name, finish, more, outs, pick=None, beside=None):
    n_parts = w.shape[0] if w.ndim == 3 else 1
    group = act.shape[0]
    n_col = lax.axis_size("col")
    own = group // (2 * n_col)
    width = w.shape[-2] if across else w.shape[-1]
    held = [((own, r.shape[1]) if r.shape[0] > own else r.shape, r.dtype) for r in more]
    out_specs = [in_vmem] * len(outs)
    scratch = [pltpu.VMEM(*h) for h in held]
    n_outs, side_in, copy_count = len(outs), (), 13
    in_specs = [anywhere] * (2 + len(more))
    if beside is not None:
        side_in, side_out, side_scratch = beside.inputs, beside.outputs, beside.scratch
        in_specs = in_specs[:2] + beside.in_specs + in_specs[2:]
        outs += side_out
        out_specs += beside.out_specs
        scratch += side_scratch
        copy_count += beside.copy_count
    return pl.pallas_call(
        functools.partial(
            scatter_kernel,
            (n_parts, across, own, width),
            finish,
            len(more),
            n_outs,
            pick,
            beside,
        ),
        out_shape=tuple(jax.ShapeDtypeStruct(*s) for s in outs),
        in_specs=in_specs,
        out_specs=tuple(out_specs),
        scratch_shapes=[
            pltpu.VMEM(act.shape, low),
            pltpu.VMEM(w.shape if pick is None else (width, act.shape[1]), low),
            pltpu.VMEM((4, own, width), low),
            pltpu.VMEM((4, own, width), f32),
            pltpu.VMEM((4, own, width), low),
            pltpu.VMEM((3, own // 2, width), low),
            pltpu.VMEM((3, own // 2, width), low),
            pltpu.VMEM((4, own, width), low),
            pltpu.VMEM((own, width), f32),
            pltpu.SemaphoreType.DMA((copy_count,)),
            pltpu.SemaphoreType.DMA((copy_count,)),
            pltpu.SemaphoreType.DMA((4 + len(held),)),
        ]
        + scratch,
        compiler_params=pltpu.CompilerParams(
            collective_id=number, has_side_effects=True, vmem_limit_bytes=60 * MIB
        ),
        cost_estimate=pl.CostEstimate(
            flops=2 * group * width * act.shape[1], bytes_accessed=40 * MIB, transcendentals=0
        ),
        name=name,
    )(act, w, *side_in, *more)


def home_kernel(rows, home, send, recv, buf, sem):
    place = Place()
    place.meet(("x", "y", "xy"))
    copies = Copies(place, send, recv)
    stay = start_home(copies, rows, home, buf, sem)
    stay.turn()
    copies.finish()
    stay.finish()


def take_home(rows, n_col):
    own, width = rows.shape
    home = (n_col * own, width // n_col)
    return pl.pallas_call(
        home_kernel,
        out_shape=jax.ShapeDtypeStruct(home, low),
        in_specs=[anywhere],
        out_specs=anywhere,
        scratch_shapes=[
            pltpu.SemaphoreType.DMA((3,)),
            pltpu.SemaphoreType.DMA((3,)),
            pltpu.VMEM((own, home[1]), low),
            pltpu.SemaphoreType.DMA((1,)),
        ],
        compiler_params=pltpu.CompilerParams(collective_id=11, has_side_effects=True),
        name="take_home",
    )(rows)


class GateReduce:
    counts = (2, 2, 3)

    def __init__(self, gates, small):
        self.n_dp = gates.shape[0]
        part = gates.shape[1:]
        self.inputs = (gates, small)
        self.outputs = ((part, low), (small.shape, f32))
        self.copy_count = 2 * (self.n_dp - 1)
        self.scratch = [
            pltpu.VMEM(gates.shape, low),
            pltpu.VMEM((self.n_dp - 1,) + part, low),
            pltpu.VMEM((self.n_dp - 1,) + small.shape, f32),
        ]

    in_specs, out_specs = [in_vmem] * 2, [in_vmem] * 2

    def turn(self):
        pass

    def names(self):
        return [f"d{d}" for d in range(1, self.n_dp)]

    def start(self, copies, gates, small, part_out, small_out, held, far, far_small):
        dp = copies.place.dp
        held[...] = gates[...]
        self.numbers = []
        for i, name in enumerate(self.names()):
            other = jnp.bitwise_xor(dp, i + 1)
            self.numbers.append(copies.start(held.at[other], far.at[i], name))
            self.numbers.append(copies.start(small, far_small.at[i], name))

    def finish(self, copies, gates, small, part_out, small_out, held, far, far_small):
        copies.land(*self.numbers)
        total = held[copies.place.dp].astype(f32)
        value = small[...]
        for i in range(self.n_dp - 1):
            total = total + far[i].astype(f32)
            value = value + far_small[i]
        part_out[...] = total.astype(low)
        small_out[...] = value


class GateGather:
    counts = (2, 2, 3)
    in_specs, out_specs = [in_vmem, anywhere], [in_vmem, anywhere]

    def __init__(self, part, grads, n_dp):
        self.n_dp = n_dp
        self.inputs = (part, grads)
        self.outputs = (((n_dp,) + part.shape, low), (grads.shape, grads.dtype))
        self.copy_count = n_dp + 2
        self.scratch = [
            pltpu.VMEM((n_dp,) + part.shape, low),
            pltpu.VMEM(grads.shape[1:], grads.dtype),
            pltpu.SemaphoreType.DMA((1,)),
        ]

    def names(self):
        return ["xy"] + [f"d{d}" for d in range(1, self.n_dp)]

    def start(self, copies, part, grads, all_out, grads_out, held, buf, sem):
        col = copies.place.col
        mine = held.at[copies.place.dp]
        self.numbers = [copies.start(part, mine, name) for name in self.names()[1:]]
        start_deal(copies, grads, grads_out)
        self.stay = Stay([(grads.at[col], grads_out.at[col])], [buf], sem)

    def turn(self):
        self.stay.turn()

    def finish(self, copies, part, grads, all_out, grads_out, held, buf, sem):
        held[copies.place.dp] = part[...]
        copies.land(*self.numbers)
        all_out[...] = held[...]
        self.stay.finish()


def square_sum(ref, row, x):
    ref[row : row + 1, :] += jnp.broadcast_to(jnp.sum(x * x, keepdims=True), (1, LANES))


def norm_scale(x):
    return lax.rsqrt(jnp.mean(x * x, axis=-1, keepdims=True) + epsilon)


def after_out_one(rows, fin, held, outs):
    x, gain = held
    resid_out, n2_out, squares = outs
    out_one = fin[rows, :]
    resid = x[rows, :].astype(f32) + out_one
    resid_out[rows, :] = resid
    n2_out[rows, :] = (resid * norm_scale(resid) * gain[1:2, :]).astype(low)
    square_sum(squares, 0, out_one)
    square_sum(squares, 1, resid)


def norm_back(d_normed, x, gain, grad_gain):
    scale = norm_scale(x)
    gained = gain * d_normed
    inner = jnp.mean(gained * x, axis=-1, keepdims=True)
    grad_gain[0:1, :] += jnp.sum(d_normed * x * scale, axis=0, keepdims=True)
    return scale * gained - x * (scale * scale * scale * inner)


def after_normed_two(rows, fin, held, outs):
    resid, upstream, gain = held
    d_resid_out, d_out, grad_gain = outs
    d_resid = upstream[rows, :].astype(f32) + norm_back(
        fin[rows, :], resid[rows, :], gain[1:2, :], grad_gain
    )
    d_resid_out[rows, :] = d_resid
    d_out[rows, :] = d_resid.astype(low)


def after_normed_one(rows, fin, held, outs):
    x, d_resid, gain = held
    back, grad_gain, squares = outs
    x_here = x[rows, :].astype(f32)
    passed = norm_back(fin[rows, :], x_here, gain[0:1, :], grad_gain)
    back[rows, :] = (d_resid[rows, :] + passed).astype(low)
    square_sum(squares, 0, x_here)


def after_out_two(rows, fin, held, outs):
    (resid,) = held
    back, squares = outs
    out_two = fin[rows, :]
    back[rows, :] = (resid[rows, :] + out_two).astype(low)
    square_sum(squares, 0, out_two)


def start_deal(copies, source, target):
    col = copies.place.col
    for name, j in (("xy", 3), ("x", 1), ("y", 2)):
        copies.start(source.at[copies.place.chip(j)], target.at[col], name)


def deal_kernel(source, target, send, recv, local, buf):
    place = Place()
    place.meet(("x", "y", "xy"))
    copies = Copies(place, send, recv)
    start_deal(copies, source, target)
    stay = Stay([(source.at[place.col], target.at[place.col])], [buf], local)
    stay.turn()
    copies.finish()
    stay.finish()


def deal_back(x, number, name):
    return pl.pallas_call(
        deal_kernel,
        out_shape=jax.ShapeDtypeStruct(x.shape, x.dtype),
        in_specs=[anywhere],
        out_specs=anywhere,
        scratch_shapes=[
            pltpu.SemaphoreType.DMA((3,)),
            pltpu.SemaphoreType.DMA((3,)),
            pltpu.SemaphoreType.DMA((1,)),
            pltpu.VMEM(x.shape[1:], x.dtype),
        ],
        compiler_params=pltpu.CompilerParams(
            collective_id=number, has_side_effects=True, vmem_limit_bytes=16 * MIB
        ),
        name=name,
    )(x)


PLANE = ("x", "y", "xy", "core", "cx", "cy", "cxy")


def sums_kernel(
    n_dp,
    gain_one,
    gain_two,
    squares_x,
    squares_one,
    squares_two,
    small,
    gates,
    rows,
    gains_out,
    squares_out,
    chans_out,
    gates_out,
    home,
    mixed,
    got,
    total,
    shared,
    ch,
    gv,
    send,
    recv,
    *bufs,
):
    place = Place()
    far = [f"d{d}" for d in range(1, n_dp)]
    place.meet(list(PLANE) + far)
    copies = Copies(place, send, recv)
    n_col, part = ch.shape[0], gains_out.shape[1]
    mixed[...] = jnp.zeros_like(mixed)
    for c in range(n_col):
        mixed[c : c + 1, :part] = gain_one[0:1, c * part : (c + 1) * part]
        mixed[n_col + c : n_col + c + 1, :part] = gain_two[0:1, c * part : (c + 1) * part]
    mixed[0:1, part:] = squares_x[0:1, :]
    mixed[1:3, part:] = squares_one[0:2, :]
    mixed[3:4, part:] = squares_two[0:1, :]
    planes = [copies.start(mixed, got.at[i], name) for i, name in enumerate(far)]
    col = place.col
    ch[col] = small[...]
    gv[col] = gates[...]
    for name in ("x", "y", "xy"):
        copies.start(ch.at[col], ch.at[col], name)
    half = n_dp // 2
    halves = (pl.ds(0, half), pl.ds(half, half))

    def gate_view(chip, h):
        return gv.at[chip, halves[h]]

    direct = {
        (name, h): copies.start(gate_view(col, h), gate_view(col, h), name)
        for h in (0, 1)
        for name in ("x", "y")
    }
    stay_home = start_home(copies, rows, home, bufs[0], bufs[1])
    stay_home.turn()
    copies.land(direct["x", 0])
    far_x = gate_view(place.chip(1), 0)
    copies.start(far_x, far_x, "y")
    copies.land(direct["y", 1])
    far_y = gate_view(place.chip(2), 1)
    copies.start(far_y, far_y, "x")
    copies.land(*planes)
    value = mixed[...]
    for i in range(n_dp - 1):
        value = value + got[i]
    total[...] = value
    others = [copies.start(total, shared.at[i], name) for i, name in enumerate(PLANE)]
    copies.land(*others)
    for i in range(len(PLANE)):
        value = value + shared[i]
    got[0] = value
    gains_out[0:1, :] = got[0, pl.ds(col, 1), :part]
    gains_out[1:2, :] = got[0, pl.ds(n_col + col, 1), :part]
    squares_out[...] = value[:, part:]
    copies.finish()
    chans_out[...] = ch[...]
    gates_out[...] = gv[...]
    stay_home.finish()


def sum_everywhere(gain_one, gain_two, squares, small, gates, rows_low, n_dp, n_col):
    count = n_dp + 22
    part = rows_low.shape[1] // n_col
    mixed = (2 * n_col, part + LANES)
    home = (n_col * rows_low.shape[0], rows_low.shape[1] // n_col)
    return pl.pallas_call(
        functools.partial(sums_kernel, n_dp),
        out_shape=(
            jax.ShapeDtypeStruct((2, part), f32),
            jax.ShapeDtypeStruct((2 * n_col, LANES), f32),
            jax.ShapeDtypeStruct((n_col,) + small.shape, f32),
            jax.ShapeDtypeStruct((n_col,) + gates.shape, low),
            jax.ShapeDtypeStruct(home, low),
        ),
        in_specs=[in_vmem] * 7 + [anywhere],
        out_specs=(in_vmem,) * 4 + (anywhere,),
        scratch_shapes=[
            pltpu.VMEM(mixed, f32),
            pltpu.VMEM((n_dp - 1,) + mixed, f32),
            pltpu.VMEM(mixed, f32),
            pltpu.VMEM((len(PLANE),) + mixed, f32),
            pltpu.VMEM((n_col,) + small.shape, f32),
            pltpu.VMEM((n_col,) + gates.shape, low),
            pltpu.SemaphoreType.DMA((count,)),
            pltpu.SemaphoreType.DMA((count,)),
            pltpu.VMEM((rows_low.shape[0], home[1]), low),
            pltpu.SemaphoreType.DMA((1,)),
        ],
        compiler_params=pltpu.CompilerParams(
            collective_id=5, has_side_effects=True, vmem_limit_bytes=24 * MIB
        ),
        name="small_sums",
    )(gain_one, gain_two, *squares, small, gates, rows_low)


def own_lanes(place, geo):
    n_col, part, bw, tiles, wide = geo
    found = [
        pl.ds(pl.multiple_of(place.col * bw + k * LANES, LANES), LANES) for k in range(bw // LANES)
    ]
    shared_tile = n_col * bw + lax.div(place.col, 2) * LANES
    return found + [pl.ds(pl.multiple_of(shared_tile, LANES), LANES)]


def one_less_exp(z):
    series = 1.0 + z / 6.0
    for n in (5.0, 4.0, 3.0, 2.0):
        series = 1.0 + z / n * series
    return jnp.where(z > -0.1, -z * series, 1.0 - jnp.exp(z))


def scan_tile(a, u, reverse):
    rows = a.shape[0]
    index = lax.broadcasted_iota(jnp.int32, a.shape, 0)
    by = 1
    while by < rows:
        turn = rows - by if reverse else by
        inside = index < rows - by if reverse else index >= by
        u = u + a * jnp.where(inside, pltpu.roll(u, turn, 0), 0.0)
        a = a * jnp.where(inside, pltpu.roll(a, turn, 0), 1.0)
        by *= 2
    return a, u


def forward_kernel(
    geo,
    x_all,
    w_rec,
    gain,
    gates,
    bias,
    soft,
    conv_w,
    conv_b,
    places,
    cotangent,
    rec_out,
    mlp_in,
    mlp_out,
    n1_out,
    x_out,
    y_out,
    pre_out,
    c_out,
    state_out,
    branch_out,
    first_out,
    g_all,
    w_out,
    w_in,
    w_down,
    xv,
    wv,
    before,
    xb,
    yv,
    prev,
    cv,
    hv,
    pv,
    bv,
    carry,
    first,
    send,
    recv,
    local,
    stay_sems,
    *bufs,
):
    place = Place()
    place.meet(AROUND + ("next", "prev"))
    copies = Copies(place, send, recv)
    n_col, part, bw, tiles, wide = geo
    chans = bw + LANES
    group, width = xv.shape
    tile = 256
    n_tiles = group // tile
    loads = [copies.keep(x_all, xv, local.at[0]), copies.keep(w_rec, wv, local.at[1])]
    halo = copies.start(x_all.at[pl.ds(group - ROWS, ROWS), :], before, "next")
    found = weight_pieces(geo, (None, rec_out, mlp_in, mlp_out), (None, w_out, w_in, w_down))
    pieces = found["rec_out"] + found["mlp_in"] + found["mlp_out"]
    dealer = Dealer(copies, 9)
    for piece in pieces[:5]:
        dealer.deal(piece)
    for load in loads:
        load.wait()
    own_block = (cotangent, block_view(cotangent, g_all, place.row, place.col, None))
    stay = Stay([own_block] + own_pieces(place, pieces), bufs, stay_sems)
    high_tile = place.col >= 2
    mine = own_lanes(place, geo)
    conv_lanes = mine[:-1] + [
        slice(n_col * bw + k * LANES, n_col * bw + (k + 1) * LANES) for k in range(bw // LANES)
    ]
    tile_cols = pl.ds(pl.multiple_of(lax.div(place.col, 2) * LANES, LANES), LANES)
    idle_tile = lax.rem(place.col, 2) == 1

    def normed(x):
        x = x.astype(f32)
        scale = lax.rsqrt(jnp.sum(x * x, axis=-1, keepdims=True) / width + epsilon)
        return (x * scale * gain[0:1, :]).astype(low)

    copies.land(halo)
    xb[0:8, :] = dot(normed(before[...]), wv[:, : 2 * bw])[ROWS - 8 :]
    carry[0:1] = jnp.zeros_like(carry[0:1])
    carry[1:2] = jnp.ones_like(carry[1:2])

    def work(i, unused):
        r0 = pl.multiple_of(i * tile, tile)
        rows = pl.ds(r0, tile)
        n1 = normed(xv[rows, :])
        xv[rows, :] = n1
        both = dot(n1, wv[...])
        xb[pl.ds(pl.multiple_of(r0 + 8, 8), tile), :] = both[:, : 2 * bw]
        yv[rows, :] = both[:, 2 * bw :]
        spot = places[rows, :]
        reach = xb[pl.ds(r0, tile + 8), :]
        conv = []
        for lane in range(2 * bw // LANES):
            at = slice(lane * LANES, (lane + 1) * LANES)
            near = reach[:, at]
            tap = conv_lanes[lane]
            total = conv_b[0:1, tap] + conv_w[0:1, tap] * near[8:]
            for t in range(1, conv_w.shape[0]):
                lagged = pltpu.roll(near, t, 0)[8:]
                total = total + jnp.where(spot >= t, conv_w[t : t + 1, tap] * lagged, 0.0)
            conv.append(total.astype(low))
        c = jnp.concatenate(conv, axis=1)
        cv[rows, :] = c
        pre = [
            jnp.concatenate(
                [dot(c[:, :bw], gates[j, place.col]), dot(c[:, bw:], gates[j, n_col, :, tile_cols])],
                axis=1,
            )
            + jnp.concatenate([bias[j : j + 1, at] for at in mine], axis=1)
            for j in range(2)
        ]
        prev[rows, :chans] = pre[0]
        prev[rows, chans:] = pre[1]
        reset = spot == 0
        for lane in range(chans // LANES):
            at = slice(lane * LANES, (lane + 1) * LANES)
            if lane * LANES < bw:
                own_c = conv[lane].astype(f32)
            else:
                own_c = jnp.where(high_tile, conv[lane + 1].astype(f32), conv[lane].astype(f32))
            log_a = -8.0 * jax.nn.sigmoid(pre[1][:, at]) * soft[0:1, mine[lane]]
            a = jnp.where(reset, 0.0, jnp.exp(log_a))
            m = jnp.where(reset, 1.0, jnp.sqrt(one_less_exp(2.0 * log_a)))
            u = own_c * jax.nn.sigmoid(pre[0][:, at]) * m
            a, u = scan_tile(a, u, False)
            h = u + a * carry[0:1, at]
            p = a * carry[1:2, at]
            hv[rows, at] = h
            pv[rows, at] = p
            carry[0:1, at] = h[tile - 1 :]
            carry[1:2, at] = p[tile - 1 :]
        return unused

    third = n_tiles // 3
    lax.fori_loop(0, third, work, 0)
    stay.turn()
    dealer.forward()
    dealer.forward()
    dealer.deal(pieces[5])
    dealer.forward()
    lax.fori_loop(third, 2 * third, work, 0)
    dealer.forward()
    dealer.deal(pieces[6])
    lax.fori_loop(2 * third, n_tiles, work, 0)
    dealer.forward()
    dealer.deal(pieces[7])
    state_in = copies.start(hv.at[pl.ds(group - 8, 8), :], first, "next")
    outs = [
        copies.keep(src, dst, local.at[10 + i])
        for i, (src, dst) in enumerate(
            ((xv, n1_out), (xb, x_out), (yv, y_out), (prev, pre_out), (cv, c_out))
        )
    ]
    copies.land(state_in)
    copies.leave(state_in)
    before_all = first[7:8, :]

    def finish(i, unused):
        rows = pl.ds(pl.multiple_of(i * tile, tile), tile)
        for lane in range(chans // LANES):
            at = slice(lane * LANES, (lane + 1) * LANES)
            state = hv[rows, at] + pv[rows, at] * before_all[:, at]
            hv[rows, at] = state
            value, _ = tanh_parts(yv[rows, at])
            b = state * value
            if lane * LANES >= bw:
                b = jnp.where(idle_tile, 0.0, b)
            bv[rows, at] = b.astype(low)
        return unused

    lax.fori_loop(0, n_tiles, finish, 0)
    outs += [
        copies.keep(hv, state_out, local.at[15]),
        copies.keep(bv, branch_out, local.at[16]),
        copies.keep(first, first_out, local.at[17]),
    ]
    dealer.forward()
    gather = block_gather(copies, cotangent, g_all)
    dealer.forward()
    dealer.forward()
    gather.pass_on()
    gather.last()
    copies.finish()
    for copy in outs:
        copy.wait()
    stay.finish()


def rec_forward(x_all, w_rec, params, places, cotangent, rec_out, mlp_in, mlp_out, geo):
    n_col, part, bw, tiles, wide = geo
    width, span, chans = part * n_col, wide * LANES, bw + LANES
    group = x_all.shape[0]

    def of(shape, dtype):
        return jax.ShapeDtypeStruct(shape, dtype)

    kept = [
        ((group, width), low),
        ((group + 8, 2 * bw), f32),
        ((group, chans), f32),
        ((group, 2 * chans), f32),
        ((group, 2 * bw), low),
        ((group, chans), f32),
        ((group, chans), low),
        ((8, chans), f32),
    ]
    dealt = [((group, width), low), ((chans, width), low), ((2, width, span), low), ((span, width), low)]
    copy_count = 1 + 6 * 8 + 12 + 1
    return pl.pallas_call(
        functools.partial(forward_kernel, geo),
        out_shape=tuple(of(*s) for s in kept + dealt),
        in_specs=[anywhere] * 2 + [in_vmem] * 7 + [anywhere] * 4,
        out_specs=(anywhere,) * 12,
        scratch_shapes=[
            pltpu.VMEM((group, width), low),
            pltpu.VMEM(w_rec.shape, low),
            pltpu.VMEM((ROWS, width), low),
            pltpu.VMEM((group + 8, 2 * bw), f32),
            pltpu.VMEM((group, chans), f32),
            pltpu.VMEM((group, 2 * chans), f32),
            pltpu.VMEM((group, 2 * bw), low),
            pltpu.VMEM((group, chans), f32),
            pltpu.VMEM((group, chans), f32),
            pltpu.VMEM((group, chans), low),
            pltpu.VMEM((8, chans), f32),
            pltpu.VMEM((8, chans), f32),
            pltpu.SemaphoreType.DMA((copy_count,)),
            pltpu.SemaphoreType.DMA((copy_count,)),
            pltpu.SemaphoreType.DMA((18,)),
            pltpu.SemaphoreType.DMA((9,)),
            pltpu.VMEM(cotangent.shape, low),
            pltpu.VMEM((bw, part), low),
            pltpu.VMEM((LANES, part), low),
        ]
        + [pltpu.VMEM((part, span // 2), low)] * 4
        + [pltpu.VMEM((span // 2, part), low)] * 2,
        compiler_params=pltpu.CompilerParams(
            collective_id=2, has_side_effects=True, vmem_limit_bytes=58 * MIB
        ),
        name="rec_forward",
    )(x_all, w_rec, *params, places, cotangent, rec_out, mlp_in, mlp_out)


def backward_kernel(
    geo,
    d_out,
    w_out,
    y_in,
    state_in,
    first_in,
    pre_in,
    c_in,
    x_in,
    gates,
    soft,
    conv_w,
    places,
    down,
    d_all,
    d_rec_out,
    gate_out,
    sums,
    down_out,
    buf,
    wv,
    dbv,
    yv,
    slv,
    hs,
    prev,
    cv,
    xb,
    ghv,
    qv,
    dpv,
    there,
    dcv,
    drv,
    gg,
    carry,
    message,
    down_buf,
    send,
    recv,
    local,
    stay_sem,
):
    place = Place()
    place.meet(["x", "y", "xy", "core", "next", "prev"])
    copies = Copies(place, send, recv)
    n_col, part, bw, tiles, wide = geo
    chans = bw + LANES
    own_rows = d_out.shape[0]
    group = yv.shape[0]
    tile = 256
    n_tiles = group // tile
    lanes = [slice(k * LANES, (k + 1) * LANES) for k in range(chans // LANES)]
    gather = slot_gather(copies, d_out, buf, own_rows)
    me = place.row * n_col + place.col
    load = copies.keep(w_out, wv, local.at[0])
    mine = copies.keep(d_out, buf.at[me], local.at[1])
    loads = [
        copies.keep(src, dst, local.at[2 + i])
        for i, (src, dst) in enumerate(
            (
                (y_in, yv),
                (state_in, hs.at[pl.ds(8, group), :]),
                (first_in, hs.at[pl.ds(0, 8), :]),
                (pre_in, prev),
                (c_in, cv),
                (x_in, xb),
            )
        )
    ]
    load.wait()
    mine.wait()
    high_tile = place.col >= 2
    idle_tile = lax.rem(place.col, 2) == 1
    mine_at = own_lanes(place, geo)
    tile_rows = pl.ds(pl.multiple_of(lax.div(place.col, 2) * LANES, LANES), LANES)

    def work(chip):
        slots = (chip, n_col + chip)
        value = dot(jnp.concatenate([buf[s] for s in slots], axis=0), wv[...], ((1,), (1,)))
        for n, s in enumerate(slots):
            rows = pl.ds(pl.multiple_of(s * own_rows, ROWS), own_rows)
            dbv[rows, :] = value[n * own_rows : (n + 1) * own_rows]

    def before_rows(k, unused):
        rows = pl.ds(pl.multiple_of(k * tile, tile), tile)
        for at in lanes:
            value, slope = tanh_parts(yv[rows, at])
            yv[rows, at] = value
            slv[rows, at] = slope
        prev[rows, :] = jax.nn.sigmoid(prev[rows, :])
        return unused

    copies.land(gather.own)
    work(place.col)
    for each in loads:
        each.wait()
    third = n_tiles // 3
    lax.fori_loop(0, third, before_rows, 0)
    x0, y0 = gather.pass_half(0)
    lax.fori_loop(third, 2 * third, before_rows, 0)
    x1, y1 = gather.pass_half(1)
    start_deal(copies, down, down_out)
    stay = Stay([(down.at[place.col], down_out.at[place.col])], [down_buf], stay_sem)
    stay.turn()
    copies.land(y0, y1)
    work(place.chip(2))
    corner = gather.last()
    copies.land(x0, x1)
    work(place.chip(1))
    lax.fori_loop(2 * third, n_tiles, before_rows, 0)
    copies.land(corner)
    out = copies.keep(buf, d_all, local.at[8])
    work(place.chip(3))

    def own(at):
        return mine_at[at.start // LANES]

    def coeffs(rows, at, spot):
        rate = prev[rows, slice(chans + at.start, chans + at.stop)]
        log_a = -8.0 * rate * soft[0:1, own(at)]
        return rate, log_a, jnp.where(spot == 0, 0.0, jnp.exp(log_a))

    carry[0:1] = jnp.zeros_like(carry[0:1])
    carry[1:2] = jnp.ones_like(carry[1:2])

    def scan_back(k, unused):
        r0 = pl.multiple_of((n_tiles - 1 - k) * tile, tile)
        rows = pl.ds(r0, tile)
        spot = places[rows, :]
        last = lax.broadcasted_iota(jnp.int32, spot.shape, 0) == tile - 1
        for at in lanes:
            d_branch = dbv[rows, at]
            if at.start >= bw:
                d_branch = jnp.where(idle_tile, 0.0, d_branch)
            value, slope = yv[rows, at], slv[rows, at]
            state = hs[pl.ds(pl.multiple_of(r0 + 8, 8), tile), at]
            d_state = d_branch * value
            drv[rows, slice(chans + at.start, chans + at.stop)] = (d_branch * state * slope).astype(low)
            _, _, a = coeffs(rows, at, spot)
            a, u = scan_tile(a, a * d_state, True)
            m = u + a * carry[0:1, at]
            q = a * carry[1:2, at]
            ghv[rows, at] = d_state + jnp.where(last, carry[0:1, at], pltpu.roll(m, tile - 1, 0))
            qv[rows, at] = jnp.where(last, carry[1:2, at], pltpu.roll(q, tile - 1, 0))
            carry[0:1, at] = m[0:1]
            carry[1:2, at] = q[0:1]
        return unused

    lax.fori_loop(0, n_tiles, scan_back, 0)
    arriving = copies.start(carry, message, "prev")
    copies.land(arriving)
    sums[...] = jnp.zeros_like(sums)
    gg[...] = jnp.zeros_like(gg)

    def through_gates(k, unused):
        r0 = pl.multiple_of(k * tile, tile)
        rows = pl.ds(r0, tile)
        spot = places[rows, :]
        reset = spot == 0
        for n, at in enumerate(lanes):
            g = ghv[rows, at] + qv[rows, at] * message[0:1, at]
            before = pltpu.roll(hs[pl.ds(r0, tile + 8), at], 1, 0)[8:]
            if at.start < bw:
                c = cv[rows, at].astype(f32)
            else:
                c = jnp.where(
                    high_tile,
                    cv[rows, slice(at.start + LANES, at.stop + LANES)].astype(f32),
                    cv[rows, at].astype(f32),
                )
            gate = prev[rows, at]
            rate, log_a, a = coeffs(rows, at, spot)
            m = jnp.where(reset, 1.0, jnp.sqrt(one_less_exp(2.0 * log_a)))
            gated = gate * m
            d_log = jnp.where(reset, 0.0, g * before * a - g * c * gate * a * a / m)
            d_pre_in = (g * c * gated * (1.0 - gate)).astype(low)
            d_pre_rate = (d_log * (-8.0 * soft[0:1, own(at)]) * rate * (1.0 - rate)).astype(low)
            dpv[rows, at] = d_pre_in
            dpv[rows, slice(chans + at.start, chans + at.stop)] = d_pre_rate
            dcv[rows, at] = g * gated
            sums[0:1, at] += jnp.sum(d_pre_in.astype(f32), axis=0, keepdims=True)
            sums[1:2, at] += jnp.sum(d_pre_rate.astype(f32), axis=0, keepdims=True)
            sums[2:3, at] += jnp.sum(d_log * (-8.0 * rate), axis=0, keepdims=True)
        return unused

    swaps = []
    for h in range(2):
        lax.fori_loop(h * n_tiles // 2, (h + 1) * n_tiles // 2, through_gates, 0)
        rows = pl.ds(h * group // 2, group // 2)
        for j in range(2):
            swaps.append(
                copies.start(
                    dpv.at[rows, pl.ds(j * chans + bw, LANES)],
                    there.at[rows, pl.ds(j * LANES, LANES)],
                    "y",
                )
            )

    def through_blocks(k, unused):
        rows = pl.ds(pl.multiple_of(k * tile, tile), tile)
        c = cv[rows, :]
        d_blk = dcv[rows, :bw]
        d_tile = dcv[rows, bw:]
        for j in range(2):
            p_blk = dpv[rows, slice(j * chans, j * chans + bw)]
            here = dpv[rows, slice(j * chans + bw, (j + 1) * chans)]
            far = there[rows, slice(j * LANES, (j + 1) * LANES)]
            five = jnp.concatenate(
                [jnp.where(high_tile, far, here), jnp.where(high_tile, here, far)], axis=1
            )
            d_blk = d_blk + dot(p_blk, gates[j, place.col], ((1,), (1,)))
            d_tile = d_tile + dot(five, gates[j, n_col, tile_rows, :], ((1,), (1,)))
            gg[j, :, :bw] += dot(c[:, :bw], p_blk, ((0,), (0,)))
            gg[j, :, bw:] += dot(c[:, bw:], here, ((0,), (0,)))
        dcv[rows, :bw] = d_blk
        dcv[rows, bw:] = d_tile
        return unused

    copies.land(swaps[0], swaps[1])
    lax.fori_loop(0, 1, through_blocks, 0)
    later = copies.start(dcv.at[pl.ds(0, 8), :], dcv.at[pl.ds(group, 8), :], "prev")
    lax.fori_loop(1, n_tiles // 2, through_blocks, 0)
    copies.land(swaps[2], swaps[3])
    lax.fori_loop(n_tiles // 2, n_tiles, through_blocks, 0)
    part_rows = gate_out.shape[1]
    for p in range(gate_out.shape[0]):
        j, first_row = divmod(p * part_rows, bw)
        gate_out[p] = gg[j, first_row : first_row + part_rows].astype(low)
    copies.land(later)

    def through_conv(k, unused):
        r0 = pl.multiple_of(k * tile, tile)
        rows = pl.ds(r0, tile)
        ext = pl.ds(r0, tile + 8)
        spot = places[ext, :]
        for at in lanes:
            reach = dcv[ext, at]
            if at.start < bw:
                x = xb[ext, at]
            else:
                x = jnp.where(high_tile, xb[ext, slice(at.start + LANES, at.stop + LANES)], xb[ext, at])
            d_c = reach[:tile]
            d_x = conv_w[0:1, own(at)] * d_c
            sums[3:4, at] += jnp.sum(d_c * x[8:], axis=0, keepdims=True)
            for t in range(1, conv_w.shape[0]):
                term = jnp.where(spot >= t, conv_w[t : t + 1, own(at)] * reach, 0.0)
                d_x = d_x + pltpu.roll(term, tile + 8 - t, 0)[:tile]
                lagged = pltpu.roll(x, t, 0)[8:]
                here = jnp.where(spot[:tile] >= t, d_c * lagged, 0.0)
                sums[3 + t : 4 + t, at] += jnp.sum(here, axis=0, keepdims=True)
            sums[7:8, at] += jnp.sum(d_c, axis=0, keepdims=True)
            drv[rows, at] = d_x.astype(low)
        return unused

    lax.fori_loop(0, n_tiles, through_conv, 0)
    for at in lanes:
        sums[2:3, at] = sums[2:3, at] * soft[1:2, own(at)]
    out_rec = copies.keep(drv, d_rec_out, local.at[9])
    copies.finish()
    out.wait()
    out_rec.wait()
    stay.finish()


def rec_backward(d_out, w_out, kept, gates, soft, conv_w, places, down, geo, n_dp):
    n_col, part, bw, tiles, wide = geo
    own, width = d_out.shape
    slots = 2 * n_col
    group, chans = slots * own, bw + LANES
    part_rows = 2 * bw // n_dp
    d_all, d_rec, gate_grads, sums, down_dealt = pl.pallas_call(
        functools.partial(backward_kernel, geo),
        out_shape=(
            jax.ShapeDtypeStruct((slots, own, width), low),
            jax.ShapeDtypeStruct((group, 2 * chans), low),
            jax.ShapeDtypeStruct((n_dp, part_rows, chans), low),
            jax.ShapeDtypeStruct((8, chans), f32),
            jax.ShapeDtypeStruct(down.shape, low),
        ),
        in_specs=[anywhere] * 8 + [in_vmem] * 4 + [anywhere],
        out_specs=(anywhere, anywhere, in_vmem, in_vmem, anywhere),
        scratch_shapes=[
            pltpu.VMEM((slots, own, width), low),
            pltpu.VMEM(w_out.shape, low),
            pltpu.VMEM((group, chans), f32),
            pltpu.VMEM((group, chans), f32),
            pltpu.VMEM((group, chans), f32),
            pltpu.VMEM((group + 8, chans), f32),
            pltpu.VMEM((group, 2 * chans), f32),
            pltpu.VMEM((group, 2 * bw), low),
            pltpu.VMEM((group + 8, 2 * bw), f32),
            pltpu.VMEM((group, chans), f32),
            pltpu.VMEM((group, chans), f32),
            pltpu.VMEM((group, 2 * chans), low),
            pltpu.VMEM((group, 2 * LANES), low),
            pltpu.VMEM((group + 8, chans), f32),
            pltpu.VMEM((group, 2 * chans), low),
            pltpu.VMEM((2, bw, chans), f32),
            pltpu.VMEM((8, chans), f32),
            pltpu.VMEM((8, chans), f32),
            pltpu.VMEM(down.shape[1:], low),
            pltpu.SemaphoreType.DMA((22,)),
            pltpu.SemaphoreType.DMA((22,)),
            pltpu.SemaphoreType.DMA((10,)),
            pltpu.SemaphoreType.DMA((1,)),
        ],
        compiler_params=pltpu.CompilerParams(
            collective_id=4, has_side_effects=True, vmem_limit_bytes=60 * MIB
        ),
        name="rec_backward",
    )(d_out, w_out, *kept, gates, soft, conv_w, places, down)
    return d_all.reshape(group, width), d_rec, gate_grads, sums, down_dealt


def outer_kernel(n_dp, first_steps, left1, right1, left2, right2, out_ref):
    def multiply(left, right):
        total = dot(left[...], right[...], ((0,), (0,)))
        rows = total.shape[0] // n_dp
        for k in range(n_dp):
            out_ref[k, 0] = total[k * rows : (k + 1) * rows].astype(out_ref.dtype)

    j = pl.program_id(1)

    @pl.when(j < first_steps)
    def _():
        multiply(left1, right1)

    @pl.when(j >= first_steps)
    def _():
        multiply(left2, right2)


def outer_one_kernel(n_dp, left, right, out_ref):
    total = dot(left[...], right[...], ((0,), (0,)))
    rows = total.shape[0] // n_dp
    for k in range(n_dp):
        out_ref[k, 0] = total[k * rows : (k + 1) * rows].astype(out_ref.dtype)


def outer(left, right, n_dp, n_col, columns, name):
    length, width = left.shape
    part = width // n_col
    count = right.shape[1]
    return pl.pallas_call(
        functools.partial(outer_one_kernel, n_dp),
        grid=(n_col, count // columns),
        out_shape=jax.ShapeDtypeStruct((n_dp, n_col, part // n_dp, count), low),
        in_specs=[
            pl.BlockSpec((length, part), lambda i, j: (0, i)),
            pl.BlockSpec((length, columns), lambda i, j: (0, j)),
        ],
        out_specs=pl.BlockSpec((n_dp, 1, part // n_dp, columns), lambda i, j: (0, i, 0, j)),
        compiler_params=pltpu.CompilerParams(vmem_limit_bytes=48 * MIB),
        cost_estimate=pl.CostEstimate(
            flops=2 * length * width * count,
            bytes_accessed=2 * (length * width + length * count + width * count),
            transcendentals=0,
        ),
        name=name,
    )(left, right)


def outer_pair(left1, right1, left2, right2, n_dp, n_col, columns, name):
    length, width = left1.shape
    part = width // n_col
    steps1, steps2 = right1.shape[1] // columns, right2.shape[1] // columns
    count = (steps1 + steps2) * columns
    left_block = pl.BlockSpec((length, part), lambda i, j: (0, i))
    return pl.pallas_call(
        functools.partial(outer_kernel, n_dp, steps1),
        grid=(n_col, steps1 + steps2),
        out_shape=jax.ShapeDtypeStruct((n_dp, n_col, part // n_dp, count), low),
        in_specs=[
            left_block,
            pl.BlockSpec((length, columns), lambda i, j: (0, jnp.minimum(j, steps1 - 1))),
            left_block,
            pl.BlockSpec((length, columns), lambda i, j: (0, jnp.maximum(j - steps1, 0))),
        ],
        out_specs=pl.BlockSpec((n_dp, 1, part // n_dp, columns), lambda i, j: (0, i, 0, j)),
        compiler_params=pltpu.CompilerParams(vmem_limit_bytes=48 * MIB),
        cost_estimate=pl.CostEstimate(
            flops=2 * length * width * count,
            bytes_accessed=2 * (2 * length * width + length * count + width * count),
            transcendentals=0,
        ),
        name=name,
    )(left1, right1, left2, right2)


def dot(a, b, dims=((1,), (0,))):
    return lax.dot_general(a, b, (dims, ((), ())), preferred_element_type=f32)


def places_of(rows, lengths):
    ends = jnp.cumsum(lengths)
    starts = ends - lengths
    inside = (rows[:, None] >= starts[None, :]) & (rows[:, None] < ends[None, :])
    places = rows - jnp.sum(jnp.where(inside, starts[None, :], 0), axis=1)
    return jnp.where(jnp.any(inside, axis=1), places, 0)


def body(
    tokens,
    cotangent,
    rec_in,
    rec_out,
    gates,
    gate_bias,
    decay,
    conv_w,
    conv_b,
    gains,
    mlp_in,
    mlp_out,
    lengths,
    order,
):
    n_dp, n_row, n_col = (lax.axis_size(a) for a in ("dp", "row", "col"))
    dp, row, col = (lax.axis_index(a) for a in ("dp", "row", "col"))
    given, part = tokens.shape
    own = given // n_col
    group = given * n_row
    width = part * n_col
    taps = conv_w.shape[0]
    blocks, bw = gates.shape[1], gates.shape[2]
    half = rec_out.shape[0]
    hidden_half = mlp_out.shape[0]
    tiles = hidden_half // LANES
    wide = -(-tiles // n_col)
    span = wide * LANES
    shared = n_col * bw
    chans = bw + LANES

    geo = (n_col, part, bw, tiles, wide)
    x_all, w_rec, gains_all = open_gather(tokens, rec_in, gains, geo)
    base = dp * group
    places = places_of(base + jnp.arange(group + 8, dtype=jnp.int32), lengths)
    places = jnp.broadcast_to(places[:, None], (group + 8, LANES))
    soft = jnp.stack([jax.nn.softplus(decay), jax.nn.sigmoid(decay)])

    n1, x_rows, y_branch, pre_both, conv_low, state, branch, first, g_all, w_out, w_in, w_down = rec_forward(
        x_all,
        w_rec,
        (gains_all, gates, gate_bias, soft, conv_w, conv_b[None, :]),
        places,
        cotangent,
        rec_out,
        mlp_in,
        mlp_out,
        geo,
    )
    rows_f, rows_b = ((own, width), f32), ((own, width), low)
    line, squares = ((8, width), f32), ((8, LANES), f32)
    resid, normed_two, squares_one = multiply_scatter(
        branch, w_out, False, 6, "out_one", after_out_one, (x_all, gains_all), (rows_f, rows_b, squares)
    )

    def spare(at):
        return spare_window(at, tiles, n_col, wide)

    n2, hidden, d_glu = glu(normed_two, w_in, w_down, g_all, spare)
    g_down = outer(g_all, hidden, n_dp, n_col, span, "outer_down")
    d_glu, hidden, g_down = lax.optimization_barrier((d_glu, hidden, g_down))
    sum_down = lax.psum_scatter(g_down, "dp", scatter_dimension=0)
    g_in = outer(n2, d_glu, n_dp, n_col, span, "outer_in")
    d_glu, g_in = lax.optimization_barrier((d_glu, g_in))
    d_resid, d_out, gain_two = multiply_scatter(
        d_glu,
        w_in,
        True,
        7,
        "d_normed_two",
        after_normed_two,
        (resid, g_all, gains_all),
        (rows_f, rows_b, line),
    )
    g_in, sum_down, d_out = lax.optimization_barrier((g_in, sum_down, d_out))
    sum_in = lax.psum_scatter(g_in, "dp", scatter_dimension=0)

    d_out_all, d_rec, gate_grads, small, down = rec_backward(
        d_out,
        w_out,
        (y_branch, state, first, pre_both, conv_low, x_rows),
        gates,
        soft,
        conv_w,
        places,
        sum_down,
        geo,
        n_dp,
    )

    def pick(at):
        tile = pl.multiple_of(bw + lax.div(at, 2) * LANES, LANES)
        return ((0, 0, bw), (tile, bw, LANES), (2 * bw, chans, chans))

    g_rec = outer_pair(n1, d_rec, d_out_all, branch, n_dp, n_col, chans, "outer_rec")
    g_rec, d_rec = lax.optimization_barrier((g_rec, d_rec))
    grad_rows, gain_one, squares_x, gate_part, small = multiply_scatter(
        d_rec,
        w_rec,
        True,
        9,
        "d_normed_one",
        after_normed_one,
        (x_all, d_resid, gains_all),
        (rows_b, line, squares),
        pick=pick,
        beside=GateReduce(gate_grads, small),
    )
    grad_input = take_home(grad_rows, n_col)
    g_rec, sum_in, grad_input, hidden = lax.optimization_barrier((g_rec, sum_in, grad_input, hidden))
    sum_rec = lax.psum_scatter(g_rec, "dp", scatter_dimension=0)
    result_rows, squares_two, gate_planes, into = multiply_scatter(
        hidden,
        w_down,
        False,
        8,
        "out_two",
        after_out_two,
        (resid,),
        (rows_b, squares),
        beside=GateGather(gate_part, sum_in, n_dp),
    )

    def windows(got, first):
        return [
            got[c][..., first + (LANES if c > n_col - 1 - (wide * n_col - tiles) else 0) : first + span]
            for c in range(n_col)
        ]

    def channels_of(got, first):
        return [got[c][..., first : first + bw] for c in range(n_col)] + [
            got[c][..., first + bw : first + chans] for c in range(0, n_col, 2)
        ]

    grad_gains, square_sums, chan_sums, gate_parts, result = sum_everywhere(
        gain_one,
        gain_two,
        (squares_x, squares_one, squares_two),
        small,
        gate_planes,
        result_rows,
        n_dp,
        n_col,
    )
    grad_mlp_in = jnp.stack(
        [jnp.concatenate(windows(into[..., j * span : (j + 1) * span], 0), axis=-1) for j in range(2)]
    ).astype(f32)
    grad_mlp_out = jnp.concatenate(windows(down, 0), axis=-1).astype(f32).T
    sum_rec, grad_mlp_in, grad_mlp_out = lax.optimization_barrier((sum_rec, grad_mlp_in, grad_mlp_out))
    recs = deal_back(sum_rec, 10, "deal_rec")
    grad_rec_in = jnp.stack(
        [jnp.concatenate(channels_of(recs, j * chans), axis=-1) for j in range(2)]
    ).astype(f32)
    grad_rec_out = jnp.concatenate(channels_of(recs, 2 * chans), axis=-1).astype(f32).T
    mine = jnp.concatenate(channels_of(chan_sums, 0), axis=-1)
    stats = jnp.sqrt(square_sums[:4, 0] / (n_dp * group * width))
    gate_parts = gate_parts.reshape(n_col, 2, bw, chans).astype(f32)
    five = jnp.concatenate([gate_parts[c, :, :, bw:] for c in range(0, n_col, 2)], axis=-1)
    grad_gates = jnp.stack([gate_parts[c, :, :, :bw] for c in range(n_col)] + [five], axis=1)
    return (
        result,
        grad_input,
        grad_rec_in,
        grad_rec_out,
        grad_gates,
        mine[0:2],
        mine[2],
        mine[3 : 3 + taps],
        mine[3 + taps],
        grad_gains,
        grad_mlp_in,
        grad_mlp_out,
        stats,
    )


def solution(mesh):
    placed = (
        P(("dp", "row"), "col"),
        P(("dp", "row"), "col"),
        P(None, "col", "row"),
        P("row", "col"),
        P(None, "row", None, None),
        P(None, "row"),
        P("row"),
        P(None, "row"),
        P("row"),
        P(None, "col"),
        P(None, "col", "row"),
        P("row", "col"),
        P(),
        P(),
    )
    return jax.shard_map(
        body,
        mesh=mesh,
        in_specs=placed,
        out_specs=(
            P(("dp", "row"), "col"),
            P(("dp", "row"), "col"),
            P(None, ("col", "dp"), "row"),
            P("row", ("col", "dp")),
            P(None, "row", None, None),
            P(None, "row"),
            P("row"),
            P(None, "row"),
            P("row"),
            P(None, "col"),
            P(None, ("col", "dp"), "row"),
            P("row", ("col", "dp")),
            P(),
        ),
        check_vma=False,
    )
```
